32 devices in a mesh: vocab: 32 (over z, y, x, core).
Axes of the slice: x: 2, y: 2, z: 4, core: 2. Of those that a mesh axis runs over, the one named last changes fastest.
Arguments:
- hidden_states: bfloat16 [512, 5120], P('vocab'), may hold values from -8 to 8
- head_weight: bfloat16 [5120, 32768], P(None, 'vocab'), may hold values from -0.25 to 0.25
- teacher_logits: bfloat16 [4, 64, 128, 128], P(None, None, 'vocab'), may hold values from -15 to 260
- block_lists: int32 [4, 64], replicated, may hold values from 0 to 255, as said below
- row_reader: int32 [4, 128], replicated, may hold values from 0 to 127, each once within a row
- tail_mass: float32 [512], replicated, may hold values from 0.05 to 0.5
- token_weight: float32 [512], replicated, may hold values from 1 to 8
Outputs:
- token_loss: float32 [512], P('vocab')
- grad_head: bfloat16 [5120, 32768], P(None, 'vocab')
- grad_hidden: bfloat16 [512, 5120], P('vocab')
The draws below stay inside these ranges and needn't reach their ends.
Inputs may be any that keep to these rules, and one draw needn't show every extreme that they name: `block_lists`: for each token block the 64 listed vocabulary blocks are distinct; at most 4 of them lie in any slab of 8 consecutive blocks starting at a multiple of 8, and in every token block some slab holds exactly 4. `row_reader`: each row is a permutation.
All inputs are finite; a program needn't handle non-finite values.
Results may differ from the reference program's by a relative error of at most 0.0048.
Values may be sent and summed in bfloat16 or wider, within the bound.
No kernel may reach another device: no remote copies, remote signals or barrier semaphores. Data moves between devices by JAX's collectives and lax.ppermute only.
A program may use at most 128 MiB of HBM per device.

```python
import math
import jax
import jax.numpy as jnp
from jax import lax

D = 5120
BLK = 128
VB_DEV = 8
VOCAB = 32768
NVB = 256
TOKEN_BLOCKS = 4
TOKENS = 512
K = 64
MOST = 4


def head_matrix(key):
    values = jax.random.normal(jax.random.fold_in(key, 101), (D, VOCAB), jnp.float32)
    return jnp.clip(values * 0.042, -0.25, 0.25)


def draw_head_weight(key, part):
    return head_matrix(key).astype(jnp.bfloat16)


def draw_hidden_states(key, part):
    values = jax.random.normal(jax.random.fold_in(key, 5), (TOKENS, D), jnp.float32)
    return jnp.clip(values, -6.0, 6.0).astype(jnp.bfloat16)


def draw_teacher_logits(key, part):
    shape = (TOKEN_BLOCKS, K, BLK, BLK)
    values = jax.random.normal(jax.random.fold_in(key, 21), shape, jnp.float32) * 3.0
    return jnp.clip(values, -15.0, 15.0).astype(jnp.bfloat16)


def draw_block_lists(key, part):
    owners = NVB // VB_DEV
    slot_positions = owners * MOST
    single_step = 262144
    preference_boost = jax.random.randint(jax.random.fold_in(key, 31), (owners,), 0, 3)
    random_jitter = jax.random.randint(jax.random.fold_in(key, 33), (TOKEN_BLOCKS, owners, MOST), 0, 2 * single_step)
    required_pick = jax.random.randint(jax.random.fold_in(key, 35), (TOKEN_BLOCKS, 1, 1), 0, owners)
    owner_sequence = jnp.arange(owners, dtype=jnp.int32)[None, :, None]
    extra_reward = jnp.where(owner_sequence == required_pick, 5 * single_step, preference_boost[None, :, None] * single_step)
    ranking_value = (extra_reward + random_jitter).reshape(TOKEN_BLOCKS, slot_positions) * slot_positions + jnp.arange(slot_positions, dtype=jnp.int32)[None, :]
    chosen = lax.top_k(ranking_value, K)[1].astype(jnp.int32)
    owner_pick = chosen // MOST
    slot_pick = chosen % MOST
    order_keys = jax.random.randint(jax.random.fold_in(key, 37), (TOKEN_BLOCKS, owners, VB_DEV), 0, 1048576) * VB_DEV + jnp.arange(VB_DEV, dtype=jnp.int32)[None, None, :]
    local_order = jnp.argsort(order_keys, axis=2).astype(jnp.int32)
    placed = jax.vmap(lambda table, owner_row, slot_row: table[owner_row, slot_row])(local_order, owner_pick, slot_pick)
    return (owner_pick * VB_DEV + placed).astype(jnp.int32)


def setup_inputs(seed: int = 0) -> dict:
    arg_keys = jax.random.split(jax.random.key(seed), 8)
    hidden_states = draw_hidden_states(jax.random.fold_in(arg_keys[7], 71), 0)
    head_weight = draw_head_weight(jax.random.fold_in(arg_keys[7], 71), 0)
    teacher_logits = draw_teacher_logits(jax.random.fold_in(arg_keys[7], 71), 0)
    block_lists = draw_block_lists(jax.random.fold_in(arg_keys[7], 71), 0)
    row_reader = jax.vmap(lambda own: jax.random.permutation(own, BLK))(jax.random.split(arg_keys[4], TOKEN_BLOCKS)).reshape((TOKEN_BLOCKS, BLK)).astype(jnp.int32)
    tail_mass = jnp.clip(jax.random.uniform(arg_keys[5], (TOKENS,), jnp.float32, 0.05, 0.5), 0.05, 0.5)
    token_weight = jnp.clip(jnp.exp(jax.random.uniform(arg_keys[6], (TOKENS,), jnp.float32, math.log(1.0), math.log(8.0))), 1.0, 8.0)
    return dict(hidden_states=hidden_states, head_weight=head_weight, teacher_logits=teacher_logits, block_lists=block_lists, row_reader=row_reader, tail_mass=tail_mass, token_weight=token_weight)


def reference(hidden_states, head_weight, teacher_logits, block_lists, row_reader, tail_mass, token_weight):
    logits = jnp.dot(hidden_states, head_weight, preferred_element_type=jnp.float32)
    vocab_blocks = VOCAB // BLK
    inverse = jnp.argsort(row_reader, axis=1).astype(jnp.int32)
    token_rows = jax.vmap(lambda stored, order: stored[:, order, :])(teacher_logits, inverse)
    block_rows = jnp.arange(TOKEN_BLOCKS, dtype=jnp.int32)[:, None]
    teacher_dense = jnp.zeros((TOKEN_BLOCKS, vocab_blocks, BLK, BLK), jnp.float32)
    teacher_dense = teacher_dense.at[block_rows, block_lists].set(token_rows.astype(jnp.float32))
    listed = jnp.zeros((TOKEN_BLOCKS, vocab_blocks), jnp.float32).at[block_rows, block_lists].set(1.0)
    teacher_values = teacher_dense.transpose(0, 2, 1, 3).reshape(TOKEN_BLOCKS, BLK, VOCAB)
    listed_mask = (jnp.repeat(listed, BLK, axis=1) > 0.5)[:, None, :]
    scores = logits.reshape(TOKEN_BLOCKS, BLK, VOCAB)
    student_max = jnp.max(scores, axis=-1, keepdims=True)
    log_norm = student_max + jnp.log(jnp.sum(jnp.exp(scores - student_max), axis=-1, keepdims=True))
    teacher_max = jnp.max(jnp.where(listed_mask, teacher_values, -jnp.inf), axis=-1, keepdims=True)
    teacher_sum = jnp.sum(jnp.where(listed_mask, jnp.exp(teacher_values - teacher_max), 0.0), axis=-1, keepdims=True)
    tail_share = tail_mass.reshape(TOKEN_BLOCKS, BLK, 1)
    unlisted = VOCAB - BLK * K
    log_teacher = jnp.where(listed_mask, jnp.log(1.0 - tail_share) + teacher_values - teacher_max - jnp.log(teacher_sum), jnp.log(tail_share / unlisted))
    teacher_prob = jnp.exp(log_teacher)
    token_loss = jnp.sum(teacher_prob * (log_teacher - scores + log_norm), axis=-1).reshape(TOKENS)
    student_prob = jnp.exp(scores - log_norm)
    weight = token_weight.reshape(TOKEN_BLOCKS, BLK, 1)
    grad_logits = (weight * (student_prob - teacher_prob)).astype(jnp.bfloat16).reshape(TOKENS, VOCAB)
    grad_head = lax.dot_general(hidden_states, grad_logits, (((0,), (0,)), ((), ())), preferred_element_type=jnp.float32).astype(jnp.bfloat16)
    grad_hidden = lax.dot_general(grad_logits, head_weight, (((1,), (1,)), ((), ())), preferred_element_type=jnp.float32).astype(jnp.bfloat16)
    return token_loss, grad_head, grad_hidden
```

```python
import jax
import jax.numpy as jnp
from jax import lax
from jax.experimental import pallas as pl
from jax.experimental.pallas import tpu as pltpu
from jax.sharding import PartitionSpec as P


def row_parts(scores, teacher_slab, listed_mask, student_exp, teacher_exp):
    return (
        jnp.sum(student_exp, axis=(2, 3)),
        jnp.sum(teacher_exp, axis=(2, 3)),
        jnp.sum(teacher_exp * scores, axis=(2, 3)),
        jnp.sum(teacher_exp * teacher_slab, axis=(2, 3)),
        jnp.sum(scores, axis=(2, 3)),
        jnp.sum(jnp.where(listed_mask, scores, 0.0), axis=(2, 3)),
    )


def plain_plan(
    hidden_states, head_weight, teacher_logits, block_lists, row_reader, tail_mass, token_weight
):
    blocks, listed_count, stored_rows, block_side = teacher_logits.shape
    slab_width = head_weight.shape[1]
    slab_blocks = slab_width // block_side
    devices = lax.axis_size("vocab")
    rank_self = lax.axis_index("vocab")
    tokens = blocks * block_side
    shard_rows = hidden_states.shape[0]
    gathered = lax.all_gather(hidden_states, "vocab", axis=0, tiled=True)
    logits = jnp.dot(gathered, head_weight, preferred_element_type=jnp.float32)
    owner_dev = block_lists // slab_blocks
    owned_here = owner_dev == rank_self
    within = block_lists - rank_self * slab_blocks
    token_iota = lax.broadcasted_iota(jnp.int32, (1, block_side, block_side), 1)
    token_map = (row_reader[:, None, :] == token_iota).astype(jnp.bfloat16)
    place_iota = lax.broadcasted_iota(jnp.int32, (1, slab_blocks, 1), 1)
    block_iota = lax.broadcasted_iota(jnp.int32, (1, devices * slab_blocks, 1), 1)
    picker = (block_lists[:, None, :] == block_iota).astype(jnp.bfloat16)
    outgoing = jnp.einsum(
        "tnk,tkrc->tnrc", picker, teacher_logits, preferred_element_type=jnp.float32
    ).astype(jnp.bfloat16)
    incoming = lax.all_to_all(outgoing, "vocab", split_axis=1, concat_axis=2, tiled=True)
    teacher_slab = jnp.einsum(
        "tpj,tbjc->tpbc", token_map, incoming, preferred_element_type=jnp.float32
    )
    listed = jnp.sum(
        ((within[:, None, :] == place_iota) & owned_here[:, None, :]).astype(jnp.int32), axis=2
    )
    scores = logits.reshape(blocks, block_side, slab_blocks, block_side)
    listed_mask = (listed > 0)[:, None, :, None]
    local_smax = jnp.max(scores, axis=(2, 3))
    local_tmax = jnp.max(jnp.where(listed_mask, teacher_slab, -1e30), axis=(2, 3))
    student_max, teacher_max = lax.pmax((local_smax, local_tmax), "vocab")
    student_exp = jnp.exp(scores - student_max[:, :, None, None])
    teacher_exp = jnp.exp(
        jnp.where(listed_mask, teacher_slab - teacher_max[:, :, None, None], -jnp.inf)
    )
    parts = row_parts(scores, teacher_slab, listed_mask, student_exp, teacher_exp)
    student_sum, teacher_sum, cross_sum, self_sum, logit_total, listed_total = lax.psum(
        (parts[0], parts[1], parts[2], parts[3], parts[4], parts[5]), "vocab"
    )
    tail_share = tail_mass.reshape(blocks, block_side)
    unlisted = float(devices * slab_width - block_side * listed_count)
    kept_mass = 1.0 - tail_share
    log_norm = student_max + jnp.log(student_sum)
    row_loss = (
        kept_mass * (jnp.log(kept_mass) - teacher_max - jnp.log(teacher_sum))
        + kept_mass * self_sum / teacher_sum
        + tail_share * jnp.log(tail_share / unlisted)
        - kept_mass * cross_sum / teacher_sum
        - tail_share / unlisted * (logit_total - listed_total)
        + log_norm
    )
    token_loss = lax.dynamic_slice_in_dim(
        row_loss.reshape(tokens), rank_self * shard_rows, shard_rows, 0
    )
    student_prob = student_exp / student_sum[:, :, None, None]
    teacher_prob = jnp.where(
        listed_mask,
        (kept_mass / teacher_sum)[:, :, None, None] * teacher_exp,
        (tail_share / unlisted)[:, :, None, None],
    )
    weight = token_weight.reshape(blocks, block_side)[:, :, None, None]
    grad_logits = (
        (weight * (student_prob - teacher_prob)).astype(jnp.bfloat16).reshape(tokens, slab_width)
    )
    grad_head = lax.dot_general(
        gathered, grad_logits, (((0,), (0,)), ((), ())), preferred_element_type=jnp.float32
    ).astype(jnp.bfloat16)
    grad_hidden = lax.psum_scatter(
        lax.dot_general(
            grad_logits, head_weight, (((1,), (1,)), ((), ())), preferred_element_type=jnp.float32
        ),
        "vocab",
        scatter_dimension=0,
        tiled=True,
    ).astype(jnp.bfloat16)
    return (token_loss, grad_head, grad_hidden)


CORES = 2
CHIPS = 4
GROUP = CORES * CHIPS
SLOTS = 4
VMEM_LIMIT = 48 * 1024 * 1024


def kernel_params():
    return pltpu.CompilerParams(vmem_limit_bytes=VMEM_LIMIT)


def vmem_spec():
    return pl.BlockSpec(memory_space=pltpu.VMEM)


def smem_spec():
    return pl.BlockSpec(memory_space=pltpu.SMEM)


def shift(x, distance):
    n = lax.axis_size("vocab")
    return lax.ppermute(x, "vocab", [(i, i ^ distance) for i in range(n)])


def tile_of(size):
    return 512 if size % 512 == 0 else 128


def token_places(place, rows, side):
    row = lax.broadcasted_iota(jnp.int32, (side, 1), 0)
    group = row // rows
    chip = (group % CHIPS) ^ place[1]
    core = (group // CHIPS) ^ place[0]
    return (chip * CORES + core) * rows + row % rows


def pick_column(match, values):
    return jnp.sum(jnp.where(match, values, 0.0), axis=1, keepdims=True)


def teacher_kernel(
    unlisted, rows, pos_ref, place_ref, blocks_ref, stat_ref, reader_ref, tail_ref, prob_ref, entropy_ref
):
    layers, slots, side, _ = blocks_ref.shape
    pos = [pos_ref[i] for i in range(3)]
    lane = lax.broadcasted_iota(jnp.int32, (1, side), 1)
    where_token = token_places(pos, rows, side)
    for k in range(layers):
        block = pos[2] ^ k
        match = reader_ref[block] == where_token
        onehot = jnp.where(match, 1.0, 0.0).astype(jnp.bfloat16)
        normaliser = pick_column(match, stat_ref[0, block])
        tail = pick_column(lane == where_token, tail_ref[block])
        kept = 1.0 - tail
        rest = tail / unlisted
        span = pl.ds(k * side, side)
        prob_ref[span, :] = jnp.broadcast_to(rest, (side, prob_ref.shape[1]))
        for s in range(slots):
            place = place_ref[block, s]
            values = jnp.dot(onehot, blocks_ref[block, s], preferred_element_type=jnp.float32)
            prob = kept * jnp.exp(values - normaliser)

            @pl.when(place >= 0)
            def _():
                prob_ref[span, pl.ds(pl.multiple_of(place * side, side), side)] = prob

        if k == 0:
            mean = pick_column(match, stat_ref[1, block])
            entropy = kept * (jnp.log(kept) - normaliser + mean) + tail * jnp.log(rest)
            entropy_ref[...] = jnp.broadcast_to(entropy[:rows], entropy_ref.shape)


def assemble(pieces, rows, out_ref):
    layers = pieces[0].shape[0] // rows
    for k in range(layers):
        for p, piece in enumerate(pieces):
            out_ref[pl.ds((k * GROUP + p) * rows, rows), :] = piece[pl.ds(k * rows, rows), :]


def logits_kernel(rows, *refs):
    pieces = refs[:GROUP]
    w_ref, prob_ref, logits_ref, stat_ref, hidden = refs[GROUP:]
    step = pl.program_id(0)
    assemble(pieces, rows, hidden)
    part = jnp.dot(hidden[...], w_ref[...], preferred_element_type=jnp.float32)

    @pl.when(step == 0)
    def _():
        logits_ref[...] = part

    @pl.when(step > 0)
    def _():
        logits_ref[...] += part

    @pl.when(step == pl.num_programs(0) - 1)
    def _():
        logits = logits_ref[...]
        top = jnp.max(logits, axis=1, keepdims=True)
        norm = top + jnp.log(jnp.sum(jnp.exp(logits - top), axis=1, keepdims=True))
        cross = jnp.sum(prob_ref[...] * logits, axis=1, keepdims=True)
        lane = lax.broadcasted_iota(jnp.int32, (1, 128), 1)
        both = jnp.where(lane == 0, norm, jnp.where(lane == 1, cross, 0.0))
        stat_ref[...] = both.T[:2]


def grad_kernel(
    rows, pos_ref, own_ref, sib_ref, logits_ref, prob_ref, weight_ref, entropy_ref, grad_ref, loss_ref
):
    tokens = logits_ref.shape[0]
    devices = tokens // rows
    layers, _, side = weight_ref.shape
    layer_bits = (devices // GROUP).bit_length() - 1
    pos = [pos_ref[i] for i in range(3)]
    lane = lax.broadcasted_iota(jnp.int32, (1, 128), 1)
    stat = jnp.concatenate(
        [own_ref[...], sib_ref[...], jnp.zeros((128 - 2 * devices, tokens), jnp.float32)], axis=0
    ).T
    pairs = [(1 + i, 3 + i) for i in range(layer_bits)]
    pairs += [(1 + layer_bits, 0), (2 + layer_bits, 1), (3 + layer_bits, 2)]
    for lane_bit, block_bit in pairs:
        halves = stat.reshape(devices >> (block_bit + 1), 2, rows << block_bit, 128)
        swapped = jnp.stack([halves[:, 1], halves[:, 0]], axis=1).reshape(tokens, 128)
        stat = jnp.where((lane >> lane_bit) & 1 == 1, swapped, stat)
    used = lane < 2 * devices
    is_norm = used & (lane % 2 == 0)
    top = jnp.max(jnp.where(is_norm, stat, -jnp.inf), axis=1, keepdims=True)
    total = jnp.sum(jnp.where(is_norm, jnp.exp(stat - top), 0.0), axis=1, keepdims=True)
    log_norm = top + jnp.log(total)
    cross = jnp.sum(jnp.where(used & (lane % 2 == 1), stat, 0.0), axis=1, keepdims=True)
    loss_ref[...] = entropy_ref[...] - cross[:rows] + log_norm[:rows]
    where_token = token_places(pos, rows, side)
    for k in range(layers):
        span = pl.ds(k * side, side)
        weight = pick_column(lane == where_token, weight_ref[pos[2] ^ k])
        student = jnp.exp(logits_ref[span, :] - log_norm[k * side : (k + 1) * side])
        grad_ref[span, :] = (weight * (student - prob_ref[span, :])).astype(grad_ref.dtype)


def partial_kernel(rows, core_ref, grad_ref, sib_ref, w_ref, sib_w_ref, *refs):
    outs, swapped = refs[:CHIPS], refs[CHIPS]
    layers = outs[0].shape[0]
    half = CHIPS * rows

    @pl.when(pl.program_id(0) == 0)
    def _():
        for k in range(layers):
            for core in range(CORES):
                swapped[pl.ds((k * CORES + core) * half, half), :] = sib_ref[
                    pl.ds((k * CORES + 1 - core) * half, half), :
                ]

    contract = (((1,), (1,)), ((), ()))
    total = lax.dot_general(
        grad_ref[...], w_ref[...], contract, preferred_element_type=jnp.float32
    ) + lax.dot_general(
        swapped[...], sib_w_ref[...], contract, preferred_element_type=jnp.float32
    )
    for j, out in enumerate(outs):
        for k in range(layers):
            for core in range(CORES):
                start = (k * GROUP + core * CHIPS + j) * rows
                out[k, core] = total[start : start + rows].astype(out.dtype)


def head_kernel(rows, *refs):
    pieces = refs[:GROUP]
    grad_ref, out_ref, hidden = refs[GROUP:]
    assemble(pieces, rows, hidden)
    out_ref[...] = lax.dot_general(
        hidden[...], grad_ref[...], (((0,), (0,)), ((), ())), preferred_element_type=jnp.float32
    ).astype(out_ref.dtype)


def chip_sum_kernel(own_ref, *refs):
    arrived, outs = refs[: CHIPS - 1], refs[CHIPS - 1 :]
    for k, out in enumerate(outs):
        total = own_ref[k]
        for part in arrived:
            total = total + part[k].astype(jnp.float32)
        out[...] = total.astype(out.dtype)


def layer_sum_kernel(own_ref, *refs):
    arrived, (mine, theirs) = refs[:-2], refs[-2:]
    total = own_ref[...]
    for part in arrived:
        total = total + part[...].astype(jnp.float32)
    mine[...] = total[0].astype(mine.dtype)
    theirs[...] = total[1].astype(theirs.dtype)


def split_three(x):
    high = lax.reduce_precision(x, 8, 7)
    middle = lax.reduce_precision(x - high, 8, 7)
    low = x - high - middle
    return jnp.stack([high, middle, low]).astype(jnp.bfloat16)


def send_teacher(teacher_logits, block_lists, places):
    blocks, listed_count, stored, side = teacher_logits.shape
    n = lax.axis_size("vocab")
    rank = lax.axis_index("vocab")
    owner = block_lists // places
    earlier = jnp.tril(jnp.ones((listed_count, listed_count), jnp.bool_), -1)
    slot = jnp.sum((owner[:, :, None] == owner[:, None, :]) & earlier, axis=2, dtype=jnp.int32)
    code = owner * SLOTS + slot
    picker = (code[:, None, :] == jnp.arange(n * SLOTS, dtype=jnp.int32)[None, :, None]).astype(jnp.bfloat16)
    packed = jnp.einsum(
        "tsk,tkrc->tsrc", picker, teacher_logits, preferred_element_type=jnp.float32
    ).astype(jnp.bfloat16)
    packed = packed.reshape(blocks, n, SLOTS * stored, side).transpose(1, 0, 2, 3)
    values = teacher_logits.astype(jnp.float32)
    top = jnp.max(values, axis=(1, 3))
    powers = jnp.exp(values - top[:, None, :, None])
    total = jnp.sum(powers, axis=(1, 3))
    mean = jnp.sum(powers * values, axis=(1, 3)) / total
    stat = split_three(jnp.stack([top + jnp.log(total), mean])).reshape(-1)
    stat = jnp.pad(stat, (0, side - stat.shape[0]))
    payload = jnp.concatenate(
        [packed.reshape(n, -1, side), jnp.broadcast_to(stat, (n, 1, side))], axis=1
    )
    arrived = lax.all_to_all(payload, "vocab", split_axis=0, concat_axis=0, tiled=True)
    arrived_blocks = (
        arrived[:, :-1]
        .reshape(n, blocks, SLOTS, stored, side)
        .transpose(1, 2, 0, 3, 4)
        .reshape(blocks, SLOTS, n * stored, side)
    )
    arrived_stat = (
        arrived[:, -1, : 6 * blocks * stored]
        .astype(jnp.float32)
        .reshape(n, 3, 2, blocks, stored)
        .sum(axis=1)
        .transpose(1, 2, 0, 3)
        .reshape(2, blocks, 1, n * stored)
    )
    mine = code[:, None, :] == rank * SLOTS + jnp.arange(SLOTS, dtype=jnp.int32)[None, :, None]
    place = jnp.sum(jnp.where(mine, (block_lists % places + 1)[:, None, :], 0), axis=2) - 1
    return arrived_blocks, arrived_stat, place.astype(jnp.int32)


def levels_plan(
    hidden_states, head_weight, teacher_logits, block_lists, row_reader, tail_mass, token_weight
):
    blocks, listed_count, stored, side = teacher_logits.shape
    rows, depth = hidden_states.shape
    slab = head_weight.shape[1]
    n = lax.axis_size("vocab")
    rank = lax.axis_index("vocab")
    tokens = n * rows
    layers = n // GROUP
    half = depth // CORES
    bf16, f32 = jnp.bfloat16, jnp.float32
    core, chip, layer = rank % CORES, (rank // CORES) % CHIPS, rank // GROUP
    pos = jnp.stack([core, chip, layer]).astype(jnp.int32)
    unlisted = float(n * slab - side * listed_count)

    column = [hidden_states] + [shift(hidden_states, k * GROUP) for k in range(1, layers)]
    column = jnp.concatenate(column, axis=0)
    pieces = [column] + [shift(column, j * CORES) for j in range(1, CHIPS)]
    pieces = pieces + [shift(piece, 1) for piece in pieces]

    arrived_blocks, arrived_stat, place = send_teacher(teacher_logits, block_lists, slab // side)
    sib_w = shift(lax.dynamic_slice(head_weight, ((1 - core) * half, 0), (half, slab)), 1)

    prob, entropy = pl.pallas_call(
        lambda *refs: teacher_kernel(unlisted, rows, *refs),
        out_shape=(
            jax.ShapeDtypeStruct((tokens, slab), f32),
            jax.ShapeDtypeStruct((rows, side), f32),
        ),
        in_specs=[smem_spec(), smem_spec()] + [vmem_spec()] * 4,
        out_specs=(vmem_spec(), vmem_spec()),
        compiler_params=kernel_params(),
        cost_estimate=pl.CostEstimate(
            flops=2 * tokens * side * side * SLOTS, bytes_accessed=4 * tokens * slab, transcendentals=0
        ),
        name="teacher_prob",
    )(
        pos,
        place,
        arrived_blocks,
        arrived_stat,
        row_reader.reshape(blocks, 1, side),
        tail_mass.reshape(blocks, 1, side),
    )

    tile = tile_of(depth)
    piece_specs = [pl.BlockSpec((layers * rows, tile), lambda t: (0, t)) for _ in range(GROUP)]
    whole = lambda t: (0, 0)
    logits, stat = pl.pallas_call(
        lambda *refs: logits_kernel(rows, *refs),
        grid=(depth // tile,),
        out_shape=(
            jax.ShapeDtypeStruct((tokens, slab), f32),
            jax.ShapeDtypeStruct((2, tokens), f32),
        ),
        in_specs=piece_specs
        + [pl.BlockSpec((tile, slab), lambda t: (t, 0)), pl.BlockSpec((tokens, slab), whole)],
        out_specs=(pl.BlockSpec((tokens, slab), whole), pl.BlockSpec((2, tokens), whole)),
        scratch_shapes=[pltpu.VMEM((tokens, tile), bf16)],
        compiler_params=kernel_params(),
        cost_estimate=pl.CostEstimate(
            flops=2 * tokens * depth * slab,
            bytes_accessed=2 * depth * (slab + tokens) + 4 * tokens * slab,
            transcendentals=tokens * slab,
        ),
        name="logits",
    )(*pieces, head_weight, prob)

    stat = jnp.concatenate([stat] + [shift(stat, k * GROUP) for k in range(1, layers)], axis=0)
    stat = jnp.concatenate([stat] + [shift(stat, j * CORES) for j in range(1, CHIPS)], axis=0)
    sib_stat = shift(stat, 1)

    grad, loss = pl.pallas_call(
        lambda *refs: grad_kernel(rows, *refs),
        out_shape=(
            jax.ShapeDtypeStruct((tokens, slab), bf16),
            jax.ShapeDtypeStruct((rows, side), f32),
        ),
        in_specs=[smem_spec()] + [vmem_spec()] * 6,
        out_specs=(vmem_spec(), vmem_spec()),
        compiler_params=kernel_params(),
        cost_estimate=pl.CostEstimate(
            flops=4 * tokens * slab, bytes_accessed=10 * tokens * slab, transcendentals=tokens * slab
        ),
        name="grad_logits",
    )(pos, stat, sib_stat, logits, prob, token_weight.reshape(blocks, 1, side), entropy)
    sib_grad = shift(grad, 1)

    tile = tile_of(half)
    steps = half // tile
    out_block = pl.BlockSpec((layers, CORES, rows, tile), lambda t, core: (0, 0, 0, t))
    partial = pl.pallas_call(
        lambda *refs: partial_kernel(rows, *refs),
        grid_spec=pltpu.PrefetchScalarGridSpec(
            num_scalar_prefetch=1,
            grid=(steps,),
            in_specs=[
                pl.BlockSpec((tokens, slab), lambda t, core: (0, 0)),
                pl.BlockSpec((tokens, slab), lambda t, core: (0, 0)),
                pl.BlockSpec((tile, slab), lambda t, core: (core[0] * steps + t, 0)),
                pl.BlockSpec((tile, slab), lambda t, core: (t, 0)),
            ],
            out_specs=[out_block] * CHIPS,
            scratch_shapes=[pltpu.VMEM((tokens, slab), bf16)],
        ),
        out_shape=[
            jax.ShapeDtypeStruct((layers, CORES, rows, half), f32 if j == 0 else bf16)
            for j in range(CHIPS)
        ],
        compiler_params=kernel_params(),
        cost_estimate=pl.CostEstimate(
            flops=4 * tokens * half * slab, bytes_accessed=4 * half * slab, transcendentals=0
        ),
        name="grad_hidden_partial",
    )(pos[:1], grad, sib_grad, head_weight, sib_w)

    arrived = [shift(partial[j], j * CORES) for j in range(1, CHIPS)]
    chip_block = pl.BlockSpec((layers, CORES, rows, tile), lambda t: (0, 0, 0, t))
    layer_block = pl.BlockSpec((CORES, rows, tile), lambda t: (0, 0, t))
    summed = pl.pallas_call(
        chip_sum_kernel,
        grid=(steps,),
        in_specs=[chip_block] * CHIPS,
        out_specs=[layer_block] * layers,
        out_shape=[
            jax.ShapeDtypeStruct((CORES, rows, half), f32 if k == 0 else bf16) for k in range(layers)
        ],
        compiler_params=kernel_params(),
        cost_estimate=pl.CostEstimate(
            flops=tokens * half, bytes_accessed=3 * tokens * half, transcendentals=0
        ),
        name="chip_sum",
    )(partial[0], *arrived)
    arrived = [shift(summed[k], k * GROUP) for k in range(1, layers)]
    row_block = pl.BlockSpec((rows, tile), lambda t: (0, t))
    mine, theirs = pl.pallas_call(
        layer_sum_kernel,
        grid=(steps,),
        in_specs=[layer_block] * layers,
        out_specs=[row_block] * CORES,
        out_shape=[jax.ShapeDtypeStruct((rows, half), bf16)] * CORES,
        compiler_params=kernel_params(),
        cost_estimate=pl.CostEstimate(
            flops=CORES * layers * rows * half, bytes_accessed=3 * CORES * layers * rows * half, transcendentals=0
        ),
        name="layer_sum",
    )(summed[0], *arrived)
    other = shift(theirs, 1)

    tile = tile_of(depth)
    grad_head = pl.pallas_call(
        lambda *refs: head_kernel(rows, *refs),
        grid=(depth // tile,),
        in_specs=piece_specs + [pl.BlockSpec((tokens, slab), whole)],
        out_specs=pl.BlockSpec((tile, slab), lambda t: (t, 0)),
        out_shape=jax.ShapeDtypeStruct((depth, slab), bf16),
        scratch_shapes=[pltpu.VMEM((tokens, tile), bf16)],
        compiler_params=kernel_params(),
        cost_estimate=pl.CostEstimate(
            flops=2 * tokens * depth * slab, bytes_accessed=2 * depth * (slab + tokens), transcendentals=0
        ),
        name="grad_head",
    )(*pieces, grad)

    low, high = jnp.where(core == 0, mine, other), jnp.where(core == 0, other, mine)
    return loss[:, 0], grad_head, jnp.concatenate([low, high], axis=1)


def fits_levels(hidden_states, teacher_logits):
    n = lax.axis_size("vocab")
    rows = hidden_states.shape[0]
    blocks, _, stored, side = teacher_logits.shape
    return (
        n == blocks * GROUP
        and blocks & (blocks - 1) == 0
        and rows * GROUP == side
        and rows % 16 == 0
        and 2 * n <= side
        and 6 * blocks * stored <= side
        and hidden_states.shape[1] % (CORES * 128) == 0
    )


def on_device(
    hidden_states, head_weight, teacher_logits, block_lists, row_reader, tail_mass, token_weight
):
    plan = levels_plan if fits_levels(hidden_states, teacher_logits) else plain_plan
    return plan(
        hidden_states, head_weight, teacher_logits, block_lists, row_reader, tail_mass, token_weight
    )


def solution(mesh):
    in_specs = (
        P("vocab", None),
        P(None, "vocab"),
        P(None, None, "vocab", None),
        P(),
        P(),
        P(),
        P(),
    )
    out_specs = (P("vocab"), P(None, "vocab"), P("vocab", None))
    return jax.shard_map(
        on_device, mesh=mesh, in_specs=in_specs, out_specs=out_specs, check_vma=False
    )
```

```python
import functools

import jax
import jax.numpy as jnp
from jax import lax
from jax.experimental import pallas as pl
from jax.experimental.pallas import tpu as pltpu
from jax.sharding import PartitionSpec as P


def row_parts(scores, teacher_slab, listed_mask, student_exp, teacher_exp):
    return (
        jnp.sum(student_exp, axis=(2, 3)),
        jnp.sum(teacher_exp, axis=(2, 3)),
        jnp.sum(teacher_exp * scores, axis=(2, 3)),
        jnp.sum(teacher_exp * teacher_slab, axis=(2, 3)),
        jnp.sum(scores, axis=(2, 3)),
        jnp.sum(jnp.where(listed_mask, scores, 0.0), axis=(2, 3)),
    )


def plain_plan(
    hidden_states, head_weight, teacher_logits, block_lists, row_reader, tail_mass, token_weight
):
    blocks, listed_count, stored_rows, block_side = teacher_logits.shape
    slab_width = head_weight.shape[1]
    slab_blocks = slab_width // block_side
    devices = lax.axis_size("vocab")
    rank_self = lax.axis_index("vocab")
    tokens = blocks * block_side
    shard_rows = hidden_states.shape[0]
    gathered = lax.all_gather(hidden_states, "vocab", axis=0, tiled=True)
    logits = jnp.dot(gathered, head_weight, preferred_element_type=jnp.float32)
    owner_dev = block_lists // slab_blocks
    owned_here = owner_dev == rank_self
    within = block_lists - rank_self * slab_blocks
    token_iota = lax.broadcasted_iota(jnp.int32, (1, block_side, block_side), 1)
    token_map = (row_reader[:, None, :] == token_iota).astype(jnp.bfloat16)
    place_iota = lax.broadcasted_iota(jnp.int32, (1, slab_blocks, 1), 1)
    block_iota = lax.broadcasted_iota(jnp.int32, (1, devices * slab_blocks, 1), 1)
    picker = (block_lists[:, None, :] == block_iota).astype(jnp.bfloat16)
    outgoing = jnp.einsum(
        "tnk,tkrc->tnrc", picker, teacher_logits, preferred_element_type=jnp.float32
    ).astype(jnp.bfloat16)
    incoming = lax.all_to_all(outgoing, "vocab", split_axis=1, concat_axis=2, tiled=True)
    teacher_slab = jnp.einsum(
        "tpj,tbjc->tpbc", token_map, incoming, preferred_element_type=jnp.float32
    )
    listed = jnp.sum(
        ((within[:, None, :] == place_iota) & owned_here[:, None, :]).astype(jnp.int32), axis=2
    )
    scores = logits.reshape(blocks, block_side, slab_blocks, block_side)
    listed_mask = (listed > 0)[:, None, :, None]
    local_smax = jnp.max(scores, axis=(2, 3))
    local_tmax = jnp.max(jnp.where(listed_mask, teacher_slab, -1e30), axis=(2, 3))
    student_max, teacher_max = lax.pmax((local_smax, local_tmax), "vocab")
    student_exp = jnp.exp(scores - student_max[:, :, None, None])
    teacher_exp = jnp.exp(
        jnp.where(listed_mask, teacher_slab - teacher_max[:, :, None, None], -jnp.inf)
    )
    parts = row_parts(scores, teacher_slab, listed_mask, student_exp, teacher_exp)
    student_sum, teacher_sum, cross_sum, self_sum, logit_total, listed_total = lax.psum(
        (parts[0], parts[1], parts[2], parts[3], parts[4], parts[5]), "vocab"
    )
    tail_share = tail_mass.reshape(blocks, block_side)
    unlisted = float(devices * slab_width - block_side * listed_count)
    kept_mass = 1.0 - tail_share
    log_norm = student_max + jnp.log(student_sum)
    row_loss = (
        kept_mass * (jnp.log(kept_mass) - teacher_max - jnp.log(teacher_sum))
        + kept_mass * self_sum / teacher_sum
        + tail_share * jnp.log(tail_share / unlisted)
        - kept_mass * cross_sum / teacher_sum
        - tail_share / unlisted * (logit_total - listed_total)
        + log_norm
    )
    token_loss = lax.dynamic_slice_in_dim(
        row_loss.reshape(tokens), rank_self * shard_rows, shard_rows, 0
    )
    student_prob = student_exp / student_sum[:, :, None, None]
    teacher_prob = jnp.where(
        listed_mask,
        (kept_mass / teacher_sum)[:, :, None, None] * teacher_exp,
        (tail_share / unlisted)[:, :, None, None],
    )
    weight = token_weight.reshape(blocks, block_side)[:, :, None, None]
    grad_logits = (
        (weight * (student_prob - teacher_prob)).astype(jnp.bfloat16).reshape(tokens, slab_width)
    )
    grad_head = lax.dot_general(
        gathered, grad_logits, (((0,), (0,)), ((), ())), preferred_element_type=jnp.float32
    ).astype(jnp.bfloat16)
    grad_hidden = lax.psum_scatter(
        lax.dot_general(
            grad_logits, head_weight, (((1,), (1,)), ((), ())), preferred_element_type=jnp.float32
        ),
        "vocab",
        scatter_dimension=0,
        tiled=True,
    ).astype(jnp.bfloat16)
    return (token_loss, grad_head, grad_hidden)


CORES = 2
CHIPS = 4
GROUP = CORES * CHIPS
SLOTS = 4
VMEM_LIMIT = 30 * 1024 * 1024
HIDDEN_CHUNKS = 2
PARTIAL_CHUNKS = (3, 2)


def kernel_params():
    return pltpu.CompilerParams(vmem_limit_bytes=VMEM_LIMIT)


def vmem_spec():
    return pl.BlockSpec(memory_space=pltpu.VMEM)


def smem_spec():
    return pl.BlockSpec(memory_space=pltpu.SMEM)


def shift(x, distance):
    n = lax.axis_size("vocab")
    return lax.ppermute(x, "vocab", [(i, i ^ distance) for i in range(n)])


def tile_of(size):
    return 512 if size % 512 == 0 else 128


def token_places(place, rows, side):
    row = lax.broadcasted_iota(jnp.int32, (side, 1), 0)
    group = row // rows
    chip = (group % CHIPS) ^ place[1]
    core = (group // CHIPS) ^ place[0]
    return (chip * CORES + core) * rows + row % rows


def pick_column(match, values):
    return jnp.sum(jnp.where(match, values, 0.0), axis=1, keepdims=True)


def teacher_kernel(
    unlisted, rows, pos_ref, place_ref, blocks_ref, stat_ref, reader_ref, tail_ref, prob_ref, entropy_ref
):
    layers, slots, side, _ = blocks_ref.shape
    pos = [pos_ref[i] for i in range(3)]
    lane = lax.broadcasted_iota(jnp.int32, (1, side), 1)
    where_token = token_places(pos, rows, side)
    for k in range(layers):
        block = pos[2] ^ k
        match = reader_ref[block] == where_token
        onehot = jnp.where(match, 1.0, 0.0).astype(jnp.bfloat16)
        normaliser = pick_column(match, stat_ref[0, block])
        tail = pick_column(lane == where_token, tail_ref[block])
        kept = 1.0 - tail
        rest = tail / unlisted
        span = pl.ds(k * side, side)
        prob_ref[span, :] = jnp.broadcast_to(rest, (side, prob_ref.shape[1]))
        for s in range(slots):
            place = place_ref[block, s]
            values = jnp.dot(onehot, blocks_ref[block, s], preferred_element_type=jnp.float32)
            prob = kept * jnp.exp(values - normaliser)

            @pl.when(place >= 0)
            def _():
                prob_ref[span, pl.ds(pl.multiple_of(place * side, side), side)] = prob

        if k == 0:
            mean = pick_column(match, stat_ref[1, block])
            entropy = kept * (jnp.log(kept) - normaliser + mean) + tail * jnp.log(rest)
            entropy_ref[...] = jnp.broadcast_to(entropy[:rows], entropy_ref.shape)


def assemble(pieces, rows, out_ref):
    layers = pieces[0].shape[0] // rows
    for k in range(layers):
        for p, piece in enumerate(pieces):
            out_ref[pl.ds((k * GROUP + p) * rows, rows), :] = piece[pl.ds(k * rows, rows), :]


def logits_kernel(rows, last, *refs):
    pieces, w_ref, refs = refs[:GROUP], refs[GROUP], refs[GROUP + 1 :]
    if last:
        before_ref, prob_ref, logits_ref, stat_ref, hidden, cross_ref = refs
    else:
        logits_ref, hidden = refs
    step = pl.program_id(0)

    @pl.when(step == 0)
    def _():
        assemble(pieces, rows, hidden)

    part = jnp.dot(hidden[...], w_ref[...], preferred_element_type=jnp.float32)
    if not last:
        logits_ref[...] = part
        return
    part = part + before_ref[...]
    width = part.shape[1]
    logits_ref[:, pl.ds(pl.multiple_of(step * width, width), width)] = part
    product = part * prob_ref[...]
    folded = product[:, :128]
    for i in range(1, width // 128):
        folded = folded + product[:, i * 128 : (i + 1) * 128]

    @pl.when(step == 0)
    def _():
        cross_ref[...] = folded

    @pl.when(step > 0)
    def _():
        cross_ref[...] += folded

    @pl.when(step == pl.num_programs(0) - 1)
    def _():
        logits = logits_ref[...]
        top = jnp.max(logits, axis=1, keepdims=True)
        norm = top + jnp.log(jnp.sum(jnp.exp(logits - top), axis=1, keepdims=True))
        cross = jnp.sum(cross_ref[...], axis=1, keepdims=True)
        lane = lax.broadcasted_iota(jnp.int32, (1, 128), 1)
        both = jnp.where(lane == 0, norm, jnp.where(lane == 1, cross, 0.0))
        stat_ref[...] = both.T[:2]


def grad_kernel(
    rows, pos_ref, own_ref, sib_ref, logits_ref, prob_ref, weight_ref, entropy_ref, grad_ref, loss_ref
):
    tokens = logits_ref.shape[0]
    devices = tokens // rows
    layers, _, side = weight_ref.shape
    layer_bits = (devices // GROUP).bit_length() - 1
    pos = [pos_ref[i] for i in range(3)]
    lane = lax.broadcasted_iota(jnp.int32, (1, 128), 1)
    stat = jnp.concatenate(
        [own_ref[...], sib_ref[...], jnp.zeros((128 - 2 * devices, tokens), jnp.float32)], axis=0
    ).T
    pairs = [(1 + i, 3 + i) for i in range(layer_bits)]
    pairs += [(1 + layer_bits, 0), (2 + layer_bits, 1), (3 + layer_bits, 2)]
    for lane_bit, block_bit in pairs:
        halves = stat.reshape(devices >> (block_bit + 1), 2, rows << block_bit, 128)
        swapped = jnp.stack([halves[:, 1], halves[:, 0]], axis=1).reshape(tokens, 128)
        stat = jnp.where((lane >> lane_bit) & 1 == 1, swapped, stat)
    used = lane < 2 * devices
    is_norm = used & (lane % 2 == 0)
    top = jnp.max(jnp.where(is_norm, stat, -jnp.inf), axis=1, keepdims=True)
    total = jnp.sum(jnp.where(is_norm, jnp.exp(stat - top), 0.0), axis=1, keepdims=True)
    log_norm = top + jnp.log(total)
    cross = jnp.sum(jnp.where(used & (lane % 2 == 1), stat, 0.0), axis=1, keepdims=True)
    loss_ref[...] = entropy_ref[...] - cross[:rows] + log_norm[:rows]
    where_token = token_places(pos, rows, side)
    for k in range(layers):
        span = pl.ds(k * side, side)
        weight = pick_column(lane == where_token, weight_ref[pos[2] ^ k])
        student = jnp.exp(logits_ref[span, :] - log_norm[k * side : (k + 1) * side])
        grad_ref[span, :] = (weight * (student - prob_ref[span, :])).astype(grad_ref.dtype)


def partial_kernel(rows, core_ref, grad_ref, sib_ref, w_ref, sib_w_ref, *refs):
    outs, swapped = refs[:CHIPS], refs[CHIPS]
    layers = outs[0].shape[0]
    half = CHIPS * rows

    @pl.when(pl.program_id(0) == 0)
    def _():
        for k in range(layers):
            for core in range(CORES):
                swapped[pl.ds((k * CORES + core) * half, half), :] = sib_ref[
                    pl.ds((k * CORES + 1 - core) * half, half), :
                ]

    contract = (((1,), (1,)), ((), ()))
    total = lax.dot_general(
        grad_ref[...], w_ref[...], contract, preferred_element_type=jnp.float32
    ) + lax.dot_general(
        swapped[...], sib_w_ref[...], contract, preferred_element_type=jnp.float32
    )
    for j, out in enumerate(outs):
        for k in range(layers):
            for core in range(CORES):
                start = (k * GROUP + core * CHIPS + j) * rows
                out[k, core] = total[start : start + rows].astype(out.dtype)


def head_kernel(rows, chunk_steps, *refs):
    pieces, (grad_ref, out_ref, hidden) = refs[:-3], refs[-3:]
    chunk = pl.program_id(0) // chunk_steps
    for i in range(len(pieces) // GROUP):

        @pl.when(chunk == i)
        def _():
            assemble(pieces[i * GROUP : (i + 1) * GROUP], rows, hidden)

    out_ref[...] = lax.dot_general(
        hidden[...], grad_ref[...], (((0,), (0,)), ((), ())), preferred_element_type=jnp.float32
    ).astype(out_ref.dtype)


def chip_sum_kernel(own_ref, *refs):
    arrived, outs = refs[: CHIPS - 1], refs[CHIPS - 1 :]
    for k, out in enumerate(outs):
        total = own_ref[k]
        for part in arrived:
            total = total + part[k].astype(jnp.float32)
        out[...] = total.astype(out.dtype)


def layer_sum_kernel(own_ref, *refs):
    arrived, (mine, theirs) = refs[:-2], refs[-2:]
    total = own_ref[...]
    for part in arrived:
        total = total + part[...].astype(jnp.float32)
    mine[...] = total[0].astype(mine.dtype)
    theirs[...] = total[1].astype(theirs.dtype)


def split_three(x):
    high = lax.reduce_precision(x, 8, 7)
    middle = lax.reduce_precision(x - high, 8, 7)
    low = x - high - middle
    return jnp.stack([high, middle, low]).astype(jnp.bfloat16)


def send_teacher(teacher_logits, block_lists, places):
    blocks, listed_count, stored, side = teacher_logits.shape
    n = lax.axis_size("vocab")
    rank = lax.axis_index("vocab")
    owner = block_lists // places
    earlier = jnp.tril(jnp.ones((listed_count, listed_count), jnp.bool_), -1)
    slot = jnp.sum((owner[:, :, None] == owner[:, None, :]) & earlier, axis=2, dtype=jnp.int32)
    code = owner * SLOTS + slot
    picker = (code[:, None, :] == jnp.arange(n * SLOTS, dtype=jnp.int32)[None, :, None]).astype(jnp.bfloat16)
    packed = jnp.einsum(
        "tsk,tkrc->tsrc", picker, teacher_logits, preferred_element_type=jnp.float32
    ).astype(jnp.bfloat16)
    packed = packed.reshape(blocks, n, SLOTS * stored, side).transpose(1, 0, 2, 3)
    values = teacher_logits.astype(jnp.float32)
    top = jnp.max(values, axis=(1, 3))
    powers = jnp.exp(values - top[:, None, :, None])
    total = jnp.sum(powers, axis=(1, 3))
    mean = jnp.sum(powers * values, axis=(1, 3)) / total
    stat = split_three(jnp.stack([top + jnp.log(total), mean])).reshape(-1)
    stat = jnp.pad(stat, (0, side - stat.shape[0]))
    payload = jnp.concatenate(
        [packed.reshape(n, -1, side), jnp.broadcast_to(stat, (n, 1, side))], axis=1
    )
    arrived = lax.all_to_all(payload, "vocab", split_axis=0, concat_axis=0, tiled=True)
    arrived_blocks = (
        arrived[:, :-1]
        .reshape(n, blocks, SLOTS, stored, side)
        .transpose(1, 2, 0, 3, 4)
        .reshape(blocks, SLOTS, n * stored, side)
    )
    arrived_stat = (
        arrived[:, -1, : 6 * blocks * stored]
        .astype(jnp.float32)
        .reshape(n, 3, 2, blocks, stored)
        .sum(axis=1)
        .transpose(1, 2, 0, 3)
        .reshape(2, blocks, 1, n * stored)
    )
    mine = code[:, None, :] == rank * SLOTS + jnp.arange(SLOTS, dtype=jnp.int32)[None, :, None]
    place = jnp.sum(jnp.where(mine, (block_lists % places + 1)[:, None, :], 0), axis=2) - 1
    return arrived_blocks, arrived_stat, place.astype(jnp.int32)


def levels_plan(
    hidden_states, head_weight, teacher_logits, block_lists, row_reader, tail_mass, token_weight
):
    blocks, listed_count, stored, side = teacher_logits.shape
    rows, depth = hidden_states.shape
    slab = head_weight.shape[1]
    n = lax.axis_size("vocab")
    rank = lax.axis_index("vocab")
    tokens = n * rows
    layers = n // GROUP
    half = depth // CORES
    bf16, f32 = jnp.bfloat16, jnp.float32
    core, chip, layer = rank % CORES, (rank // CORES) % CHIPS, rank // GROUP
    pos = jnp.stack([core, chip, layer]).astype(jnp.int32)
    unlisted = float(n * slab - side * listed_count)

    chunks = HIDDEN_CHUNKS if depth % (HIDDEN_CHUNKS * 256) == 0 else 1
    chunk = depth // chunks
    pieces = []
    for i in range(chunks):
        own = hidden_states[:, i * chunk : (i + 1) * chunk]
        column = [own] + [shift(own, k * GROUP) for k in range(1, layers)]
        column = jnp.concatenate(column, axis=0)
        plane = [column] + [shift(column, j * CORES) for j in range(1, CHIPS)]
        pieces.append(plane + [shift(piece, 1) for piece in plane])

    arrived_blocks, arrived_stat, place = send_teacher(teacher_logits, block_lists, slab // side)
    sib_w = shift(lax.dynamic_slice(head_weight, ((1 - core) * half, 0), (half, slab)), 1)

    prob, entropy = pl.pallas_call(
        lambda *refs: teacher_kernel(unlisted, rows, *refs),
        out_shape=(
            jax.ShapeDtypeStruct((tokens, slab), f32),
            jax.ShapeDtypeStruct((rows, side), f32),
        ),
        in_specs=[smem_spec(), smem_spec()] + [vmem_spec()] * 4,
        out_specs=(vmem_spec(), vmem_spec()),
        compiler_params=kernel_params(),
        cost_estimate=pl.CostEstimate(
            flops=2 * tokens * side * side * SLOTS, bytes_accessed=4 * tokens * slab, transcendentals=0
        ),
        name="teacher_prob",
    )(
        pos,
        place,
        arrived_blocks,
        arrived_stat,
        row_reader.reshape(blocks, 1, side),
        tail_mass.reshape(blocks, 1, side),
    )

    width = 256 if slab % 256 == 0 else 128
    logits = None
    for i in range(chunks):
        last = i == chunks - 1
        whole = lambda t: (0, 0)
        across = pl.BlockSpec((tokens, width), lambda t: (0, t))
        in_specs = [pl.BlockSpec((layers * rows, chunk), whole) for _ in range(GROUP)]
        in_specs.append(pl.BlockSpec((chunk, width), lambda t, i=i: (i, t)))
        operands = pieces[i] + [head_weight]
        scratch = [pltpu.VMEM((tokens, chunk), bf16)]
        out_shape = [jax.ShapeDtypeStruct((tokens, slab), f32)]
        out_specs = [across]
        if last:
            before = jnp.zeros((tokens, slab), f32) if logits is None else logits
            in_specs += [across, across]
            operands += [before, prob]
            scratch.append(pltpu.VMEM((tokens, 128), f32))
            out_shape.append(jax.ShapeDtypeStruct((2, tokens), f32))
            out_specs = [pl.BlockSpec((tokens, slab), whole), pl.BlockSpec((2, tokens), whole)]
        outs = pl.pallas_call(
            functools.partial(logits_kernel, rows, last),
            grid=(slab // width,),
            out_shape=out_shape,
            in_specs=in_specs,
            out_specs=out_specs,
            scratch_shapes=scratch,
            compiler_params=kernel_params(),
            cost_estimate=pl.CostEstimate(
                flops=2 * tokens * chunk * slab,
                bytes_accessed=2 * chunk * (slab + tokens) + 4 * tokens * slab,
                transcendentals=tokens * slab if last else 0,
            ),
            name="logits",
        )(*operands)
        logits = outs[0]
    stat = outs[1]

    distances = [1 << i for i in range((n // GROUP).bit_length() - 1)]
    distances = [d * GROUP for d in distances] + [CORES, 2 * CORES]
    for distance in distances:
        stat = jnp.concatenate([stat, shift(stat, distance)], axis=0)
    sib_stat = shift(stat, 1)

    grad, loss = pl.pallas_call(
        lambda *refs: grad_kernel(rows, *refs),
        out_shape=(
            jax.ShapeDtypeStruct((tokens, slab), bf16),
            jax.ShapeDtypeStruct((rows, side), f32),
        ),
        in_specs=[smem_spec()] + [vmem_spec()] * 6,
        out_specs=(vmem_spec(), vmem_spec()),
        compiler_params=kernel_params(),
        cost_estimate=pl.CostEstimate(
            flops=4 * tokens * slab, bytes_accessed=10 * tokens * slab, transcendentals=tokens * slab
        ),
        name="grad_logits",
    )(pos, stat, sib_stat, logits, prob, token_weight.reshape(blocks, 1, side), entropy)
    sib_grad = shift(grad, 1)

    tile = tile_of(half)
    steps = half // tile
    sizes = PARTIAL_CHUNKS if sum(PARTIAL_CHUNKS) == steps else (steps,)
    sent = []
    for i, size in enumerate(sizes):
        first = sum(sizes[:i])
        out_block = pl.BlockSpec((layers, CORES, rows, tile), lambda t, core: (0, 0, 0, t))
        partial = pl.pallas_call(
            functools.partial(partial_kernel, rows),
            grid_spec=pltpu.PrefetchScalarGridSpec(
                num_scalar_prefetch=1,
                grid=(size,),
                in_specs=[
                    pl.BlockSpec((tokens, slab), lambda t, core: (0, 0)),
                    pl.BlockSpec((tokens, slab), lambda t, core: (0, 0)),
                    pl.BlockSpec((tile, slab), lambda t, core, first=first: (core[0] * steps + first + t, 0)),
                    pl.BlockSpec((tile, slab), lambda t, core, first=first: (first + t, 0)),
                ],
                out_specs=[out_block] * CHIPS,
                scratch_shapes=[pltpu.VMEM((tokens, slab), bf16)],
            ),
            out_shape=[
                jax.ShapeDtypeStruct((layers, CORES, rows, size * tile), f32 if j == 0 else bf16)
                for j in range(CHIPS)
            ],
            compiler_params=kernel_params(),
            cost_estimate=pl.CostEstimate(
                flops=4 * tokens * size * tile * slab, bytes_accessed=4 * size * tile * slab, transcendentals=0
            ),
            name="grad_hidden_partial",
        )(pos[:1], grad, sib_grad, head_weight, sib_w)
        sent.append([partial[0]] + [shift(partial[j], j * CORES) for j in range(1, CHIPS)])

    head_tile = chunk // 2 if chunk % 512 == 0 else chunk
    per_chunk = chunk // head_tile
    piece_specs = [
        pl.BlockSpec(
            (layers * rows, head_tile),
            lambda t, i=i: (0, jnp.clip(t - i * per_chunk, 0, per_chunk - 1)),
        )
        for i in range(chunks)
        for _ in range(GROUP)
    ]
    grad_head = pl.pallas_call(
        functools.partial(head_kernel, rows, per_chunk),
        grid=(depth // head_tile,),
        in_specs=piece_specs + [pl.BlockSpec((tokens, slab), lambda t: (0, 0))],
        out_specs=pl.BlockSpec((head_tile, slab), lambda t: (t, 0)),
        out_shape=jax.ShapeDtypeStruct((depth, slab), bf16),
        scratch_shapes=[pltpu.VMEM((tokens, head_tile), bf16)],
        compiler_params=kernel_params(),
        cost_estimate=pl.CostEstimate(
            flops=2 * tokens * depth * slab, bytes_accessed=2 * depth * (slab + tokens), transcendentals=0
        ),
        name="grad_head",
    )(*[piece for some in pieces for piece in some], grad)
    sent, grad_head = lax.optimization_barrier((sent, grad_head))

    mine, other = [], []
    for size, parts in zip(sizes, sent):
        chip_block = pl.BlockSpec((layers, CORES, rows, tile), lambda t: (0, 0, 0, t))
        layer_block = pl.BlockSpec((CORES, rows, tile), lambda t: (0, 0, t))
        summed = pl.pallas_call(
            chip_sum_kernel,
            grid=(size,),
            in_specs=[chip_block] * CHIPS,
            out_specs=[layer_block] * layers,
            out_shape=[
                jax.ShapeDtypeStruct((CORES, rows, size * tile), f32 if k == 0 else bf16)
                for k in range(layers)
            ],
            compiler_params=kernel_params(),
            cost_estimate=pl.CostEstimate(
                flops=tokens * size * tile, bytes_accessed=3 * tokens * size * tile, transcendentals=0
            ),
            name="chip_sum",
        )(*parts)
        arrived = [shift(summed[k], k * GROUP) for k in range(1, layers)]
        row_block = pl.BlockSpec((rows, tile), lambda t: (0, t))
        ours, theirs = pl.pallas_call(
            layer_sum_kernel,
            grid=(size,),
            in_specs=[layer_block] * layers,
            out_specs=[row_block] * CORES,
            out_shape=[jax.ShapeDtypeStruct((rows, size * tile), bf16)] * CORES,
            compiler_params=kernel_params(),
            cost_estimate=pl.CostEstimate(
                flops=CORES * layers * rows * size * tile,
                bytes_accessed=3 * CORES * layers * rows * size * tile,
                transcendentals=0,
            ),
            name="layer_sum",
        )(summed[0], *arrived)
        mine.append(ours)
        other.append(shift(theirs, 1))
    mine, other = jnp.concatenate(mine, axis=1), jnp.concatenate(other, axis=1)

    low, high = jnp.where(core == 0, mine, other), jnp.where(core == 0, other, mine)
    return loss[:, 0], grad_head, jnp.concatenate([low, high], axis=1)


def fits_levels(hidden_states, teacher_logits):
    n = lax.axis_size("vocab")
    rows = hidden_states.shape[0]
    blocks, _, stored, side = teacher_logits.shape
    return (
        n == blocks * GROUP
        and blocks & (blocks - 1) == 0
        and rows * GROUP == side
        and rows % 16 == 0
        and 2 * n <= side
        and 6 * blocks * stored <= side
        and hidden_states.shape[1] % (CORES * 128) == 0
    )


def on_device(
    hidden_states, head_weight, teacher_logits, block_lists, row_reader, tail_mass, token_weight
):
    plan = levels_plan if fits_levels(hidden_states, teacher_logits) else plain_plan
    return plan(
        hidden_states, head_weight, teacher_logits, block_lists, row_reader, tail_mass, token_weight
    )


def solution(mesh):
    in_specs = (
        P("vocab", None),
        P(None, "vocab"),
        P(None, None, "vocab", None),
        P(),
        P(),
        P(),
        P(),
    )
    out_specs = (P("vocab"), P(None, "vocab"), P("vocab", None))
    return jax.shard_map(
        on_device, mesh=mesh, in_specs=in_specs, out_specs=out_specs, check_vma=False
    )
```

```python
import functools

import jax
import jax.numpy as jnp
from jax import lax
from jax.experimental import pallas as pl
from jax.experimental.pallas import tpu as pltpu
from jax.sharding import PartitionSpec as P


def row_parts(scores, teacher_slab, listed_mask, student_exp, teacher_exp):
    return (
        jnp.sum(student_exp, axis=(2, 3)),
        jnp.sum(teacher_exp, axis=(2, 3)),
        jnp.sum(teacher_exp * scores, axis=(2, 3)),
        jnp.sum(teacher_exp * teacher_slab, axis=(2, 3)),
        jnp.sum(scores, axis=(2, 3)),
        jnp.sum(jnp.where(listed_mask, scores, 0.0), axis=(2, 3)),
    )


def plain_plan(
    hidden_states, head_weight, teacher_logits, block_lists, row_reader, tail_mass, token_weight
):
    blocks, listed_count, stored_rows, block_side = teacher_logits.shape
    slab_width = head_weight.shape[1]
    slab_blocks = slab_width // block_side
    devices = lax.axis_size("vocab")
    rank_self = lax.axis_index("vocab")
    tokens = blocks * block_side
    shard_rows = hidden_states.shape[0]
    gathered = lax.all_gather(hidden_states, "vocab", axis=0, tiled=True)
    logits = jnp.dot(gathered, head_weight, preferred_element_type=jnp.float32)
    owner_dev = block_lists // slab_blocks
    owned_here = owner_dev == rank_self
    within = block_lists - rank_self * slab_blocks
    token_iota = lax.broadcasted_iota(jnp.int32, (1, block_side, block_side), 1)
    token_map = (row_reader[:, None, :] == token_iota).astype(jnp.bfloat16)
    place_iota = lax.broadcasted_iota(jnp.int32, (1, slab_blocks, 1), 1)
    block_iota = lax.broadcasted_iota(jnp.int32, (1, devices * slab_blocks, 1), 1)
    picker = (block_lists[:, None, :] == block_iota).astype(jnp.bfloat16)
    outgoing = jnp.einsum(
        "tnk,tkrc->tnrc", picker, teacher_logits, preferred_element_type=jnp.float32
    ).astype(jnp.bfloat16)
    incoming = lax.all_to_all(outgoing, "vocab", split_axis=1, concat_axis=2, tiled=True)
    teacher_slab = jnp.einsum(
        "tpj,tbjc->tpbc", token_map, incoming, preferred_element_type=jnp.float32
    )
    listed = jnp.sum(
        ((within[:, None, :] == place_iota) & owned_here[:, None, :]).astype(jnp.int32), axis=2
    )
    scores = logits.reshape(blocks, block_side, slab_blocks, block_side)
    listed_mask = (listed > 0)[:, None, :, None]
    local_smax = jnp.max(scores, axis=(2, 3))
    local_tmax = jnp.max(jnp.where(listed_mask, teacher_slab, -1e30), axis=(2, 3))
    student_max, teacher_max = lax.pmax((local_smax, local_tmax), "vocab")
    student_exp = jnp.exp(scores - student_max[:, :, None, None])
    teacher_exp = jnp.exp(
        jnp.where(listed_mask, teacher_slab - teacher_max[:, :, None, None], -jnp.inf)
    )
    parts = row_parts(scores, teacher_slab, listed_mask, student_exp, teacher_exp)
    student_sum, teacher_sum, cross_sum, self_sum, logit_total, listed_total = lax.psum(
        (parts[0], parts[1], parts[2], parts[3], parts[4], parts[5]), "vocab"
    )
    tail_share = tail_mass.reshape(blocks, block_side)
    unlisted = float(devices * slab_width - block_side * listed_count)
    kept_mass = 1.0 - tail_share
    log_norm = student_max + jnp.log(student_sum)
    row_loss = (
        kept_mass * (jnp.log(kept_mass) - teacher_max - jnp.log(teacher_sum))
        + kept_mass * self_sum / teacher_sum
        + tail_share * jnp.log(tail_share / unlisted)
        - kept_mass * cross_sum / teacher_sum
        - tail_share / unlisted * (logit_total - listed_total)
        + log_norm
    )
    token_loss = lax.dynamic_slice_in_dim(
        row_loss.reshape(tokens), rank_self * shard_rows, shard_rows, 0
    )
    student_prob = student_exp / student_sum[:, :, None, None]
    teacher_prob = jnp.where(
        listed_mask,
        (kept_mass / teacher_sum)[:, :, None, None] * teacher_exp,
        (tail_share / unlisted)[:, :, None, None],
    )
    weight = token_weight.reshape(blocks, block_side)[:, :, None, None]
    grad_logits = (
        (weight * (student_prob - teacher_prob)).astype(jnp.bfloat16).reshape(tokens, slab_width)
    )
    grad_head = lax.dot_general(
        gathered, grad_logits, (((0,), (0,)), ((), ())), preferred_element_type=jnp.float32
    ).astype(jnp.bfloat16)
    grad_hidden = lax.psum_scatter(
        lax.dot_general(
            grad_logits, head_weight, (((1,), (1,)), ((), ())), preferred_element_type=jnp.float32
        ),
        "vocab",
        scatter_dimension=0,
        tiled=True,
    ).astype(jnp.bfloat16)
    return (token_loss, grad_head, grad_hidden)


CORES = 2
CHIPS = 4
GROUP = CORES * CHIPS
SLOTS = 4
VMEM_LIMIT = 56 * 1024 * 1024


def kernel_params():
    return pltpu.CompilerParams(vmem_limit_bytes=VMEM_LIMIT)


def vmem_spec():
    return pl.BlockSpec(memory_space=pltpu.VMEM)


def smem_spec():
    return pl.BlockSpec(memory_space=pltpu.SMEM)


def shift(x, distance):
    n = lax.axis_size("vocab")
    return lax.ppermute(x, "vocab", [(i, i ^ distance) for i in range(n)])


def token_places(place, rows, side):
    row = lax.broadcasted_iota(jnp.int32, (side, 1), 0)
    group = row // rows
    chip = (group % CHIPS) ^ place[1]
    core = (group // CHIPS) ^ place[0]
    return (chip * CORES + core) * rows + row % rows


def pick_column(match, values):
    return jnp.sum(jnp.where(match, values, 0.0), axis=1, keepdims=True)


def teacher_kernel(
    unlisted, rows, pos_ref, place_ref, blocks_ref, stat_ref, reader_ref, tail_ref, prob_ref, entropy_ref
):
    layers, slots, side, _ = blocks_ref.shape
    pos = [pos_ref[i] for i in range(3)]
    lane = lax.broadcasted_iota(jnp.int32, (1, side), 1)
    where_token = token_places(pos, rows, side)
    for k in range(layers):
        block = pos[2] ^ k
        match = reader_ref[block] == where_token
        onehot = jnp.where(match, 1.0, 0.0).astype(jnp.bfloat16)
        normaliser = pick_column(match, stat_ref[0, block])
        tail = pick_column(lane == where_token, tail_ref[block])
        kept = 1.0 - tail
        rest = tail / unlisted
        span = pl.ds(k * side, side)
        prob_ref[span, :] = jnp.broadcast_to(rest, (side, prob_ref.shape[1]))
        for s in range(slots):
            place = place_ref[block, s]
            values = jnp.dot(onehot, blocks_ref[block, s], preferred_element_type=jnp.float32)
            prob = kept * jnp.exp(values - normaliser)

            @pl.when(place >= 0)
            def _():
                prob_ref[span, pl.ds(pl.multiple_of(place * side, side), side)] = prob

        if k == 0:
            mean = pick_column(match, stat_ref[1, block])
            entropy = kept * (jnp.log(kept) - normaliser + mean) + tail * jnp.log(rest)
            entropy_ref[...] = jnp.broadcast_to(entropy[:rows], entropy_ref.shape)


def assemble(pieces, places, rows, out_ref):
    for piece, blocks in zip(pieces, places):
        for i, block in enumerate(blocks):
            out_ref[pl.ds(block * rows, rows), :] = piece[pl.ds(i * rows, rows), :]


def logits_kernel(rows, places, last, *refs):
    count = len(places)
    pieces, w_ref, refs = refs[:count], refs[count], refs[count + 1 :]
    if last:
        before_ref, prob_ref, logits_ref, stat_ref, hidden, cross_ref = refs
    else:
        logits_ref, hidden = refs
    step = pl.program_id(0)

    @pl.when(step == 0)
    def _():
        assemble(pieces, places, rows, hidden)

    part = jnp.dot(hidden[...], w_ref[...], preferred_element_type=jnp.float32)
    if not last:
        logits_ref[...] = part
        return
    part = part + before_ref[...]
    width = part.shape[1]
    logits_ref[:, pl.ds(pl.multiple_of(step * width, width), width)] = part
    product = part * prob_ref[...]
    folded = product[:, :128]
    for i in range(1, width // 128):
        folded = folded + product[:, i * 128 : (i + 1) * 128]

    @pl.when(step == 0)
    def _():
        cross_ref[...] = folded

    @pl.when(step > 0)
    def _():
        cross_ref[...] += folded

    @pl.when(step == pl.num_programs(0) - 1)
    def _():
        logits = logits_ref[...]
        top = jnp.max(logits, axis=1, keepdims=True)
        norm = top + jnp.log(jnp.sum(jnp.exp(logits - top), axis=1, keepdims=True))
        cross = jnp.sum(cross_ref[...], axis=1, keepdims=True)
        lane = lax.broadcasted_iota(jnp.int32, (1, 128), 1)
        both = jnp.where(lane == 0, norm, jnp.where(lane == 1, cross, 0.0))
        both = both.T
        tokens = logits.shape[0]
        packed = [both[i : i + 1, t : t + 128] for i in range(2) for t in range(0, tokens, 128)]
        stat_ref[...] = jnp.broadcast_to(jnp.concatenate(packed, axis=0)[None], stat_ref.shape)


def grad_kernel(
    rows, pos_ref, stat_ref, logits_ref, prob_ref, weight_ref, entropy_ref, grad_ref, loss_ref
):
    tokens = logits_ref.shape[0]
    devices = tokens // rows
    layers, _, side = weight_ref.shape
    layer_bits = (devices // GROUP).bit_length() - 1
    pos = [pos_ref[i] for i in range(3)]
    rank = pos_ref[3]
    lane = lax.broadcasted_iota(jnp.int32, (1, 128), 1)
    per_stat = stat_ref.shape[1] // 2
    norms, crosses = [
        jnp.concatenate([stat_ref[:, i * per_stat + t, :] for t in range(per_stat)], axis=1) for i in range(2)
    ]
    stat = jnp.concatenate(
        [norms, crosses, jnp.zeros((128 - 2 * devices, tokens), jnp.float32)], axis=0
    ).T
    pairs = [(0, 2), (1, 0), (2, 1)] + [(3 + i, 3 + i) for i in range(layer_bits)]
    for index_bit, block_bit in pairs:
        halves = stat.reshape(devices >> (block_bit + 1), 2, rows << block_bit, 128)
        swapped = jnp.stack([halves[:, 1], halves[:, 0]], axis=1).reshape(tokens, 128)
        stat = jnp.where(((lane ^ rank) >> index_bit) & 1 == 1, swapped, stat)
    is_norm = lane < devices
    is_cross = (lane >= devices) & (lane < 2 * devices)
    top = jnp.max(jnp.where(is_norm, stat, -jnp.inf), axis=1, keepdims=True)
    total = jnp.sum(jnp.where(is_norm, jnp.exp(stat - top), 0.0), axis=1, keepdims=True)
    log_norm = top + jnp.log(total)
    cross = jnp.sum(jnp.where(is_cross, stat, 0.0), axis=1, keepdims=True)
    loss_ref[...] = entropy_ref[...] - cross[:rows] + log_norm[:rows]
    where_token = token_places(pos, rows, side)
    for k in range(layers):
        span = pl.ds(k * side, side)
        weight = pick_column(lane == where_token, weight_ref[pos[2] ^ k])
        student = jnp.exp(logits_ref[span, :] - log_norm[k * side : (k + 1) * side])
        grad_ref[span, :] = (weight * (student - prob_ref[span, :])).astype(grad_ref.dtype)


def partial_kernel(rows, by_layer, pos_ref, grad_ref, sib_ref, w_ref, sib_w_ref, out_ref, swapped):
    layers = out_ref.shape[0] if by_layer else out_ref.shape[1]
    half = CHIPS * rows

    @pl.when(pl.program_id(0) == 0)
    def _():
        for k in range(layers):
            for core in range(CORES):
                swapped[pl.ds((k * CORES + core) * half, half), :] = sib_ref[
                    pl.ds((k * CORES + 1 - core) * half, half), :
                ]

    contract = (((1,), (1,)), ((), ()))
    total = lax.dot_general(
        grad_ref[...], w_ref[...], contract, preferred_element_type=jnp.float32
    ) + lax.dot_general(
        swapped[...], sib_w_ref[...], contract, preferred_element_type=jnp.float32
    )
    for k in range(layers):
        for j in range(CHIPS):
            for core in range(CORES):
                start = (k * GROUP + core * CHIPS + j) * rows
                part = total[start : start + rows].astype(out_ref.dtype)
                if by_layer:
                    out_ref[pos_ref[2] ^ k, j, core] = part
                else:
                    out_ref[pos_ref[1] ^ j, k, core] = part


def head_kernel(rows, places, *refs):
    pieces, (grad_ref, out_ref, hidden) = refs[:-3], refs[-3:]
    step = pl.program_id(0)
    done, first = 0, 0
    for blocks, steps in places:
        some = pieces[done : done + len(blocks)]

        @pl.when((step >= first) & (step < first + steps))
        def _():
            assemble(some, blocks, rows, hidden)

        done, first = done + len(blocks), first + steps
    out_ref[...] = lax.dot_general(
        hidden[...], grad_ref[...], (((0,), (0,)), ((), ())), preferred_element_type=jnp.float32
    ).astype(out_ref.dtype)


def total_of(parts_ref, index=()):
    total = parts_ref[(0, *index)].astype(jnp.float32)
    for i in range(1, parts_ref.shape[0]):
        total = total + parts_ref[(i, *index)].astype(jnp.float32)
    return total


def first_sum_kernel(axis, pos_ref, parts_ref, out_ref):
    for i in range(out_ref.shape[0]):
        out_ref[pos_ref[axis] ^ i] = total_of(parts_ref, (i,)).astype(out_ref.dtype)


def last_sum_kernel(*refs):
    parts, (mine, theirs) = refs[:-2], refs[-2:]
    first = 0
    for part in parts:
        total = total_of(part)
        span = pl.ds(first, total.shape[-1])
        mine[:, span] = total[0].astype(mine.dtype)
        theirs[:, span] = total[1].astype(theirs.dtype)
        first += total.shape[-1]


def split_three(x):
    high = lax.reduce_precision(x, 8, 7)
    middle = lax.reduce_precision(x - high, 8, 7)
    low = x - high - middle
    return jnp.stack([high, middle, low]).astype(jnp.bfloat16)


def send_teacher(teacher_logits, block_lists, places):
    blocks, listed_count, stored, side = teacher_logits.shape
    n = lax.axis_size("vocab")
    rank = lax.axis_index("vocab")
    owner = block_lists // places
    earlier = jnp.tril(jnp.ones((listed_count, listed_count), jnp.bool_), -1)
    slot = jnp.sum((owner[:, :, None] == owner[:, None, :]) & earlier, axis=2, dtype=jnp.int32)
    code = owner * SLOTS + slot
    picker = (code[:, None, :] == jnp.arange(n * SLOTS, dtype=jnp.int32)[None, :, None]).astype(jnp.bfloat16)
    packed = jnp.einsum(
        "tsk,tkrc->tsrc", picker, teacher_logits, preferred_element_type=jnp.float32
    ).astype(jnp.bfloat16)
    packed = packed.reshape(blocks, n, SLOTS * stored, side).transpose(1, 0, 2, 3)
    values = teacher_logits.astype(jnp.float32)
    top = jnp.max(values, axis=(1, 3))
    powers = jnp.exp(values - top[:, None, :, None])
    total = jnp.sum(powers, axis=(1, 3))
    mean = jnp.sum(powers * values, axis=(1, 3)) / total
    stat = split_three(jnp.stack([top + jnp.log(total), mean])).reshape(-1)
    stat = jnp.pad(stat, (0, side - stat.shape[0]))
    payload = jnp.concatenate(
        [packed.reshape(n, -1, side), jnp.broadcast_to(stat, (n, 1, side))], axis=1
    )
    arrived = lax.all_to_all(payload, "vocab", split_axis=0, concat_axis=0, tiled=True)
    arrived_blocks = (
        arrived[:, :-1]
        .reshape(n, blocks, SLOTS, stored, side)
        .transpose(1, 2, 0, 3, 4)
        .reshape(blocks, SLOTS, n * stored, side)
    )
    arrived_stat = (
        arrived[:, -1, : 6 * blocks * stored]
        .astype(jnp.float32)
        .reshape(n, 3, 2, blocks, stored)
        .sum(axis=1)
        .transpose(1, 2, 0, 3)
        .reshape(2, blocks, 1, n * stored)
    )
    mine = code[:, None, :] == rank * SLOTS + jnp.arange(SLOTS, dtype=jnp.int32)[None, :, None]
    place = jnp.sum(jnp.where(mine, (block_lists % places + 1)[:, None, :], 0), axis=2) - 1
    return arrived_blocks, arrived_stat, place.astype(jnp.int32)


def levels_plan(
    hidden_states, head_weight, teacher_logits, block_lists, row_reader, tail_mass, token_weight
):
    blocks, listed_count, stored, side = teacher_logits.shape
    rows, depth = hidden_states.shape
    slab = head_weight.shape[1]
    n = lax.axis_size("vocab")
    rank = lax.axis_index("vocab")
    tokens = n * rows
    layers = n // GROUP
    half = depth // CORES
    bf16, f32 = jnp.bfloat16, jnp.float32
    core, chip, layer = rank % CORES, (rank // CORES) % CHIPS, rank // GROUP
    pos = jnp.stack([core, chip, layer, rank]).astype(jnp.int32)
    unlisted = float(n * slab - side * listed_count)
    in_layer = [[(o * CHIPS + q) * CORES + c for q in range(CHIPS)] for o in range(layers) for c in range(CORES)]
    across = [[o * GROUP + i for o in range(layers)] for i in range(GROUP)]

    wide = depth * 3 // 4
    own = hidden_states[:, :wide]
    column = [own] + [shift(own, k * GROUP) for k in range(1, layers)]
    column = jnp.concatenate(column, axis=0)
    plane = hidden_states[:, wide:]
    for j in (1, 2):
        plane = jnp.concatenate([plane, shift(plane, j * CORES)], axis=0)

    arrived_blocks, arrived_stat, place = send_teacher(teacher_logits, block_lists, slab // side)

    column, plane, late_weight = lax.optimization_barrier((column, plane, head_weight))
    wide_pieces = [column] + [shift(column, j * CORES) for j in range(1, CHIPS)]
    wide_pieces += [shift(piece, 1) for piece in wide_pieces]
    wide_places = [[k * GROUP + p for k in range(layers)] for p in range(GROUP)]
    narrow_pieces = [plane]
    narrow_layers = [[0]]
    for k in [1 << i for i in reversed(range((layers - 1).bit_length()))]:
        if k > 1:
            narrow_pieces = [jnp.concatenate([plane, shift(plane, k * GROUP)], axis=0)]
            plane = narrow_pieces[0]
            narrow_layers = [narrow_layers[0] + [i ^ k for i in narrow_layers[0]]]
        else:
            narrow_pieces.append(shift(plane, GROUP))
            narrow_layers.append([i ^ 1 for i in narrow_layers[0]])
    narrow_pieces += [shift(piece, 1) for piece in narrow_pieces]
    narrow_places = [
        [k * GROUP + c * CHIPS + j for k in some for j in range(CHIPS)] for c in range(CORES) for some in narrow_layers
    ]
    sib_w = shift(lax.dynamic_slice(late_weight, ((1 - core) * half, 0), (half, slab)), 1)

    prob, entropy = pl.pallas_call(
        lambda *refs: teacher_kernel(unlisted, rows, *refs),
        out_shape=(
            jax.ShapeDtypeStruct((tokens, slab), f32),
            jax.ShapeDtypeStruct((rows, side), f32),
        ),
        in_specs=[smem_spec(), smem_spec()] + [vmem_spec()] * 4,
        out_specs=(vmem_spec(), vmem_spec()),
        compiler_params=kernel_params(),
        cost_estimate=pl.CostEstimate(
            flops=2 * tokens * side * side * SLOTS, bytes_accessed=4 * tokens * slab, transcendentals=0
        ),
        name="teacher_prob",
    )(
        pos,
        place,
        arrived_blocks,
        arrived_stat,
        row_reader.reshape(blocks, 1, side),
        tail_mass.reshape(blocks, 1, side),
    )

    width = 256 if slab % 256 == 0 else 128
    whole = lambda t: (0, 0)
    tile_out = pl.BlockSpec((tokens, width), lambda t: (0, t))
    narrow = depth - wide

    def logits_call(pieces, places, chunk, first, before=None):
        last = before is not None
        out_shape = [jax.ShapeDtypeStruct((tokens, slab), f32)]
        out_specs = [tile_out]
        scratch = [pltpu.VMEM((tokens, chunk), bf16)]
        if last:
            scratch.append(pltpu.VMEM((tokens, 128), f32))
            out_shape.append(jax.ShapeDtypeStruct((n, 2 * tokens // 128, 128), f32))
            out_specs = [
                pl.BlockSpec((tokens, slab), whole),
                pl.BlockSpec((n, 2 * tokens // 128, 128), lambda t: (0, 0, 0)),
            ]
        return pl.pallas_call(
            functools.partial(logits_kernel, rows, places, last),
            grid=(slab // width,),
            out_shape=out_shape,
            in_specs=[pl.BlockSpec(piece.shape, whole) for piece in pieces]
            + [pl.BlockSpec((chunk, width), lambda t: (first // chunk, t))]
            + [tile_out] * (2 * last),
            out_specs=out_specs,
            scratch_shapes=scratch,
            compiler_params=kernel_params(),
            cost_estimate=pl.CostEstimate(
                flops=2 * tokens * chunk * slab,
                bytes_accessed=2 * chunk * (slab + tokens) + 4 * tokens * slab,
                transcendentals=tokens * slab if last else 0,
            ),
            name="logits",
        )(*pieces, head_weight, *((before, prob) if last else ()))

    (logits,) = logits_call(narrow_pieces, narrow_places, narrow, wide)
    logits, stat = logits_call(wide_pieces, wide_places, wide, 0, logits)
    stat = lax.all_to_all(stat, "vocab", split_axis=0, concat_axis=0, tiled=True)

    grad, loss = pl.pallas_call(
        lambda *refs: grad_kernel(rows, *refs),
        out_shape=(
            jax.ShapeDtypeStruct((tokens, slab), bf16),
            jax.ShapeDtypeStruct((rows, side), f32),
        ),
        in_specs=[smem_spec()] + [vmem_spec()] * 5,
        out_specs=(vmem_spec(), vmem_spec()),
        compiler_params=kernel_params(),
        cost_estimate=pl.CostEstimate(
            flops=4 * tokens * slab, bytes_accessed=10 * tokens * slab, transcendentals=tokens * slab
        ),
        name="grad_logits",
    )(pos, stat, logits, prob, token_weight.reshape(blocks, 1, side), entropy)
    sib_grad = shift(grad, 1)

    back = half // 10 * 3 // 256 * 256
    sent = []
    for first, size, by_layer in ((0, half - back, False), (half - back, back, True)):
        tile = size // 2 if size % 256 == 0 and size > 1024 else size
        steps = size // tile
        shape = (layers, CHIPS, CORES, rows) if by_layer else (CHIPS, layers, CORES, rows)
        partial = pl.pallas_call(
            functools.partial(partial_kernel, rows, by_layer),
            grid_spec=pltpu.PrefetchScalarGridSpec(
                num_scalar_prefetch=1,
                grid=(steps,),
                in_specs=[
                    pl.BlockSpec((tokens, slab), lambda t, pos: (0, 0)),
                    pl.BlockSpec((tokens, slab), lambda t, pos: (0, 0)),
                    pl.BlockSpec(
                        (pl.Element(tile), pl.Element(slab)),
                        lambda t, pos, first=first, tile=tile: (pl.multiple_of(pos[0] * half + first + t * tile, 128), 0),
                    ),
                    pl.BlockSpec(
                        (pl.Element(tile), pl.Element(slab)),
                        lambda t, pos, first=first, tile=tile: (pl.multiple_of(first + t * tile, 128), 0),
                    ),
                ],
                out_specs=pl.BlockSpec((*shape, tile), lambda t, pos: (0, 0, 0, 0, t)),
                scratch_shapes=[pltpu.VMEM((tokens, slab), bf16)],
            ),
            out_shape=jax.ShapeDtypeStruct((*shape, size), bf16),
            compiler_params=kernel_params(),
            cost_estimate=pl.CostEstimate(
                flops=4 * tokens * size * slab, bytes_accessed=4 * size * slab, transcendentals=0
            ),
            name="grad_hidden_partial",
        )(pos, grad, sib_grad, head_weight, sib_w)
        groups = across if by_layer else in_layer
        sent.append(
            lax.all_to_all(
                partial, "vocab", split_axis=0, concat_axis=0, axis_index_groups=groups, tiled=True
            )
        )

    _, late_grad = lax.optimization_barrier((partial, grad))
    head_tile = narrow
    places = [(wide_places, wide // head_tile), (narrow_places, narrow // head_tile)]
    piece_specs = [
        pl.BlockSpec((piece.shape[0], head_tile), lambda t: (0, jnp.minimum(t, wide // head_tile - 1)))
        for piece in wide_pieces
    ] + [
        pl.BlockSpec((piece.shape[0], head_tile), lambda t: (0, jnp.maximum(t - wide // head_tile, 0)))
        for piece in narrow_pieces
    ]
    grad_head = pl.pallas_call(
        functools.partial(head_kernel, rows, places),
        grid=(depth // head_tile,),
        in_specs=piece_specs + [pl.BlockSpec((tokens, slab), whole)],
        out_specs=pl.BlockSpec((head_tile, slab), lambda t: (t, 0)),
        out_shape=jax.ShapeDtypeStruct((depth, slab), bf16),
        scratch_shapes=[pltpu.VMEM((tokens, head_tile), bf16)],
        compiler_params=kernel_params(),
        cost_estimate=pl.CostEstimate(
            flops=2 * tokens * depth * slab, bytes_accessed=2 * depth * (slab + tokens), transcendentals=0
        ),
        name="grad_head",
    )(*wide_pieces, *narrow_pieces, late_grad)
    sent, grad_head = lax.optimization_barrier((sent, grad_head))

    arrived = []
    for parts, by_layer in zip(sent, (False, True)):
        size = parts.shape[-1]
        tile = size // 2 if size % 256 == 0 and size > 1024 else size
        count = parts.shape[1]
        summed = pl.pallas_call(
            functools.partial(first_sum_kernel, 1 if by_layer else 2),
            grid=(size // tile,),
            in_specs=[
                smem_spec(),
                pl.BlockSpec((*parts.shape[:-1], tile), lambda t: (0, 0, 0, 0, t)),
            ],
            out_specs=pl.BlockSpec((count, CORES, rows, tile), lambda t: (0, 0, 0, t)),
            out_shape=jax.ShapeDtypeStruct((count, CORES, rows, size), bf16),
            compiler_params=kernel_params(),
            cost_estimate=pl.CostEstimate(
                flops=tokens * size, bytes_accessed=3 * tokens * size, transcendentals=0
            ),
            name="first_sum",
        )(pos, parts)
        groups = in_layer if by_layer else across
        arrived.append(
            lax.all_to_all(
                summed, "vocab", split_axis=0, concat_axis=0, axis_index_groups=groups, tiled=True
            )
        )
    mine, theirs = pl.pallas_call(
        last_sum_kernel,
        in_specs=[vmem_spec()] * 2,
        out_specs=[vmem_spec()] * 2,
        out_shape=[jax.ShapeDtypeStruct((rows, half), bf16)] * 2,
        compiler_params=kernel_params(),
        cost_estimate=pl.CostEstimate(
            flops=CORES * layers * rows * half, bytes_accessed=3 * CORES * layers * rows * half, transcendentals=0
        ),
        name="last_sum",
    )(*arrived)
    other = shift(theirs, 1)

    low, high = jnp.where(core == 0, mine, other), jnp.where(core == 0, other, mine)
    return loss[:, 0], grad_head, jnp.concatenate([low, high], axis=1)


def fits_levels(hidden_states, teacher_logits):
    n = lax.axis_size("vocab")
    rows = hidden_states.shape[0]
    blocks, _, stored, side = teacher_logits.shape
    return (
        n == blocks * GROUP
        and blocks & (blocks - 1) == 0
        and rows * GROUP == side
        and rows % 16 == 0
        and 2 * n <= side
        and 6 * blocks * stored <= side
        and hidden_states.shape[1] % (CORES * 1280) == 0
    )


def on_device(
    hidden_states, head_weight, teacher_logits, block_lists, row_reader, tail_mass, token_weight
):
    plan = levels_plan if fits_levels(hidden_states, teacher_logits) else plain_plan
    return plan(
        hidden_states, head_weight, teacher_logits, block_lists, row_reader, tail_mass, token_weight
    )


def solution(mesh):
    in_specs = (
        P("vocab", None),
        P(None, "vocab"),
        P(None, None, "vocab", None),
        P(),
        P(),
        P(),
        P(),
    )
    out_specs = (P("vocab"), P(None, "vocab"), P("vocab", None))
    return jax.shard_map(
        on_device, mesh=mesh, in_specs=in_specs, out_specs=out_specs, check_vma=False
    )
```

```python
import functools

import jax
import jax.numpy as jnp
from jax import lax
from jax.experimental import pallas as pl
from jax.experimental.pallas import tpu as pltpu
from jax.sharding import PartitionSpec as P


def row_parts(scores, teacher_slab, listed_mask, student_exp, teacher_exp):
    return (
        jnp.sum(student_exp, axis=(2, 3)),
        jnp.sum(teacher_exp, axis=(2, 3)),
        jnp.sum(teacher_exp * scores, axis=(2, 3)),
        jnp.sum(teacher_exp * teacher_slab, axis=(2, 3)),
        jnp.sum(scores, axis=(2, 3)),
        jnp.sum(jnp.where(listed_mask, scores, 0.0), axis=(2, 3)),
    )


def plain_plan(
    hidden_states, head_weight, teacher_logits, block_lists, row_reader, tail_mass, token_weight
):
    blocks, listed_count, stored_rows, block_side = teacher_logits.shape
    slab_width = head_weight.shape[1]
    slab_blocks = slab_width // block_side
    devices = lax.axis_size("vocab")
    rank_self = lax.axis_index("vocab")
    tokens = blocks * block_side
    shard_rows = hidden_states.shape[0]
    gathered = lax.all_gather(hidden_states, "vocab", axis=0, tiled=True)
    logits = jnp.dot(gathered, head_weight, preferred_element_type=jnp.float32)
    owner_dev = block_lists // slab_blocks
    owned_here = owner_dev == rank_self
    within = block_lists - rank_self * slab_blocks
    token_iota = lax.broadcasted_iota(jnp.int32, (1, block_side, block_side), 1)
    token_map = (row_reader[:, None, :] == token_iota).astype(jnp.bfloat16)
    place_iota = lax.broadcasted_iota(jnp.int32, (1, slab_blocks, 1), 1)
    block_iota = lax.broadcasted_iota(jnp.int32, (1, devices * slab_blocks, 1), 1)
    picker = (block_lists[:, None, :] == block_iota).astype(jnp.bfloat16)
    outgoing = jnp.einsum(
        "tnk,tkrc->tnrc", picker, teacher_logits, preferred_element_type=jnp.float32
    ).astype(jnp.bfloat16)
    incoming = lax.all_to_all(outgoing, "vocab", split_axis=1, concat_axis=2, tiled=True)
    teacher_slab = jnp.einsum(
        "tpj,tbjc->tpbc", token_map, incoming, preferred_element_type=jnp.float32
    )
    listed = jnp.sum(
        ((within[:, None, :] == place_iota) & owned_here[:, None, :]).astype(jnp.int32), axis=2
    )
    scores = logits.reshape(blocks, block_side, slab_blocks, block_side)
    listed_mask = (listed > 0)[:, None, :, None]
    local_smax = jnp.max(scores, axis=(2, 3))
    local_tmax = jnp.max(jnp.where(listed_mask, teacher_slab, -1e30), axis=(2, 3))
    student_max, teacher_max = lax.pmax((local_smax, local_tmax), "vocab")
    student_exp = jnp.exp(scores - student_max[:, :, None, None])
    teacher_exp = jnp.exp(
        jnp.where(listed_mask, teacher_slab - teacher_max[:, :, None, None], -jnp.inf)
    )
    parts = row_parts(scores, teacher_slab, listed_mask, student_exp, teacher_exp)
    student_sum, teacher_sum, cross_sum, self_sum, logit_total, listed_total = lax.psum(
        (parts[0], parts[1], parts[2], parts[3], parts[4], parts[5]), "vocab"
    )
    tail_share = tail_mass.reshape(blocks, block_side)
    unlisted = float(devices * slab_width - block_side * listed_count)
    kept_mass = 1.0 - tail_share
    log_norm = student_max + jnp.log(student_sum)
    row_loss = (
        kept_mass * (jnp.log(kept_mass) - teacher_max - jnp.log(teacher_sum))
        + kept_mass * self_sum / teacher_sum
        + tail_share * jnp.log(tail_share / unlisted)
        - kept_mass * cross_sum / teacher_sum
        - tail_share / unlisted * (logit_total - listed_total)
        + log_norm
    )
    token_loss = lax.dynamic_slice_in_dim(
        row_loss.reshape(tokens), rank_self * shard_rows, shard_rows, 0
    )
    student_prob = student_exp / student_sum[:, :, None, None]
    teacher_prob = jnp.where(
        listed_mask,
        (kept_mass / teacher_sum)[:, :, None, None] * teacher_exp,
        (tail_share / unlisted)[:, :, None, None],
    )
    weight = token_weight.reshape(blocks, block_side)[:, :, None, None]
    grad_logits = (
        (weight * (student_prob - teacher_prob)).astype(jnp.bfloat16).reshape(tokens, slab_width)
    )
    grad_head = lax.dot_general(
        gathered, grad_logits, (((0,), (0,)), ((), ())), preferred_element_type=jnp.float32
    ).astype(jnp.bfloat16)
    grad_hidden = lax.psum_scatter(
        lax.dot_general(
            grad_logits, head_weight, (((1,), (1,)), ((), ())), preferred_element_type=jnp.float32
        ),
        "vocab",
        scatter_dimension=0,
        tiled=True,
    ).astype(jnp.bfloat16)
    return (token_loss, grad_head, grad_hidden)


CORES = 2
CHIPS = 4
GROUP = CORES * CHIPS
SLOTS = 4
VMEM_LIMIT = 30 * 1024 * 1024


def kernel_params():
    return pltpu.CompilerParams(vmem_limit_bytes=VMEM_LIMIT)


def vmem_spec():
    return pl.BlockSpec(memory_space=pltpu.VMEM)


def hbm_spec():
    return pl.BlockSpec(memory_space=pltpu.HBM)


def smem_spec():
    return pl.BlockSpec(memory_space=pltpu.SMEM)


def shift(x, distance):
    n = lax.axis_size("vocab")
    return lax.ppermute(x, "vocab", [(i, i ^ distance) for i in range(n)])


def token_places(place, rows, side):
    row = lax.broadcasted_iota(jnp.int32, (side, 1), 0)
    group = row // rows
    chip = (group % CHIPS) ^ place[1]
    core = (group // CHIPS) ^ place[0]
    return (chip * CORES + core) * rows + row % rows


def pick_column(match, values):
    return jnp.sum(jnp.where(match, values, 0.0), axis=1, keepdims=True)


def teacher_kernel(
    unlisted, rows, pos_ref, place_ref, blocks_ref, stat_ref, reader_ref, tail_ref, prob_ref, entropy_ref
):
    layers, slots, side, _ = blocks_ref.shape
    pos = [pos_ref[i] for i in range(3)]
    lane = lax.broadcasted_iota(jnp.int32, (1, side), 1)
    where_token = token_places(pos, rows, side)
    for k in range(layers):
        block = pos[2] ^ k
        match = reader_ref[block] == where_token
        onehot = jnp.where(match, 1.0, 0.0).astype(jnp.bfloat16)
        normaliser = pick_column(match, stat_ref[0, block])
        tail = pick_column(lane == where_token, tail_ref[block])
        kept = 1.0 - tail
        rest = tail / unlisted
        span = pl.ds(k * side, side)
        prob_ref[span, :] = jnp.broadcast_to(rest, (side, prob_ref.shape[1]))
        for s in range(slots):
            place = place_ref[block, s]
            values = jnp.dot(onehot, blocks_ref[block, s], preferred_element_type=jnp.float32)
            prob = kept * jnp.exp(values - normaliser)

            @pl.when(place >= 0)
            def _():
                prob_ref[span, pl.ds(pl.multiple_of(place * side, side), side)] = prob

        if k == 0:
            mean = pick_column(match, stat_ref[1, block])
            entropy = kept * (jnp.log(kept) - normaliser + mean) + tail * jnp.log(rest)
            entropy_ref[...] = jnp.broadcast_to(entropy[:rows], entropy_ref.shape)


def assemble(pieces, layer, rows, out_ref):
    layers = out_ref.shape[0] // (GROUP * rows)
    for core, piece in enumerate(pieces):
        for chip in range(CHIPS):
            for i in range(layers):
                block = (layer ^ i) * GROUP + core * CHIPS + chip
                out_ref[pl.ds(pl.multiple_of(block * rows, rows), rows), :] = piece[
                    pl.ds((chip * layers + i) * rows, rows), :
                ]


def logits_kernel(rows, by_rank, first, last, pos_ref, *refs):
    pieces, w_ref, refs = refs[:CORES], refs[CORES], refs[CORES + 1 :]
    if last:
        before_ref, prob_ref, logits_ref, stat_ref, hidden, tiles, sems, cross_ref = refs
    else:
        logits_ref, hidden, tiles, sems = refs
    step, steps = pl.program_id(0), w_ref.shape[1] // tiles.shape[2]
    chunk, width = tiles.shape[1:]

    def copy(t, slot):
        column = pl.multiple_of(t * width, width)
        return pltpu.make_async_copy(
            w_ref.at[pl.ds(first, chunk), pl.ds(column, width)], tiles.at[slot], sems.at[slot]
        )

    @pl.when(step == 0)
    def _():
        for t in range(min(2, steps)):
            copy(t, t).start()
        assemble(pieces, pos_ref[2] if by_rank else 0, rows, hidden)

    copy(step, step % 2).wait()
    part = jnp.dot(hidden[...], tiles[step % 2], preferred_element_type=jnp.float32)

    @pl.when(step + 2 < steps)
    def _():
        copy(step + 2, step % 2).start()

    if not last:
        logits_ref[...] = part
        return
    part = part + before_ref[...]
    logits_ref[:, pl.ds(pl.multiple_of(step * width, width), width)] = part
    product = part * prob_ref[...]
    folded = product[:, :128]
    for i in range(1, width // 128):
        folded = folded + product[:, i * 128 : (i + 1) * 128]

    @pl.when(step == 0)
    def _():
        cross_ref[...] = folded

    @pl.when(step > 0)
    def _():
        cross_ref[...] += folded

    @pl.when(step == pl.num_programs(0) - 1)
    def _():
        logits = logits_ref[...]
        top = jnp.max(logits, axis=1, keepdims=True)
        norm = top + jnp.log(jnp.sum(jnp.exp(logits - top), axis=1, keepdims=True))
        cross = jnp.sum(cross_ref[...], axis=1, keepdims=True)
        lane = lax.broadcasted_iota(jnp.int32, (1, 128), 1)
        both = jnp.where(lane == 0, norm, jnp.where(lane == 1, cross, 0.0))
        both = both.T
        tokens = logits.shape[0]
        packed = [both[i : i + 1, t : t + 128] for i in range(2) for t in range(0, tokens, 128)]
        stat_ref[...] = jnp.broadcast_to(jnp.concatenate(packed, axis=0)[None], stat_ref.shape)


def grad_kernel(
    rows, pos_ref, stat_ref, logits_ref, prob_ref, weight_ref, entropy_ref, grad_ref, loss_ref
):
    tokens = logits_ref.shape[0]
    devices = tokens // rows
    layers, _, side = weight_ref.shape
    layer_bits = (devices // GROUP).bit_length() - 1
    pos = [pos_ref[i] for i in range(3)]
    rank = pos_ref[3]
    lane = lax.broadcasted_iota(jnp.int32, (1, 128), 1)
    per_stat = stat_ref.shape[1] // 2
    norms, crosses = [
        jnp.concatenate([stat_ref[:, i * per_stat + t, :] for t in range(per_stat)], axis=1) for i in range(2)
    ]
    stat = jnp.concatenate(
        [norms, crosses, jnp.zeros((128 - 2 * devices, tokens), jnp.float32)], axis=0
    ).T
    pairs = [(0, 2), (1, 0), (2, 1)] + [(3 + i, 3 + i) for i in range(layer_bits)]
    for index_bit, block_bit in pairs:
        halves = stat.reshape(devices >> (block_bit + 1), 2, rows << block_bit, 128)
        swapped = jnp.stack([halves[:, 1], halves[:, 0]], axis=1).reshape(tokens, 128)
        stat = jnp.where(((lane ^ rank) >> index_bit) & 1 == 1, swapped, stat)
    is_norm = lane < devices
    is_cross = (lane >= devices) & (lane < 2 * devices)
    top = jnp.max(jnp.where(is_norm, stat, -jnp.inf), axis=1, keepdims=True)
    total = jnp.sum(jnp.where(is_norm, jnp.exp(stat - top), 0.0), axis=1, keepdims=True)
    log_norm = top + jnp.log(total)
    cross = jnp.sum(jnp.where(is_cross, stat, 0.0), axis=1, keepdims=True)
    loss_ref[...] = entropy_ref[...] - cross[:rows] + log_norm[:rows]
    where_token = token_places(pos, rows, side)
    for k in range(layers):
        span = pl.ds(k * side, side)
        weight = pick_column(lane == where_token, weight_ref[pos[2] ^ k])
        student = jnp.exp(logits_ref[span, :] - log_norm[k * side : (k + 1) * side])
        grad_ref[span, :] = (weight * (student - prob_ref[span, :])).astype(grad_ref.dtype)


def partial_kernel(rows, first, steps, stacked, pos_ref, grad_ref, sib_ref, w_ref, sib_w_ref, *refs):
    outs, (swapped, tiles, sems) = refs[:-3], refs[-3:]
    tokens = grad_ref.shape[0]
    layers = tokens // (GROUP * rows)
    half = CHIPS * rows
    step = pl.program_id(0)
    tile = tiles.shape[1]
    start = pos_ref[0] * (w_ref.shape[0] // CORES) + first

    def copy(t, slot):
        row = pl.multiple_of(start + t * tile, 128)
        return pltpu.make_async_copy(w_ref.at[pl.ds(row, tile), :], tiles.at[slot], sems.at[slot])

    @pl.when(step == 0)
    def _():
        for t in range(min(2, steps)):
            copy(t, t).start()
        for k in range(layers):
            for core in range(CORES):
                swapped[pl.ds((k * CORES + core) * half, half), :] = sib_ref[
                    pl.ds((k * CORES + 1 - core) * half, half), :
                ]

    contract = (((1,), (1,)), ((), ()))
    span = pl.ds(pl.multiple_of(first + step * tile, tile), tile)
    total = lax.dot_general(swapped[...], sib_w_ref[span, :], contract, preferred_element_type=jnp.float32)
    copy(step, step % 2).wait()
    total += lax.dot_general(grad_ref[...], tiles[step % 2], contract, preferred_element_type=jnp.float32)

    @pl.when(step + 2 < steps)
    def _():
        copy(step + 2, step % 2).start()

    for j in range(CHIPS):
        for k in range(layers):
            for core in range(CORES):
                row = (k * GROUP + core * CHIPS + j) * rows
                part = total[row : row + rows]
                if stacked:
                    outs[0][pos_ref[1] ^ j, k, core] = part.astype(outs[0].dtype)
                else:
                    outs[j][k, core] = part.astype(outs[j].dtype)


def head_kernel(rows, chunk_steps, pos_ref, *refs):
    pieces, (grad_ref, out_ref, hidden) = refs[:-3], refs[-3:]
    chunk = pl.program_id(0) // chunk_steps

    @pl.when(chunk == 0)
    def _():
        assemble(pieces[:CORES], 0, rows, hidden)

    @pl.when(chunk == 1)
    def _():
        assemble(pieces[CORES:], pos_ref[2], rows, hidden)

    out_ref[...] = lax.dot_general(
        hidden[...], grad_ref[...], (((0,), (0,)), ((), ())), preferred_element_type=jnp.float32
    ).astype(out_ref.dtype)


def total_of(parts_ref, index=()):
    total = parts_ref[(0, *index)].astype(jnp.float32)
    for i in range(1, parts_ref.shape[0]):
        total = total + parts_ref[(i, *index)].astype(jnp.float32)
    return total


def chip_sum_kernel(own_ref, *refs):
    arrived, outs = refs[: CHIPS - 1], refs[CHIPS - 1 :]
    for k, out in enumerate(outs):
        total = own_ref[k]
        for part in arrived:
            total = total + part[k].astype(jnp.float32)
        out[...] = total.astype(out.dtype)


def chip_sum_stacked_kernel(pos_ref, parts_ref, out_ref):
    for k in range(out_ref.shape[0]):
        out_ref[pos_ref[2] ^ k] = total_of(parts_ref, (k,)).astype(out_ref.dtype)


def last_sum_kernel(own_ref, *refs):
    arrived, (stacked_ref, mine, theirs) = refs[:-3], refs[-3:]
    first = own_ref[...]
    for part in arrived:
        first = first + part[...].astype(jnp.float32)
    second = total_of(stacked_ref)
    split, end = first.shape[-1], mine.shape[1]
    for core, out in enumerate((mine, theirs)):
        out[:, :split] = first[core].astype(out.dtype)
        out[:, split:end] = second[core].astype(out.dtype)


def split_three(x):
    high = lax.reduce_precision(x, 8, 7)
    middle = lax.reduce_precision(x - high, 8, 7)
    low = x - high - middle
    return jnp.stack([high, middle, low]).astype(jnp.bfloat16)


def send_teacher(teacher_logits, block_lists, places, after):
    blocks, listed_count, stored, side = teacher_logits.shape
    n = lax.axis_size("vocab")
    rank = lax.axis_index("vocab")
    owner = block_lists // places
    earlier = jnp.tril(jnp.ones((listed_count, listed_count), jnp.bool_), -1)
    slot = jnp.sum((owner[:, :, None] == owner[:, None, :]) & earlier, axis=2, dtype=jnp.int32)
    code = owner * SLOTS + slot
    picker = (code[:, None, :] == jnp.arange(n * SLOTS, dtype=jnp.int32)[None, :, None]).astype(jnp.bfloat16)
    packed = jnp.einsum(
        "tsk,tkrc->tsrc", picker, teacher_logits, preferred_element_type=jnp.float32
    ).astype(jnp.bfloat16)
    packed = packed.reshape(blocks, n, SLOTS * stored, side).transpose(1, 0, 2, 3)
    values = teacher_logits.astype(jnp.float32)
    top = jnp.max(values, axis=(1, 3))
    powers = jnp.exp(values - top[:, None, :, None])
    total = jnp.sum(powers, axis=(1, 3))
    mean = jnp.sum(powers * values, axis=(1, 3)) / total
    stat = split_three(jnp.stack([top + jnp.log(total), mean])).reshape(-1)
    stat = jnp.pad(stat, (0, side - stat.shape[0]))
    payload = jnp.concatenate(
        [packed.reshape(n, -1, side), jnp.broadcast_to(stat, (n, 1, side))], axis=1
    )
    payload, _ = lax.optimization_barrier((payload, after))
    arrived = lax.all_to_all(payload, "vocab", split_axis=0, concat_axis=0, tiled=True)
    arrived_blocks = (
        arrived[:, :-1]
        .reshape(n, blocks, SLOTS, stored, side)
        .transpose(1, 2, 0, 3, 4)
        .reshape(blocks, SLOTS, n * stored, side)
    )
    arrived_stat = (
        arrived[:, -1, : 6 * blocks * stored]
        .astype(jnp.float32)
        .reshape(n, 3, 2, blocks, stored)
        .sum(axis=1)
        .transpose(1, 2, 0, 3)
        .reshape(2, blocks, 1, n * stored)
    )
    mine = code[:, None, :] == rank * SLOTS + jnp.arange(SLOTS, dtype=jnp.int32)[None, :, None]
    place = jnp.sum(jnp.where(mine, (block_lists % places + 1)[:, None, :], 0), axis=2) - 1
    return arrived_blocks, arrived_stat, place.astype(jnp.int32)


def levels_plan(
    hidden_states, head_weight, teacher_logits, block_lists, row_reader, tail_mass, token_weight
):
    blocks, listed_count, stored, side = teacher_logits.shape
    rows, depth = hidden_states.shape
    slab = head_weight.shape[1]
    n = lax.axis_size("vocab")
    rank = lax.axis_index("vocab")
    tokens = n * rows
    layers = n // GROUP
    half = depth // CORES
    bf16, f32 = jnp.bfloat16, jnp.float32
    core, chip, layer = rank % CORES, (rank // CORES) % CHIPS, rank // GROUP
    pos = jnp.stack([core, chip, layer, rank]).astype(jnp.int32)
    unlisted = float(n * slab - side * listed_count)
    in_layer = [[(o * CHIPS + q) * CORES + c for q in range(CHIPS)] for o in range(layers) for c in range(CORES)]
    across = [[o * GROUP + i for o in range(layers)] for i in range(GROUP)]

    chunk = depth // 2
    column = hidden_states[:, :chunk]
    column = jnp.concatenate([column] + [shift(column, k * GROUP) for k in range(1, layers)], axis=0)
    late_column = jnp.broadcast_to(hidden_states[None, :, chunk:], (layers, rows, chunk))
    late_column = lax.all_to_all(
        late_column.reshape(layers * rows, chunk),
        "vocab",
        split_axis=0,
        concat_axis=0,
        axis_index_groups=across,
        tiled=True,
    )
    sib_w = shift(lax.dynamic_slice(head_weight, ((1 - core) * half, 0), (half, slab)), 1)
    plane = [column] + [shift(column, j * CORES) for j in range(1, CHIPS)]
    arrived_blocks, arrived_stat, place = send_teacher(
        teacher_logits, block_lists, slab // side, late_column
    )
    late_column, plane[1], sib_w = lax.optimization_barrier((late_column, plane[1], sib_w))
    late_plane = [late_column] + [shift(late_column, j * CORES) for j in range(1, CHIPS)]
    plane = jnp.concatenate(plane, axis=0)
    hidden = [plane, shift(plane, 1)]

    prob, entropy = pl.pallas_call(
        lambda *refs: teacher_kernel(unlisted, rows, *refs),
        out_shape=(
            jax.ShapeDtypeStruct((tokens, slab), f32),
            jax.ShapeDtypeStruct((rows, side), f32),
        ),
        in_specs=[smem_spec(), smem_spec()] + [vmem_spec()] * 4,
        out_specs=(vmem_spec(), vmem_spec()),
        compiler_params=kernel_params(),
        cost_estimate=pl.CostEstimate(
            flops=2 * tokens * side * side * SLOTS, bytes_accessed=4 * tokens * slab, transcendentals=0
        ),
        name="teacher_prob",
    )(
        pos,
        place,
        arrived_blocks,
        arrived_stat,
        row_reader.reshape(blocks, 1, side),
        tail_mass.reshape(blocks, 1, side),
    )

    width = 256 if slab % 256 == 0 else 128
    whole = lambda t: (0, 0)
    tile_out = pl.BlockSpec((tokens, width), lambda t: (0, t))

    def logits_call(pieces, first, before=None):
        last = before is not None
        out_shape = [jax.ShapeDtypeStruct((tokens, slab), f32)]
        out_specs = [tile_out]
        scratch = [
            pltpu.VMEM((tokens, chunk), bf16),
            pltpu.VMEM((2, chunk, width), bf16),
            pltpu.SemaphoreType.DMA((2,)),
        ]
        if last:
            scratch.append(pltpu.VMEM((tokens, 128), f32))
            out_shape.append(jax.ShapeDtypeStruct((n, 2 * tokens // 128, 128), f32))
            out_specs = [
                pl.BlockSpec((tokens, slab), whole),
                pl.BlockSpec((n, 2 * tokens // 128, 128), lambda t: (0, 0, 0)),
            ]
        return pl.pallas_call(
            functools.partial(logits_kernel, rows, last, first, last),
            grid=(slab // width,),
            out_shape=out_shape,
            in_specs=[smem_spec()] + [vmem_spec()] * CORES + [hbm_spec()] + [tile_out] * (2 * last),
            out_specs=out_specs,
            scratch_shapes=scratch,
            compiler_params=kernel_params(),
            cost_estimate=pl.CostEstimate(
                flops=2 * tokens * chunk * slab,
                bytes_accessed=2 * chunk * (slab + tokens) + 4 * tokens * slab,
                transcendentals=tokens * slab if last else 0,
            ),
            name="logits",
        )(pos, *pieces, head_weight, *((before, prob) if last else ()))

    (logits,) = logits_call(hidden, 0)
    late_plane, logits, prob = lax.optimization_barrier((late_plane, logits, prob))
    late_plane = jnp.concatenate(late_plane, axis=0)
    late_hidden = [late_plane, shift(late_plane, 1)]
    logits, stat = logits_call(late_hidden, chunk, logits)
    stat = lax.all_to_all(stat, "vocab", split_axis=0, concat_axis=0, tiled=True)

    grad, loss = pl.pallas_call(
        lambda *refs: grad_kernel(rows, *refs),
        out_shape=(
            jax.ShapeDtypeStruct((tokens, slab), bf16),
            jax.ShapeDtypeStruct((rows, side), f32),
        ),
        in_specs=[smem_spec()] + [vmem_spec()] * 5,
        out_specs=(vmem_spec(), vmem_spec()),
        compiler_params=kernel_params(),
        cost_estimate=pl.CostEstimate(
            flops=4 * tokens * slab, bytes_accessed=10 * tokens * slab, transcendentals=tokens * slab
        ),
        name="grad_logits",
    )(pos, stat, logits, prob, token_weight.reshape(blocks, 1, side), entropy)
    sib_grad = shift(grad, 1)

    tile = half // 5
    sizes = (3 * tile, 2 * tile)
    late_grad, later_sib_w = grad, sib_w
    partials = []
    for i, size in enumerate(sizes):
        first = sum(sizes[:i])
        stacked = i == 1
        if stacked:
            shapes = [(CHIPS, layers, CORES, rows)]
        else:
            shapes = [(layers, CORES, rows)] * CHIPS
        outs = pl.pallas_call(
            functools.partial(partial_kernel, rows, first, size // tile, stacked),
            grid=(size // tile,),
            in_specs=[smem_spec(), vmem_spec(), vmem_spec(), hbm_spec(), vmem_spec()],
            out_specs=[
                pl.BlockSpec((*shape, tile), lambda t, count=len(shape): (0,) * count + (t,)) for shape in shapes
            ],
            out_shape=[
                jax.ShapeDtypeStruct((*shape, size), f32 if j == 0 and not stacked else bf16)
                for j, shape in enumerate(shapes)
            ],
            scratch_shapes=[
                pltpu.VMEM((tokens, slab), bf16),
                pltpu.VMEM((2, tile, slab), bf16),
                pltpu.SemaphoreType.DMA((2,)),
            ],
            compiler_params=kernel_params(),
            cost_estimate=pl.CostEstimate(
                flops=4 * tokens * size * slab, bytes_accessed=4 * size * slab, transcendentals=0
            ),
            name="grad_hidden_partial",
        )(pos, late_grad, sib_grad, head_weight, later_sib_w)
        *outs, late_grad, later_sib_w = lax.optimization_barrier((*outs, late_grad, later_sib_w))
        partials.append(outs)
    arrived = [shift(partials[0][j], j * CORES) for j in range(1, CHIPS)]
    late_arrived = lax.all_to_all(
        partials[1][0], "vocab", split_axis=0, concat_axis=0, axis_index_groups=in_layer, tiled=True
    )

    head_tile = chunk // 2
    piece_specs = [
        pl.BlockSpec((tokens // CORES, head_tile), lambda t, i=i: (0, jnp.clip(t - 2 * i, 0, 1)))
        for i in (0, 0, 1, 1)
    ]
    grad_head = pl.pallas_call(
        functools.partial(head_kernel, rows, 2),
        grid=(4,),
        in_specs=[smem_spec()] + piece_specs + [vmem_spec()],
        out_specs=pl.BlockSpec((head_tile, slab), lambda t: (t, 0)),
        out_shape=jax.ShapeDtypeStruct((depth, slab), bf16),
        scratch_shapes=[pltpu.VMEM((tokens, head_tile), bf16)],
        compiler_params=kernel_params(),
        cost_estimate=pl.CostEstimate(
            flops=2 * tokens * depth * slab, bytes_accessed=2 * depth * (slab + tokens), transcendentals=0
        ),
        name="grad_head",
    )(pos, *hidden, *late_hidden, late_grad)
    arrived, grad_head = lax.optimization_barrier((arrived, grad_head))

    summed = pl.pallas_call(
        chip_sum_kernel,
        in_specs=[vmem_spec()] * CHIPS,
        out_specs=[vmem_spec()] * layers,
        out_shape=[
            jax.ShapeDtypeStruct((CORES, rows, sizes[0]), f32 if k == 0 else bf16) for k in range(layers)
        ],
        compiler_params=kernel_params(),
        cost_estimate=pl.CostEstimate(
            flops=tokens * sizes[0], bytes_accessed=3 * tokens * sizes[0], transcendentals=0
        ),
        name="chip_sum",
    )(partials[0][0], *arrived)
    arrived = [shift(summed[k], k * GROUP) for k in range(1, layers)]
    late_summed = pl.pallas_call(
        chip_sum_stacked_kernel,
        in_specs=[smem_spec(), vmem_spec()],
        out_specs=vmem_spec(),
        out_shape=jax.ShapeDtypeStruct((layers, CORES, rows, sizes[1]), bf16),
        compiler_params=kernel_params(),
        cost_estimate=pl.CostEstimate(
            flops=tokens * sizes[1], bytes_accessed=3 * tokens * sizes[1], transcendentals=0
        ),
        name="chip_sum",
    )(pos, late_arrived)
    late_arrived = lax.all_to_all(
        late_summed, "vocab", split_axis=0, concat_axis=0, axis_index_groups=across, tiled=True
    )
    mine, theirs = pl.pallas_call(
        last_sum_kernel,
        in_specs=[vmem_spec()] * (layers + 1),
        out_specs=[vmem_spec()] * 2,
        out_shape=[jax.ShapeDtypeStruct((rows, half), bf16)] * 2,
        compiler_params=kernel_params(),
        cost_estimate=pl.CostEstimate(
            flops=CORES * layers * rows * half, bytes_accessed=3 * CORES * layers * rows * half, transcendentals=0
        ),
        name="last_sum",
    )(summed[0], *arrived, late_arrived)
    other = shift(theirs, 1)

    low, high = jnp.where(core == 0, mine, other), jnp.where(core == 0, other, mine)
    return loss[:, 0], grad_head, jnp.concatenate([low, high], axis=1)


def fits_levels(hidden_states, teacher_logits):
    n = lax.axis_size("vocab")
    rows = hidden_states.shape[0]
    blocks, _, stored, side = teacher_logits.shape
    return (
        n == blocks * GROUP
        and blocks & (blocks - 1) == 0
        and rows * GROUP == side
        and rows % 16 == 0
        and 2 * n <= side
        and 6 * blocks * stored <= side
        and hidden_states.shape[1] % (CORES * 1280) == 0
    )


def on_device(
    hidden_states, head_weight, teacher_logits, block_lists, row_reader, tail_mass, token_weight
):
    plan = levels_plan if fits_levels(hidden_states, teacher_logits) else plain_plan
    return plan(
        hidden_states, head_weight, teacher_logits, block_lists, row_reader, tail_mass, token_weight
    )


def solution(mesh):
    in_specs = (
        P("vocab", None),
        P(None, "vocab"),
        P(None, None, "vocab", None),
        P(),
        P(),
        P(),
        P(),
    )
    out_specs = (P("vocab"), P(None, "vocab"), P("vocab", None))
    return jax.shard_map(
        on_device, mesh=mesh, in_specs=in_specs, out_specs=out_specs, check_vma=False
    )
```

```python
import functools

import jax
import jax.numpy as jnp
from jax import lax
from jax.experimental import pallas as pl
from jax.experimental.pallas import tpu as pltpu
from jax.sharding import PartitionSpec as P


def row_parts(scores, teacher_slab, listed_mask, student_exp, teacher_exp):
    return (
        jnp.sum(student_exp, axis=(2, 3)),
        jnp.sum(teacher_exp, axis=(2, 3)),
        jnp.sum(teacher_exp * scores, axis=(2, 3)),
        jnp.sum(teacher_exp * teacher_slab, axis=(2, 3)),
        jnp.sum(scores, axis=(2, 3)),
        jnp.sum(jnp.where(listed_mask, scores, 0.0), axis=(2, 3)),
    )


def plain_plan(
    hidden_states, head_weight, teacher_logits, block_lists, row_reader, tail_mass, token_weight
):
    blocks, listed_count, stored_rows, block_side = teacher_logits.shape
    slab_width = head_weight.shape[1]
    slab_blocks = slab_width // block_side
    devices = lax.axis_size("vocab")
    rank_self = lax.axis_index("vocab")
    tokens = blocks * block_side
    shard_rows = hidden_states.shape[0]
    gathered = lax.all_gather(hidden_states, "vocab", axis=0, tiled=True)
    logits = jnp.dot(gathered, head_weight, preferred_element_type=jnp.float32)
    owner_dev = block_lists // slab_blocks
    owned_here = owner_dev == rank_self
    within = block_lists - rank_self * slab_blocks
    token_iota = lax.broadcasted_iota(jnp.int32, (1, block_side, block_side), 1)
    token_map = (row_reader[:, None, :] == token_iota).astype(jnp.bfloat16)
    place_iota = lax.broadcasted_iota(jnp.int32, (1, slab_blocks, 1), 1)
    block_iota = lax.broadcasted_iota(jnp.int32, (1, devices * slab_blocks, 1), 1)
    picker = (block_lists[:, None, :] == block_iota).astype(jnp.bfloat16)
    outgoing = jnp.einsum(
        "tnk,tkrc->tnrc", picker, teacher_logits, preferred_element_type=jnp.float32
    ).astype(jnp.bfloat16)
    incoming = lax.all_to_all(outgoing, "vocab", split_axis=1, concat_axis=2, tiled=True)
    teacher_slab = jnp.einsum(
        "tpj,tbjc->tpbc", token_map, incoming, preferred_element_type=jnp.float32
    )
    listed = jnp.sum(
        ((within[:, None, :] == place_iota) & owned_here[:, None, :]).astype(jnp.int32), axis=2
    )
    scores = logits.reshape(blocks, block_side, slab_blocks, block_side)
    listed_mask = (listed > 0)[:, None, :, None]
    local_smax = jnp.max(scores, axis=(2, 3))
    local_tmax = jnp.max(jnp.where(listed_mask, teacher_slab, -1e30), axis=(2, 3))
    student_max, teacher_max = lax.pmax((local_smax, local_tmax), "vocab")
    student_exp = jnp.exp(scores - student_max[:, :, None, None])
    teacher_exp = jnp.exp(
        jnp.where(listed_mask, teacher_slab - teacher_max[:, :, None, None], -jnp.inf)
    )
    parts = row_parts(scores, teacher_slab, listed_mask, student_exp, teacher_exp)
    student_sum, teacher_sum, cross_sum, self_sum, logit_total, listed_total = lax.psum(
        (parts[0], parts[1], parts[2], parts[3], parts[4], parts[5]), "vocab"
    )
    tail_share = tail_mass.reshape(blocks, block_side)
    unlisted = float(devices * slab_width - block_side * listed_count)
    kept_mass = 1.0 - tail_share
    log_norm = student_max + jnp.log(student_sum)
    row_loss = (
        kept_mass * (jnp.log(kept_mass) - teacher_max - jnp.log(teacher_sum))
        + kept_mass * self_sum / teacher_sum
        + tail_share * jnp.log(tail_share / unlisted)
        - kept_mass * cross_sum / teacher_sum
        - tail_share / unlisted * (logit_total - listed_total)
        + log_norm
    )
    token_loss = lax.dynamic_slice_in_dim(
        row_loss.reshape(tokens), rank_self * shard_rows, shard_rows, 0
    )
    student_prob = student_exp / student_sum[:, :, None, None]
    teacher_prob = jnp.where(
        listed_mask,
        (kept_mass / teacher_sum)[:, :, None, None] * teacher_exp,
        (tail_share / unlisted)[:, :, None, None],
    )
    weight = token_weight.reshape(blocks, block_side)[:, :, None, None]
    grad_logits = (
        (weight * (student_prob - teacher_prob)).astype(jnp.bfloat16).reshape(tokens, slab_width)
    )
    grad_head = lax.dot_general(
        gathered, grad_logits, (((0,), (0,)), ((), ())), preferred_element_type=jnp.float32
    ).astype(jnp.bfloat16)
    grad_hidden = lax.psum_scatter(
        lax.dot_general(
            grad_logits, head_weight, (((1,), (1,)), ((), ())), preferred_element_type=jnp.float32
        ),
        "vocab",
        scatter_dimension=0,
        tiled=True,
    ).astype(jnp.bfloat16)
    return (token_loss, grad_head, grad_hidden)


CORES = 2
CHIPS = 4
GROUP = CORES * CHIPS
SLOTS = 4
LIGHT = pl.CostEstimate(flops=1, bytes_accessed=1, transcendentals=0)
SMALL_VMEM = 24 * 1024 * 1024
LARGE_VMEM = 56 * 1024 * 1024


def kernel_params(limit=SMALL_VMEM):
    return pltpu.CompilerParams(vmem_limit_bytes=limit)


def vmem_spec():
    return pl.BlockSpec(memory_space=pltpu.VMEM)


def hbm_spec():
    return pl.BlockSpec(memory_space=pltpu.HBM)


def smem_spec():
    return pl.BlockSpec(memory_space=pltpu.SMEM)


def shift(x, distance):
    n = lax.axis_size("vocab")
    return lax.ppermute(x, "vocab", [(i, i ^ distance) for i in range(n)])


def token_places(place, rows, side):
    row = lax.broadcasted_iota(jnp.int32, (side, 1), 0)
    group = row // rows
    chip = (group % CHIPS) ^ place[1]
    core = (group // CHIPS) ^ place[0]
    return (chip * CORES + core) * rows + row % rows


def pick_column(match, values):
    return jnp.sum(jnp.where(match, values, 0.0), axis=1, keepdims=True)


def teacher_kernel(
    unlisted, rows, pos_ref, place_ref, blocks_ref, stat_ref, reader_ref, tail_ref, prob_ref, entropy_ref
):
    layers, slots, side, _ = blocks_ref.shape
    pos = [pos_ref[i] for i in range(3)]
    lane = lax.broadcasted_iota(jnp.int32, (1, side), 1)
    where_token = token_places(pos, rows, side)
    for k in range(layers):
        block = pos[2] ^ k
        match = reader_ref[block] == where_token
        onehot = jnp.where(match, 1.0, 0.0).astype(jnp.bfloat16)
        normaliser = pick_column(match, stat_ref[0, block])
        tail = pick_column(lane == where_token, tail_ref[block])
        kept = 1.0 - tail
        rest = tail / unlisted
        span = pl.ds(k * side, side)
        prob_ref[span, :] = jnp.broadcast_to(rest, (side, prob_ref.shape[1]))
        for s in range(slots):
            place = place_ref[block, s]
            values = jnp.dot(onehot, blocks_ref[block, s], preferred_element_type=jnp.float32)
            prob = kept * jnp.exp(values - normaliser)

            @pl.when(place >= 0)
            def _():
                prob_ref[span, pl.ds(pl.multiple_of(place * side, side), side)] = prob

        if k == 0:
            mean = pick_column(match, stat_ref[1, block])
            entropy = kept * (jnp.log(kept) - normaliser + mean) + tail * jnp.log(rest)
            entropy_ref[...] = jnp.broadcast_to(entropy[:rows], entropy_ref.shape)


def assemble(pieces, rows, out_ref):
    layers = out_ref.shape[0] // (GROUP * rows)
    for core, piece in enumerate(pieces):
        for chip in range(CHIPS):
            for i in range(layers):
                block = i * GROUP + core * CHIPS + chip
                out_ref[pl.ds(block * rows, rows), :] = piece[
                    pl.ds((chip * layers + i) * rows, rows), :
                ]


def logits_kernel(rows, first, last, *refs):
    pieces, w_ref, refs = refs[:CORES], refs[CORES], refs[CORES + 1 :]
    if last:
        before_ref, prob_ref, logits_ref, stat_ref, hidden, tiles, sems, cross_ref = refs
    else:
        logits_ref, hidden, tiles, sems = refs
    step, steps = pl.program_id(0), w_ref.shape[1] // tiles.shape[2]
    chunk, width = tiles.shape[1:]

    def copy(t, slot):
        column = pl.multiple_of(t * width, width)
        return pltpu.make_async_copy(
            w_ref.at[pl.ds(first, chunk), pl.ds(column, width)], tiles.at[slot], sems.at[slot]
        )

    @pl.when(step == 0)
    def _():
        for t in range(min(2, steps)):
            copy(t, t).start()
        assemble(pieces, rows, hidden)

    copy(step, step % 2).wait()
    part = jnp.dot(hidden[...], tiles[step % 2], preferred_element_type=jnp.float32)

    @pl.when(step + 2 < steps)
    def _():
        copy(step + 2, step % 2).start()

    if not last:
        logits_ref[...] = part
        return
    part = part + before_ref[...]
    logits_ref[:, pl.ds(pl.multiple_of(step * width, width), width)] = part
    product = part * prob_ref[...]
    folded = product[:, :128]
    for i in range(1, width // 128):
        folded = folded + product[:, i * 128 : (i + 1) * 128]

    @pl.when(step == 0)
    def _():
        cross_ref[...] = folded

    @pl.when(step > 0)
    def _():
        cross_ref[...] += folded

    @pl.when(step == pl.num_programs(0) - 1)
    def _():
        logits = logits_ref[...]
        top = jnp.max(logits, axis=1, keepdims=True)
        norm = top + jnp.log(jnp.sum(jnp.exp(logits - top), axis=1, keepdims=True))
        cross = jnp.sum(cross_ref[...], axis=1, keepdims=True)
        lane = lax.broadcasted_iota(jnp.int32, (1, 128), 1)
        both = jnp.where(lane == 0, norm, jnp.where(lane == 1, cross, 0.0))
        both = both.T
        tokens = logits.shape[0]
        packed = [both[i : i + 1, t : t + 128] for i in range(2) for t in range(0, tokens, 128)]
        stat_ref[...] = jnp.broadcast_to(jnp.concatenate(packed, axis=0)[None], stat_ref.shape)


def grad_kernel(
    rows, pos_ref, stat_ref, logits_ref, prob_ref, weight_ref, entropy_ref, grad_ref, loss_ref
):
    tokens = logits_ref.shape[0]
    devices = tokens // rows
    layers, _, side = weight_ref.shape
    layer_bits = (devices // GROUP).bit_length() - 1
    pos = [pos_ref[i] for i in range(3)]
    rank = pos_ref[3]
    lane = lax.broadcasted_iota(jnp.int32, (1, 128), 1)
    per_stat = stat_ref.shape[1] // 2
    norms, crosses = [
        jnp.concatenate([stat_ref[:, i * per_stat + t, :] for t in range(per_stat)], axis=1) for i in range(2)
    ]
    stat = jnp.concatenate(
        [norms, crosses, jnp.zeros((128 - 2 * devices, tokens), jnp.float32)], axis=0
    ).T
    pairs = [(0, 2), (1, 0), (2, 1)] + [(3 + i, 3 + i) for i in range(layer_bits)]
    for index_bit, block_bit in pairs:
        halves = stat.reshape(devices >> (block_bit + 1), 2, rows << block_bit, 128)
        swapped = jnp.stack([halves[:, 1], halves[:, 0]], axis=1).reshape(tokens, 128)
        stat = jnp.where(((lane ^ rank) >> index_bit) & 1 == 1, swapped, stat)
    is_norm = lane < devices
    is_cross = (lane >= devices) & (lane < 2 * devices)
    top = jnp.max(jnp.where(is_norm, stat, -jnp.inf), axis=1, keepdims=True)
    total = jnp.sum(jnp.where(is_norm, jnp.exp(stat - top), 0.0), axis=1, keepdims=True)
    log_norm = top + jnp.log(total)
    cross = jnp.sum(jnp.where(is_cross, stat, 0.0), axis=1, keepdims=True)
    loss_ref[...] = entropy_ref[...] - cross[:rows] + log_norm[:rows]
    where_token = token_places(pos, rows, side)
    for k in range(layers):
        span = pl.ds(k * side, side)
        weight = pick_column(lane == where_token, weight_ref[pos[2] ^ k])
        student = jnp.exp(logits_ref[span, :] - log_norm[k * side : (k + 1) * side])
        grad_ref[span, :] = (weight * (student - prob_ref[span, :])).astype(grad_ref.dtype)


def partial_kernel(rows, stacked, pos_ref, grad_ref, sib_ref, w_ref, sib_w_ref, *refs):
    outs, swapped = refs[:-1], refs[-1]
    layers = grad_ref.shape[0] // (GROUP * rows)
    half = CHIPS * rows

    @pl.when(pl.program_id(0) == 0)
    def _():
        for k in range(layers):
            for core in range(CORES):
                swapped[pl.ds((k * CORES + core) * half, half), :] = sib_ref[
                    pl.ds((k * CORES + 1 - core) * half, half), :
                ]

    contract = (((1,), (1,)), ((), ()))
    total = lax.dot_general(
        grad_ref[...], w_ref[...], contract, preferred_element_type=jnp.float32
    ) + lax.dot_general(swapped[...], sib_w_ref[...], contract, preferred_element_type=jnp.float32)
    for j in range(CHIPS):
        for k in range(layers):
            for core in range(CORES):
                row = (k * GROUP + core * CHIPS + j) * rows
                part = total[row : row + rows]
                if stacked:
                    outs[0][pos_ref[1] ^ j, k, core] = part.astype(outs[0].dtype)
                else:
                    outs[j][k, core] = part.astype(outs[j].dtype)


def head_kernel(rows, chunk_steps, *refs):
    pieces, (grad_ref, out_ref, hidden) = refs[:-3], refs[-3:]
    chunk = pl.program_id(0) // chunk_steps

    @pl.when(chunk == 0)
    def _():
        assemble(pieces[:CORES], rows, hidden)

    @pl.when(chunk == 1)
    def _():
        assemble(pieces[CORES:], rows, hidden)

    out_ref[...] = lax.dot_general(
        hidden[...], grad_ref[...], (((0,), (0,)), ((), ())), preferred_element_type=jnp.float32
    ).astype(out_ref.dtype)


def total_of(parts_ref, index=()):
    total = parts_ref[(0, *index)].astype(jnp.float32)
    for i in range(1, parts_ref.shape[0]):
        total = total + parts_ref[(i, *index)].astype(jnp.float32)
    return total


def chip_sum_kernel(own_ref, *refs):
    arrived, outs = refs[: CHIPS - 1], refs[CHIPS - 1 :]
    for k, out in enumerate(outs):
        total = own_ref[k]
        for part in arrived:
            total = total + part[k].astype(jnp.float32)
        out[...] = total.astype(out.dtype)


def chip_sum_stacked_kernel(pos_ref, parts_ref, out_ref):
    for k in range(out_ref.shape[0]):
        out_ref[pos_ref[2] ^ k] = total_of(parts_ref, (k,)).astype(out_ref.dtype)


def last_sum_kernel(own_ref, *refs):
    arrived, (stacked_ref, mine, theirs) = refs[:-3], refs[-3:]
    first = own_ref[...]
    for part in arrived:
        first = first + part[...].astype(jnp.float32)
    second = total_of(stacked_ref)
    split, end = first.shape[-1], mine.shape[1]
    for core, out in enumerate((mine, theirs)):
        out[:, :split] = first[core].astype(out.dtype)
        out[:, split:end] = second[core].astype(out.dtype)


def split_three(x):
    high = lax.reduce_precision(x, 8, 7)
    middle = lax.reduce_precision(x - high, 8, 7)
    low = x - high - middle
    return jnp.stack([high, middle, low]).astype(jnp.bfloat16)


def send_teacher(teacher_logits, block_lists, places, after):
    blocks, listed_count, stored, side = teacher_logits.shape
    n = lax.axis_size("vocab")
    rank = lax.axis_index("vocab")
    owner = block_lists // places
    earlier = jnp.tril(jnp.ones((listed_count, listed_count), jnp.bool_), -1)
    slot = jnp.sum((owner[:, :, None] == owner[:, None, :]) & earlier, axis=2, dtype=jnp.int32)
    code = owner * SLOTS + slot
    picker = (code[:, None, :] == jnp.arange(n * SLOTS, dtype=jnp.int32)[None, :, None]).astype(jnp.bfloat16)
    packed = jnp.einsum(
        "tsk,tkrc->tsrc", picker, teacher_logits, preferred_element_type=jnp.float32
    ).astype(jnp.bfloat16)
    packed = packed.reshape(blocks, n, SLOTS * stored, side).transpose(1, 0, 2, 3)
    values = teacher_logits.astype(jnp.float32)
    top = jnp.max(values, axis=(1, 3))
    powers = jnp.exp(values - top[:, None, :, None])
    total = jnp.sum(powers, axis=(1, 3))
    mean = jnp.sum(powers * values, axis=(1, 3)) / total
    stat = split_three(jnp.stack([top + jnp.log(total), mean])).reshape(-1)
    stat = jnp.pad(stat, (0, side - stat.shape[0]))
    payload = jnp.concatenate(
        [packed.reshape(n, -1, side), jnp.broadcast_to(stat, (n, 1, side))], axis=1
    )
    payload, _ = lax.optimization_barrier((payload, after))
    arrived = lax.all_to_all(payload, "vocab", split_axis=0, concat_axis=0, tiled=True)
    arrived_blocks = (
        arrived[:, :-1]
        .reshape(n, blocks, SLOTS, stored, side)
        .transpose(1, 2, 0, 3, 4)
        .reshape(blocks, SLOTS, n * stored, side)
    )
    arrived_stat = (
        arrived[:, -1, : 6 * blocks * stored]
        .astype(jnp.float32)
        .reshape(n, 3, 2, blocks, stored)
        .sum(axis=1)
        .transpose(1, 2, 0, 3)
        .reshape(2, blocks, 1, n * stored)
    )
    mine = code[:, None, :] == rank * SLOTS + jnp.arange(SLOTS, dtype=jnp.int32)[None, :, None]
    place = jnp.sum(jnp.where(mine, (block_lists % places + 1)[:, None, :], 0), axis=2) - 1
    return arrived_blocks, arrived_stat, place.astype(jnp.int32)


def levels_plan(
    hidden_states, head_weight, teacher_logits, block_lists, row_reader, tail_mass, token_weight
):
    blocks, listed_count, stored, side = teacher_logits.shape
    rows, depth = hidden_states.shape
    slab = head_weight.shape[1]
    n = lax.axis_size("vocab")
    rank = lax.axis_index("vocab")
    tokens = n * rows
    layers = n // GROUP
    half = depth // CORES
    bf16, f32 = jnp.bfloat16, jnp.float32
    core, chip, layer = rank % CORES, (rank // CORES) % CHIPS, rank // GROUP
    pos = jnp.stack([core, chip, layer, rank]).astype(jnp.int32)
    unlisted = float(n * slab - side * listed_count)
    in_layer = [[(o * CHIPS + q) * CORES + c for q in range(CHIPS)] for o in range(layers) for c in range(CORES)]
    across = [[o * GROUP + i for o in range(layers)] for i in range(GROUP)]

    chunk = depth // 2
    column = hidden_states[:, :chunk]
    column = jnp.concatenate([column] + [shift(column, k * GROUP) for k in range(1, layers)], axis=0)
    sib_w = shift(head_weight, 1)
    late_column, column = lax.optimization_barrier((hidden_states[:, chunk:], column))
    plane = [column] + [shift(column, j * CORES) for j in range(1, CHIPS)]
    for k in [1 << i for i in range((layers - 1).bit_length())]:
        late_column = jnp.concatenate([late_column, shift(late_column, k * GROUP)], axis=0)
    arrived_blocks, arrived_stat, place = send_teacher(teacher_logits, block_lists, slab // side, column)
    late_column, plane[1], sib_w = lax.optimization_barrier((late_column, plane[1], sib_w))
    late_plane = [late_column] + [shift(late_column, j * CORES) for j in range(1, CHIPS)]
    plane = jnp.concatenate(plane, axis=0)
    hidden = [plane, shift(plane, 1)]

    prob, entropy = pl.pallas_call(
        lambda *refs: teacher_kernel(unlisted, rows, *refs),
        out_shape=(
            jax.ShapeDtypeStruct((tokens, slab), f32),
            jax.ShapeDtypeStruct((rows, side), f32),
        ),
        in_specs=[smem_spec(), smem_spec()] + [vmem_spec()] * 4,
        out_specs=(vmem_spec(), vmem_spec()),
        compiler_params=kernel_params(),
        cost_estimate=LIGHT,
        name="teacher_prob",
    )(
        pos,
        place,
        arrived_blocks,
        arrived_stat,
        row_reader.reshape(blocks, 1, side),
        tail_mass.reshape(blocks, 1, side),
    )

    width = 256 if slab % 256 == 0 else 128
    whole = lambda t: (0, 0)
    tile_out = pl.BlockSpec((tokens, width), lambda t: (0, t))

    def logits_call(pieces, first, before=None):
        last = before is not None
        out_shape = [jax.ShapeDtypeStruct((tokens, slab), f32)]
        out_specs = [tile_out]
        scratch = [
            pltpu.VMEM((tokens, chunk), bf16),
            pltpu.VMEM((2, chunk, width), bf16),
            pltpu.SemaphoreType.DMA((2,)),
        ]
        if last:
            scratch.append(pltpu.VMEM((tokens, 128), f32))
            out_shape.append(jax.ShapeDtypeStruct((n, 2 * tokens // 128, 128), f32))
            out_specs = [
                pl.BlockSpec((tokens, slab), whole),
                pl.BlockSpec((n, 2 * tokens // 128, 128), lambda t: (0, 0, 0)),
            ]
        return pl.pallas_call(
            functools.partial(logits_kernel, rows, first, last),
            grid=(slab // width,),
            out_shape=out_shape,
            in_specs=[vmem_spec()] * CORES + [hbm_spec()] + [tile_out] * (2 * last),
            out_specs=out_specs,
            scratch_shapes=scratch,
            compiler_params=kernel_params(LARGE_VMEM),
            cost_estimate=LIGHT,
            name="logits",
        )(*pieces, head_weight, *((before, prob) if last else ()))

    (logits,) = logits_call(hidden, 0)
    late_plane, logits, prob = lax.optimization_barrier((late_plane, logits, prob))
    late_plane = jnp.concatenate(late_plane, axis=0)
    late_hidden = [late_plane, shift(late_plane, 1)]
    logits, stat = logits_call(late_hidden, chunk, logits)
    stat = lax.all_to_all(stat, "vocab", split_axis=0, concat_axis=0, tiled=True)

    grad, loss = pl.pallas_call(
        lambda *refs: grad_kernel(rows, *refs),
        out_shape=(
            jax.ShapeDtypeStruct((tokens, slab), bf16),
            jax.ShapeDtypeStruct((rows, side), f32),
        ),
        in_specs=[smem_spec()] + [vmem_spec()] * 5,
        out_specs=(vmem_spec(), vmem_spec()),
        compiler_params=kernel_params(),
        cost_estimate=LIGHT,
        name="grad_logits",
    )(pos, stat, logits, prob, token_weight.reshape(blocks, 1, side), entropy)
    sib_grad = shift(grad, 1)

    tile = half // 5
    sizes = (3 * tile, 2 * tile)
    late_grad, later_sib_w = grad, sib_w
    partials = []
    for i, size in enumerate(sizes):
        first = sum(sizes[:i])
        stacked = i == 1
        if stacked:
            shapes = [(CHIPS, layers, CORES, rows)]
        else:
            shapes = [(layers, CORES, rows)] * CHIPS
        w_block = pl.BlockSpec((tile, slab), lambda t, pos, first=first: (pos[0] * 5 + first // tile + t, 0))
        outs = pl.pallas_call(
            functools.partial(partial_kernel, rows, stacked),
            grid_spec=pltpu.PrefetchScalarGridSpec(
                num_scalar_prefetch=1,
                grid=(size // tile,),
                in_specs=[pl.BlockSpec((tokens, slab), lambda t, pos: (0, 0))] * 2 + [w_block] * 2,
                out_specs=[
                    pl.BlockSpec((*shape, tile), lambda t, pos, count=len(shape): (0,) * count + (t,))
                    for shape in shapes
                ],
                scratch_shapes=[pltpu.VMEM((tokens, slab), bf16)],
            ),
            out_shape=[
                jax.ShapeDtypeStruct((*shape, size), f32 if j == 0 and not stacked else bf16)
                for j, shape in enumerate(shapes)
            ],
            compiler_params=kernel_params(LARGE_VMEM),
            cost_estimate=LIGHT,
            name="grad_hidden_partial",
        )(pos, late_grad, sib_grad, head_weight, later_sib_w)
        if stacked:
            outs, late_grad = lax.optimization_barrier((outs, late_grad))
        else:
            arrived = [shift(outs[j], j * CORES) for j in range(1, CHIPS)]
            arrived[1], late_grad, later_sib_w = lax.optimization_barrier((arrived[1], late_grad, later_sib_w))
        partials.append(outs)
    late_arrived = lax.all_to_all(
        partials[1][0], "vocab", split_axis=0, concat_axis=0, axis_index_groups=in_layer, tiled=True
    )

    head_tile = chunk // 2
    piece_specs = [
        pl.BlockSpec((tokens // CORES, head_tile), lambda t, i=i: (0, jnp.clip(t - 2 * i, 0, 1)))
        for i in (0, 0, 1, 1)
    ]
    grad_head = pl.pallas_call(
        functools.partial(head_kernel, rows, 2),
        grid=(4,),
        in_specs=piece_specs + [pl.BlockSpec((tokens, slab), whole)],
        out_specs=pl.BlockSpec((head_tile, slab), lambda t: (t, 0)),
        out_shape=jax.ShapeDtypeStruct((depth, slab), bf16),
        scratch_shapes=[pltpu.VMEM((tokens, head_tile), bf16)],
        compiler_params=kernel_params(LARGE_VMEM),
        cost_estimate=LIGHT,
        name="grad_head",
    )(*hidden, *late_hidden, late_grad)
    arrived, grad_head = lax.optimization_barrier((arrived, grad_head))

    summed = pl.pallas_call(
        chip_sum_kernel,
        in_specs=[vmem_spec()] * CHIPS,
        out_specs=[vmem_spec()] * layers,
        out_shape=[
            jax.ShapeDtypeStruct((CORES, rows, sizes[0]), f32 if k == 0 else bf16) for k in range(layers)
        ],
        compiler_params=kernel_params(),
        cost_estimate=LIGHT,
        name="chip_sum",
    )(partials[0][0], *arrived)
    arrived = [shift(summed[k], k * GROUP) for k in range(1, layers)]
    late_summed = pl.pallas_call(
        chip_sum_stacked_kernel,
        in_specs=[smem_spec(), vmem_spec()],
        out_specs=vmem_spec(),
        out_shape=jax.ShapeDtypeStruct((layers, CORES, rows, sizes[1]), bf16),
        compiler_params=kernel_params(),
        cost_estimate=LIGHT,
        name="chip_sum",
    )(pos, late_arrived)
    late_arrived = lax.all_to_all(
        late_summed, "vocab", split_axis=0, concat_axis=0, axis_index_groups=across, tiled=True
    )
    mine, theirs = pl.pallas_call(
        last_sum_kernel,
        in_specs=[vmem_spec()] * (layers + 1),
        out_specs=[vmem_spec()] * 2,
        out_shape=[jax.ShapeDtypeStruct((rows, half), bf16)] * 2,
        compiler_params=kernel_params(),
        cost_estimate=LIGHT,
        name="last_sum",
    )(summed[0], *arrived, late_arrived)
    other = shift(theirs, 1)

    low, high = jnp.where(core == 0, mine, other), jnp.where(core == 0, other, mine)
    return loss[:, 0], grad_head, jnp.concatenate([low, high], axis=1)


def fits_levels(hidden_states, teacher_logits):
    n = lax.axis_size("vocab")
    rows = hidden_states.shape[0]
    blocks, _, stored, side = teacher_logits.shape
    return (
        n == blocks * GROUP
        and blocks & (blocks - 1) == 0
        and rows * GROUP == side
        and rows % 16 == 0
        and 2 * n <= side
        and 6 * blocks * stored <= side
        and hidden_states.shape[1] % (CORES * 1280) == 0
    )


def on_device(
    hidden_states, head_weight, teacher_logits, block_lists, row_reader, tail_mass, token_weight
):
    plan = levels_plan if fits_levels(hidden_states, teacher_logits) else plain_plan
    return plan(
        hidden_states, head_weight, teacher_logits, block_lists, row_reader, tail_mass, token_weight
    )


def solution(mesh):
    in_specs = (
        P("vocab", None),
        P(None, "vocab"),
        P(None, None, "vocab", None),
        P(),
        P(),
        P(),
        P(),
    )
    out_specs = (P("vocab"), P(None, "vocab"), P("vocab", None))
    return jax.shard_map(
        on_device, mesh=mesh, in_specs=in_specs, out_specs=out_specs, check_vma=False
    )
```

```python
import functools

import jax
import jax.numpy as jnp
from jax import lax
from jax.experimental import pallas as pl
from jax.experimental.pallas import tpu as pltpu
from jax.sharding import PartitionSpec as P


def row_parts(scores, teacher_slab, listed_mask, student_exp, teacher_exp):
    return (
        jnp.sum(student_exp, axis=(2, 3)),
        jnp.sum(teacher_exp, axis=(2, 3)),
        jnp.sum(teacher_exp * scores, axis=(2, 3)),
        jnp.sum(teacher_exp * teacher_slab, axis=(2, 3)),
        jnp.sum(scores, axis=(2, 3)),
        jnp.sum(jnp.where(listed_mask, scores, 0.0), axis=(2, 3)),
    )


def plain_plan(
    hidden_states, head_weight, teacher_logits, block_lists, row_reader, tail_mass, token_weight
):
    blocks, listed_count, stored_rows, block_side = teacher_logits.shape
    slab_width = head_weight.shape[1]
    slab_blocks = slab_width // block_side
    devices = lax.axis_size("vocab")
    rank_self = lax.axis_index("vocab")
    tokens = blocks * block_side
    shard_rows = hidden_states.shape[0]
    gathered = lax.all_gather(hidden_states, "vocab", axis=0, tiled=True)
    logits = jnp.dot(gathered, head_weight, preferred_element_type=jnp.float32)
    owner_dev = block_lists // slab_blocks
    owned_here = owner_dev == rank_self
    within = block_lists - rank_self * slab_blocks
    token_iota = lax.broadcasted_iota(jnp.int32, (1, block_side, block_side), 1)
    token_map = (row_reader[:, None, :] == token_iota).astype(jnp.bfloat16)
    place_iota = lax.broadcasted_iota(jnp.int32, (1, slab_blocks, 1), 1)
    block_iota = lax.broadcasted_iota(jnp.int32, (1, devices * slab_blocks, 1), 1)
    picker = (block_lists[:, None, :] == block_iota).astype(jnp.bfloat16)
    outgoing = jnp.einsum(
        "tnk,tkrc->tnrc", picker, teacher_logits, preferred_element_type=jnp.float32
    ).astype(jnp.bfloat16)
    incoming = lax.all_to_all(outgoing, "vocab", split_axis=1, concat_axis=2, tiled=True)
    teacher_slab = jnp.einsum(
        "tpj,tbjc->tpbc", token_map, incoming, preferred_element_type=jnp.float32
    )
    listed = jnp.sum(
        ((within[:, None, :] == place_iota) & owned_here[:, None, :]).astype(jnp.int32), axis=2
    )
    scores = logits.reshape(blocks, block_side, slab_blocks, block_side)
    listed_mask = (listed > 0)[:, None, :, None]
    local_smax = jnp.max(scores, axis=(2, 3))
    local_tmax = jnp.max(jnp.where(listed_mask, teacher_slab, -1e30), axis=(2, 3))
    student_max, teacher_max = lax.pmax((local_smax, local_tmax), "vocab")
    student_exp = jnp.exp(scores - student_max[:, :, None, None])
    teacher_exp = jnp.exp(
        jnp.where(listed_mask, teacher_slab - teacher_max[:, :, None, None], -jnp.inf)
    )
    parts = row_parts(scores, teacher_slab, listed_mask, student_exp, teacher_exp)
    student_sum, teacher_sum, cross_sum, self_sum, logit_total, listed_total = lax.psum(
        (parts[0], parts[1], parts[2], parts[3], parts[4], parts[5]), "vocab"
    )
    tail_share = tail_mass.reshape(blocks, block_side)
    unlisted = float(devices * slab_width - block_side * listed_count)
    kept_mass = 1.0 - tail_share
    log_norm = student_max + jnp.log(student_sum)
    row_loss = (
        kept_mass * (jnp.log(kept_mass) - teacher_max - jnp.log(teacher_sum))
        + kept_mass * self_sum / teacher_sum
        + tail_share * jnp.log(tail_share / unlisted)
        - kept_mass * cross_sum / teacher_sum
        - tail_share / unlisted * (logit_total - listed_total)
        + log_norm
    )
    token_loss = lax.dynamic_slice_in_dim(
        row_loss.reshape(tokens), rank_self * shard_rows, shard_rows, 0
    )
    student_prob = student_exp / student_sum[:, :, None, None]
    teacher_prob = jnp.where(
        listed_mask,
        (kept_mass / teacher_sum)[:, :, None, None] * teacher_exp,
        (tail_share / unlisted)[:, :, None, None],
    )
    weight = token_weight.reshape(blocks, block_side)[:, :, None, None]
    grad_logits = (
        (weight * (student_prob - teacher_prob)).astype(jnp.bfloat16).reshape(tokens, slab_width)
    )
    grad_head = lax.dot_general(
        gathered, grad_logits, (((0,), (0,)), ((), ())), preferred_element_type=jnp.float32
    ).astype(jnp.bfloat16)
    grad_hidden = lax.psum_scatter(
        lax.dot_general(
            grad_logits, head_weight, (((1,), (1,)), ((), ())), preferred_element_type=jnp.float32
        ),
        "vocab",
        scatter_dimension=0,
        tiled=True,
    ).astype(jnp.bfloat16)
    return (token_loss, grad_head, grad_hidden)


CORES = 2
CHIPS = 4
GROUP = CORES * CHIPS
SLOTS = 4
LIGHT = pl.CostEstimate(flops=1, bytes_accessed=1, transcendentals=0)
SMALL_VMEM = 16 * 1024 * 1024
LOGITS_VMEM = 48 * 1024 * 1024
LARGE_VMEM = 52 * 1024 * 1024


def kernel_params(limit=SMALL_VMEM):
    return pltpu.CompilerParams(vmem_limit_bytes=limit)


def vmem_spec():
    return pl.BlockSpec(memory_space=pltpu.VMEM)


def hbm_spec():
    return pl.BlockSpec(memory_space=pltpu.HBM)


def smem_spec():
    return pl.BlockSpec(memory_space=pltpu.SMEM)


def shift(x, distance):
    n = lax.axis_size("vocab")
    return lax.ppermute(x, "vocab", [(i, i ^ distance) for i in range(n)])


def token_places(place, rows, side):
    row = lax.broadcasted_iota(jnp.int32, (side, 1), 0)
    group = row // rows
    chip = (group % CHIPS) ^ place[1]
    core = (group // CHIPS) ^ place[0]
    return (chip * CORES + core) * rows + row % rows


def pick_column(match, values):
    return jnp.sum(jnp.where(match, values, 0.0), axis=1, keepdims=True)


def teacher_kernel(
    unlisted, rows, pos_ref, place_ref, blocks_ref, stat_ref, reader_ref, tail_ref, prob_ref, entropy_ref
):
    layers, slots, side, _ = blocks_ref.shape
    pos = [pos_ref[i] for i in range(3)]
    lane = lax.broadcasted_iota(jnp.int32, (1, side), 1)
    where_token = token_places(pos, rows, side)
    for k in range(layers):
        block = pos[2] ^ k
        match = reader_ref[block] == where_token
        onehot = jnp.where(match, 1.0, 0.0).astype(jnp.bfloat16)
        normaliser = pick_column(match, stat_ref[0, block])
        tail = pick_column(lane == where_token, tail_ref[block])
        kept = 1.0 - tail
        rest = tail / unlisted
        span = pl.ds(k * side, side)
        prob_ref[span, :] = jnp.broadcast_to(rest, (side, prob_ref.shape[1]))
        for s in range(slots):
            place = place_ref[block, s]
            values = jnp.dot(onehot, blocks_ref[block, s], preferred_element_type=jnp.float32)
            prob = kept * jnp.exp(values - normaliser)

            @pl.when(place >= 0)
            def _():
                prob_ref[span, pl.ds(pl.multiple_of(place * side, side), side)] = prob

        if k == 0:
            mean = pick_column(match, stat_ref[1, block])
            entropy = kept * (jnp.log(kept) - normaliser + mean) + tail * jnp.log(rest)
            entropy_ref[...] = jnp.broadcast_to(entropy[:rows], entropy_ref.shape)


def piece_blocks(layers):
    first = [
        [k * GROUP + core * CHIPS + x + 2 * y for x in range(2) for k in range(layers)]
        for core in range(CORES)
        for y in range(2)
    ]
    second = [
        [k * GROUP + core * CHIPS + x + 2 * y for y in range(2) for k in range(layers)]
        for core in range(CORES)
        for x in range(2)
    ]
    return first, second


def assemble(pieces, places, rows, out_ref, columns=slice(None)):
    for piece, blocks in zip(pieces, places):
        for i, block in enumerate(blocks):
            out_ref[pl.ds(block * rows, rows), columns] = piece[pl.ds(i * rows, rows), :]


def logits_kernel(rows, places, *refs):
    count = 2 * len(places[0])
    pieces, refs = refs[:count], refs[count:]
    w_ref, prob_ref, logits_ref, stat_ref, hidden, weight, sems, cross_ref = refs
    half, width = w_ref.shape[0] // 2, prob_ref.shape[1]
    tiles = w_ref.shape[1] // width
    step = pl.program_id(0)

    def copy(i):
        span = pl.ds(i * half, half)
        return pltpu.make_async_copy(w_ref.at[span, :], weight.at[span, :], sems.at[i])

    @pl.when(step == 0)
    def _():
        copy(0).start()
        copy(1).start()
        for i, some in enumerate(places):
            mine = pieces[i * len(some) : (i + 1) * len(some)]
            assemble(mine, some, rows, hidden, slice(i * half, (i + 1) * half))
        copy(0).wait()

    @pl.when(step == tiles)
    def _():
        copy(1).wait()

    @pl.when(step < tiles)
    def _():
        span = pl.ds(pl.multiple_of(step * width, width), width)
        logits_ref[:, span] = jnp.dot(
            hidden[:, :half], weight[:half, span], preferred_element_type=jnp.float32
        )

    @pl.when(step >= tiles)
    def _():
        span = pl.ds(pl.multiple_of((step - tiles) * width, width), width)
        total = logits_ref[:, span] + jnp.dot(
            hidden[:, half:], weight[half:, span], preferred_element_type=jnp.float32
        )
        logits_ref[:, span] = total
        product = total * prob_ref[...]
        folded = product[:, :128]
        for i in range(1, width // 128):
            folded = folded + product[:, i * 128 : (i + 1) * 128]
        cross_ref[...] = jnp.where(step == tiles, 0.0, cross_ref[...]) + folded

    @pl.when(step == 2 * tiles - 1)
    def _():
        logits = logits_ref[...]
        top = jnp.max(logits, axis=1, keepdims=True)
        norm = top + jnp.log(jnp.sum(jnp.exp(logits - top), axis=1, keepdims=True))
        cross = jnp.sum(cross_ref[...], axis=1, keepdims=True)
        lane = lax.broadcasted_iota(jnp.int32, (1, 128), 1)
        both = jnp.where(lane == 0, norm, jnp.where(lane == 1, cross, 0.0)).T
        tokens = logits.shape[0]
        packed = [both[i : i + 1, t : t + 128] for i in range(2) for t in range(0, tokens, 128)]
        stat_ref[...] = jnp.broadcast_to(jnp.concatenate(packed, axis=0)[None], stat_ref.shape)


def grad_kernel(
    rows, pos_ref, stat_ref, logits_ref, prob_ref, weight_ref, entropy_ref, grad_ref, loss_ref
):
    tokens = logits_ref.shape[0]
    devices = tokens // rows
    layers, _, side = weight_ref.shape
    layer_bits = (devices // GROUP).bit_length() - 1
    pos = [pos_ref[i] for i in range(3)]
    rank = pos_ref[3]
    lane = lax.broadcasted_iota(jnp.int32, (1, 128), 1)
    per_stat = stat_ref.shape[1] // 2
    norms, crosses = [
        jnp.concatenate([stat_ref[:, i * per_stat + t, :] for t in range(per_stat)], axis=1) for i in range(2)
    ]
    stat = jnp.concatenate(
        [norms, crosses, jnp.zeros((128 - 2 * devices, tokens), jnp.float32)], axis=0
    ).T
    pairs = [(0, 2), (1, 0), (2, 1)] + [(3 + i, 3 + i) for i in range(layer_bits)]
    for index_bit, block_bit in pairs:
        halves = stat.reshape(devices >> (block_bit + 1), 2, rows << block_bit, 128)
        swapped = jnp.stack([halves[:, 1], halves[:, 0]], axis=1).reshape(tokens, 128)
        stat = jnp.where(((lane ^ rank) >> index_bit) & 1 == 1, swapped, stat)
    is_norm = lane < devices
    is_cross = (lane >= devices) & (lane < 2 * devices)
    top = jnp.max(jnp.where(is_norm, stat, -jnp.inf), axis=1, keepdims=True)
    total = jnp.sum(jnp.where(is_norm, jnp.exp(stat - top), 0.0), axis=1, keepdims=True)
    log_norm = top + jnp.log(total)
    cross = jnp.sum(jnp.where(is_cross, stat, 0.0), axis=1, keepdims=True)
    loss_ref[...] = entropy_ref[...] - cross[:rows] + log_norm[:rows]
    where_token = token_places(pos, rows, side)
    for k in range(layers):
        span = pl.ds(k * side, side)
        weight = pick_column(lane == where_token, weight_ref[pos[2] ^ k])
        student = jnp.exp(logits_ref[span, :] - log_norm[k * side : (k + 1) * side])
        grad_ref[span, :] = (weight * (student - prob_ref[span, :])).astype(grad_ref.dtype)


def partial_kernel(rows, core_ref, grad_ref, sib_ref, w_ref, sib_w_ref, *refs):
    outs, swapped = refs[:CHIPS], refs[CHIPS]
    layers = outs[0].shape[0]
    half = CHIPS * rows

    @pl.when(pl.program_id(0) == 0)
    def _():
        for k in range(layers):
            for core in range(CORES):
                swapped[pl.ds((k * CORES + core) * half, half), :] = sib_ref[
                    pl.ds((k * CORES + 1 - core) * half, half), :
                ]

    contract = (((1,), (1,)), ((), ()))
    total = lax.dot_general(
        grad_ref[...], w_ref[...], contract, preferred_element_type=jnp.float32
    ) + lax.dot_general(
        swapped[...], sib_w_ref[...], contract, preferred_element_type=jnp.float32
    )
    for j, out in enumerate(outs):
        for k in range(layers):
            for core in range(CORES):
                start = (k * GROUP + core * CHIPS + j) * rows
                out[k, core] = total[start : start + rows].astype(out.dtype)


def head_kernel(rows, places, *refs):
    pieces, (grad_ref, out_ref, hidden) = refs[:-3], refs[-3:]
    half = pl.program_id(0) // 2
    for i, some in enumerate(places):

        @pl.when(half == i)
        def _():
            assemble(pieces[i * len(some) : (i + 1) * len(some)], some, rows, hidden)

    out_ref[...] = lax.dot_general(
        hidden[...], grad_ref[...], (((0,), (0,)), ((), ())), preferred_element_type=jnp.float32
    ).astype(out_ref.dtype)


def chip_sum_kernel(own_ref, *refs):
    arrived, outs = refs[: CHIPS - 1], refs[CHIPS - 1 :]
    for k, out in enumerate(outs):
        total = own_ref[k]
        for part in arrived:
            total = total + part[k].astype(jnp.float32)
        out[...] = total.astype(out.dtype)


def layer_sum_kernel(own_ref, *refs):
    arrived, (mine, theirs) = refs[:-2], refs[-2:]
    total = own_ref[...]
    for part in arrived:
        total = total + part[...].astype(jnp.float32)
    mine[...] = total[0].astype(mine.dtype)
    theirs[...] = total[1].astype(theirs.dtype)


def split_three(x):
    high = lax.reduce_precision(x, 8, 7)
    middle = lax.reduce_precision(x - high, 8, 7)
    low = x - high - middle
    return jnp.stack([high, middle, low]).astype(jnp.bfloat16)


def pack_teacher(teacher_logits, block_lists, places, layer):
    blocks, listed_count, stored, side = teacher_logits.shape
    n = lax.axis_size("vocab")
    rank = lax.axis_index("vocab")
    owner = block_lists // places
    earlier = jnp.tril(jnp.ones((listed_count, listed_count), jnp.bool_), -1)
    slot = jnp.sum((owner[:, :, None] == owner[:, None, :]) & earlier, axis=2, dtype=jnp.int32)
    code = (owner ^ (layer * GROUP)) * SLOTS + slot
    picker = (code[:, None, :] == jnp.arange(n * SLOTS, dtype=jnp.int32)[None, :, None]).astype(jnp.bfloat16)
    packed = jnp.einsum(
        "tsk,tkrc->tsrc", picker, teacher_logits, preferred_element_type=jnp.float32
    ).astype(jnp.bfloat16)
    packed = packed.reshape(blocks, n, SLOTS * stored, side).transpose(1, 0, 2, 3)
    values = teacher_logits.astype(jnp.float32)
    top = jnp.max(values, axis=(1, 3))
    powers = jnp.exp(values - top[:, None, :, None])
    total = jnp.sum(powers, axis=(1, 3))
    mean = jnp.sum(powers * values, axis=(1, 3)) / total
    stat = split_three(jnp.stack([top + jnp.log(total), mean])).reshape(-1)
    stat = jnp.pad(stat, (0, side - stat.shape[0]))
    payload = jnp.concatenate(
        [packed.reshape(n, -1, side), jnp.broadcast_to(stat, (n, 1, side))], axis=1
    )
    mine = (owner * SLOTS + slot)[:, None, :] == rank * SLOTS + jnp.arange(SLOTS, dtype=jnp.int32)[None, :, None]
    place = jnp.sum(jnp.where(mine, (block_lists % places + 1)[:, None, :], 0), axis=2) - 1
    return payload.reshape(n // GROUP, GROUP, -1, side), place.astype(jnp.int32)


def unpack_teacher(arrived, blocks, stored):
    n, _, side = arrived.shape
    arrived_blocks = (
        arrived[:, :-1]
        .reshape(n, blocks, SLOTS, stored, side)
        .transpose(1, 2, 0, 3, 4)
        .reshape(blocks, SLOTS, n * stored, side)
    )
    arrived_stat = (
        arrived[:, -1, : 6 * blocks * stored]
        .astype(jnp.float32)
        .reshape(n, 3, 2, blocks, stored)
        .sum(axis=1)
        .transpose(1, 2, 0, 3)
        .reshape(2, blocks, 1, n * stored)
    )
    return arrived_blocks, arrived_stat


def by_distance(x, layer, layers):
    shape = x.shape
    for i in range((layers - 1).bit_length()):
        pairs = x.reshape(shape[0], layers >> (i + 1), 2, -1)
        x = jnp.where((layer >> i) & 1 == 1, pairs[:, :, ::-1], pairs).reshape(shape)
    return x


def levels_plan(
    hidden_states, head_weight, teacher_logits, block_lists, row_reader, tail_mass, token_weight
):
    blocks, listed_count, stored, side = teacher_logits.shape
    rows, depth = hidden_states.shape
    slab = head_weight.shape[1]
    n = lax.axis_size("vocab")
    rank = lax.axis_index("vocab")
    tokens = n * rows
    layers = n // GROUP
    half = depth // CORES
    bf16, f32 = jnp.bfloat16, jnp.float32
    core, chip, layer = rank % CORES, (rank // CORES) % CHIPS, rank // GROUP
    pos = jnp.stack([core, chip, layer, rank]).astype(jnp.int32)
    unlisted = float(n * slab - side * listed_count)
    in_layer = [[o * GROUP + i for i in range(GROUP)] for o in range(layers)]
    X, Y = CORES, 2 * CORES

    column = [hidden_states] + [shift(hidden_states, k * GROUP) for k in range(1, layers)]
    sib_w = shift(head_weight, 1)
    payload, place = pack_teacher(teacher_logits, block_lists, slab // side, layer)
    payload = lax.all_to_all(
        payload, "vocab", split_axis=1, concat_axis=1, axis_index_groups=in_layer, tiled=True
    )
    column = jnp.concatenate(column, axis=0)
    column, payload = lax.optimization_barrier((column, payload))
    first, second = [column[:, :half]], [column[:, half:]]
    first_x, second_y = shift(first[0], X), shift(second[0], Y)
    crossed = [payload[k] for k in range(layers)]
    early = [shift(crossed[k], k * GROUP) for k in range(1, layers - 1)]
    first_x, second_y, sib_w, *early = lax.optimization_barrier((first_x, second_y, sib_w, *early))
    first = [jnp.concatenate([first[0], first_x], axis=0)]
    second = [jnp.concatenate([second[0], second_y], axis=0)]
    first.append(shift(first[0], Y))
    second.append(shift(second[0], X))
    late = [shift(crossed[k], k * GROUP) for k in range(max(layers - 1, 1), layers)]
    arrived = jnp.stack([crossed[0], *early, *late]).reshape(n, -1, side)
    arrived_blocks, arrived_stat = unpack_teacher(arrived, blocks, stored)
    first_sib, second_sib = [shift(first[0], 1)], [shift(second[0], 1)]

    prob, entropy = pl.pallas_call(
        lambda *refs: teacher_kernel(unlisted, rows, *refs),
        out_shape=(
            jax.ShapeDtypeStruct((tokens, slab), f32),
            jax.ShapeDtypeStruct((rows, side), f32),
        ),
        in_specs=[smem_spec(), smem_spec()] + [vmem_spec()] * 4,
        out_specs=(vmem_spec(), vmem_spec()),
        compiler_params=kernel_params(),
        cost_estimate=LIGHT,
        name="teacher_prob",
    )(
        pos,
        place,
        arrived_blocks,
        arrived_stat,
        by_distance(row_reader, layer, layers).reshape(blocks, 1, side),
        tail_mass.reshape(blocks, 1, side),
    )

    first[1], second[1], first_sib[0], second_sib[0], prob = lax.optimization_barrier(
        (first[1], second[1], first_sib[0], second_sib[0], prob)
    )
    first_sib.append(shift(first[1], 1))
    second_sib.append(shift(second[1], 1))
    pieces = first + first_sib + second + second_sib
    places = piece_blocks(layers)

    width = 256 if slab % 256 == 0 else 128
    tiles = slab // width
    whole = lambda t: (0, 0)
    logits, stat = pl.pallas_call(
        functools.partial(logits_kernel, rows, places),
        grid=(2 * tiles,),
        out_shape=[
            jax.ShapeDtypeStruct((tokens, slab), f32),
            jax.ShapeDtypeStruct((n, 2 * tokens // 128, 128), f32),
        ],
        in_specs=[vmem_spec()] * len(pieces)
        + [hbm_spec(), pl.BlockSpec((tokens, width), lambda t: (0, jnp.maximum(t - tiles, 0)))],
        out_specs=[
            pl.BlockSpec((tokens, slab), whole),
            pl.BlockSpec((n, 2 * tokens // 128, 128), lambda t: (0, 0, 0)),
        ],
        scratch_shapes=[
            pltpu.VMEM((tokens, depth), bf16),
            pltpu.VMEM((depth, slab), bf16),
            pltpu.SemaphoreType.DMA((2,)),
            pltpu.VMEM((tokens, 128), f32),
        ],
        compiler_params=kernel_params(LOGITS_VMEM),
        cost_estimate=LIGHT,
        name="logits",
    )(*pieces, head_weight, prob)
    stat = lax.all_to_all(stat, "vocab", split_axis=0, concat_axis=0, tiled=True)

    grad, loss = pl.pallas_call(
        lambda *refs: grad_kernel(rows, *refs),
        out_shape=(
            jax.ShapeDtypeStruct((tokens, slab), bf16),
            jax.ShapeDtypeStruct((rows, side), f32),
        ),
        in_specs=[smem_spec()] + [vmem_spec()] * 5,
        out_specs=(vmem_spec(), vmem_spec()),
        compiler_params=kernel_params(),
        cost_estimate=LIGHT,
        name="grad_logits",
    )(pos, stat, logits, prob, token_weight.reshape(blocks, 1, side), entropy)
    sib_grad = shift(grad, 1)

    tile = half // 5
    out_block = pl.BlockSpec((layers, CORES, rows, tile), lambda t, pos: (0, 0, 0, t))
    partial = pl.pallas_call(
        functools.partial(partial_kernel, rows),
        grid_spec=pltpu.PrefetchScalarGridSpec(
            num_scalar_prefetch=1,
            grid=(5,),
            in_specs=[pl.BlockSpec((tokens, slab), lambda t, pos: (0, 0))] * 2
            + [pl.BlockSpec((tile, slab), lambda t, pos: (pos[0] * 5 + t, 0))] * 2,
            out_specs=[out_block] * CHIPS,
            scratch_shapes=[pltpu.VMEM((tokens, slab), bf16)],
        ),
        out_shape=[
            jax.ShapeDtypeStruct((layers, CORES, rows, half), f32 if j == 0 else bf16) for j in range(CHIPS)
        ],
        compiler_params=kernel_params(LARGE_VMEM),
        cost_estimate=LIGHT,
        name="grad_hidden_partial",
    )(pos, grad, sib_grad, head_weight, sib_w)
    *partial, late_grad = lax.optimization_barrier((*partial, grad))
    arrived = [shift(partial[j], j * CORES) for j in range(1, CHIPS)]

    head_tile = half // 2
    per_half = len(pieces) // 2
    grad_head = pl.pallas_call(
        functools.partial(head_kernel, rows, places),
        grid=(4,),
        in_specs=[
            pl.BlockSpec((piece.shape[0], head_tile), lambda t, i=i: (0, jnp.clip(t - 2 * (i // per_half), 0, 1)))
            for i, piece in enumerate(pieces)
        ]
        + [pl.BlockSpec((tokens, slab), whole)],
        out_specs=pl.BlockSpec((head_tile, slab), lambda t: (t, 0)),
        out_shape=jax.ShapeDtypeStruct((depth, slab), bf16),
        scratch_shapes=[pltpu.VMEM((tokens, head_tile), bf16)],
        compiler_params=kernel_params(LARGE_VMEM),
        cost_estimate=LIGHT,
        name="grad_head",
    )(*pieces, late_grad)
    arrived, grad_head = lax.optimization_barrier((arrived, grad_head))

    summed = pl.pallas_call(
        chip_sum_kernel,
        in_specs=[vmem_spec()] * CHIPS,
        out_specs=[vmem_spec()] * layers,
        out_shape=[
            jax.ShapeDtypeStruct((CORES, rows, half), f32 if k == 0 else bf16) for k in range(layers)
        ],
        compiler_params=kernel_params(),
        cost_estimate=LIGHT,
        name="chip_sum",
    )(partial[0], *arrived)
    arrived = [shift(summed[k], k * GROUP) for k in range(1, layers)]
    mine, theirs = pl.pallas_call(
        layer_sum_kernel,
        in_specs=[vmem_spec()] * layers,
        out_specs=[vmem_spec()] * 2,
        out_shape=[jax.ShapeDtypeStruct((rows, half), bf16)] * 2,
        compiler_params=kernel_params(),
        cost_estimate=LIGHT,
        name="layer_sum",
    )(summed[0], *arrived)
    other = shift(theirs, 1)

    low, high = jnp.where(core == 0, mine, other), jnp.where(core == 0, other, mine)
    return loss[:, 0], grad_head, jnp.concatenate([low, high], axis=1)


def fits_levels(hidden_states, teacher_logits):
    n = lax.axis_size("vocab")
    rows = hidden_states.shape[0]
    blocks, _, stored, side = teacher_logits.shape
    return (
        n == blocks * GROUP
        and blocks & (blocks - 1) == 0
        and rows * GROUP == side
        and rows % 16 == 0
        and 2 * n <= side
        and 6 * blocks * stored <= side
        and hidden_states.shape[1] % (CORES * 1280) == 0
    )


def on_device(
    hidden_states, head_weight, teacher_logits, block_lists, row_reader, tail_mass, token_weight
):
    plan = levels_plan if fits_levels(hidden_states, teacher_logits) else plain_plan
    return plan(
        hidden_states, head_weight, teacher_logits, block_lists, row_reader, tail_mass, token_weight
    )


def solution(mesh):
    in_specs = (
        P("vocab", None),
        P(None, "vocab"),
        P(None, None, "vocab", None),
        P(),
        P(),
        P(),
        P(),
    )
    out_specs = (P("vocab"), P(None, "vocab"), P("vocab", None))
    return jax.shard_map(
        on_device, mesh=mesh, in_specs=in_specs, out_specs=out_specs, check_vma=False
    )
```

```python
import functools

import jax
import jax.numpy as jnp
from jax import lax
from jax.experimental import pallas as pl
from jax.experimental.pallas import tpu as pltpu
from jax.sharding import PartitionSpec as P


def row_parts(scores, teacher_slab, listed_mask, student_exp, teacher_exp):
    return (
        jnp.sum(student_exp, axis=(2, 3)),
        jnp.sum(teacher_exp, axis=(2, 3)),
        jnp.sum(teacher_exp * scores, axis=(2, 3)),
        jnp.sum(teacher_exp * teacher_slab, axis=(2, 3)),
        jnp.sum(scores, axis=(2, 3)),
        jnp.sum(jnp.where(listed_mask, scores, 0.0), axis=(2, 3)),
    )


def plain_plan(
    hidden_states, head_weight, teacher_logits, block_lists, row_reader, tail_mass, token_weight
):
    blocks, listed_count, stored_rows, block_side = teacher_logits.shape
    slab_width = head_weight.shape[1]
    slab_blocks = slab_width // block_side
    devices = lax.axis_size("vocab")
    rank_self = lax.axis_index("vocab")
    tokens = blocks * block_side
    shard_rows = hidden_states.shape[0]
    gathered = lax.all_gather(hidden_states, "vocab", axis=0, tiled=True)
    logits = jnp.dot(gathered, head_weight, preferred_element_type=jnp.float32)
    owner_dev = block_lists // slab_blocks
    owned_here = owner_dev == rank_self
    within = block_lists - rank_self * slab_blocks
    token_iota = lax.broadcasted_iota(jnp.int32, (1, block_side, block_side), 1)
    token_map = (row_reader[:, None, :] == token_iota).astype(jnp.bfloat16)
    place_iota = lax.broadcasted_iota(jnp.int32, (1, slab_blocks, 1), 1)
    block_iota = lax.broadcasted_iota(jnp.int32, (1, devices * slab_blocks, 1), 1)
    picker = (block_lists[:, None, :] == block_iota).astype(jnp.bfloat16)
    outgoing = jnp.einsum(
        "tnk,tkrc->tnrc", picker, teacher_logits, preferred_element_type=jnp.float32
    ).astype(jnp.bfloat16)
    incoming = lax.all_to_all(outgoing, "vocab", split_axis=1, concat_axis=2, tiled=True)
    teacher_slab = jnp.einsum(
        "tpj,tbjc->tpbc", token_map, incoming, preferred_element_type=jnp.float32
    )
    listed = jnp.sum(
        ((within[:, None, :] == place_iota) & owned_here[:, None, :]).astype(jnp.int32), axis=2
    )
    scores = logits.reshape(blocks, block_side, slab_blocks, block_side)
    listed_mask = (listed > 0)[:, None, :, None]
    local_smax = jnp.max(scores, axis=(2, 3))
    local_tmax = jnp.max(jnp.where(listed_mask, teacher_slab, -1e30), axis=(2, 3))
    student_max, teacher_max = lax.pmax((local_smax, local_tmax), "vocab")
    student_exp = jnp.exp(scores - student_max[:, :, None, None])
    teacher_exp = jnp.exp(
        jnp.where(listed_mask, teacher_slab - teacher_max[:, :, None, None], -jnp.inf)
    )
    parts = row_parts(scores, teacher_slab, listed_mask, student_exp, teacher_exp)
    student_sum, teacher_sum, cross_sum, self_sum, logit_total, listed_total = lax.psum(
        (parts[0], parts[1], parts[2], parts[3], parts[4], parts[5]), "vocab"
    )
    tail_share = tail_mass.reshape(blocks, block_side)
    unlisted = float(devices * slab_width - block_side * listed_count)
    kept_mass = 1.0 - tail_share
    log_norm = student_max + jnp.log(student_sum)
    row_loss = (
        kept_mass * (jnp.log(kept_mass) - teacher_max - jnp.log(teacher_sum))
        + kept_mass * self_sum / teacher_sum
        + tail_share * jnp.log(tail_share / unlisted)
        - kept_mass * cross_sum / teacher_sum
        - tail_share / unlisted * (logit_total - listed_total)
        + log_norm
    )
    token_loss = lax.dynamic_slice_in_dim(
        row_loss.reshape(tokens), rank_self * shard_rows, shard_rows, 0
    )
    student_prob = student_exp / student_sum[:, :, None, None]
    teacher_prob = jnp.where(
        listed_mask,
        (kept_mass / teacher_sum)[:, :, None, None] * teacher_exp,
        (tail_share / unlisted)[:, :, None, None],
    )
    weight = token_weight.reshape(blocks, block_side)[:, :, None, None]
    grad_logits = (
        (weight * (student_prob - teacher_prob)).astype(jnp.bfloat16).reshape(tokens, slab_width)
    )
    grad_head = lax.dot_general(
        gathered, grad_logits, (((0,), (0,)), ((), ())), preferred_element_type=jnp.float32
    ).astype(jnp.bfloat16)
    grad_hidden = lax.psum_scatter(
        lax.dot_general(
            grad_logits, head_weight, (((1,), (1,)), ((), ())), preferred_element_type=jnp.float32
        ),
        "vocab",
        scatter_dimension=0,
        tiled=True,
    ).astype(jnp.bfloat16)
    return (token_loss, grad_head, grad_hidden)


CORES = 2
CHIPS = 4
GROUP = CORES * CHIPS
SLOTS = 4
LIGHT = pl.CostEstimate(flops=1, bytes_accessed=1, transcendentals=0)
SMALL_VMEM = 16 * 1024 * 1024
LOGITS_VMEM = 56 * 1024 * 1024
LARGE_VMEM = 52 * 1024 * 1024


def kernel_params(limit=SMALL_VMEM):
    return pltpu.CompilerParams(vmem_limit_bytes=limit)


def vmem_spec():
    return pl.BlockSpec(memory_space=pltpu.VMEM)


def hbm_spec():
    return pl.BlockSpec(memory_space=pltpu.HBM)


def smem_spec():
    return pl.BlockSpec(memory_space=pltpu.SMEM)


def shift(x, distance):
    n = lax.axis_size("vocab")
    return lax.ppermute(x, "vocab", [(i, i ^ distance) for i in range(n)])


def token_places(place, rows, side):
    row = lax.broadcasted_iota(jnp.int32, (side, 1), 0)
    group = row // rows
    chip = (group % CHIPS) ^ place[1]
    core = (group // CHIPS) ^ place[0]
    return (chip * CORES + core) * rows + row % rows


def pick_column(match, values):
    return jnp.sum(jnp.where(match, values, 0.0), axis=1, keepdims=True)


def teacher_kernel(
    unlisted, rows, pos_ref, place_ref, blocks_ref, stat_ref, reader_ref, tail_ref, prob_ref, entropy_ref
):
    layers, slots, side, _ = blocks_ref.shape
    pos = [pos_ref[i] for i in range(3)]
    lane = lax.broadcasted_iota(jnp.int32, (1, side), 1)
    where_token = token_places(pos, rows, side)
    for k in range(layers):
        block = pos[2] ^ k
        match = reader_ref[block] == where_token
        onehot = jnp.where(match, 1.0, 0.0).astype(jnp.bfloat16)
        normaliser = pick_column(match, stat_ref[0, block])
        tail = pick_column(lane == where_token, tail_ref[block])
        kept = 1.0 - tail
        rest = tail / unlisted
        span = pl.ds(k * side, side)
        prob_ref[span, :] = jnp.broadcast_to(rest, (side, prob_ref.shape[1]))
        for s in range(slots):
            place = place_ref[block, s]
            values = jnp.dot(onehot, blocks_ref[block, s], preferred_element_type=jnp.float32)
            prob = kept * jnp.exp(values - normaliser)

            @pl.when(place >= 0)
            def _():
                prob_ref[span, pl.ds(pl.multiple_of(place * side, side), side)] = prob

        if k == 0:
            mean = pick_column(match, stat_ref[1, block])
            entropy = kept * (jnp.log(kept) - normaliser + mean) + tail * jnp.log(rest)
            entropy_ref[...] = jnp.broadcast_to(entropy[:rows], entropy_ref.shape)


def piece_blocks(layers):
    first = [
        [k * GROUP + core * CHIPS + x + 2 * y for x in range(2) for k in range(layers)]
        for core in range(CORES)
        for y in range(2)
    ]
    second = [
        [k * GROUP + core * CHIPS + x + 2 * y for y in range(2) for k in range(layers)]
        for core in range(CORES)
        for x in range(2)
    ]
    return first, second


def assemble(pieces, places, rows, out_ref, columns=slice(None)):
    for piece, blocks in zip(pieces, places):
        for i, block in enumerate(blocks):
            out_ref[pl.ds(block * rows, rows), columns] = piece[pl.ds(i * rows, rows), :]


def logits_kernel(rows, places, width, *refs):
    count = 2 * len(places[0])
    pieces, refs = refs[:count], refs[count:]
    w_ref, logits_ref, stat_ref, hidden, weight, sems = refs
    half = w_ref.shape[0] // 2
    tiles = w_ref.shape[1] // width
    step = pl.program_id(0)

    def copy(i):
        span = pl.ds(i * half, half)
        return pltpu.make_async_copy(w_ref.at[span, :], weight.at[span, :], sems.at[i])

    @pl.when(step == 0)
    def _():
        copy(0).start()
        copy(1).start()
        for i, some in enumerate(places):
            mine = pieces[i * len(some) : (i + 1) * len(some)]
            assemble(mine, some, rows, hidden, slice(i * half, (i + 1) * half))
        copy(0).wait()

    @pl.when(step == tiles)
    def _():
        copy(1).wait()

    @pl.when(step < tiles)
    def _():
        span = pl.ds(pl.multiple_of(step * width, width), width)
        logits_ref[:, span] = jnp.dot(
            hidden[:, :half], weight[:half, span], preferred_element_type=jnp.float32
        )

    @pl.when(step >= tiles)
    def _():
        span = pl.ds(pl.multiple_of((step - tiles) * width, width), width)
        total = logits_ref[:, span] + jnp.dot(
            hidden[:, half:], weight[half:, span], preferred_element_type=jnp.float32
        )
        logits_ref[:, span] = total

    @pl.when(step == 2 * tiles - 1)
    def _():
        logits = logits_ref[...]
        top = jnp.max(logits, axis=1, keepdims=True)
        norm = top + jnp.log(jnp.sum(jnp.exp(logits - top), axis=1, keepdims=True))
        tokens = logits.shape[0]
        norm = jnp.broadcast_to(norm, (tokens, 128)).T
        packed = jnp.concatenate([norm[:1, t : t + 128] for t in range(0, tokens, 128)], axis=0)
        stat_ref[...] = jnp.broadcast_to(packed[None], stat_ref.shape)


def grad_kernel(
    rows, pos_ref, stat_ref, logits_ref, prob_ref, weight_ref, entropy_ref, grad_ref, loss_ref, cross_ref
):
    tokens = logits_ref.shape[0]
    devices = tokens // rows
    layers, _, side = weight_ref.shape
    layer_bits = (devices // GROUP).bit_length() - 1
    pos = [pos_ref[i] for i in range(3)]
    rank = pos_ref[3]
    lane = lax.broadcasted_iota(jnp.int32, (1, 128), 1)
    norms = jnp.concatenate([stat_ref[:, t, :] for t in range(stat_ref.shape[1])], axis=1)
    stat = jnp.concatenate([norms, jnp.zeros((128 - devices, tokens), jnp.float32)], axis=0).T
    pairs = [(0, 2), (1, 0), (2, 1)] + [(3 + i, 3 + i) for i in range(layer_bits)]
    for index_bit, block_bit in pairs:
        halves = stat.reshape(devices >> (block_bit + 1), 2, rows << block_bit, 128)
        swapped = jnp.stack([halves[:, 1], halves[:, 0]], axis=1).reshape(tokens, 128)
        stat = jnp.where(((lane ^ rank) >> index_bit) & 1 == 1, swapped, stat)
    is_norm = lane < devices
    top = jnp.max(jnp.where(is_norm, stat, -jnp.inf), axis=1, keepdims=True)
    total = jnp.sum(jnp.where(is_norm, jnp.exp(stat - top), 0.0), axis=1, keepdims=True)
    log_norm = top + jnp.log(total)
    loss_ref[...] = entropy_ref[...] + log_norm[:rows]
    crosses = []
    where_token = token_places(pos, rows, side)
    for k in range(layers):
        span = pl.ds(k * side, side)
        weight = pick_column(lane == where_token, weight_ref[pos[2] ^ k])
        logits, prob = logits_ref[span, :], prob_ref[span, :]
        crosses.append(jnp.sum(prob * logits, axis=1, keepdims=True))
        student = jnp.exp(logits - log_norm[k * side : (k + 1) * side])
        grad_ref[span, :] = (weight * (student - prob)).astype(grad_ref.dtype)
    cross = jnp.broadcast_to(jnp.concatenate(crosses, axis=0), (tokens, 128)).T
    cross_ref[...] = cross[:1]


def partial_kernel(rows, core_ref, grad_ref, sib_ref, w_ref, sib_w_ref, *refs):
    outs, swapped = refs[:CHIPS], refs[CHIPS]
    layers = outs[0].shape[0]
    half = CHIPS * rows

    @pl.when(pl.program_id(0) == 0)
    def _():
        for k in range(layers):
            for core in range(CORES):
                swapped[pl.ds((k * CORES + core) * half, half), :] = sib_ref[
                    pl.ds((k * CORES + 1 - core) * half, half), :
                ]

    contract = (((1,), (1,)), ((), ()))
    total = lax.dot_general(
        grad_ref[...], w_ref[...], contract, preferred_element_type=jnp.float32
    ) + lax.dot_general(
        swapped[...], sib_w_ref[...], contract, preferred_element_type=jnp.float32
    )
    for j, out in enumerate(outs):
        for k in range(layers):
            for core in range(CORES):
                start = (k * GROUP + core * CHIPS + j) * rows
                out[k, core] = total[start : start + rows].astype(out.dtype)


def head_kernel(rows, places, *refs):
    pieces, (grad_ref, out_ref, hidden) = refs[:-3], refs[-3:]
    half = pl.program_id(0) // 2
    for i, some in enumerate(places):

        @pl.when(half == i)
        def _():
            assemble(pieces[i * len(some) : (i + 1) * len(some)], some, rows, hidden)

    out_ref[...] = lax.dot_general(
        hidden[...], grad_ref[...], (((0,), (0,)), ((), ())), preferred_element_type=jnp.float32
    ).astype(out_ref.dtype)


def chip_sum_kernel(own_ref, *refs):
    arrived, outs = refs[: CHIPS - 1], refs[CHIPS - 1 :]
    for k, out in enumerate(outs):
        total = own_ref[k]
        for part in arrived:
            total = total + part[k].astype(jnp.float32)
        out[...] = total.astype(out.dtype)


def layer_sum_kernel(own_ref, *refs):
    arrived, (mine, theirs) = refs[:-2], refs[-2:]
    total = own_ref[...]
    for part in arrived:
        total = total + part[...].astype(jnp.float32)
    mine[...] = total[0].astype(mine.dtype)
    theirs[...] = total[1].astype(theirs.dtype)


def split_three(x):
    high = lax.reduce_precision(x, 8, 7)
    middle = lax.reduce_precision(x - high, 8, 7)
    low = x - high - middle
    return jnp.stack([high, middle, low]).astype(jnp.bfloat16)


def pack_teacher(teacher_logits, block_lists, places):
    blocks, listed_count, stored, side = teacher_logits.shape
    n = lax.axis_size("vocab")
    rank = lax.axis_index("vocab")
    owner = block_lists // places
    earlier = jnp.tril(jnp.ones((listed_count, listed_count), jnp.bool_), -1)
    slot = jnp.sum((owner[:, :, None] == owner[:, None, :]) & earlier, axis=2, dtype=jnp.int32)
    code = owner * SLOTS + slot
    picker = (code[:, None, :] == jnp.arange(n * SLOTS, dtype=jnp.int32)[None, :, None]).astype(jnp.bfloat16)
    packed = jnp.einsum(
        "tsk,tkrc->tsrc", picker, teacher_logits, preferred_element_type=jnp.float32
    ).astype(jnp.bfloat16)
    packed = packed.reshape(blocks, n, SLOTS * stored, side).transpose(1, 0, 2, 3)
    values = teacher_logits.astype(jnp.float32)
    top = jnp.max(values, axis=(1, 3))
    powers = jnp.exp(values - top[:, None, :, None])
    total = jnp.sum(powers, axis=(1, 3))
    mean = jnp.sum(powers * values, axis=(1, 3)) / total
    stat = split_three(jnp.stack([top + jnp.log(total), mean])).reshape(-1)
    stat = jnp.pad(stat, (0, side - stat.shape[0]))
    payload = jnp.concatenate(
        [packed.reshape(n, -1, side), jnp.broadcast_to(stat, (n, 1, side))], axis=1
    )
    mine = code[:, None, :] == rank * SLOTS + jnp.arange(SLOTS, dtype=jnp.int32)[None, :, None]
    place = jnp.sum(jnp.where(mine, (block_lists % places + 1)[:, None, :], 0), axis=2) - 1
    return payload.reshape(n // GROUP, GROUP, -1, side), place.astype(jnp.int32)


def unpack_teacher(arrived, blocks, stored):
    n, _, side = arrived.shape
    arrived_blocks = (
        arrived[:, :-1]
        .reshape(n, blocks, SLOTS, stored, side)
        .transpose(1, 2, 0, 3, 4)
        .reshape(blocks, SLOTS, n * stored, side)
    )
    arrived_stat = (
        arrived[:, -1, : 6 * blocks * stored]
        .astype(jnp.float32)
        .reshape(n, 3, 2, blocks, stored)
        .sum(axis=1)
        .transpose(1, 2, 0, 3)
        .reshape(2, blocks, 1, n * stored)
    )
    return arrived_blocks, arrived_stat


def by_device(x, rank):
    n = x.shape[0]
    for i in range((n - 1).bit_length()):
        pairs = x.reshape(n >> (i + 1), 2, -1)
        x = jnp.where((rank >> i) & 1 == 1, pairs[:, ::-1], pairs).reshape(x.shape)
    return x


def levels_plan(
    hidden_states, head_weight, teacher_logits, block_lists, row_reader, tail_mass, token_weight
):
    blocks, listed_count, stored, side = teacher_logits.shape
    rows, depth = hidden_states.shape
    slab = head_weight.shape[1]
    n = lax.axis_size("vocab")
    rank = lax.axis_index("vocab")
    tokens = n * rows
    layers = n // GROUP
    half = depth // CORES
    bf16, f32 = jnp.bfloat16, jnp.float32
    core, chip, layer = rank % CORES, (rank // CORES) % CHIPS, rank // GROUP
    pos = jnp.stack([core, chip, layer, rank]).astype(jnp.int32)
    unlisted = float(n * slab - side * listed_count)
    across = [[o * GROUP + i for o in range(layers)] for i in range(GROUP)]
    in_layer = [[o * GROUP + i for i in range(GROUP)] for o in range(layers)]
    X, Y = CORES, 2 * CORES

    column = [hidden_states] + [shift(hidden_states, k * GROUP) for k in range(1, layers)]
    sib_w = shift(head_weight, 1)
    payload, place = pack_teacher(teacher_logits, block_lists, slab // side)
    payload = lax.all_to_all(
        payload, "vocab", split_axis=1, concat_axis=1, axis_index_groups=in_layer, tiled=True
    )
    column = lax.optimization_barrier(jnp.concatenate(column, axis=0))
    first, second = [column[:, :half]], [column[:, half:]]
    first_x, second_y = shift(first[0], X), shift(second[0], Y)
    first_x, second_y, sib_w, payload = lax.optimization_barrier((first_x, second_y, sib_w, payload))
    first = [jnp.concatenate([first[0], first_x], axis=0)]
    second = [jnp.concatenate([second[0], second_y], axis=0)]
    first.append(shift(first[0], Y))
    second.append(shift(second[0], X))
    first_sib, second_sib = [shift(first[0], 1)], [shift(second[0], 1)]
    arrived = lax.all_to_all(
        payload, "vocab", split_axis=0, concat_axis=0, axis_index_groups=across, tiled=True
    )
    first[1], second[1], first_sib[0], second_sib[0], arrived = lax.optimization_barrier(
        (first[1], second[1], first_sib[0], second_sib[0], arrived)
    )
    first_sib.append(shift(first[1], 1))
    second_sib.append(shift(second[1], 1))
    pieces = first + first_sib + second + second_sib
    places = piece_blocks(layers)
    width = 256 if slab % 256 == 0 else 128
    tiles = slab // width
    whole = lambda t: (0, 0)
    logits, stat = pl.pallas_call(
        functools.partial(logits_kernel, rows, places, width),
        grid=(2 * tiles,),
        out_shape=[
            jax.ShapeDtypeStruct((tokens, slab), f32),
            jax.ShapeDtypeStruct((n, tokens // 128, 128), f32),
        ],
        in_specs=[vmem_spec()] * len(pieces)
        + [hbm_spec()],
        out_specs=[
            pl.BlockSpec((tokens, slab), whole),
            pl.BlockSpec((n, tokens // 128, 128), lambda t: (0, 0, 0)),
        ],
        scratch_shapes=[
            pltpu.VMEM((tokens, depth), bf16),
            pltpu.VMEM((depth, slab), bf16),
            pltpu.SemaphoreType.DMA((2,)),
        ],
        compiler_params=kernel_params(LOGITS_VMEM),
        cost_estimate=LIGHT,
        name="logits",
    )(*pieces, head_weight)
    stat, arrived = lax.optimization_barrier((stat, arrived))
    stat = lax.all_to_all(stat, "vocab", split_axis=0, concat_axis=0, tiled=True)
    arrived_blocks, arrived_stat = unpack_teacher(arrived.reshape(n, -1, side), blocks, stored)
    prob, entropy = pl.pallas_call(
        lambda *refs: teacher_kernel(unlisted, rows, *refs),
        out_shape=(
            jax.ShapeDtypeStruct((tokens, slab), f32),
            jax.ShapeDtypeStruct((rows, side), f32),
        ),
        in_specs=[smem_spec(), smem_spec()] + [vmem_spec()] * 4,
        out_specs=(vmem_spec(), vmem_spec()),
        compiler_params=kernel_params(),
        cost_estimate=LIGHT,
        name="teacher_prob",
    )(
        pos,
        place,
        arrived_blocks,
        arrived_stat,
        row_reader.reshape(blocks, 1, side),
        tail_mass.reshape(blocks, 1, side),
    )

    grad, loss, cross = pl.pallas_call(
        lambda *refs: grad_kernel(rows, *refs),
        out_shape=(
            jax.ShapeDtypeStruct((tokens, slab), bf16),
            jax.ShapeDtypeStruct((rows, side), f32),
            jax.ShapeDtypeStruct((1, tokens), f32),
        ),
        in_specs=[smem_spec()] + [vmem_spec()] * 5,
        out_specs=[vmem_spec()] * 3,
        compiler_params=kernel_params(),
        cost_estimate=LIGHT,
        name="grad_logits",
    )(pos, stat, logits, prob, token_weight.reshape(blocks, 1, side), entropy)
    sib_grad = shift(grad, 1)

    tile = half // 5
    out_block = pl.BlockSpec((layers, CORES, rows, tile), lambda t, pos: (0, 0, 0, t))
    partial = pl.pallas_call(
        functools.partial(partial_kernel, rows),
        grid_spec=pltpu.PrefetchScalarGridSpec(
            num_scalar_prefetch=1,
            grid=(5,),
            in_specs=[pl.BlockSpec((tokens, slab), lambda t, pos: (0, 0))] * 2
            + [pl.BlockSpec((tile, slab), lambda t, pos: (pos[0] * 5 + t, 0))] * 2,
            out_specs=[out_block] * CHIPS,
            scratch_shapes=[pltpu.VMEM((tokens, slab), bf16)],
        ),
        out_shape=[
            jax.ShapeDtypeStruct((layers, CORES, rows, half), f32 if j == 0 else bf16) for j in range(CHIPS)
        ],
        compiler_params=kernel_params(LARGE_VMEM),
        cost_estimate=LIGHT,
        name="grad_hidden_partial",
    )(pos, grad, sib_grad, head_weight, sib_w)
    *partial, late_grad, cross = lax.optimization_barrier((*partial, grad, cross))
    cross = cross.reshape(layers, CORES, CHIPS, rows).transpose(0, 2, 1, 3).reshape(n, rows)
    cross = lax.all_to_all(by_device(cross, rank), "vocab", split_axis=0, concat_axis=0, tiled=True)
    token_loss = loss[:, 0] - jnp.sum(cross, axis=0)
    arrived = [shift(partial[j], j * CORES) for j in range(1, CHIPS)]

    head_tile = half // 2
    per_half = len(pieces) // 2
    grad_head = pl.pallas_call(
        functools.partial(head_kernel, rows, places),
        grid=(4,),
        in_specs=[
            pl.BlockSpec((piece.shape[0], head_tile), lambda t, i=i: (0, jnp.clip(t - 2 * (i // per_half), 0, 1)))
            for i, piece in enumerate(pieces)
        ]
        + [pl.BlockSpec((tokens, slab), whole)],
        out_specs=pl.BlockSpec((head_tile, slab), lambda t: (t, 0)),
        out_shape=jax.ShapeDtypeStruct((depth, slab), bf16),
        scratch_shapes=[pltpu.VMEM((tokens, head_tile), bf16)],
        compiler_params=kernel_params(LARGE_VMEM),
        cost_estimate=LIGHT,
        name="grad_head",
    )(*pieces, late_grad)
    arrived, grad_head, token_loss = lax.optimization_barrier((arrived, grad_head, token_loss))

    summed = pl.pallas_call(
        chip_sum_kernel,
        in_specs=[vmem_spec()] * CHIPS,
        out_specs=[vmem_spec()] * layers,
        out_shape=[
            jax.ShapeDtypeStruct((CORES, rows, half), f32 if k == 0 else bf16) for k in range(layers)
        ],
        compiler_params=kernel_params(),
        cost_estimate=LIGHT,
        name="chip_sum",
    )(partial[0], *arrived)
    arrived = [shift(summed[k], k * GROUP) for k in range(1, layers)]
    mine, theirs = pl.pallas_call(
        layer_sum_kernel,
        in_specs=[vmem_spec()] * layers,
        out_specs=[vmem_spec()] * 2,
        out_shape=[jax.ShapeDtypeStruct((rows, half), bf16)] * 2,
        compiler_params=kernel_params(),
        cost_estimate=LIGHT,
        name="layer_sum",
    )(summed[0], *arrived)
    other = shift(theirs, 1)

    low, high = jnp.where(core == 0, mine, other), jnp.where(core == 0, other, mine)
    return token_loss, grad_head, jnp.concatenate([low, high], axis=1)


def fits_levels(hidden_states, teacher_logits):
    n = lax.axis_size("vocab")
    rows = hidden_states.shape[0]
    blocks, _, stored, side = teacher_logits.shape
    return (
        n == blocks * GROUP
        and blocks & (blocks - 1) == 0
        and rows * GROUP == side
        and rows % 16 == 0
        and 2 * n <= side
        and 6 * blocks * stored <= side
        and hidden_states.shape[1] % (CORES * 1280) == 0
    )


def on_device(
    hidden_states, head_weight, teacher_logits, block_lists, row_reader, tail_mass, token_weight
):
    plan = levels_plan if fits_levels(hidden_states, teacher_logits) else plain_plan
    return plan(
        hidden_states, head_weight, teacher_logits, block_lists, row_reader, tail_mass, token_weight
    )


def solution(mesh):
    in_specs = (
        P("vocab", None),
        P(None, "vocab"),
        P(None, None, "vocab", None),
        P(),
        P(),
        P(),
        P(),
    )
    out_specs = (P("vocab"), P(None, "vocab"), P("vocab", None))
    return jax.shard_map(
        on_device, mesh=mesh, in_specs=in_specs, out_specs=out_specs, check_vma=False
    )
```

```python
import functools

import jax
import jax.numpy as jnp
from jax import lax
from jax.experimental import pallas as pl
from jax.experimental.pallas import tpu as pltpu
from jax.sharding import PartitionSpec as P


def row_parts(scores, teacher_slab, listed_mask, student_exp, teacher_exp):
    return (
        jnp.sum(student_exp, axis=(2, 3)),
        jnp.sum(teacher_exp, axis=(2, 3)),
        jnp.sum(teacher_exp * scores, axis=(2, 3)),
        jnp.sum(teacher_exp * teacher_slab, axis=(2, 3)),
        jnp.sum(scores, axis=(2, 3)),
        jnp.sum(jnp.where(listed_mask, scores, 0.0), axis=(2, 3)),
    )


def plain_plan(
    hidden_states, head_weight, teacher_logits, block_lists, row_reader, tail_mass, token_weight
):
    blocks, listed_count, stored_rows, block_side = teacher_logits.shape
    slab_width = head_weight.shape[1]
    slab_blocks = slab_width // block_side
    devices = lax.axis_size("vocab")
    rank_self = lax.axis_index("vocab")
    tokens = blocks * block_side
    shard_rows = hidden_states.shape[0]
    gathered = lax.all_gather(hidden_states, "vocab", axis=0, tiled=True)
    logits = jnp.dot(gathered, head_weight, preferred_element_type=jnp.float32)
    owner_dev = block_lists // slab_blocks
    owned_here = owner_dev == rank_self
    within = block_lists - rank_self * slab_blocks
    token_iota = lax.broadcasted_iota(jnp.int32, (1, block_side, block_side), 1)
    token_map = (row_reader[:, None, :] == token_iota).astype(jnp.bfloat16)
    place_iota = lax.broadcasted_iota(jnp.int32, (1, slab_blocks, 1), 1)
    block_iota = lax.broadcasted_iota(jnp.int32, (1, devices * slab_blocks, 1), 1)
    picker = (block_lists[:, None, :] == block_iota).astype(jnp.bfloat16)
    outgoing = jnp.einsum(
        "tnk,tkrc->tnrc", picker, teacher_logits, preferred_element_type=jnp.float32
    ).astype(jnp.bfloat16)
    incoming = lax.all_to_all(outgoing, "vocab", split_axis=1, concat_axis=2, tiled=True)
    teacher_slab = jnp.einsum(
        "tpj,tbjc->tpbc", token_map, incoming, preferred_element_type=jnp.float32
    )
    listed = jnp.sum(
        ((within[:, None, :] == place_iota) & owned_here[:, None, :]).astype(jnp.int32), axis=2
    )
    scores = logits.reshape(blocks, block_side, slab_blocks, block_side)
    listed_mask = (listed > 0)[:, None, :, None]
    local_smax = jnp.max(scores, axis=(2, 3))
    local_tmax = jnp.max(jnp.where(listed_mask, teacher_slab, -1e30), axis=(2, 3))
    student_max, teacher_max = lax.pmax((local_smax, local_tmax), "vocab")
    student_exp = jnp.exp(scores - student_max[:, :, None, None])
    teacher_exp = jnp.exp(
        jnp.where(listed_mask, teacher_slab - teacher_max[:, :, None, None], -jnp.inf)
    )
    parts = row_parts(scores, teacher_slab, listed_mask, student_exp, teacher_exp)
    student_sum, teacher_sum, cross_sum, self_sum, logit_total, listed_total = lax.psum(
        (parts[0], parts[1], parts[2], parts[3], parts[4], parts[5]), "vocab"
    )
    tail_share = tail_mass.reshape(blocks, block_side)
    unlisted = float(devices * slab_width - block_side * listed_count)
    kept_mass = 1.0 - tail_share
    log_norm = student_max + jnp.log(student_sum)
    row_loss = (
        kept_mass * (jnp.log(kept_mass) - teacher_max - jnp.log(teacher_sum))
        + kept_mass * self_sum / teacher_sum
        + tail_share * jnp.log(tail_share / unlisted)
        - kept_mass * cross_sum / teacher_sum
        - tail_share / unlisted * (logit_total - listed_total)
        + log_norm
    )
    token_loss = lax.dynamic_slice_in_dim(
        row_loss.reshape(tokens), rank_self * shard_rows, shard_rows, 0
    )
    student_prob = student_exp / student_sum[:, :, None, None]
    teacher_prob = jnp.where(
        listed_mask,
        (kept_mass / teacher_sum)[:, :, None, None] * teacher_exp,
        (tail_share / unlisted)[:, :, None, None],
    )
    weight = token_weight.reshape(blocks, block_side)[:, :, None, None]
    grad_logits = (
        (weight * (student_prob - teacher_prob)).astype(jnp.bfloat16).reshape(tokens, slab_width)
    )
    grad_head = lax.dot_general(
        gathered, grad_logits, (((0,), (0,)), ((), ())), preferred_element_type=jnp.float32
    ).astype(jnp.bfloat16)
    grad_hidden = lax.psum_scatter(
        lax.dot_general(
            grad_logits, head_weight, (((1,), (1,)), ((), ())), preferred_element_type=jnp.float32
        ),
        "vocab",
        scatter_dimension=0,
        tiled=True,
    ).astype(jnp.bfloat16)
    return (token_loss, grad_head, grad_hidden)


CORES = 2
CHIPS = 4
GROUP = CORES * CHIPS
SLOTS = 4
LIGHT = pl.CostEstimate(flops=1, bytes_accessed=1, transcendentals=0)
SMALL_VMEM = 16 * 1024 * 1024
LARGE_VMEM = 48 * 1024 * 1024
ALL_VMEM = 60 * 1024 * 1024
STAT_ROWS = 16


def kernel_params(limit=SMALL_VMEM):
    return pltpu.CompilerParams(vmem_limit_bytes=limit)


def vmem_spec():
    return pl.BlockSpec(memory_space=pltpu.VMEM)


def hbm_spec():
    return pl.BlockSpec(memory_space=pltpu.HBM)


def smem_spec():
    return pl.BlockSpec(memory_space=pltpu.SMEM)


def shift(x, distance):
    n = lax.axis_size("vocab")
    return lax.ppermute(x, "vocab", [(i, i ^ distance) for i in range(n)])


def token_places(place, rows, side):
    row = lax.broadcasted_iota(jnp.int32, (side, 1), 0)
    group = row // rows
    chip = (group % CHIPS) ^ place[1]
    core = (group // CHIPS) ^ place[0]
    return (chip * CORES + core) * rows + row % rows


def pick_column(match, values):
    return jnp.sum(jnp.where(match, values, 0.0), axis=1, keepdims=True)


def teacher_kernel(
    unlisted, rows, pos_ref, place_ref, blocks_ref, stat_ref, reader_ref, tail_ref, prob_ref, entropy_ref
):
    layers, slots, side, _ = blocks_ref.shape
    pos = [pos_ref[i] for i in range(3)]
    lane = lax.broadcasted_iota(jnp.int32, (1, side), 1)
    where_token = token_places(pos, rows, side)
    for k in range(layers):
        block = pos[2] ^ k
        match = reader_ref[block] == where_token
        onehot = jnp.where(match, 1.0, 0.0).astype(jnp.bfloat16)
        normaliser = pick_column(match, stat_ref[0, block])
        tail = pick_column(lane == where_token, tail_ref[block])
        kept = 1.0 - tail
        rest = tail / unlisted
        span = pl.ds(k * side, side)
        prob_ref[span, :] = jnp.broadcast_to(rest, (side, prob_ref.shape[1]))
        for s in range(slots):
            place = place_ref[block, s]
            values = jnp.dot(onehot, blocks_ref[block, s], preferred_element_type=jnp.float32)
            prob = kept * jnp.exp(values - normaliser)

            @pl.when(place >= 0)
            def _():
                prob_ref[span, pl.ds(pl.multiple_of(place * side, side), side)] = prob

        if k == 0:
            mean = pick_column(match, stat_ref[1, block])
            entropy = kept * (jnp.log(kept) - normaliser + mean) + tail * jnp.log(rest)
            entropy_ref[...] = jnp.broadcast_to(entropy[:rows], entropy_ref.shape)


def piece_blocks(layers):
    first = [
        [k * GROUP + core * CHIPS + x + 2 * y for x in range(2) for k in range(layers)]
        for core in range(CORES)
        for y in range(2)
    ]
    second = [
        [k * GROUP + core * CHIPS + x + 2 * y for y in range(2) for k in range(layers)]
        for core in range(CORES)
        for x in range(2)
    ]
    return first, second


def assemble(pieces, places, rows, out_ref, columns=slice(None)):
    for piece, blocks in zip(pieces, places):
        for i, block in enumerate(blocks):
            out_ref[pl.ds(block * rows, rows), columns] = piece[pl.ds(i * rows, rows), :]


def products_kernel(width, last, *refs):
    pieces, w_ref, refs = refs[:4], refs[4], refs[5:]
    if last:
        rows, places, before_ref, prob_ref, logits_ref, stat_ref, hidden, weight, sems, out_ref = last + refs
    else:
        out_ref, hidden, weight, sems = refs
    half = w_ref.shape[0] // 2
    tiles = w_ref.shape[1] // width
    step = pl.program_id(0)
    i = step // tiles

    def copy(i):
        span = pl.ds(i * half, half)
        return pltpu.make_async_copy(w_ref.at[span, :], weight.at[i], sems.at[i])

    @pl.when(step == 0)
    def _():
        copy(0).start()
        copy(1).start()
        for p, piece in enumerate(pieces):
            size = piece.shape[0]
            hidden[p // 2, pl.ds(p % 2 * size, size), :] = piece[...]
        copy(0).wait()

    @pl.when(step == tiles)
    def _():
        copy(1).wait()

    span = pl.ds(pl.multiple_of(step % tiles * width, width), width)
    out_ref[i, :, span] = jnp.dot(hidden[i], weight[i, :, span], preferred_element_type=jnp.float32)

    if last:

        @pl.when(step == 2 * tiles - 1)
        def _():
            sources = {}
            for i, some in enumerate(places):
                for p, blocks in enumerate(some):
                    for g, block in enumerate(blocks):
                        sources.setdefault(block, []).append((i, p % 2, (p // 2 * len(blocks) + g) * rows))
            for block, parts in sources.items():
                total = None
                for i, late, row in parts:
                    part = (out_ref if late else before_ref)[i, pl.ds(row, rows), :]
                    total = part if total is None else total + part
                logits_ref[pl.ds(block * rows, rows), :] = total
            logits = logits_ref[...]
            top = jnp.max(logits, axis=1, keepdims=True)
            norm = top + jnp.log(jnp.sum(jnp.exp(logits - top), axis=1, keepdims=True))
            tokens = logits.shape[0]
            cross = jnp.sum(logits * prob_ref[...], axis=1, keepdims=True)
            lane = lax.broadcasted_iota(jnp.int32, (1, 128), 1)
            both = jnp.where(lane == 0, norm, jnp.where(lane == 1, cross, 0.0)).T
            packed = [both[i : i + 1, t : t + 128] for i in range(2) for t in range(0, tokens, 128)]
            packed = jnp.concatenate(packed, axis=0)
            stat_ref[...] = jnp.broadcast_to(packed[None], stat_ref.shape)


def grad_kernel(
    rows, pos_ref, stat_ref, logits_ref, prob_ref, weight_ref, entropy_ref, grad_ref, loss_ref, norm_ref
):
    layers, _, side = weight_ref.shape
    tokens = layers * side
    devices = tokens // rows
    layer_bits = (layers - 1).bit_length()
    pos = [pos_ref[i] for i in range(3)]
    rank = pos_ref[3]
    lane = lax.broadcasted_iota(jnp.int32, (1, 128), 1)
    step = pl.program_id(0)

    @pl.when(step == 0)
    def _():
        per_stat = stat_ref.shape[1] // 2
        norms, crosses = [
            jnp.concatenate([stat_ref[:, i * per_stat + t, :] for t in range(per_stat)], axis=1) for i in range(2)
        ]
        stat = jnp.concatenate(
            [norms, crosses, jnp.zeros((128 - 2 * devices, tokens), jnp.float32)], axis=0
        ).T
        pairs = [(0, 2), (1, 0), (2, 1)] + [(3 + i, 3 + i) for i in range(layer_bits)]
        for index_bit, block_bit in pairs:
            halves = stat.reshape(devices >> (block_bit + 1), 2, rows << block_bit, 128)
            swapped = jnp.stack([halves[:, 1], halves[:, 0]], axis=1).reshape(tokens, 128)
            stat = jnp.where(((lane ^ rank) >> index_bit) & 1 == 1, swapped, stat)
        is_norm = lane < devices
        is_cross = (lane >= devices) & (lane < 2 * devices)
        top = jnp.max(jnp.where(is_norm, stat, -jnp.inf), axis=1, keepdims=True)
        total = jnp.sum(jnp.where(is_norm, jnp.exp(stat - top), 0.0), axis=1, keepdims=True)
        log_norm = top + jnp.log(total)
        cross = jnp.sum(jnp.where(is_cross, stat, 0.0), axis=1, keepdims=True)
        loss_ref[...] = entropy_ref[...] - cross[:rows] + log_norm[:rows]
        norm_ref[...] = jnp.broadcast_to(log_norm, norm_ref.shape)

    weight = pick_column(lane == token_places(pos, rows, side), weight_ref[pos[2] ^ step])
    norm = norm_ref[pl.ds(pl.multiple_of(step * side, side), side), :][:, :1]
    student = jnp.exp(logits_ref[...] - norm)
    grad_ref[...] = (weight * (student - prob_ref[...])).astype(grad_ref.dtype)


def partial_kernel(rows, core_ref, grad_ref, sib_ref, w_ref, sib_w_ref, *refs):
    outs, swapped = refs[:CHIPS], refs[CHIPS]
    layers = outs[0].shape[0]
    half = CHIPS * rows

    @pl.when(pl.program_id(0) == 0)
    def _():
        for k in range(layers):
            for core in range(CORES):
                swapped[pl.ds((k * CORES + core) * half, half), :] = sib_ref[
                    pl.ds((k * CORES + 1 - core) * half, half), :
                ]

    contract = (((1,), (1,)), ((), ()))
    total = lax.dot_general(
        grad_ref[...], w_ref[...], contract, preferred_element_type=jnp.float32
    ) + lax.dot_general(
        swapped[...], sib_w_ref[...], contract, preferred_element_type=jnp.float32
    )
    for j, out in enumerate(outs):
        for k in range(layers):
            for core in range(CORES):
                start = (k * GROUP + core * CHIPS + j) * rows
                out[k, core] = total[start : start + rows].astype(out.dtype)


def head_kernel(rows, places, *refs):
    pieces, (grad_ref, out_ref, hidden) = refs[:-3], refs[-3:]
    half = pl.program_id(0) // 2
    for i, some in enumerate(places):

        @pl.when(half == i)
        def _():
            assemble(pieces[i * len(some) : (i + 1) * len(some)], some, rows, hidden)

    out_ref[...] = lax.dot_general(
        hidden[...], grad_ref[...], (((0,), (0,)), ((), ())), preferred_element_type=jnp.float32
    ).astype(out_ref.dtype)


def chip_sum_kernel(own_ref, *refs):
    arrived, outs = refs[: CHIPS - 1], refs[CHIPS - 1 :]
    for k, out in enumerate(outs):
        total = own_ref[k]
        for part in arrived:
            total = total + part[k].astype(jnp.float32)
        out[...] = total.astype(out.dtype)


def layer_sum_kernel(own_ref, *refs):
    arrived, (mine, theirs) = refs[:-2], refs[-2:]
    total = own_ref[...]
    for part in arrived:
        total = total + part[...].astype(jnp.float32)
    mine[...] = total[0].astype(mine.dtype)
    theirs[...] = total[1].astype(theirs.dtype)


def pack_kernel(code_ref, x_ref, out_ref):
    blocks, count, side = x_ref.shape
    chips, layers, size, _ = out_ref.shape
    slot_rows = (size - STAT_ROWS) // blocks
    stored = slot_rows // SLOTS
    target = lax.broadcasted_iota(jnp.int32, (chips * layers * slot_rows, 1), 0)
    row = lax.broadcasted_iota(jnp.int32, (count, 1), 0) % stored
    lane = lax.broadcasted_iota(jnp.int32, (1, side), 1)
    stat = jnp.zeros((1, side), jnp.float32)
    for t in range(blocks):
        onehot = jnp.where(code_ref[t] == target, 1.0, 0.0).astype(x_ref.dtype)
        packed = jnp.dot(onehot, x_ref[t], preferred_element_type=jnp.float32).astype(out_ref.dtype)
        for device in range(chips * layers):
            out_ref[device % chips, device // chips, pl.ds(t * slot_rows, slot_rows), :] = packed[
                device * slot_rows : (device + 1) * slot_rows
            ]
        values = x_ref[t].astype(jnp.float32)
        row_top = jnp.max(values, axis=1, keepdims=True)
        tops = [jnp.max(jnp.where(row == r, row_top, -jnp.inf), axis=0, keepdims=True) for r in range(stored)]
        top = jnp.zeros_like(row_top)
        for r in range(stored):
            top = jnp.where(row == r, tops[r], top)
        powers = jnp.exp(values - top)
        sums = jnp.sum(powers, axis=1, keepdims=True)
        weighted = jnp.sum(powers * values, axis=1, keepdims=True)
        for r in range(stored):
            total = jnp.sum(jnp.where(row == r, sums, 0.0), axis=0, keepdims=True)
            mean = jnp.sum(jnp.where(row == r, weighted, 0.0), axis=0, keepdims=True) / total
            stat = jnp.where(lane == t * stored + r, tops[r] + jnp.log(total), stat)
            stat = jnp.where(lane == (blocks + t) * stored + r, mean, stat)
    high = stat.astype(jnp.bfloat16).astype(jnp.float32)
    middle = (stat - high).astype(jnp.bfloat16).astype(jnp.float32)
    low = stat - high - middle
    parts = jnp.concatenate([high, middle, low, jnp.zeros((STAT_ROWS - 3, side), jnp.float32)], axis=0)
    parts = parts.astype(out_ref.dtype)
    for chip in range(chips):
        for layer in range(layers):
            out_ref[chip, layer, pl.ds(size - STAT_ROWS, STAT_ROWS), :] = parts


def pack_teacher(teacher_logits, block_lists, places, layer):
    blocks, listed_count, stored, side = teacher_logits.shape
    n = lax.axis_size("vocab")
    rank = lax.axis_index("vocab")
    owner = block_lists // places
    earlier = jnp.tril(jnp.ones((listed_count, listed_count), jnp.bool_), -1)
    slot = jnp.sum((owner[:, :, None] == owner[:, None, :]) & earlier, axis=2, dtype=jnp.int32)
    code = (owner ^ (layer * GROUP)) * SLOTS + slot
    code = (code[:, :, None] * stored + jnp.arange(stored, dtype=jnp.int32)).reshape(blocks, 1, -1)
    payload = pl.pallas_call(
        pack_kernel,
        in_specs=[vmem_spec()] * 2,
        out_specs=vmem_spec(),
        out_shape=jax.ShapeDtypeStruct(
            (GROUP, n // GROUP, blocks * SLOTS * stored + STAT_ROWS, side), teacher_logits.dtype
        ),
        compiler_params=kernel_params(),
        cost_estimate=LIGHT,
        name="pack_teacher",
    )(code, teacher_logits.reshape(blocks, listed_count * stored, side))
    mine = (owner * SLOTS + slot)[:, None, :] == rank * SLOTS + jnp.arange(SLOTS, dtype=jnp.int32)[None, :, None]
    place = jnp.sum(jnp.where(mine, (block_lists % places + 1)[:, None, :], 0), axis=2) - 1
    return payload, place.astype(jnp.int32)


def unpack_teacher(arrived, blocks, stored):
    n, _, side = arrived.shape
    arrived_blocks = (
        arrived[:, :-STAT_ROWS]
        .reshape(n, blocks, SLOTS, stored, side)
        .transpose(1, 2, 0, 3, 4)
        .reshape(blocks, SLOTS, n * stored, side)
    )
    arrived_stat = (
        arrived[:, -STAT_ROWS : 3 - STAT_ROWS, : 2 * blocks * stored]
        .astype(jnp.float32)
        .sum(axis=1)
        .reshape(n, 2, blocks, stored)
        .transpose(1, 2, 0, 3)
        .reshape(2, blocks, 1, n * stored)
    )
    return arrived_blocks, arrived_stat


def by_distance(x, layer, layers):
    shape = x.shape
    for i in range((layers - 1).bit_length()):
        pairs = x.reshape(shape[0], layers >> (i + 1), 2, -1)
        x = jnp.where((layer >> i) & 1 == 1, pairs[:, :, ::-1], pairs).reshape(shape)
    return x


def levels_plan(
    hidden_states, head_weight, teacher_logits, block_lists, row_reader, tail_mass, token_weight
):
    blocks, listed_count, stored, side = teacher_logits.shape
    rows, depth = hidden_states.shape
    slab = head_weight.shape[1]
    n = lax.axis_size("vocab")
    rank = lax.axis_index("vocab")
    tokens = n * rows
    layers = n // GROUP
    half = depth // CORES
    bf16, f32 = jnp.bfloat16, jnp.float32
    core, chip, layer = rank % CORES, (rank // CORES) % CHIPS, rank // GROUP
    pos = jnp.stack([core, chip, layer, rank]).astype(jnp.int32)
    unlisted = float(n * slab - side * listed_count)
    in_layer = [[o * GROUP + i for i in range(GROUP)] for o in range(layers)]
    X, Y = CORES, 2 * CORES

    column = [hidden_states] + [shift(hidden_states, k * GROUP) for k in range(1, layers)]
    sib_w = shift(head_weight, 1)
    payload, place = pack_teacher(teacher_logits, block_lists, slab // side, layer)
    payload = lax.all_to_all(
        payload, "vocab", split_axis=0, concat_axis=0, axis_index_groups=in_layer, tiled=True
    )
    column = jnp.concatenate(column, axis=0)
    column, payload = lax.optimization_barrier((column, payload))
    first, second = [column[:, :half]], [column[:, half:]]
    first_x, second_y = shift(first[0], X), shift(second[0], Y)
    crossed = [payload[:, k] for k in range(layers)]
    early = [shift(crossed[k], k * GROUP) for k in range(1, layers - 1)]
    first_x, second_y, sib_w, *early = lax.optimization_barrier((first_x, second_y, sib_w, *early))
    first = [jnp.concatenate([first[0], first_x], axis=0)]
    second = [jnp.concatenate([second[0], second_y], axis=0)]
    first.append(shift(first[0], Y))
    second.append(shift(second[0], X))
    late = [shift(crossed[k], k * GROUP) for k in range(max(layers - 1, 1), layers)]
    arrived = jnp.stack([crossed[0], *early, *late]).reshape(n, -1, side)
    arrived_blocks, arrived_stat = unpack_teacher(arrived, blocks, stored)
    first_sib, second_sib = [shift(first[0], 1)], [shift(second[0], 1)]

    prob, entropy = pl.pallas_call(
        lambda *refs: teacher_kernel(unlisted, rows, *refs),
        out_shape=(
            jax.ShapeDtypeStruct((tokens, slab), f32),
            jax.ShapeDtypeStruct((rows, side), f32),
        ),
        in_specs=[smem_spec(), smem_spec()] + [vmem_spec()] * 4,
        out_specs=(vmem_spec(), vmem_spec()),
        compiler_params=kernel_params(),
        cost_estimate=LIGHT,
        name="teacher_prob",
    )(
        pos,
        place,
        arrived_blocks,
        arrived_stat,
        by_distance(row_reader, layer, layers).reshape(blocks, 1, side),
        tail_mass.reshape(blocks, 1, side),
    )

    width = 256 if slab % 256 == 0 else 128
    tiles = slab // width
    product = jax.ShapeDtypeStruct((2, tokens // 2, slab), f32)
    whole = lambda t: (0, 0)
    weight_scratch = [
        pltpu.VMEM((2, tokens // 2, half), bf16),
        pltpu.VMEM((2, half, slab), bf16),
        pltpu.SemaphoreType.DMA((2,)),
    ]
    before = pl.pallas_call(
        functools.partial(products_kernel, width, None),
        grid=(2 * tiles,),
        out_shape=product,
        in_specs=[vmem_spec()] * 4 + [hbm_spec()],
        out_specs=pl.BlockSpec(product.shape, lambda t: (0, 0, 0)),
        scratch_shapes=weight_scratch,
        compiler_params=kernel_params(LARGE_VMEM),
        cost_estimate=LIGHT,
        name="first_products",
    )(first[0], first_sib[0], second[0], second_sib[0], head_weight)
    first[1], second[1], first_sib[0], second_sib[0], prob, before = lax.optimization_barrier(
        (first[1], second[1], first_sib[0], second_sib[0], prob, before)
    )
    first_sib.append(shift(first[1], 1))
    second_sib.append(shift(second[1], 1))
    pieces = first + first_sib + second + second_sib
    places = piece_blocks(layers)

    logits, stat = pl.pallas_call(
        functools.partial(products_kernel, width, (rows, places)),
        grid=(2 * tiles,),
        out_shape=[
            jax.ShapeDtypeStruct((tokens, slab), f32),
            jax.ShapeDtypeStruct((n, 2 * tokens // 128, 128), f32),
        ],
        in_specs=[vmem_spec()] * 4 + [hbm_spec()] + [vmem_spec()] * 2,
        out_specs=[
            pl.BlockSpec((tokens, slab), whole),
            pl.BlockSpec((n, 2 * tokens // 128, 128), lambda t: (0, 0, 0)),
        ],
        scratch_shapes=weight_scratch + [pltpu.VMEM(product.shape, f32)],
        compiler_params=kernel_params(LARGE_VMEM),
        cost_estimate=LIGHT,
        name="logits",
    )(first[1], first_sib[1], second[1], second_sib[1], head_weight, before, prob)
    stat = lax.all_to_all(stat, "vocab", split_axis=0, concat_axis=0, tiled=True)

    block = pl.BlockSpec((side, slab), lambda t: (t, 0))
    grad, loss = pl.pallas_call(
        functools.partial(grad_kernel, rows),
        grid=(layers,),
        out_shape=(
            jax.ShapeDtypeStruct((tokens, slab), bf16),
            jax.ShapeDtypeStruct((rows, side), f32),
        ),
        in_specs=[smem_spec(), pl.BlockSpec(stat.shape, lambda t: (0, 0, 0)), block, block]
        + [pl.BlockSpec((blocks, 1, side), lambda t: (0, 0, 0)), pl.BlockSpec((rows, side), whole)],
        out_specs=(block, pl.BlockSpec((rows, side), whole)),
        scratch_shapes=[pltpu.VMEM((tokens, 128), f32)],
        compiler_params=kernel_params(ALL_VMEM),
        cost_estimate=LIGHT,
        name="grad_logits",
    )(pos, stat, logits, prob, token_weight.reshape(blocks, 1, side), entropy)
    sib_grad = shift(grad, 1)

    tile = half // 5
    out_block = pl.BlockSpec((layers, CORES, rows, tile), lambda t, pos: (0, 0, 0, t))
    partial = pl.pallas_call(
        functools.partial(partial_kernel, rows),
        grid_spec=pltpu.PrefetchScalarGridSpec(
            num_scalar_prefetch=1,
            grid=(5,),
            in_specs=[pl.BlockSpec((tokens, slab), lambda t, pos: (0, 0))] * 2
            + [pl.BlockSpec((tile, slab), lambda t, pos: (pos[0] * 5 + t, 0))] * 2,
            out_specs=[out_block] * CHIPS,
            scratch_shapes=[pltpu.VMEM((tokens, slab), bf16)],
        ),
        out_shape=[
            jax.ShapeDtypeStruct((layers, CORES, rows, half), f32 if j == 0 else bf16) for j in range(CHIPS)
        ],
        compiler_params=kernel_params(LARGE_VMEM),
        cost_estimate=LIGHT,
        name="grad_hidden_partial",
    )(pos, grad, sib_grad, head_weight, sib_w)
    *partial, late_grad = lax.optimization_barrier((*partial, grad))
    arrived = [shift(partial[j], j * CORES) for j in range(1, CHIPS)]

    head_tile = half // 2
    per_half = len(pieces) // 2
    grad_head = pl.pallas_call(
        functools.partial(head_kernel, rows, places),
        grid=(4,),
        in_specs=[
            pl.BlockSpec((piece.shape[0], head_tile), lambda t, i=i: (0, jnp.clip(t - 2 * (i // per_half), 0, 1)))
            for i, piece in enumerate(pieces)
        ]
        + [pl.BlockSpec((tokens, slab), whole)],
        out_specs=pl.BlockSpec((head_tile, slab), lambda t: (t, 0)),
        out_shape=jax.ShapeDtypeStruct((depth, slab), bf16),
        scratch_shapes=[pltpu.VMEM((tokens, head_tile), bf16)],
        compiler_params=kernel_params(LARGE_VMEM),
        cost_estimate=LIGHT,
        name="grad_head",
    )(*pieces, late_grad)
    arrived, grad_head = lax.optimization_barrier((arrived, grad_head))

    summed = pl.pallas_call(
        chip_sum_kernel,
        in_specs=[vmem_spec()] * CHIPS,
        out_specs=[vmem_spec()] * layers,
        out_shape=[
            jax.ShapeDtypeStruct((CORES, rows, half), f32 if k == 0 else bf16) for k in range(layers)
        ],
        compiler_params=kernel_params(),
        cost_estimate=LIGHT,
        name="chip_sum",
    )(partial[0], *arrived)
    arrived = [shift(summed[k], k * GROUP) for k in range(1, layers)]
    mine, theirs = pl.pallas_call(
        layer_sum_kernel,
        in_specs=[vmem_spec()] * layers,
        out_specs=[vmem_spec()] * 2,
        out_shape=[jax.ShapeDtypeStruct((rows, half), bf16)] * 2,
        compiler_params=kernel_params(),
        cost_estimate=LIGHT,
        name="layer_sum",
    )(summed[0], *arrived)
    other = shift(theirs, 1)

    low, high = jnp.where(core == 0, mine, other), jnp.where(core == 0, other, mine)
    return loss[:, 0], grad_head, jnp.concatenate([low, high], axis=1)


def fits_levels(hidden_states, teacher_logits):
    n = lax.axis_size("vocab")
    rows = hidden_states.shape[0]
    blocks, _, stored, side = teacher_logits.shape
    return (
        n == blocks * GROUP
        and blocks & (blocks - 1) == 0
        and rows * GROUP == side
        and rows % 16 == 0
        and 2 * n <= side
        and 6 * blocks * stored <= side
        and hidden_states.shape[1] % (CORES * 1280) == 0
    )


def on_device(
    hidden_states, head_weight, teacher_logits, block_lists, row_reader, tail_mass, token_weight
):
    plan = levels_plan if fits_levels(hidden_states, teacher_logits) else plain_plan
    return plan(
        hidden_states, head_weight, teacher_logits, block_lists, row_reader, tail_mass, token_weight
    )


def solution(mesh):
    in_specs = (
        P("vocab", None),
        P(None, "vocab"),
        P(None, None, "vocab", None),
        P(),
        P(),
        P(),
        P(),
    )
    out_specs = (P("vocab"), P(None, "vocab"), P("vocab", None))
    return jax.shard_map(
        on_device, mesh=mesh, in_specs=in_specs, out_specs=out_specs, check_vma=False
    )
```

```python
import functools

import jax
import jax.numpy as jnp
from jax import lax
from jax.experimental import pallas as pl
from jax.experimental.pallas import tpu as pltpu
from jax.sharding import PartitionSpec as P


def row_parts(scores, teacher_slab, listed_mask, student_exp, teacher_exp):
    return (
        jnp.sum(student_exp, axis=(2, 3)),
        jnp.sum(teacher_exp, axis=(2, 3)),
        jnp.sum(teacher_exp * scores, axis=(2, 3)),
        jnp.sum(teacher_exp * teacher_slab, axis=(2, 3)),
        jnp.sum(scores, axis=(2, 3)),
        jnp.sum(jnp.where(listed_mask, scores, 0.0), axis=(2, 3)),
    )


def plain_plan(
    hidden_states, head_weight, teacher_logits, block_lists, row_reader, tail_mass, token_weight
):
    blocks, listed_count, stored_rows, block_side = teacher_logits.shape
    slab_width = head_weight.shape[1]
    slab_blocks = slab_width // block_side
    devices = lax.axis_size("vocab")
    rank_self = lax.axis_index("vocab")
    tokens = blocks * block_side
    shard_rows = hidden_states.shape[0]
    gathered = lax.all_gather(hidden_states, "vocab", axis=0, tiled=True)
    logits = jnp.dot(gathered, head_weight, preferred_element_type=jnp.float32)
    owner_dev = block_lists // slab_blocks
    owned_here = owner_dev == rank_self
    within = block_lists - rank_self * slab_blocks
    token_iota = lax.broadcasted_iota(jnp.int32, (1, block_side, block_side), 1)
    token_map = (row_reader[:, None, :] == token_iota).astype(jnp.bfloat16)
    place_iota = lax.broadcasted_iota(jnp.int32, (1, slab_blocks, 1), 1)
    block_iota = lax.broadcasted_iota(jnp.int32, (1, devices * slab_blocks, 1), 1)
    picker = (block_lists[:, None, :] == block_iota).astype(jnp.bfloat16)
    outgoing = jnp.einsum(
        "tnk,tkrc->tnrc", picker, teacher_logits, preferred_element_type=jnp.float32
    ).astype(jnp.bfloat16)
    incoming = lax.all_to_all(outgoing, "vocab", split_axis=1, concat_axis=2, tiled=True)
    teacher_slab = jnp.einsum(
        "tpj,tbjc->tpbc", token_map, incoming, preferred_element_type=jnp.float32
    )
    listed = jnp.sum(
        ((within[:, None, :] == place_iota) & owned_here[:, None, :]).astype(jnp.int32), axis=2
    )
    scores = logits.reshape(blocks, block_side, slab_blocks, block_side)
    listed_mask = (listed > 0)[:, None, :, None]
    local_smax = jnp.max(scores, axis=(2, 3))
    local_tmax = jnp.max(jnp.where(listed_mask, teacher_slab, -1e30), axis=(2, 3))
    student_max, teacher_max = lax.pmax((local_smax, local_tmax), "vocab")
    student_exp = jnp.exp(scores - student_max[:, :, None, None])
    teacher_exp = jnp.exp(
        jnp.where(listed_mask, teacher_slab - teacher_max[:, :, None, None], -jnp.inf)
    )
    parts = row_parts(scores, teacher_slab, listed_mask, student_exp, teacher_exp)
    student_sum, teacher_sum, cross_sum, self_sum, logit_total, listed_total = lax.psum(
        (parts[0], parts[1], parts[2], parts[3], parts[4], parts[5]), "vocab"
    )
    tail_share = tail_mass.reshape(blocks, block_side)
    unlisted = float(devices * slab_width - block_side * listed_count)
    kept_mass = 1.0 - tail_share
    log_norm = student_max + jnp.log(student_sum)
    row_loss = (
        kept_mass * (jnp.log(kept_mass) - teacher_max - jnp.log(teacher_sum))
        + kept_mass * self_sum / teacher_sum
        + tail_share * jnp.log(tail_share / unlisted)
        - kept_mass * cross_sum / teacher_sum
        - tail_share / unlisted * (logit_total - listed_total)
        + log_norm
    )
    token_loss = lax.dynamic_slice_in_dim(
        row_loss.reshape(tokens), rank_self * shard_rows, shard_rows, 0
    )
    student_prob = student_exp / student_sum[:, :, None, None]
    teacher_prob = jnp.where(
        listed_mask,
        (kept_mass / teacher_sum)[:, :, None, None] * teacher_exp,
        (tail_share / unlisted)[:, :, None, None],
    )
    weight = token_weight.reshape(blocks, block_side)[:, :, None, None]
    grad_logits = (
        (weight * (student_prob - teacher_prob)).astype(jnp.bfloat16).reshape(tokens, slab_width)
    )
    grad_head = lax.dot_general(
        gathered, grad_logits, (((0,), (0,)), ((), ())), preferred_element_type=jnp.float32
    ).astype(jnp.bfloat16)
    grad_hidden = lax.psum_scatter(
        lax.dot_general(
            grad_logits, head_weight, (((1,), (1,)), ((), ())), preferred_element_type=jnp.float32
        ),
        "vocab",
        scatter_dimension=0,
        tiled=True,
    ).astype(jnp.bfloat16)
    return (token_loss, grad_head, grad_hidden)


CORES = 2
CHIPS = 4
GROUP = CORES * CHIPS
SLOTS = 4
LIGHT = pl.CostEstimate(flops=1, bytes_accessed=1, transcendentals=0)
SMALL_VMEM = 16 * 1024 * 1024
LOGITS_VMEM = 46 * 1024 * 1024
LARGE_VMEM = 48 * 1024 * 1024
STAT_ROWS = 16


def kernel_params(limit=SMALL_VMEM):
    return pltpu.CompilerParams(vmem_limit_bytes=limit)


def vmem_spec():
    return pl.BlockSpec(memory_space=pltpu.VMEM)


def hbm_spec():
    return pl.BlockSpec(memory_space=pltpu.HBM)


def smem_spec():
    return pl.BlockSpec(memory_space=pltpu.SMEM)


def shift(x, distance):
    n = lax.axis_size("vocab")
    return lax.ppermute(x, "vocab", [(i, i ^ distance) for i in range(n)])


def token_places(place, rows, side):
    row = lax.broadcasted_iota(jnp.int32, (side, 1), 0)
    group = row // rows
    chip = (group % CHIPS) ^ place[1]
    core = (group // CHIPS) ^ place[0]
    return (chip * CORES + core) * rows + row % rows


def pick_column(match, values):
    return jnp.sum(jnp.where(match, values, 0.0), axis=1, keepdims=True)


def teacher_kernel(
    unlisted, rows, pos_ref, place_ref, blocks_ref, stat_ref, reader_ref, tail_ref, prob_ref, entropy_ref
):
    layers, slots, side, _ = blocks_ref.shape
    pos = [pos_ref[i] for i in range(3)]
    lane = lax.broadcasted_iota(jnp.int32, (1, side), 1)
    where_token = token_places(pos, rows, side)
    for k in range(layers):
        block = pos[2] ^ k
        match = reader_ref[block] == where_token
        onehot = jnp.where(match, 1.0, 0.0).astype(jnp.bfloat16)
        normaliser = pick_column(match, stat_ref[0, block])
        tail = pick_column(lane == where_token, tail_ref[block])
        kept = 1.0 - tail
        rest = tail / unlisted
        span = pl.ds(k * side, side)
        prob_ref[span, :] = jnp.broadcast_to(rest, (side, prob_ref.shape[1]))
        for s in range(slots):
            place = place_ref[block, s]
            values = jnp.dot(onehot, blocks_ref[block, s], preferred_element_type=jnp.float32)
            prob = kept * jnp.exp(values - normaliser)

            @pl.when(place >= 0)
            def _():
                prob_ref[span, pl.ds(pl.multiple_of(place * side, side), side)] = prob

        if k == 0:
            mean = pick_column(match, stat_ref[1, block])
            entropy = kept * (jnp.log(kept) - normaliser + mean) + tail * jnp.log(rest)
            entropy_ref[...] = jnp.broadcast_to(entropy[:rows], entropy_ref.shape)


def assemble(pieces, rows, out_ref):
    layers = pieces[0].shape[0] // rows
    for k in range(layers):
        for p, piece in enumerate(pieces):
            out_ref[pl.ds((k * GROUP + p) * rows, rows), :] = piece[pl.ds(k * rows, rows), :]


def logits_kernel(rows, *refs):
    pieces, refs = refs[:GROUP], refs[GROUP:]
    w_ref, prob_ref, logits_ref, stat_ref, hidden, weight, sems, cross_ref = refs
    half, width = w_ref.shape[0] // 2, prob_ref.shape[1]
    tiles = w_ref.shape[1] // width
    step = pl.program_id(0)

    def copy(i):
        span = pl.ds(i * half, half)
        return pltpu.make_async_copy(w_ref.at[span, :], weight.at[span, :], sems.at[i])

    @pl.when(step == 0)
    def _():
        copy(0).start()
        copy(1).start()
        assemble(pieces, rows, hidden)
        copy(0).wait()

    @pl.when(step == tiles)
    def _():
        copy(1).wait()

    @pl.when(step < tiles)
    def _():
        span = pl.ds(pl.multiple_of(step * width, width), width)
        logits_ref[:, span] = jnp.dot(
            hidden[:, :half], weight[:half, span], preferred_element_type=jnp.float32
        )

    @pl.when(step >= tiles)
    def _():
        span = pl.ds(pl.multiple_of((step - tiles) * width, width), width)
        total = logits_ref[:, span] + jnp.dot(
            hidden[:, half:], weight[half:, span], preferred_element_type=jnp.float32
        )
        logits_ref[:, span] = total
        product = total * prob_ref[...]
        folded = product[:, :128]
        for i in range(1, width // 128):
            folded = folded + product[:, i * 128 : (i + 1) * 128]
        cross_ref[...] = jnp.where(step == tiles, 0.0, cross_ref[...]) + folded

    @pl.when(step == 2 * tiles - 1)
    def _():
        logits = logits_ref[...]
        top = jnp.max(logits, axis=1, keepdims=True)
        norm = top + jnp.log(jnp.sum(jnp.exp(logits - top), axis=1, keepdims=True))
        cross = jnp.sum(cross_ref[...], axis=1, keepdims=True)
        lane = lax.broadcasted_iota(jnp.int32, (1, 128), 1)
        both = jnp.where(lane == 0, norm, jnp.where(lane == 1, cross, 0.0)).T
        tokens = logits.shape[0]
        packed = [both[i : i + 1, t : t + 128] for i in range(2) for t in range(0, tokens, 128)]
        stat_ref[...] = jnp.broadcast_to(jnp.concatenate(packed, axis=0)[None], stat_ref.shape)


def grad_kernel(
    rows, pos_ref, stat_ref, logits_ref, prob_ref, weight_ref, entropy_ref, grad_ref, loss_ref
):
    tokens = logits_ref.shape[0]
    devices = tokens // rows
    layers, _, side = weight_ref.shape
    layer_bits = (devices // GROUP).bit_length() - 1
    pos = [pos_ref[i] for i in range(3)]
    rank = pos_ref[3]
    lane = lax.broadcasted_iota(jnp.int32, (1, 128), 1)
    per_stat = stat_ref.shape[1] // 2
    norms, crosses = [
        jnp.concatenate([stat_ref[:, i * per_stat + t, :] for t in range(per_stat)], axis=1) for i in range(2)
    ]
    stat = jnp.concatenate(
        [norms, crosses, jnp.zeros((128 - 2 * devices, tokens), jnp.float32)], axis=0
    ).T
    pairs = [(0, 2), (1, 0), (2, 1)] + [(3 + i, 3 + i) for i in range(layer_bits)]
    for index_bit, block_bit in pairs:
        halves = stat.reshape(devices >> (block_bit + 1), 2, rows << block_bit, 128)
        swapped = jnp.stack([halves[:, 1], halves[:, 0]], axis=1).reshape(tokens, 128)
        stat = jnp.where(((lane ^ rank) >> index_bit) & 1 == 1, swapped, stat)
    is_norm = lane < devices
    is_cross = (lane >= devices) & (lane < 2 * devices)
    top = jnp.max(jnp.where(is_norm, stat, -jnp.inf), axis=1, keepdims=True)
    total = jnp.sum(jnp.where(is_norm, jnp.exp(stat - top), 0.0), axis=1, keepdims=True)
    log_norm = top + jnp.log(total)
    cross = jnp.sum(jnp.where(is_cross, stat, 0.0), axis=1, keepdims=True)
    loss_ref[...] = entropy_ref[...] - cross[:rows] + log_norm[:rows]
    where_token = token_places(pos, rows, side)
    for k in range(layers):
        span = pl.ds(k * side, side)
        weight = pick_column(lane == where_token, weight_ref[pos[2] ^ k])
        student = jnp.exp(logits_ref[span, :] - log_norm[k * side : (k + 1) * side])
        grad_ref[span, :] = (weight * (student - prob_ref[span, :])).astype(grad_ref.dtype)


def partial_kernel(rows, core_ref, grad_ref, sib_ref, w_ref, sib_w_ref, *refs):
    outs, swapped = refs[:CHIPS], refs[CHIPS]
    layers = outs[0].shape[0]
    half = CHIPS * rows

    @pl.when(pl.program_id(0) == 0)
    def _():
        for k in range(layers):
            for core in range(CORES):
                swapped[pl.ds((k * CORES + core) * half, half), :] = sib_ref[
                    pl.ds((k * CORES + 1 - core) * half, half), :
                ]

    contract = (((1,), (1,)), ((), ()))
    total = lax.dot_general(
        grad_ref[...], w_ref[...], contract, preferred_element_type=jnp.float32
    ) + lax.dot_general(
        swapped[...], sib_w_ref[...], contract, preferred_element_type=jnp.float32
    )
    for j, out in enumerate(outs):
        for k in range(layers):
            for core in range(CORES):
                start = (k * GROUP + core * CHIPS + j) * rows
                out[k, core] = total[start : start + rows].astype(out.dtype)


def head_kernel(rows, *refs):
    pieces, (grad_ref, out_ref, hidden) = refs[:-3], refs[-3:]
    assemble(pieces, rows, hidden)
    out_ref[...] = lax.dot_general(
        hidden[...], grad_ref[...], (((0,), (0,)), ((), ())), preferred_element_type=jnp.float32
    ).astype(out_ref.dtype)


def chip_sum_kernel(own_ref, *refs):
    arrived, outs = refs[: CHIPS - 1], refs[CHIPS - 1 :]
    for k, out in enumerate(outs):
        total = own_ref[k]
        for part in arrived:
            total = total + part[k].astype(jnp.float32)
        out[...] = total.astype(out.dtype)


def layer_sum_kernel(own_ref, *refs):
    arrived, (mine, theirs) = refs[:-2], refs[-2:]
    total = own_ref[...]
    for part in arrived:
        total = total + part[...].astype(jnp.float32)
    mine[...] = total[0].astype(mine.dtype)
    theirs[...] = total[1].astype(theirs.dtype)


def pack_kernel(code_ref, x_ref, out_ref):
    blocks, count, side = x_ref.shape
    devices, size, _ = out_ref.shape
    slot_rows = (size - STAT_ROWS) // blocks
    stored = slot_rows // SLOTS
    target = lax.broadcasted_iota(jnp.int32, (devices * slot_rows, 1), 0)
    row = lax.broadcasted_iota(jnp.int32, (count, 1), 0) % stored
    lane = lax.broadcasted_iota(jnp.int32, (1, side), 1)
    stat = jnp.zeros((1, side), jnp.float32)
    for t in range(blocks):
        onehot = jnp.where(code_ref[t] == target, 1.0, 0.0).astype(x_ref.dtype)
        packed = jnp.dot(onehot, x_ref[t], preferred_element_type=jnp.float32).astype(out_ref.dtype)
        for device in range(devices):
            out_ref[device, pl.ds(t * slot_rows, slot_rows), :] = packed[
                device * slot_rows : (device + 1) * slot_rows
            ]
        values = x_ref[t].astype(jnp.float32)
        row_top = jnp.max(values, axis=1, keepdims=True)
        tops = [jnp.max(jnp.where(row == r, row_top, -jnp.inf), axis=0, keepdims=True) for r in range(stored)]
        top = jnp.zeros_like(row_top)
        for r in range(stored):
            top = jnp.where(row == r, tops[r], top)
        powers = jnp.exp(values - top)
        sums = jnp.sum(powers, axis=1, keepdims=True)
        weighted = jnp.sum(powers * values, axis=1, keepdims=True)
        for r in range(stored):
            total = jnp.sum(jnp.where(row == r, sums, 0.0), axis=0, keepdims=True)
            mean = jnp.sum(jnp.where(row == r, weighted, 0.0), axis=0, keepdims=True) / total
            stat = jnp.where(lane == t * stored + r, tops[r] + jnp.log(total), stat)
            stat = jnp.where(lane == (blocks + t) * stored + r, mean, stat)
    high = stat.astype(jnp.bfloat16).astype(jnp.float32)
    middle = (stat - high).astype(jnp.bfloat16).astype(jnp.float32)
    low = stat - high - middle
    parts = jnp.concatenate([high, middle, low, jnp.zeros((STAT_ROWS - 3, side), jnp.float32)], axis=0)
    parts = parts.astype(out_ref.dtype)
    for device in range(devices):
        out_ref[device, pl.ds(size - STAT_ROWS, STAT_ROWS), :] = parts


def pack_teacher(teacher_logits, block_lists, places):
    blocks, listed_count, stored, side = teacher_logits.shape
    n = lax.axis_size("vocab")
    rank = lax.axis_index("vocab")
    owner = block_lists // places
    earlier = jnp.tril(jnp.ones((listed_count, listed_count), jnp.bool_), -1)
    slot = jnp.sum((owner[:, :, None] == owner[:, None, :]) & earlier, axis=2, dtype=jnp.int32)
    code = owner * SLOTS + slot
    rows_code = (code[:, :, None] * stored + jnp.arange(stored, dtype=jnp.int32)).reshape(blocks, 1, -1)
    payload = pl.pallas_call(
        pack_kernel,
        in_specs=[vmem_spec()] * 2,
        out_specs=vmem_spec(),
        out_shape=jax.ShapeDtypeStruct(
            (n, blocks * SLOTS * stored + STAT_ROWS, side), teacher_logits.dtype
        ),
        compiler_params=kernel_params(),
        cost_estimate=LIGHT,
        name="pack_teacher",
    )(rows_code, teacher_logits.reshape(blocks, listed_count * stored, side))
    mine = code[:, None, :] == rank * SLOTS + jnp.arange(SLOTS, dtype=jnp.int32)[None, :, None]
    place = jnp.sum(jnp.where(mine, (block_lists % places + 1)[:, None, :], 0), axis=2) - 1
    return payload, place.astype(jnp.int32)


def unpack_teacher(arrived, blocks, stored):
    n, _, side = arrived.shape
    arrived_blocks = (
        arrived[:, :-3]
        .reshape(n, blocks, SLOTS, stored, side)
        .transpose(1, 2, 0, 3, 4)
        .reshape(blocks, SLOTS, n * stored, side)
    )
    arrived_stat = (
        arrived[:, -3:, : 2 * blocks * stored]
        .astype(jnp.float32)
        .sum(axis=1)
        .reshape(n, 2, blocks, stored)
        .transpose(1, 2, 0, 3)
        .reshape(2, blocks, 1, n * stored)
    )
    return arrived_blocks, arrived_stat


def levels_plan(
    hidden_states, head_weight, teacher_logits, block_lists, row_reader, tail_mass, token_weight
):
    blocks, listed_count, stored, side = teacher_logits.shape
    rows, depth = hidden_states.shape
    slab = head_weight.shape[1]
    n = lax.axis_size("vocab")
    rank = lax.axis_index("vocab")
    tokens = n * rows
    layers = n // GROUP
    half = depth // CORES
    bf16, f32 = jnp.bfloat16, jnp.float32
    core, chip, layer = rank % CORES, (rank // CORES) % CHIPS, rank // GROUP
    pos = jnp.stack([core, chip, layer, rank]).astype(jnp.int32)
    unlisted = float(n * slab - side * listed_count)

    column = [hidden_states] + [shift(hidden_states, k * GROUP) for k in range(1, layers)]
    sib_w = shift(head_weight, 1)
    column = jnp.concatenate(column, axis=0)
    plane = [column] + [shift(column, j * CORES) for j in range(1, CHIPS)]
    payload, place = pack_teacher(teacher_logits, block_lists, slab // side)
    payload, _ = lax.optimization_barrier((payload, column))
    arrived = lax.all_to_all(
        payload[:, : 3 - STAT_ROWS], "vocab", split_axis=0, concat_axis=0, tiled=True
    )
    arrived_blocks, arrived_stat = unpack_teacher(arrived, blocks, stored)

    prob, entropy = pl.pallas_call(
        lambda *refs: teacher_kernel(unlisted, rows, *refs),
        out_shape=(
            jax.ShapeDtypeStruct((tokens, slab), f32),
            jax.ShapeDtypeStruct((rows, side), f32),
        ),
        in_specs=[smem_spec(), smem_spec()] + [vmem_spec()] * 4,
        out_specs=(vmem_spec(), vmem_spec()),
        compiler_params=kernel_params(),
        cost_estimate=LIGHT,
        name="teacher_prob",
    )(
        pos,
        place,
        arrived_blocks,
        arrived_stat,
        row_reader.reshape(blocks, 1, side),
        tail_mass.reshape(blocks, 1, side),
    )

    plane[-1], prob, sib_w = lax.optimization_barrier((plane[-1], prob, sib_w))
    pieces = plane + [shift(piece, 1) for piece in plane]

    width = 256 if slab % 256 == 0 else 128
    tiles = slab // width
    whole = lambda t: (0, 0)
    logits, stat = pl.pallas_call(
        functools.partial(logits_kernel, rows),
        grid=(2 * tiles,),
        out_shape=[
            jax.ShapeDtypeStruct((tokens, slab), f32),
            jax.ShapeDtypeStruct((n, 2 * tokens // 128, 128), f32),
        ],
        in_specs=[vmem_spec()] * len(pieces)
        + [hbm_spec(), pl.BlockSpec((tokens, width), lambda t: (0, jnp.maximum(t - tiles, 0)))],
        out_specs=[
            pl.BlockSpec((tokens, slab), whole),
            pl.BlockSpec((n, 2 * tokens // 128, 128), lambda t: (0, 0, 0)),
        ],
        scratch_shapes=[
            pltpu.VMEM((tokens, depth), bf16),
            pltpu.VMEM((depth, slab), bf16),
            pltpu.SemaphoreType.DMA((2,)),
            pltpu.VMEM((tokens, 128), f32),
        ],
        compiler_params=kernel_params(LOGITS_VMEM),
        cost_estimate=LIGHT,
        name="logits",
    )(*pieces, head_weight, prob)
    stat = lax.all_to_all(stat, "vocab", split_axis=0, concat_axis=0, tiled=True)

    grad, loss = pl.pallas_call(
        lambda *refs: grad_kernel(rows, *refs),
        out_shape=(
            jax.ShapeDtypeStruct((tokens, slab), bf16),
            jax.ShapeDtypeStruct((rows, side), f32),
        ),
        in_specs=[smem_spec()] + [vmem_spec()] * 5,
        out_specs=(vmem_spec(), vmem_spec()),
        compiler_params=kernel_params(),
        cost_estimate=LIGHT,
        name="grad_logits",
    )(pos, stat, logits, prob, token_weight.reshape(blocks, 1, side), entropy)
    sib_grad = shift(grad, 1)

    tile = half // 5
    out_block = pl.BlockSpec((layers, CORES, rows, tile), lambda t, pos: (0, 0, 0, t))
    partial = pl.pallas_call(
        functools.partial(partial_kernel, rows),
        grid_spec=pltpu.PrefetchScalarGridSpec(
            num_scalar_prefetch=1,
            grid=(5,),
            in_specs=[pl.BlockSpec((tokens, slab), lambda t, pos: (0, 0))] * 2
            + [pl.BlockSpec((tile, slab), lambda t, pos: (pos[0] * 5 + t, 0))] * 2,
            out_specs=[out_block] * CHIPS,
            scratch_shapes=[pltpu.VMEM((tokens, slab), bf16)],
        ),
        out_shape=[
            jax.ShapeDtypeStruct((layers, CORES, rows, half), f32 if j == 0 else bf16) for j in range(CHIPS)
        ],
        compiler_params=kernel_params(LARGE_VMEM),
        cost_estimate=LIGHT,
        name="grad_hidden_partial",
    )(pos, grad, sib_grad, head_weight, sib_w)
    *partial, late_grad = lax.optimization_barrier((*partial, grad))
    arrived = [shift(partial[j], j * CORES) for j in range(1, CHIPS)]

    head_tile = half // 2
    grad_head = pl.pallas_call(
        functools.partial(head_kernel, rows),
        grid=(4,),
        in_specs=[pl.BlockSpec((layers * rows, head_tile), lambda t: (0, t)) for _ in pieces]
        + [pl.BlockSpec((tokens, slab), whole)],
        out_specs=pl.BlockSpec((head_tile, slab), lambda t: (t, 0)),
        out_shape=jax.ShapeDtypeStruct((depth, slab), bf16),
        scratch_shapes=[pltpu.VMEM((tokens, head_tile), bf16)],
        compiler_params=kernel_params(LARGE_VMEM),
        cost_estimate=LIGHT,
        name="grad_head",
    )(*pieces, late_grad)
    arrived, grad_head = lax.optimization_barrier((arrived, grad_head))

    summed = pl.pallas_call(
        chip_sum_kernel,
        in_specs=[vmem_spec()] * CHIPS,
        out_specs=[vmem_spec()] * layers,
        out_shape=[
            jax.ShapeDtypeStruct((CORES, rows, half), f32 if k == 0 else bf16) for k in range(layers)
        ],
        compiler_params=kernel_params(),
        cost_estimate=LIGHT,
        name="chip_sum",
    )(partial[0], *arrived)
    arrived = [shift(summed[k], k * GROUP) for k in range(1, layers)]
    mine, theirs = pl.pallas_call(
        layer_sum_kernel,
        in_specs=[vmem_spec()] * layers,
        out_specs=[vmem_spec()] * 2,
        out_shape=[jax.ShapeDtypeStruct((rows, half), bf16)] * 2,
        compiler_params=kernel_params(),
        cost_estimate=LIGHT,
        name="layer_sum",
    )(summed[0], *arrived)
    other = shift(theirs, 1)

    low, high = jnp.where(core == 0, mine, other), jnp.where(core == 0, other, mine)
    return loss[:, 0], grad_head, jnp.concatenate([low, high], axis=1)


def fits_levels(hidden_states, teacher_logits):
    n = lax.axis_size("vocab")
    rows = hidden_states.shape[0]
    blocks, _, stored, side = teacher_logits.shape
    return (
        n == blocks * GROUP
        and blocks & (blocks - 1) == 0
        and rows * GROUP == side
        and rows % 16 == 0
        and 2 * n <= side
        and 6 * blocks * stored <= side
        and hidden_states.shape[1] % (CORES * 1280) == 0
    )


def on_device(
    hidden_states, head_weight, teacher_logits, block_lists, row_reader, tail_mass, token_weight
):
    plan = levels_plan if fits_levels(hidden_states, teacher_logits) else plain_plan
    return plan(
        hidden_states, head_weight, teacher_logits, block_lists, row_reader, tail_mass, token_weight
    )


def solution(mesh):
    in_specs = (
        P("vocab", None),
        P(None, "vocab"),
        P(None, None, "vocab", None),
        P(),
        P(),
        P(),
        P(),
    )
    out_specs = (P("vocab"), P(None, "vocab"), P("vocab", None))
    return jax.shard_map(
        on_device, mesh=mesh, in_specs=in_specs, out_specs=out_specs, check_vma=False
    )
```

```python
import functools

import jax
import jax.numpy as jnp
from jax import lax
from jax.experimental import pallas as pl
from jax.experimental.pallas import tpu as pltpu
from jax.sharding import PartitionSpec as P


def row_parts(scores, teacher_slab, listed_mask, student_exp, teacher_exp):
    return (
        jnp.sum(student_exp, axis=(2, 3)),
        jnp.sum(teacher_exp, axis=(2, 3)),
        jnp.sum(teacher_exp * scores, axis=(2, 3)),
        jnp.sum(teacher_exp * teacher_slab, axis=(2, 3)),
        jnp.sum(scores, axis=(2, 3)),
        jnp.sum(jnp.where(listed_mask, scores, 0.0), axis=(2, 3)),
    )


def plain_plan(
    hidden_states, head_weight, teacher_logits, block_lists, row_reader, tail_mass, token_weight
):
    blocks, listed_count, stored_rows, block_side = teacher_logits.shape
    slab_width = head_weight.shape[1]
    slab_blocks = slab_width // block_side
    devices = lax.axis_size("vocab")
    rank_self = lax.axis_index("vocab")
    tokens = blocks * block_side
    shard_rows = hidden_states.shape[0]
    gathered = lax.all_gather(hidden_states, "vocab", axis=0, tiled=True)
    logits = jnp.dot(gathered, head_weight, preferred_element_type=jnp.float32)
    owner_dev = block_lists // slab_blocks
    owned_here = owner_dev == rank_self
    within = block_lists - rank_self * slab_blocks
    token_iota = lax.broadcasted_iota(jnp.int32, (1, block_side, block_side), 1)
    token_map = (row_reader[:, None, :] == token_iota).astype(jnp.bfloat16)
    place_iota = lax.broadcasted_iota(jnp.int32, (1, slab_blocks, 1), 1)
    block_iota = lax.broadcasted_iota(jnp.int32, (1, devices * slab_blocks, 1), 1)
    picker = (block_lists[:, None, :] == block_iota).astype(jnp.bfloat16)
    outgoing = jnp.einsum(
        "tnk,tkrc->tnrc", picker, teacher_logits, preferred_element_type=jnp.float32
    ).astype(jnp.bfloat16)
    incoming = lax.all_to_all(outgoing, "vocab", split_axis=1, concat_axis=2, tiled=True)
    teacher_slab = jnp.einsum(
        "tpj,tbjc->tpbc", token_map, incoming, preferred_element_type=jnp.float32
    )
    listed = jnp.sum(
        ((within[:, None, :] == place_iota) & owned_here[:, None, :]).astype(jnp.int32), axis=2
    )
    scores = logits.reshape(blocks, block_side, slab_blocks, block_side)
    listed_mask = (listed > 0)[:, None, :, None]
    local_smax = jnp.max(scores, axis=(2, 3))
    local_tmax = jnp.max(jnp.where(listed_mask, teacher_slab, -1e30), axis=(2, 3))
    student_max, teacher_max = lax.pmax((local_smax, local_tmax), "vocab")
    student_exp = jnp.exp(scores - student_max[:, :, None, None])
    teacher_exp = jnp.exp(
        jnp.where(listed_mask, teacher_slab - teacher_max[:, :, None, None], -jnp.inf)
    )
    parts = row_parts(scores, teacher_slab, listed_mask, student_exp, teacher_exp)
    student_sum, teacher_sum, cross_sum, self_sum, logit_total, listed_total = lax.psum(
        (parts[0], parts[1], parts[2], parts[3], parts[4], parts[5]), "vocab"
    )
    tail_share = tail_mass.reshape(blocks, block_side)
    unlisted = float(devices * slab_width - block_side * listed_count)
    kept_mass = 1.0 - tail_share
    log_norm = student_max + jnp.log(student_sum)
    row_loss = (
        kept_mass * (jnp.log(kept_mass) - teacher_max - jnp.log(teacher_sum))
        + kept_mass * self_sum / teacher_sum
        + tail_share * jnp.log(tail_share / unlisted)
        - kept_mass * cross_sum / teacher_sum
        - tail_share / unlisted * (logit_total - listed_total)
        + log_norm
    )
    token_loss = lax.dynamic_slice_in_dim(
        row_loss.reshape(tokens), rank_self * shard_rows, shard_rows, 0
    )
    student_prob = student_exp / student_sum[:, :, None, None]
    teacher_prob = jnp.where(
        listed_mask,
        (kept_mass / teacher_sum)[:, :, None, None] * teacher_exp,
        (tail_share / unlisted)[:, :, None, None],
    )
    weight = token_weight.reshape(blocks, block_side)[:, :, None, None]
    grad_logits = (
        (weight * (student_prob - teacher_prob)).astype(jnp.bfloat16).reshape(tokens, slab_width)
    )
    grad_head = lax.dot_general(
        gathered, grad_logits, (((0,), (0,)), ((), ())), preferred_element_type=jnp.float32
    ).astype(jnp.bfloat16)
    grad_hidden = lax.psum_scatter(
        lax.dot_general(
            grad_logits, head_weight, (((1,), (1,)), ((), ())), preferred_element_type=jnp.float32
        ),
        "vocab",
        scatter_dimension=0,
        tiled=True,
    ).astype(jnp.bfloat16)
    return (token_loss, grad_head, grad_hidden)


CORES = 2
CHIPS = 4
GROUP = CORES * CHIPS
SLOTS = 4
LIGHT = pl.CostEstimate(flops=1, bytes_accessed=1, transcendentals=0)
SMALL_VMEM = 16 * 1024 * 1024
LOGITS_VMEM = 46 * 1024 * 1024
LARGE_VMEM = 48 * 1024 * 1024
STAT_ROWS = 16


def kernel_params(limit=SMALL_VMEM):
    return pltpu.CompilerParams(vmem_limit_bytes=limit)


def vmem_spec():
    return pl.BlockSpec(memory_space=pltpu.VMEM)


def hbm_spec():
    return pl.BlockSpec(memory_space=pltpu.HBM)


def smem_spec():
    return pl.BlockSpec(memory_space=pltpu.SMEM)


def shift(x, distance):
    n = lax.axis_size("vocab")
    return lax.ppermute(x, "vocab", [(i, i ^ distance) for i in range(n)])


def token_places(place, rows, side):
    row = lax.broadcasted_iota(jnp.int32, (side, 1), 0)
    group = row // rows
    chip = (group % CHIPS) ^ place[1]
    core = (group // CHIPS) ^ place[0]
    return (chip * CORES + core) * rows + row % rows


def pick_column(match, values):
    return jnp.sum(jnp.where(match, values, 0.0), axis=1, keepdims=True)


def teacher_kernel(
    unlisted, rows, pos_ref, place_ref, blocks_ref, stat_ref, reader_ref, tail_ref, prob_ref, entropy_ref
):
    layers, slots, side, _ = blocks_ref.shape
    pos = [pos_ref[i] for i in range(3)]
    lane = lax.broadcasted_iota(jnp.int32, (1, side), 1)
    where_token = token_places(pos, rows, side)
    for k in range(layers):
        block = pos[2] ^ k
        match = reader_ref[block] == where_token
        onehot = jnp.where(match, 1.0, 0.0).astype(jnp.bfloat16)
        normaliser = pick_column(match, stat_ref[0, block])
        tail = pick_column(lane == where_token, tail_ref[block])
        kept = 1.0 - tail
        rest = tail / unlisted
        span = pl.ds(k * side, side)
        prob_ref[span, :] = jnp.broadcast_to(rest, (side, prob_ref.shape[1]))
        for s in range(slots):
            place = place_ref[block, s]
            values = jnp.dot(onehot, blocks_ref[block, s], preferred_element_type=jnp.float32)
            prob = kept * jnp.exp(values - normaliser)

            @pl.when(place >= 0)
            def _():
                prob_ref[span, pl.ds(pl.multiple_of(place * side, side), side)] = prob

        if k == 0:
            mean = pick_column(match, stat_ref[1, block])
            entropy = kept * (jnp.log(kept) - normaliser + mean) + tail * jnp.log(rest)
            entropy_ref[...] = jnp.broadcast_to(entropy[:rows], entropy_ref.shape)


def assemble(pieces, by_layer, rows, out_ref, columns=slice(None)):
    count = len(pieces) // CORES
    groups = pieces[0].shape[0] // rows
    for p, piece in enumerate(pieces):
        core, i = p // count, p % count
        for g in range(groups):
            layer, chip = (i, g) if by_layer else (g, i)
            block = layer * GROUP + core * CHIPS + chip
            out_ref[pl.ds(block * rows, rows), columns] = piece[pl.ds(g * rows, rows), :]


def logits_kernel(rows, wide_count, *refs):
    pieces, refs = refs[:-8], refs[-8:]
    w_ref, prob_ref, logits_ref, stat_ref, hidden, weight, sems, cross_ref = refs
    wide_pieces, narrow_pieces = pieces[:wide_count], pieces[wide_count:]
    depth = w_ref.shape[0]
    wide, width = wide_pieces[0].shape[1], prob_ref.shape[1]
    tiles = w_ref.shape[1] // width
    step = pl.program_id(0)
    parts = [slice(wide, depth), slice(0, wide)]

    def copy(i):
        span = pl.ds(parts[i].start, parts[i].stop - parts[i].start)
        return pltpu.make_async_copy(w_ref.at[span, :], weight.at[span, :], sems.at[i])

    @pl.when(step == 0)
    def _():
        copy(0).start()
        copy(1).start()
        assemble(narrow_pieces, True, rows, hidden, parts[0])
        assemble(wide_pieces, False, rows, hidden, parts[1])
        copy(0).wait()

    @pl.when(step == tiles)
    def _():
        copy(1).wait()

    @pl.when(step < tiles)
    def _():
        span = pl.ds(pl.multiple_of(step * width, width), width)
        logits_ref[:, span] = jnp.dot(
            hidden[:, parts[0]], weight[parts[0], span], preferred_element_type=jnp.float32
        )

    @pl.when(step >= tiles)
    def _():
        span = pl.ds(pl.multiple_of((step - tiles) * width, width), width)
        total = logits_ref[:, span] + jnp.dot(
            hidden[:, parts[1]], weight[parts[1], span], preferred_element_type=jnp.float32
        )
        logits_ref[:, span] = total
        product = total * prob_ref[...]
        folded = product[:, :128]
        for i in range(1, width // 128):
            folded = folded + product[:, i * 128 : (i + 1) * 128]
        cross_ref[...] = jnp.where(step == tiles, 0.0, cross_ref[...]) + folded

    @pl.when(step == 2 * tiles - 1)
    def _():
        logits = logits_ref[...]
        top = jnp.max(logits, axis=1, keepdims=True)
        norm = top + jnp.log(jnp.sum(jnp.exp(logits - top), axis=1, keepdims=True))
        cross = jnp.sum(cross_ref[...], axis=1, keepdims=True)
        lane = lax.broadcasted_iota(jnp.int32, (1, 128), 1)
        both = jnp.where(lane == 0, norm, jnp.where(lane == 1, cross, 0.0)).T
        tokens = logits.shape[0]
        packed = [both[i : i + 1, t : t + 128] for i in range(2) for t in range(0, tokens, 128)]
        stat_ref[...] = jnp.broadcast_to(jnp.concatenate(packed, axis=0)[None], stat_ref.shape)


def grad_kernel(
    rows, pos_ref, stat_ref, logits_ref, prob_ref, weight_ref, entropy_ref, grad_ref, loss_ref
):
    tokens = logits_ref.shape[0]
    devices = tokens // rows
    layers, _, side = weight_ref.shape
    layer_bits = (devices // GROUP).bit_length() - 1
    pos = [pos_ref[i] for i in range(3)]
    rank = pos_ref[3]
    lane = lax.broadcasted_iota(jnp.int32, (1, 128), 1)
    per_stat = stat_ref.shape[1] // 2
    norms, crosses = [
        jnp.concatenate([stat_ref[:, i * per_stat + t, :] for t in range(per_stat)], axis=1) for i in range(2)
    ]
    stat = jnp.concatenate(
        [norms, crosses, jnp.zeros((128 - 2 * devices, tokens), jnp.float32)], axis=0
    ).T
    pairs = [(0, 2), (1, 0), (2, 1)] + [(3 + i, 3 + i) for i in range(layer_bits)]
    for index_bit, block_bit in pairs:
        halves = stat.reshape(devices >> (block_bit + 1), 2, rows << block_bit, 128)
        swapped = jnp.stack([halves[:, 1], halves[:, 0]], axis=1).reshape(tokens, 128)
        stat = jnp.where(((lane ^ rank) >> index_bit) & 1 == 1, swapped, stat)
    is_norm = lane < devices
    is_cross = (lane >= devices) & (lane < 2 * devices)
    top = jnp.max(jnp.where(is_norm, stat, -jnp.inf), axis=1, keepdims=True)
    total = jnp.sum(jnp.where(is_norm, jnp.exp(stat - top), 0.0), axis=1, keepdims=True)
    log_norm = top + jnp.log(total)
    cross = jnp.sum(jnp.where(is_cross, stat, 0.0), axis=1, keepdims=True)
    loss_ref[...] = entropy_ref[...] - cross[:rows] + log_norm[:rows]
    where_token = token_places(pos, rows, side)
    for k in range(layers):
        span = pl.ds(k * side, side)
        weight = pick_column(lane == where_token, weight_ref[pos[2] ^ k])
        student = jnp.exp(logits_ref[span, :] - log_norm[k * side : (k + 1) * side])
        grad_ref[span, :] = (weight * (student - prob_ref[span, :])).astype(grad_ref.dtype)


def partial_kernel(rows, wide_steps, core_ref, grad_ref, sib_ref, w_ref, sib_w_ref, *refs):
    outs, swapped = refs[:-1], refs[-1]
    wide_outs, narrow_outs = outs[:CHIPS], outs[CHIPS:]
    layers = len(narrow_outs)
    half = CHIPS * rows
    step = pl.program_id(0)

    @pl.when(step == 0)
    def _():
        for k in range(layers):
            for core in range(CORES):
                swapped[pl.ds((k * CORES + core) * half, half), :] = sib_ref[
                    pl.ds((k * CORES + 1 - core) * half, half), :
                ]

    contract = (((1,), (1,)), ((), ()))
    total = lax.dot_general(
        grad_ref[...], w_ref[...], contract, preferred_element_type=jnp.float32
    ) + lax.dot_general(swapped[...], sib_w_ref[...], contract, preferred_element_type=jnp.float32)

    def parts():
        for k in range(layers):
            for core in range(CORES):
                for j in range(CHIPS):
                    start = (k * GROUP + core * CHIPS + j) * rows
                    yield k, core, j, total[start : start + rows]

    @pl.when(step < wide_steps)
    def _():
        for k, core, j, part in parts():
            wide_outs[j][k, core] = part.astype(wide_outs[j].dtype)

    @pl.when(step >= wide_steps)
    def _():
        for k, core, j, part in parts():
            narrow_outs[k][j, core] = part.astype(narrow_outs[k].dtype)


def head_kernel(rows, wide_count, wide_steps, *refs):
    pieces, (grad_ref, out_ref, hidden) = refs[:-3], refs[-3:]
    step = pl.program_id(0)

    @pl.when(step < wide_steps)
    def _():
        assemble(pieces[:wide_count], False, rows, hidden)

    @pl.when(step >= wide_steps)
    def _():
        assemble(pieces[wide_count:], True, rows, hidden)

    out_ref[...] = lax.dot_general(
        hidden[...], grad_ref[...], (((0,), (0,)), ((), ())), preferred_element_type=jnp.float32
    ).astype(out_ref.dtype)


def sum_of(parts, index=...):
    total = parts[0][index]
    for part in parts[1:]:
        total = total + part[index].astype(jnp.float32)
    return total


def first_sum_kernel(layers, *refs):
    wide, narrow, outs = refs[:CHIPS], refs[CHIPS : CHIPS + layers], refs[CHIPS + layers :]
    for k, out in enumerate(outs[:layers]):
        out[...] = sum_of(wide, k).astype(out.dtype)
    for j, out in enumerate(outs[layers:]):
        out[...] = sum_of(narrow, j).astype(out.dtype)


def last_sum_kernel(layers, *refs):
    wide, narrow, (mine, theirs) = refs[:layers], refs[layers:-2], refs[-2:]
    split = wide[0].shape[-1]
    for parts, columns in ((wide, slice(0, split)), (narrow, slice(split, mine.shape[1]))):
        total = sum_of(parts)
        mine[:, columns] = total[0].astype(mine.dtype)
        theirs[:, columns] = total[1].astype(theirs.dtype)


def pack_kernel(code_ref, x_ref, out_ref):
    blocks, count, side = x_ref.shape
    devices, size, _ = out_ref.shape
    slot_rows = (size - STAT_ROWS) // blocks
    stored = slot_rows // SLOTS
    target = lax.broadcasted_iota(jnp.int32, (devices * slot_rows, 1), 0)
    row = lax.broadcasted_iota(jnp.int32, (count, 1), 0) % stored
    lane = lax.broadcasted_iota(jnp.int32, (1, side), 1)
    stat = jnp.zeros((1, side), jnp.float32)
    for t in range(blocks):
        onehot = jnp.where(code_ref[t] == target, 1.0, 0.0).astype(x_ref.dtype)
        packed = jnp.dot(onehot, x_ref[t], preferred_element_type=jnp.float32).astype(out_ref.dtype)
        for device in range(devices):
            out_ref[device, pl.ds(t * slot_rows, slot_rows), :] = packed[
                device * slot_rows : (device + 1) * slot_rows
            ]
        values = x_ref[t].astype(jnp.float32)
        row_top = jnp.max(values, axis=1, keepdims=True)
        tops = [jnp.max(jnp.where(row == r, row_top, -jnp.inf), axis=0, keepdims=True) for r in range(stored)]
        top = jnp.zeros_like(row_top)
        for r in range(stored):
            top = jnp.where(row == r, tops[r], top)
        powers = jnp.exp(values - top)
        sums = jnp.sum(powers, axis=1, keepdims=True)
        weighted = jnp.sum(powers * values, axis=1, keepdims=True)
        for r in range(stored):
            total = jnp.sum(jnp.where(row == r, sums, 0.0), axis=0, keepdims=True)
            mean = jnp.sum(jnp.where(row == r, weighted, 0.0), axis=0, keepdims=True) / total
            stat = jnp.where(lane == t * stored + r, tops[r] + jnp.log(total), stat)
            stat = jnp.where(lane == (blocks + t) * stored + r, mean, stat)
    high = stat.astype(jnp.bfloat16).astype(jnp.float32)
    middle = (stat - high).astype(jnp.bfloat16).astype(jnp.float32)
    low = stat - high - middle
    parts = jnp.concatenate([high, middle, low, jnp.zeros((STAT_ROWS - 3, side), jnp.float32)], axis=0)
    parts = parts.astype(out_ref.dtype)
    for device in range(devices):
        out_ref[device, pl.ds(size - STAT_ROWS, STAT_ROWS), :] = parts


def pack_teacher(teacher_logits, block_lists, places):
    blocks, listed_count, stored, side = teacher_logits.shape
    n = lax.axis_size("vocab")
    rank = lax.axis_index("vocab")
    owner = block_lists // places
    earlier = jnp.tril(jnp.ones((listed_count, listed_count), jnp.bool_), -1)
    slot = jnp.sum((owner[:, :, None] == owner[:, None, :]) & earlier, axis=2, dtype=jnp.int32)
    code = owner * SLOTS + slot
    rows_code = (code[:, :, None] * stored + jnp.arange(stored, dtype=jnp.int32)).reshape(blocks, 1, -1)
    payload = pl.pallas_call(
        pack_kernel,
        in_specs=[vmem_spec()] * 2,
        out_specs=vmem_spec(),
        out_shape=jax.ShapeDtypeStruct(
            (n, blocks * SLOTS * stored + STAT_ROWS, side), teacher_logits.dtype
        ),
        compiler_params=kernel_params(),
        cost_estimate=LIGHT,
        name="pack_teacher",
    )(rows_code, teacher_logits.reshape(blocks, listed_count * stored, side))
    mine = code[:, None, :] == rank * SLOTS + jnp.arange(SLOTS, dtype=jnp.int32)[None, :, None]
    place = jnp.sum(jnp.where(mine, (block_lists % places + 1)[:, None, :], 0), axis=2) - 1
    return payload, place.astype(jnp.int32)


def unpack_teacher(arrived, blocks, stored):
    n, _, side = arrived.shape
    arrived_blocks = (
        arrived[:, :-3]
        .reshape(n, blocks, SLOTS, stored, side)
        .transpose(1, 2, 0, 3, 4)
        .reshape(blocks, SLOTS, n * stored, side)
    )
    arrived_stat = (
        arrived[:, -3:, : 2 * blocks * stored]
        .astype(jnp.float32)
        .sum(axis=1)
        .reshape(n, 2, blocks, stored)
        .transpose(1, 2, 0, 3)
        .reshape(2, blocks, 1, n * stored)
    )
    return arrived_blocks, arrived_stat


def levels_plan(
    hidden_states, head_weight, teacher_logits, block_lists, row_reader, tail_mass, token_weight
):
    blocks, listed_count, stored, side = teacher_logits.shape
    rows, depth = hidden_states.shape
    slab = head_weight.shape[1]
    n = lax.axis_size("vocab")
    rank = lax.axis_index("vocab")
    tokens = n * rows
    layers = n // GROUP
    half = depth // CORES
    bf16, f32 = jnp.bfloat16, jnp.float32
    core, chip, layer = rank % CORES, (rank // CORES) % CHIPS, rank // GROUP
    pos = jnp.stack([core, chip, layer, rank]).astype(jnp.int32)
    unlisted = float(n * slab - side * listed_count)

    narrow = depth * 3 // 10 // 512 * 512
    wide = depth - narrow
    column = [hidden_states[:, :wide]]
    column += [shift(column[0], k * GROUP) for k in range(1, layers)]
    plane = [hidden_states[:, wide:]]
    plane += [shift(plane[0], j * CORES) for j in range(1, CHIPS)]
    payload, place = pack_teacher(teacher_logits, block_lists, slab // side)
    column, plane = jnp.concatenate(column, axis=0), jnp.concatenate(plane, axis=0)
    column, plane, payload = lax.optimization_barrier((column, plane, payload[:, : 3 - STAT_ROWS]))
    wide_pieces = [column] + [shift(column, j * CORES) for j in range(1, CHIPS)]
    narrow_pieces = [plane] + [shift(plane, k * GROUP) for k in range(1, layers)]
    narrow_pieces[1], payload = lax.optimization_barrier((narrow_pieces[1], payload))
    arrived = lax.all_to_all(payload, "vocab", split_axis=0, concat_axis=0, tiled=True)
    arrived_blocks, arrived_stat = unpack_teacher(arrived, blocks, stored)

    prob, entropy = pl.pallas_call(
        lambda *refs: teacher_kernel(unlisted, rows, *refs),
        out_shape=(
            jax.ShapeDtypeStruct((tokens, slab), f32),
            jax.ShapeDtypeStruct((rows, side), f32),
        ),
        in_specs=[smem_spec(), smem_spec()] + [vmem_spec()] * 4,
        out_specs=(vmem_spec(), vmem_spec()),
        compiler_params=kernel_params(),
        cost_estimate=LIGHT,
        name="teacher_prob",
    )(
        pos,
        place,
        arrived_blocks,
        arrived_stat,
        row_reader.reshape(blocks, 1, side),
        tail_mass.reshape(blocks, 1, side),
    )

    wide_pieces, narrow_pieces, prob = lax.optimization_barrier((wide_pieces, narrow_pieces, prob))
    wide_pieces = list(wide_pieces) + [shift(piece, 1) for piece in wide_pieces]
    narrow_pieces = list(narrow_pieces) + [shift(piece, 1) for piece in narrow_pieces]
    wide_pieces, narrow_pieces, late_weight = lax.optimization_barrier((wide_pieces, narrow_pieces, head_weight))
    sib_w = shift(late_weight, 1)
    pieces = wide_pieces + narrow_pieces

    width = 256 if slab % 256 == 0 else 128
    tiles = slab // width
    whole = lambda t: (0, 0)
    logits, stat = pl.pallas_call(
        functools.partial(logits_kernel, rows, len(wide_pieces)),
        grid=(2 * tiles,),
        out_shape=[
            jax.ShapeDtypeStruct((tokens, slab), f32),
            jax.ShapeDtypeStruct((n, 2 * tokens // 128, 128), f32),
        ],
        in_specs=[vmem_spec()] * len(pieces)
        + [hbm_spec(), pl.BlockSpec((tokens, width), lambda t: (0, jnp.maximum(t - tiles, 0)))],
        out_specs=[
            pl.BlockSpec((tokens, slab), whole),
            pl.BlockSpec((n, 2 * tokens // 128, 128), lambda t: (0, 0, 0)),
        ],
        scratch_shapes=[
            pltpu.VMEM((tokens, depth), bf16),
            pltpu.VMEM((depth, slab), bf16),
            pltpu.SemaphoreType.DMA((2,)),
            pltpu.VMEM((tokens, 128), f32),
        ],
        compiler_params=kernel_params(LOGITS_VMEM),
        cost_estimate=LIGHT,
        name="logits",
    )(*pieces, head_weight, prob)
    stat = lax.all_to_all(stat, "vocab", split_axis=0, concat_axis=0, tiled=True)

    grad, loss = pl.pallas_call(
        lambda *refs: grad_kernel(rows, *refs),
        out_shape=(
            jax.ShapeDtypeStruct((tokens, slab), bf16),
            jax.ShapeDtypeStruct((rows, side), f32),
        ),
        in_specs=[smem_spec()] + [vmem_spec()] * 5,
        out_specs=(vmem_spec(), vmem_spec()),
        compiler_params=kernel_params(),
        cost_estimate=LIGHT,
        name="grad_logits",
    )(pos, stat, logits, prob, token_weight.reshape(blocks, 1, side), entropy)
    sib_grad = shift(grad, 1)

    tile = half // 5
    wide_steps = 3
    sizes = (wide_steps * tile, half - wide_steps * tile)
    wide_block = pl.BlockSpec(
        (layers, CORES, rows, tile), lambda t, pos: (0, 0, 0, jnp.minimum(t, wide_steps - 1))
    )
    narrow_block = pl.BlockSpec(
        (CHIPS, CORES, rows, tile), lambda t, pos: (0, 0, 0, jnp.maximum(t - wide_steps, 0))
    )
    partial = pl.pallas_call(
        functools.partial(partial_kernel, rows, wide_steps),
        grid_spec=pltpu.PrefetchScalarGridSpec(
            num_scalar_prefetch=1,
            grid=(5,),
            in_specs=[pl.BlockSpec((tokens, slab), lambda t, pos: (0, 0))] * 2
            + [pl.BlockSpec((tile, slab), lambda t, pos: (pos[0] * 5 + t, 0))] * 2,
            out_specs=[wide_block] * CHIPS + [narrow_block] * layers,
            scratch_shapes=[pltpu.VMEM((tokens, slab), bf16)],
        ),
        out_shape=[
            jax.ShapeDtypeStruct((layers, CORES, rows, sizes[0]), bf16 if j else f32) for j in range(CHIPS)
        ]
        + [jax.ShapeDtypeStruct((CHIPS, CORES, rows, sizes[1]), bf16 if k else f32) for k in range(layers)],
        compiler_params=kernel_params(LARGE_VMEM),
        cost_estimate=LIGHT,
        name="grad_hidden_partial",
    )(pos, grad, sib_grad, head_weight, sib_w)
    *partial, late_grad = lax.optimization_barrier((*partial, grad))
    wide_sums = [shift(partial[j], j * CORES) for j in range(1, CHIPS)]
    narrow_sums = [shift(partial[CHIPS + k], k * GROUP) for k in range(1, layers)]

    head_tile = 512
    head_steps = wide // head_tile
    grad_head = pl.pallas_call(
        functools.partial(head_kernel, rows, len(wide_pieces), head_steps),
        grid=(depth // head_tile,),
        in_specs=[
            pl.BlockSpec((piece.shape[0], head_tile), lambda t: (0, jnp.minimum(t, head_steps - 1)))
            for piece in wide_pieces
        ]
        + [
            pl.BlockSpec((piece.shape[0], head_tile), lambda t: (0, jnp.maximum(t - head_steps, 0)))
            for piece in narrow_pieces
        ]
        + [pl.BlockSpec((tokens, slab), whole)],
        out_specs=pl.BlockSpec((head_tile, slab), lambda t: (t, 0)),
        out_shape=jax.ShapeDtypeStruct((depth, slab), bf16),
        scratch_shapes=[pltpu.VMEM((tokens, head_tile), bf16)],
        compiler_params=kernel_params(LARGE_VMEM),
        cost_estimate=LIGHT,
        name="grad_head",
    )(*pieces, late_grad)
    wide_sums, narrow_sums, grad_head = lax.optimization_barrier((wide_sums, narrow_sums, grad_head))

    summed = pl.pallas_call(
        functools.partial(first_sum_kernel, layers),
        in_specs=[vmem_spec()] * (CHIPS + layers),
        out_specs=[vmem_spec()] * (CHIPS + layers),
        out_shape=[jax.ShapeDtypeStruct((CORES, rows, sizes[0]), bf16 if k else f32) for k in range(layers)]
        + [jax.ShapeDtypeStruct((CORES, rows, sizes[1]), bf16 if j else f32) for j in range(CHIPS)],
        compiler_params=kernel_params(),
        cost_estimate=LIGHT,
        name="first_sum",
    )(partial[0], *wide_sums, partial[CHIPS], *narrow_sums)
    wide_sums = [shift(summed[k], k * GROUP) for k in range(1, layers)]
    narrow_sums = [shift(summed[layers + j], j * CORES) for j in range(1, CHIPS)]
    mine, theirs = pl.pallas_call(
        functools.partial(last_sum_kernel, layers),
        in_specs=[vmem_spec()] * (CHIPS + layers),
        out_specs=[vmem_spec()] * 2,
        out_shape=[jax.ShapeDtypeStruct((rows, half), bf16)] * 2,
        compiler_params=kernel_params(),
        cost_estimate=LIGHT,
        name="last_sum",
    )(summed[0], *wide_sums, summed[layers], *narrow_sums)
    other = shift(theirs, 1)

    low, high = jnp.where(core == 0, mine, other), jnp.where(core == 0, other, mine)
    return loss[:, 0], grad_head, jnp.concatenate([low, high], axis=1)


def fits_levels(hidden_states, teacher_logits):
    n = lax.axis_size("vocab")
    rows = hidden_states.shape[0]
    blocks, _, stored, side = teacher_logits.shape
    return (
        n == blocks * GROUP
        and blocks & (blocks - 1) == 0
        and rows * GROUP == side
        and rows % 16 == 0
        and 2 * n <= side
        and 6 * blocks * stored <= side
        and hidden_states.shape[1] % (CORES * 1280) == 0
    )


def on_device(
    hidden_states, head_weight, teacher_logits, block_lists, row_reader, tail_mass, token_weight
):
    plan = levels_plan if fits_levels(hidden_states, teacher_logits) else plain_plan
    return plan(
        hidden_states, head_weight, teacher_logits, block_lists, row_reader, tail_mass, token_weight
    )


def solution(mesh):
    in_specs = (
        P("vocab", None),
        P(None, "vocab"),
        P(None, None, "vocab", None),
        P(),
        P(),
        P(),
        P(),
    )
    out_specs = (P("vocab"), P(None, "vocab"), P("vocab", None))
    return jax.shard_map(
        on_device, mesh=mesh, in_specs=in_specs, out_specs=out_specs, check_vma=False
    )
```

```python
import functools

import jax
import jax.numpy as jnp
from jax import lax
from jax.experimental import pallas as pl
from jax.experimental.pallas import tpu as pltpu
from jax.sharding import PartitionSpec as P


def row_parts(scores, teacher_slab, listed_mask, student_exp, teacher_exp):
    return (
        jnp.sum(student_exp, axis=(2, 3)),
        jnp.sum(teacher_exp, axis=(2, 3)),
        jnp.sum(teacher_exp * scores, axis=(2, 3)),
        jnp.sum(teacher_exp * teacher_slab, axis=(2, 3)),
        jnp.sum(scores, axis=(2, 3)),
        jnp.sum(jnp.where(listed_mask, scores, 0.0), axis=(2, 3)),
    )


def plain_plan(
    hidden_states, head_weight, teacher_logits, block_lists, row_reader, tail_mass, token_weight
):
    blocks, listed_count, stored_rows, block_side = teacher_logits.shape
    slab_width = head_weight.shape[1]
    slab_blocks = slab_width // block_side
    devices = lax.axis_size("vocab")
    rank_self = lax.axis_index("vocab")
    tokens = blocks * block_side
    shard_rows = hidden_states.shape[0]
    gathered = lax.all_gather(hidden_states, "vocab", axis=0, tiled=True)
    logits = jnp.dot(gathered, head_weight, preferred_element_type=jnp.float32)
    owner_dev = block_lists // slab_blocks
    owned_here = owner_dev == rank_self
    within = block_lists - rank_self * slab_blocks
    token_iota = lax.broadcasted_iota(jnp.int32, (1, block_side, block_side), 1)
    token_map = (row_reader[:, None, :] == token_iota).astype(jnp.bfloat16)
    place_iota = lax.broadcasted_iota(jnp.int32, (1, slab_blocks, 1), 1)
    block_iota = lax.broadcasted_iota(jnp.int32, (1, devices * slab_blocks, 1), 1)
    picker = (block_lists[:, None, :] == block_iota).astype(jnp.bfloat16)
    outgoing = jnp.einsum(
        "tnk,tkrc->tnrc", picker, teacher_logits, preferred_element_type=jnp.float32
    ).astype(jnp.bfloat16)
    incoming = lax.all_to_all(outgoing, "vocab", split_axis=1, concat_axis=2, tiled=True)
    teacher_slab = jnp.einsum(
        "tpj,tbjc->tpbc", token_map, incoming, preferred_element_type=jnp.float32
    )
    listed = jnp.sum(
        ((within[:, None, :] == place_iota) & owned_here[:, None, :]).astype(jnp.int32), axis=2
    )
    scores = logits.reshape(blocks, block_side, slab_blocks, block_side)
    listed_mask = (listed > 0)[:, None, :, None]
    local_smax = jnp.max(scores, axis=(2, 3))
    local_tmax = jnp.max(jnp.where(listed_mask, teacher_slab, -1e30), axis=(2, 3))
    student_max, teacher_max = lax.pmax((local_smax, local_tmax), "vocab")
    student_exp = jnp.exp(scores - student_max[:, :, None, None])
    teacher_exp = jnp.exp(
        jnp.where(listed_mask, teacher_slab - teacher_max[:, :, None, None], -jnp.inf)
    )
    parts = row_parts(scores, teacher_slab, listed_mask, student_exp, teacher_exp)
    student_sum, teacher_sum, cross_sum, self_sum, logit_total, listed_total = lax.psum(
        (parts[0], parts[1], parts[2], parts[3], parts[4], parts[5]), "vocab"
    )
    tail_share = tail_mass.reshape(blocks, block_side)
    unlisted = float(devices * slab_width - block_side * listed_count)
    kept_mass = 1.0 - tail_share
    log_norm = student_max + jnp.log(student_sum)
    row_loss = (
        kept_mass * (jnp.log(kept_mass) - teacher_max - jnp.log(teacher_sum))
        + kept_mass * self_sum / teacher_sum
        + tail_share * jnp.log(tail_share / unlisted)
        - kept_mass * cross_sum / teacher_sum
        - tail_share / unlisted * (logit_total - listed_total)
        + log_norm
    )
    token_loss = lax.dynamic_slice_in_dim(
        row_loss.reshape(tokens), rank_self * shard_rows, shard_rows, 0
    )
    student_prob = student_exp / student_sum[:, :, None, None]
    teacher_prob = jnp.where(
        listed_mask,
        (kept_mass / teacher_sum)[:, :, None, None] * teacher_exp,
        (tail_share / unlisted)[:, :, None, None],
    )
    weight = token_weight.reshape(blocks, block_side)[:, :, None, None]
    grad_logits = (
        (weight * (student_prob - teacher_prob)).astype(jnp.bfloat16).reshape(tokens, slab_width)
    )
    grad_head = lax.dot_general(
        gathered, grad_logits, (((0,), (0,)), ((), ())), preferred_element_type=jnp.float32
    ).astype(jnp.bfloat16)
    grad_hidden = lax.psum_scatter(
        lax.dot_general(
            grad_logits, head_weight, (((1,), (1,)), ((), ())), preferred_element_type=jnp.float32
        ),
        "vocab",
        scatter_dimension=0,
        tiled=True,
    ).astype(jnp.bfloat16)
    return (token_loss, grad_head, grad_hidden)


CORES = 2
CHIPS = 4
GROUP = CORES * CHIPS
SLOTS = 4
LIGHT = pl.CostEstimate(flops=1, bytes_accessed=1, transcendentals=0)
SMALL_VMEM = 16 * 1024 * 1024
LOGITS_VMEM = 46 * 1024 * 1024
LARGE_VMEM = 48 * 1024 * 1024
STAT_ROWS = 16


def kernel_params(limit=SMALL_VMEM):
    return pltpu.CompilerParams(vmem_limit_bytes=limit)


def vmem_spec():
    return pl.BlockSpec(memory_space=pltpu.VMEM)


def hbm_spec():
    return pl.BlockSpec(memory_space=pltpu.HBM)


def smem_spec():
    return pl.BlockSpec(memory_space=pltpu.SMEM)


def shift(x, distance):
    n = lax.axis_size("vocab")
    return lax.ppermute(x, "vocab", [(i, i ^ distance) for i in range(n)])


def token_places(place, rows, side):
    row = lax.broadcasted_iota(jnp.int32, (side, 1), 0)
    group = row // rows
    chip = (group % CHIPS) ^ place[1]
    core = (group // CHIPS) ^ place[0]
    return (chip * CORES + core) * rows + row % rows


def pick_column(match, values):
    return jnp.sum(jnp.where(match, values, 0.0), axis=1, keepdims=True)


def teacher_kernel(
    unlisted, rows, pos_ref, place_ref, blocks_ref, stat_ref, reader_ref, tail_ref, prob_ref, entropy_ref
):
    layers, slots, side, _ = blocks_ref.shape
    pos = [pos_ref[i] for i in range(3)]
    lane = lax.broadcasted_iota(jnp.int32, (1, side), 1)
    where_token = token_places(pos, rows, side)
    for k in range(layers):
        block = pos[2] ^ k
        match = reader_ref[block] == where_token
        onehot = jnp.where(match, 1.0, 0.0).astype(jnp.bfloat16)
        normaliser = pick_column(match, stat_ref[0, block])
        tail = pick_column(lane == where_token, tail_ref[block])
        kept = 1.0 - tail
        rest = tail / unlisted
        span = pl.ds(k * side, side)
        prob_ref[span, :] = jnp.broadcast_to(rest, (side, prob_ref.shape[1]))
        for s in range(slots):
            place = place_ref[block, s]
            values = jnp.dot(onehot, blocks_ref[block, s], preferred_element_type=jnp.float32)
            prob = kept * jnp.exp(values - normaliser)

            @pl.when(place >= 0)
            def _():
                prob_ref[span, pl.ds(pl.multiple_of(place * side, side), side)] = prob

        if k == 0:
            mean = pick_column(match, stat_ref[1, block])
            entropy = kept * (jnp.log(kept) - normaliser + mean) + tail * jnp.log(rest)
            entropy_ref[...] = jnp.broadcast_to(entropy[:rows], entropy_ref.shape)


def assemble(pieces, by_layer, rows, out_ref, columns=slice(None)):
    count = len(pieces) // CORES
    groups = pieces[0].shape[0] // rows
    for p, piece in enumerate(pieces):
        core, i = p // count, p % count
        for g in range(groups):
            layer, chip = (i, g) if by_layer else (g, i)
            block = layer * GROUP + core * CHIPS + chip
            out_ref[pl.ds(block * rows, rows), columns] = piece[pl.ds(g * rows, rows), :]


def cut_kernel(x_ref, narrow_ref, wide_ref):
    split = wide_ref.shape[1]
    wide_ref[...] = x_ref[:, :split]
    narrow_ref[...] = x_ref[:, split:]


def logits_kernel(rows, wide_count, *refs):
    pieces, refs = refs[:-8], refs[-8:]
    w_ref, prob_ref, logits_ref, stat_ref, hidden, weight, sems, cross_ref = refs
    wide_pieces, narrow_pieces = pieces[:wide_count], pieces[wide_count:]
    depth = w_ref.shape[0]
    wide, width = wide_pieces[0].shape[1], prob_ref.shape[1]
    tiles = w_ref.shape[1] // width
    step = pl.program_id(0)
    parts = [slice(wide, depth), slice(0, wide)]

    def copy(i):
        span = pl.ds(parts[i].start, parts[i].stop - parts[i].start)
        return pltpu.make_async_copy(w_ref.at[span, :], weight.at[span, :], sems.at[i])

    @pl.when(step == 0)
    def _():
        copy(0).start()
        copy(1).start()
        assemble(narrow_pieces, True, rows, hidden, parts[0])
        assemble(wide_pieces, False, rows, hidden, parts[1])
        copy(0).wait()

    @pl.when(step == tiles)
    def _():
        copy(1).wait()

    @pl.when(step < tiles)
    def _():
        span = pl.ds(pl.multiple_of(step * width, width), width)
        logits_ref[:, span] = jnp.dot(
            hidden[:, parts[0]], weight[parts[0], span], preferred_element_type=jnp.float32
        )

    @pl.when(step >= tiles)
    def _():
        span = pl.ds(pl.multiple_of((step - tiles) * width, width), width)
        total = logits_ref[:, span] + jnp.dot(
            hidden[:, parts[1]], weight[parts[1], span], preferred_element_type=jnp.float32
        )
        logits_ref[:, span] = total
        product = total * prob_ref[...]
        folded = product[:, :128]
        for i in range(1, width // 128):
            folded = folded + product[:, i * 128 : (i + 1) * 128]
        cross_ref[...] = jnp.where(step == tiles, 0.0, cross_ref[...]) + folded

    @pl.when(step == 2 * tiles - 1)
    def _():
        logits = logits_ref[...]
        top = jnp.max(logits, axis=1, keepdims=True)
        norm = top + jnp.log(jnp.sum(jnp.exp(logits - top), axis=1, keepdims=True))
        cross = jnp.sum(cross_ref[...], axis=1, keepdims=True)
        lane = lax.broadcasted_iota(jnp.int32, (1, 128), 1)
        both = jnp.where(lane == 0, norm, jnp.where(lane == 1, cross, 0.0)).T
        tokens = logits.shape[0]
        packed = [both[i : i + 1, t : t + 128] for i in range(2) for t in range(0, tokens, 128)]
        stat_ref[...] = jnp.broadcast_to(jnp.concatenate(packed, axis=0)[None], stat_ref.shape)


def grad_kernel(
    rows, pos_ref, stat_ref, logits_ref, prob_ref, weight_ref, entropy_ref, grad_ref, loss_ref
):
    tokens = logits_ref.shape[0]
    devices = tokens // rows
    layers, _, side = weight_ref.shape
    layer_bits = (devices // GROUP).bit_length() - 1
    pos = [pos_ref[i] for i in range(3)]
    rank = pos_ref[3]
    lane = lax.broadcasted_iota(jnp.int32, (1, 128), 1)
    per_stat = stat_ref.shape[1] // 2
    norms, crosses = [
        jnp.concatenate([stat_ref[:, i * per_stat + t, :] for t in range(per_stat)], axis=1) for i in range(2)
    ]
    stat = jnp.concatenate(
        [norms, crosses, jnp.zeros((128 - 2 * devices, tokens), jnp.float32)], axis=0
    ).T
    pairs = [(0, 2), (1, 0), (2, 1)] + [(3 + i, 3 + i) for i in range(layer_bits)]
    for index_bit, block_bit in pairs:
        halves = stat.reshape(devices >> (block_bit + 1), 2, rows << block_bit, 128)
        swapped = jnp.stack([halves[:, 1], halves[:, 0]], axis=1).reshape(tokens, 128)
        stat = jnp.where(((lane ^ rank) >> index_bit) & 1 == 1, swapped, stat)
    is_norm = lane < devices
    is_cross = (lane >= devices) & (lane < 2 * devices)
    top = jnp.max(jnp.where(is_norm, stat, -jnp.inf), axis=1, keepdims=True)
    total = jnp.sum(jnp.where(is_norm, jnp.exp(stat - top), 0.0), axis=1, keepdims=True)
    log_norm = top + jnp.log(total)
    cross = jnp.sum(jnp.where(is_cross, stat, 0.0), axis=1, keepdims=True)
    loss_ref[...] = entropy_ref[...] - cross[:rows] + log_norm[:rows]
    where_token = token_places(pos, rows, side)
    for k in range(layers):
        span = pl.ds(k * side, side)
        weight = pick_column(lane == where_token, weight_ref[pos[2] ^ k])
        student = jnp.exp(logits_ref[span, :] - log_norm[k * side : (k + 1) * side])
        grad_ref[span, :] = (weight * (student - prob_ref[span, :])).astype(grad_ref.dtype)


def partial_kernel(rows, wide_steps, core_ref, grad_ref, sib_ref, w_ref, sib_w_ref, *refs):
    outs, swapped = refs[:-1], refs[-1]
    wide_outs, narrow_outs = outs[:CHIPS], outs[CHIPS:]
    layers = len(narrow_outs)
    half = CHIPS * rows
    step = pl.program_id(0)

    @pl.when(step == 0)
    def _():
        for k in range(layers):
            for core in range(CORES):
                swapped[pl.ds((k * CORES + core) * half, half), :] = sib_ref[
                    pl.ds((k * CORES + 1 - core) * half, half), :
                ]

    contract = (((1,), (1,)), ((), ()))
    total = lax.dot_general(
        grad_ref[...], w_ref[...], contract, preferred_element_type=jnp.float32
    ) + lax.dot_general(swapped[...], sib_w_ref[...], contract, preferred_element_type=jnp.float32)

    def parts():
        for k in range(layers):
            for core in range(CORES):
                for j in range(CHIPS):
                    start = (k * GROUP + core * CHIPS + j) * rows
                    yield k, core, j, total[start : start + rows]

    @pl.when(step < wide_steps)
    def _():
        for k, core, j, part in parts():
            wide_outs[j][k, core] = part.astype(wide_outs[j].dtype)

    @pl.when(step >= wide_steps)
    def _():
        for k, core, j, part in parts():
            narrow_outs[k][j, core] = part.astype(narrow_outs[k].dtype)


def head_kernel(rows, wide_count, wide_steps, *refs):
    pieces, (grad_ref, out_ref, hidden) = refs[:-3], refs[-3:]
    step = pl.program_id(0)

    @pl.when(step < wide_steps)
    def _():
        assemble(pieces[:wide_count], False, rows, hidden)

    @pl.when(step >= wide_steps)
    def _():
        assemble(pieces[wide_count:], True, rows, hidden)

    out_ref[...] = lax.dot_general(
        hidden[...], grad_ref[...], (((0,), (0,)), ((), ())), preferred_element_type=jnp.float32
    ).astype(out_ref.dtype)


def sum_of(parts, index=...):
    total = parts[0][index]
    for part in parts[1:]:
        total = total + part[index].astype(jnp.float32)
    return total


def first_sum_kernel(layers, *refs):
    wide, narrow, outs = refs[:CHIPS], refs[CHIPS : CHIPS + layers], refs[CHIPS + layers :]
    for k, out in enumerate(outs[:layers]):
        out[...] = sum_of(wide, k).astype(out.dtype)
    for j, out in enumerate(outs[layers:]):
        out[...] = sum_of(narrow, j).astype(out.dtype)


def last_sum_kernel(layers, *refs):
    wide, narrow, (mine, theirs) = refs[:layers], refs[layers:-2], refs[-2:]
    split = wide[0].shape[-1]
    for parts, columns in ((wide, slice(0, split)), (narrow, slice(split, mine.shape[1]))):
        total = sum_of(parts)
        mine[:, columns] = total[0].astype(mine.dtype)
        theirs[:, columns] = total[1].astype(theirs.dtype)


def pack_kernel(code_ref, x_ref, out_ref):
    blocks, count, side = x_ref.shape
    devices, size, _ = out_ref.shape
    slot_rows = (size - STAT_ROWS) // blocks
    stored = slot_rows // SLOTS
    target = lax.broadcasted_iota(jnp.int32, (devices * slot_rows, 1), 0)
    row = lax.broadcasted_iota(jnp.int32, (count, 1), 0) % stored
    lane = lax.broadcasted_iota(jnp.int32, (1, side), 1)
    stat = jnp.zeros((1, side), jnp.float32)
    for t in range(blocks):
        onehot = jnp.where(code_ref[t] == target, 1.0, 0.0).astype(x_ref.dtype)
        packed = jnp.dot(onehot, x_ref[t], preferred_element_type=jnp.float32).astype(out_ref.dtype)
        for device in range(devices):
            out_ref[device, pl.ds(t * slot_rows, slot_rows), :] = packed[
                device * slot_rows : (device + 1) * slot_rows
            ]
        values = x_ref[t].astype(jnp.float32)
        row_top = jnp.max(values, axis=1, keepdims=True)
        tops = [jnp.max(jnp.where(row == r, row_top, -jnp.inf), axis=0, keepdims=True) for r in range(stored)]
        top = jnp.zeros_like(row_top)
        for r in range(stored):
            top = jnp.where(row == r, tops[r], top)
        powers = jnp.exp(values - top)
        sums = jnp.sum(powers, axis=1, keepdims=True)
        weighted = jnp.sum(powers * values, axis=1, keepdims=True)
        for r in range(stored):
            total = jnp.sum(jnp.where(row == r, sums, 0.0), axis=0, keepdims=True)
            mean = jnp.sum(jnp.where(row == r, weighted, 0.0), axis=0, keepdims=True) / total
            stat = jnp.where(lane == t * stored + r, tops[r] + jnp.log(total), stat)
            stat = jnp.where(lane == (blocks + t) * stored + r, mean, stat)
    high = stat.astype(jnp.bfloat16).astype(jnp.float32)
    middle = (stat - high).astype(jnp.bfloat16).astype(jnp.float32)
    low = stat - high - middle
    parts = jnp.concatenate([high, middle, low, jnp.zeros((STAT_ROWS - 3, side), jnp.float32)], axis=0)
    parts = parts.astype(out_ref.dtype)
    for device in range(devices):
        out_ref[device, pl.ds(size - STAT_ROWS, STAT_ROWS), :] = parts


def pack_teacher(teacher_logits, block_lists, places):
    blocks, listed_count, stored, side = teacher_logits.shape
    n = lax.axis_size("vocab")
    rank = lax.axis_index("vocab")
    owner = block_lists // places
    earlier = jnp.tril(jnp.ones((listed_count, listed_count), jnp.bool_), -1)
    slot = jnp.sum((owner[:, :, None] == owner[:, None, :]) & earlier, axis=2, dtype=jnp.int32)
    code = owner * SLOTS + slot
    rows_code = (code[:, :, None] * stored + jnp.arange(stored, dtype=jnp.int32)).reshape(blocks, 1, -1)
    payload = pl.pallas_call(
        pack_kernel,
        in_specs=[vmem_spec()] * 2,
        out_specs=vmem_spec(),
        out_shape=jax.ShapeDtypeStruct(
            (n, blocks * SLOTS * stored + STAT_ROWS, side), teacher_logits.dtype
        ),
        compiler_params=kernel_params(),
        cost_estimate=LIGHT,
        name="pack_teacher",
    )(rows_code, teacher_logits.reshape(blocks, listed_count * stored, side))
    mine = code[:, None, :] == rank * SLOTS + jnp.arange(SLOTS, dtype=jnp.int32)[None, :, None]
    place = jnp.sum(jnp.where(mine, (block_lists % places + 1)[:, None, :], 0), axis=2) - 1
    return payload, place.astype(jnp.int32)


def unpack_teacher(arrived, blocks, stored):
    n, _, side = arrived.shape
    arrived_blocks = (
        arrived[:, :-3]
        .reshape(n, blocks, SLOTS, stored, side)
        .transpose(1, 2, 0, 3, 4)
        .reshape(blocks, SLOTS, n * stored, side)
    )
    arrived_stat = (
        arrived[:, -3:, : 2 * blocks * stored]
        .astype(jnp.float32)
        .sum(axis=1)
        .reshape(n, 2, blocks, stored)
        .transpose(1, 2, 0, 3)
        .reshape(2, blocks, 1, n * stored)
    )
    return arrived_blocks, arrived_stat


def levels_plan(
    hidden_states, head_weight, teacher_logits, block_lists, row_reader, tail_mass, token_weight
):
    blocks, listed_count, stored, side = teacher_logits.shape
    rows, depth = hidden_states.shape
    slab = head_weight.shape[1]
    n = lax.axis_size("vocab")
    rank = lax.axis_index("vocab")
    tokens = n * rows
    layers = n // GROUP
    half = depth // CORES
    bf16, f32 = jnp.bfloat16, jnp.float32
    core, chip, layer = rank % CORES, (rank // CORES) % CHIPS, rank // GROUP
    pos = jnp.stack([core, chip, layer, rank]).astype(jnp.int32)
    unlisted = float(n * slab - side * listed_count)

    narrow = depth // 4
    wide = depth - narrow
    own_narrow, own_wide = pl.pallas_call(
        cut_kernel,
        in_specs=[vmem_spec()],
        out_specs=[vmem_spec()] * 2,
        out_shape=[jax.ShapeDtypeStruct((rows, size), bf16) for size in (narrow, wide)],
        compiler_params=kernel_params(),
        cost_estimate=LIGHT,
        name="cut_columns",
    )(hidden_states)
    plane = [own_narrow] + [shift(own_narrow, j * CORES) for j in range(1, CHIPS)]
    column = [own_wide] + [shift(own_wide, k * GROUP) for k in range(1, layers)]
    payload, place = pack_teacher(teacher_logits, block_lists, slab // side)
    arrived = lax.all_to_all(
        payload[:, : 3 - STAT_ROWS], "vocab", split_axis=0, concat_axis=0, tiled=True
    )
    plane, column = jnp.concatenate(plane, axis=0), jnp.concatenate(column, axis=0)
    plane, column = lax.optimization_barrier((plane, column))
    wide_pieces = [column] + [shift(column, j * CORES) for j in range(1, CHIPS)]
    narrow_pieces = [plane] + [shift(plane, k * GROUP) for k in range(1, layers)]
    arrived_blocks, arrived_stat = unpack_teacher(arrived, blocks, stored)

    prob, entropy = pl.pallas_call(
        lambda *refs: teacher_kernel(unlisted, rows, *refs),
        out_shape=(
            jax.ShapeDtypeStruct((tokens, slab), f32),
            jax.ShapeDtypeStruct((rows, side), f32),
        ),
        in_specs=[smem_spec(), smem_spec()] + [vmem_spec()] * 4,
        out_specs=(vmem_spec(), vmem_spec()),
        compiler_params=kernel_params(),
        cost_estimate=LIGHT,
        name="teacher_prob",
    )(
        pos,
        place,
        arrived_blocks,
        arrived_stat,
        row_reader.reshape(blocks, 1, side),
        tail_mass.reshape(blocks, 1, side),
    )

    wide_pieces, narrow_pieces, prob = lax.optimization_barrier((wide_pieces, narrow_pieces, prob))
    wide_pieces = list(wide_pieces) + [shift(piece, 1) for piece in wide_pieces]
    narrow_pieces = list(narrow_pieces) + [shift(piece, 1) for piece in narrow_pieces]
    wide_pieces, narrow_pieces, late_weight = lax.optimization_barrier((wide_pieces, narrow_pieces, head_weight))
    sib_w = shift(late_weight, 1)
    pieces = wide_pieces + narrow_pieces

    width = 256 if slab % 256 == 0 else 128
    tiles = slab // width
    whole = lambda t: (0, 0)
    logits, stat = pl.pallas_call(
        functools.partial(logits_kernel, rows, len(wide_pieces)),
        grid=(2 * tiles,),
        out_shape=[
            jax.ShapeDtypeStruct((tokens, slab), f32),
            jax.ShapeDtypeStruct((n, 2 * tokens // 128, 128), f32),
        ],
        in_specs=[vmem_spec()] * len(pieces)
        + [hbm_spec(), pl.BlockSpec((tokens, width), lambda t: (0, jnp.maximum(t - tiles, 0)))],
        out_specs=[
            pl.BlockSpec((tokens, slab), whole),
            pl.BlockSpec((n, 2 * tokens // 128, 128), lambda t: (0, 0, 0)),
        ],
        scratch_shapes=[
            pltpu.VMEM((tokens, depth), bf16),
            pltpu.VMEM((depth, slab), bf16),
            pltpu.SemaphoreType.DMA((2,)),
            pltpu.VMEM((tokens, 128), f32),
        ],
        compiler_params=kernel_params(LOGITS_VMEM),
        cost_estimate=LIGHT,
        name="logits",
    )(*pieces, head_weight, prob)
    stat = lax.all_to_all(stat, "vocab", split_axis=0, concat_axis=0, tiled=True)

    grad, loss = pl.pallas_call(
        lambda *refs: grad_kernel(rows, *refs),
        out_shape=(
            jax.ShapeDtypeStruct((tokens, slab), bf16),
            jax.ShapeDtypeStruct((rows, side), f32),
        ),
        in_specs=[smem_spec()] + [vmem_spec()] * 5,
        out_specs=(vmem_spec(), vmem_spec()),
        compiler_params=kernel_params(),
        cost_estimate=LIGHT,
        name="grad_logits",
    )(pos, stat, logits, prob, token_weight.reshape(blocks, 1, side), entropy)
    sib_grad = shift(grad, 1)

    tile = half // 5
    wide_steps = 3
    sizes = (wide_steps * tile, half - wide_steps * tile)
    wide_block = pl.BlockSpec(
        (layers, CORES, rows, tile), lambda t, pos: (0, 0, 0, jnp.minimum(t, wide_steps - 1))
    )
    narrow_block = pl.BlockSpec(
        (CHIPS, CORES, rows, tile), lambda t, pos: (0, 0, 0, jnp.maximum(t - wide_steps, 0))
    )
    partial = pl.pallas_call(
        functools.partial(partial_kernel, rows, wide_steps),
        grid_spec=pltpu.PrefetchScalarGridSpec(
            num_scalar_prefetch=1,
            grid=(5,),
            in_specs=[pl.BlockSpec((tokens, slab), lambda t, pos: (0, 0))] * 2
            + [pl.BlockSpec((tile, slab), lambda t, pos: (pos[0] * 5 + t, 0))] * 2,
            out_specs=[wide_block] * CHIPS + [narrow_block] * layers,
            scratch_shapes=[pltpu.VMEM((tokens, slab), bf16)],
        ),
        out_shape=[
            jax.ShapeDtypeStruct((layers, CORES, rows, sizes[0]), bf16 if j else f32) for j in range(CHIPS)
        ]
        + [jax.ShapeDtypeStruct((CHIPS, CORES, rows, sizes[1]), bf16 if k else f32) for k in range(layers)],
        compiler_params=kernel_params(LARGE_VMEM),
        cost_estimate=LIGHT,
        name="grad_hidden_partial",
    )(pos, grad, sib_grad, head_weight, sib_w)
    *partial, late_grad = lax.optimization_barrier((*partial, grad))
    wide_sums = [shift(partial[j], j * CORES) for j in range(1, CHIPS)]
    narrow_sums = [shift(partial[CHIPS + k], k * GROUP) for k in range(1, layers)]

    head_tile = narrow
    head_steps = wide // head_tile
    grad_head = pl.pallas_call(
        functools.partial(head_kernel, rows, len(wide_pieces), head_steps),
        grid=(depth // head_tile,),
        in_specs=[
            pl.BlockSpec((piece.shape[0], head_tile), lambda t: (0, jnp.minimum(t, head_steps - 1)))
            for piece in wide_pieces
        ]
        + [
            pl.BlockSpec((piece.shape[0], head_tile), lambda t: (0, jnp.maximum(t - head_steps, 0)))
            for piece in narrow_pieces
        ]
        + [pl.BlockSpec((tokens, slab), whole)],
        out_specs=pl.BlockSpec((head_tile, slab), lambda t: (t, 0)),
        out_shape=jax.ShapeDtypeStruct((depth, slab), bf16),
        scratch_shapes=[pltpu.VMEM((tokens, head_tile), bf16)],
        compiler_params=kernel_params(LARGE_VMEM),
        cost_estimate=LIGHT,
        name="grad_head",
    )(*pieces, late_grad)
    wide_sums, narrow_sums, grad_head = lax.optimization_barrier((wide_sums, narrow_sums, grad_head))

    summed = pl.pallas_call(
        functools.partial(first_sum_kernel, layers),
        in_specs=[vmem_spec()] * (CHIPS + layers),
        out_specs=[vmem_spec()] * (CHIPS + layers),
        out_shape=[jax.ShapeDtypeStruct((CORES, rows, sizes[0]), bf16 if k else f32) for k in range(layers)]
        + [jax.ShapeDtypeStruct((CORES, rows, sizes[1]), bf16 if j else f32) for j in range(CHIPS)],
        compiler_params=kernel_params(),
        cost_estimate=LIGHT,
        name="first_sum",
    )(partial[0], *wide_sums, partial[CHIPS], *narrow_sums)
    wide_sums = [shift(summed[k], k * GROUP) for k in range(1, layers)]
    narrow_sums = [shift(summed[layers + j], j * CORES) for j in range(1, CHIPS)]
    mine, theirs = pl.pallas_call(
        functools.partial(last_sum_kernel, layers),
        in_specs=[vmem_spec()] * (CHIPS + layers),
        out_specs=[vmem_spec()] * 2,
        out_shape=[jax.ShapeDtypeStruct((rows, half), bf16)] * 2,
        compiler_params=kernel_params(),
        cost_estimate=LIGHT,
        name="last_sum",
    )(summed[0], *wide_sums, summed[layers], *narrow_sums)
    other = shift(theirs, 1)

    low, high = jnp.where(core == 0, mine, other), jnp.where(core == 0, other, mine)
    return loss[:, 0], grad_head, jnp.concatenate([low, high], axis=1)


def fits_levels(hidden_states, teacher_logits):
    n = lax.axis_size("vocab")
    rows = hidden_states.shape[0]
    blocks, _, stored, side = teacher_logits.shape
    return (
        n == blocks * GROUP
        and blocks & (blocks - 1) == 0
        and rows * GROUP == side
        and rows % 16 == 0
        and 2 * n <= side
        and 6 * blocks * stored <= side
        and hidden_states.shape[1] % (CORES * 1280) == 0
    )


def on_device(
    hidden_states, head_weight, teacher_logits, block_lists, row_reader, tail_mass, token_weight
):
    plan = levels_plan if fits_levels(hidden_states, teacher_logits) else plain_plan
    return plan(
        hidden_states, head_weight, teacher_logits, block_lists, row_reader, tail_mass, token_weight
    )


def solution(mesh):
    in_specs = (
        P("vocab", None),
        P(None, "vocab"),
        P(None, None, "vocab", None),
        P(),
        P(),
        P(),
        P(),
    )
    out_specs = (P("vocab"), P(None, "vocab"), P("vocab", None))
    return jax.shard_map(
        on_device, mesh=mesh, in_specs=in_specs, out_specs=out_specs, check_vma=False
    )
```

```python
import functools

import jax
import jax.numpy as jnp
from jax import lax
from jax.experimental import pallas as pl
from jax.experimental.pallas import tpu as pltpu
from jax.sharding import PartitionSpec as P


def row_parts(scores, teacher_slab, listed_mask, student_exp, teacher_exp):
    return (
        jnp.sum(student_exp, axis=(2, 3)),
        jnp.sum(teacher_exp, axis=(2, 3)),
        jnp.sum(teacher_exp * scores, axis=(2, 3)),
        jnp.sum(teacher_exp * teacher_slab, axis=(2, 3)),
        jnp.sum(scores, axis=(2, 3)),
        jnp.sum(jnp.where(listed_mask, scores, 0.0), axis=(2, 3)),
    )


def plain_plan(
    hidden_states, head_weight, teacher_logits, block_lists, row_reader, tail_mass, token_weight
):
    blocks, listed_count, stored_rows, block_side = teacher_logits.shape
    slab_width = head_weight.shape[1]
    slab_blocks = slab_width // block_side
    devices = lax.axis_size("vocab")
    rank_self = lax.axis_index("vocab")
    tokens = blocks * block_side
    shard_rows = hidden_states.shape[0]
    gathered = lax.all_gather(hidden_states, "vocab", axis=0, tiled=True)
    logits = jnp.dot(gathered, head_weight, preferred_element_type=jnp.float32)
    owner_dev = block_lists // slab_blocks
    owned_here = owner_dev == rank_self
    within = block_lists - rank_self * slab_blocks
    token_iota = lax.broadcasted_iota(jnp.int32, (1, block_side, block_side), 1)
    token_map = (row_reader[:, None, :] == token_iota).astype(jnp.bfloat16)
    place_iota = lax.broadcasted_iota(jnp.int32, (1, slab_blocks, 1), 1)
    block_iota = lax.broadcasted_iota(jnp.int32, (1, devices * slab_blocks, 1), 1)
    picker = (block_lists[:, None, :] == block_iota).astype(jnp.bfloat16)
    outgoing = jnp.einsum(
        "tnk,tkrc->tnrc", picker, teacher_logits, preferred_element_type=jnp.float32
    ).astype(jnp.bfloat16)
    incoming = lax.all_to_all(outgoing, "vocab", split_axis=1, concat_axis=2, tiled=True)
    teacher_slab = jnp.einsum(
        "tpj,tbjc->tpbc", token_map, incoming, preferred_element_type=jnp.float32
    )
    listed = jnp.sum(
        ((within[:, None, :] == place_iota) & owned_here[:, None, :]).astype(jnp.int32), axis=2
    )
    scores = logits.reshape(blocks, block_side, slab_blocks, block_side)
    listed_mask = (listed > 0)[:, None, :, None]
    local_smax = jnp.max(scores, axis=(2, 3))
    local_tmax = jnp.max(jnp.where(listed_mask, teacher_slab, -1e30), axis=(2, 3))
    student_max, teacher_max = lax.pmax((local_smax, local_tmax), "vocab")
    student_exp = jnp.exp(scores - student_max[:, :, None, None])
    teacher_exp = jnp.exp(
        jnp.where(listed_mask, teacher_slab - teacher_max[:, :, None, None], -jnp.inf)
    )
    parts = row_parts(scores, teacher_slab, listed_mask, student_exp, teacher_exp)
    student_sum, teacher_sum, cross_sum, self_sum, logit_total, listed_total = lax.psum(
        (parts[0], parts[1], parts[2], parts[3], parts[4], parts[5]), "vocab"
    )
    tail_share = tail_mass.reshape(blocks, block_side)
    unlisted = float(devices * slab_width - block_side * listed_count)
    kept_mass = 1.0 - tail_share
    log_norm = student_max + jnp.log(student_sum)
    row_loss = (
        kept_mass * (jnp.log(kept_mass) - teacher_max - jnp.log(teacher_sum))
        + kept_mass * self_sum / teacher_sum
        + tail_share * jnp.log(tail_share / unlisted)
        - kept_mass * cross_sum / teacher_sum
        - tail_share / unlisted * (logit_total - listed_total)
        + log_norm
    )
    token_loss = lax.dynamic_slice_in_dim(
        row_loss.reshape(tokens), rank_self * shard_rows, shard_rows, 0
    )
    student_prob = student_exp / student_sum[:, :, None, None]
    teacher_prob = jnp.where(
        listed_mask,
        (kept_mass / teacher_sum)[:, :, None, None] * teacher_exp,
        (tail_share / unlisted)[:, :, None, None],
    )
    weight = token_weight.reshape(blocks, block_side)[:, :, None, None]
    grad_logits = (
        (weight * (student_prob - teacher_prob)).astype(jnp.bfloat16).reshape(tokens, slab_width)
    )
    grad_head = lax.dot_general(
        gathered, grad_logits, (((0,), (0,)), ((), ())), preferred_element_type=jnp.float32
    ).astype(jnp.bfloat16)
    grad_hidden = lax.psum_scatter(
        lax.dot_general(
            grad_logits, head_weight, (((1,), (1,)), ((), ())), preferred_element_type=jnp.float32
        ),
        "vocab",
        scatter_dimension=0,
        tiled=True,
    ).astype(jnp.bfloat16)
    return (token_loss, grad_head, grad_hidden)


CORES = 2
CHIPS = 4
GROUP = CORES * CHIPS
SLOTS = 4
LIGHT = pl.CostEstimate(flops=1, bytes_accessed=1, transcendentals=0)
SMALL_VMEM = 16 * 1024 * 1024
LOGITS_VMEM = 46 * 1024 * 1024
LARGE_VMEM = 48 * 1024 * 1024
STAT_ROWS = 16


def kernel_params(limit=SMALL_VMEM):
    return pltpu.CompilerParams(vmem_limit_bytes=limit)


def vmem_spec():
    return pl.BlockSpec(memory_space=pltpu.VMEM)


def hbm_spec():
    return pl.BlockSpec(memory_space=pltpu.HBM)


def smem_spec():
    return pl.BlockSpec(memory_space=pltpu.SMEM)


def shift(x, distance):
    n = lax.axis_size("vocab")
    return lax.ppermute(x, "vocab", [(i, i ^ distance) for i in range(n)])


def token_places(place, rows, side):
    row = lax.broadcasted_iota(jnp.int32, (side, 1), 0)
    group = row // rows
    chip = (group % CHIPS) ^ place[1]
    core = (group // CHIPS) ^ place[0]
    return (chip * CORES + core) * rows + row % rows


def pick_column(match, values):
    return jnp.sum(jnp.where(match, values, 0.0), axis=1, keepdims=True)


def teacher_kernel(
    unlisted, rows, pos_ref, place_ref, blocks_ref, stat_ref, reader_ref, tail_ref, prob_ref, entropy_ref
):
    layers, slots, side, _ = blocks_ref.shape
    pos = [pos_ref[i] for i in range(3)]
    lane = lax.broadcasted_iota(jnp.int32, (1, side), 1)
    where_token = token_places(pos, rows, side)
    for k in range(layers):
        block = pos[2] ^ k
        match = reader_ref[block] == where_token
        onehot = jnp.where(match, 1.0, 0.0).astype(jnp.bfloat16)
        normaliser = pick_column(match, stat_ref[0, block])
        tail = pick_column(lane == where_token, tail_ref[block])
        kept = 1.0 - tail
        rest = tail / unlisted
        span = pl.ds(k * side, side)
        prob_ref[span, :] = jnp.broadcast_to(rest, (side, prob_ref.shape[1]))
        for s in range(slots):
            place = place_ref[block, s]
            values = jnp.dot(onehot, blocks_ref[block, s], preferred_element_type=jnp.float32)
            prob = kept * jnp.exp(values - normaliser)

            @pl.when(place >= 0)
            def _():
                prob_ref[span, pl.ds(pl.multiple_of(place * side, side), side)] = prob

        if k == 0:
            mean = pick_column(match, stat_ref[1, block])
            entropy = kept * (jnp.log(kept) - normaliser + mean) + tail * jnp.log(rest)
            entropy_ref[...] = jnp.broadcast_to(entropy[:rows], entropy_ref.shape)


def assemble(pieces, rows, out_ref):
    layers = pieces[0].shape[0] // rows
    for k in range(layers):
        for p, piece in enumerate(pieces):
            out_ref[pl.ds((k * GROUP + p) * rows, rows), :] = piece[pl.ds(k * rows, rows), :]


def logits_kernel(rows, *refs):
    pieces, refs = refs[:GROUP], refs[GROUP:]
    w_ref, prob_ref, logits_ref, stat_ref, hidden, weight, sems, cross_ref = refs
    half, width = w_ref.shape[0] // 2, prob_ref.shape[1]
    tiles = w_ref.shape[1] // width
    step = pl.program_id(0)

    def copy(i):
        span = pl.ds(i * half, half)
        return pltpu.make_async_copy(w_ref.at[span, :], weight.at[span, :], sems.at[i])

    @pl.when(step == 0)
    def _():
        copy(0).start()
        copy(1).start()
        assemble(pieces, rows, hidden)
        copy(0).wait()

    @pl.when(step == tiles)
    def _():
        copy(1).wait()

    @pl.when(step < tiles)
    def _():
        span = pl.ds(pl.multiple_of(step * width, width), width)
        logits_ref[:, span] = jnp.dot(
            hidden[:, :half], weight[:half, span], preferred_element_type=jnp.float32
        )

    @pl.when(step >= tiles)
    def _():
        span = pl.ds(pl.multiple_of((step - tiles) * width, width), width)
        total = logits_ref[:, span] + jnp.dot(
            hidden[:, half:], weight[half:, span], preferred_element_type=jnp.float32
        )
        logits_ref[:, span] = total
        product = total * prob_ref[...]
        folded = product[:, :128]
        for i in range(1, width // 128):
            folded = folded + product[:, i * 128 : (i + 1) * 128]
        cross_ref[...] = jnp.where(step == tiles, 0.0, cross_ref[...]) + folded

    @pl.when(step == 2 * tiles - 1)
    def _():
        logits = logits_ref[...]
        top = jnp.max(logits, axis=1, keepdims=True)
        norm = top + jnp.log(jnp.sum(jnp.exp(logits - top), axis=1, keepdims=True))
        cross = jnp.sum(cross_ref[...], axis=1, keepdims=True)
        lane = lax.broadcasted_iota(jnp.int32, (1, 128), 1)
        both = jnp.where(lane == 0, norm, jnp.where(lane == 1, cross, 0.0)).T
        tokens = logits.shape[0]
        packed = [both[i : i + 1, t : t + 128] for i in range(2) for t in range(0, tokens, 128)]
        stat_ref[...] = jnp.broadcast_to(jnp.concatenate(packed, axis=0)[None], stat_ref.shape)


def grad_kernel(
    rows, pos_ref, stat_ref, logits_ref, prob_ref, weight_ref, entropy_ref, grad_ref, loss_ref
):
    tokens = logits_ref.shape[0]
    devices = tokens // rows
    layers, _, side = weight_ref.shape
    layer_bits = (devices // GROUP).bit_length() - 1
    pos = [pos_ref[i] for i in range(3)]
    rank = pos_ref[3]
    lane = lax.broadcasted_iota(jnp.int32, (1, 128), 1)
    per_stat = stat_ref.shape[1] // 2
    norms, crosses = [
        jnp.concatenate([stat_ref[:, i * per_stat + t, :] for t in range(per_stat)], axis=1) for i in range(2)
    ]
    stat = jnp.concatenate(
        [norms, crosses, jnp.zeros((128 - 2 * devices, tokens), jnp.float32)], axis=0
    ).T
    pairs = [(0, 2), (1, 0), (2, 1)] + [(3 + i, 3 + i) for i in range(layer_bits)]
    for index_bit, block_bit in pairs:
        halves = stat.reshape(devices >> (block_bit + 1), 2, rows << block_bit, 128)
        swapped = jnp.stack([halves[:, 1], halves[:, 0]], axis=1).reshape(tokens, 128)
        stat = jnp.where(((lane ^ rank) >> index_bit) & 1 == 1, swapped, stat)
    is_norm = lane < devices
    is_cross = (lane >= devices) & (lane < 2 * devices)
    top = jnp.max(jnp.where(is_norm, stat, -jnp.inf), axis=1, keepdims=True)
    total = jnp.sum(jnp.where(is_norm, jnp.exp(stat - top), 0.0), axis=1, keepdims=True)
    log_norm = top + jnp.log(total)
    cross = jnp.sum(jnp.where(is_cross, stat, 0.0), axis=1, keepdims=True)
    loss_ref[...] = entropy_ref[...] - cross[:rows] + log_norm[:rows]
    where_token = token_places(pos, rows, side)
    for k in range(layers):
        span = pl.ds(k * side, side)
        weight = pick_column(lane == where_token, weight_ref[pos[2] ^ k])
        student = jnp.exp(logits_ref[span, :] - log_norm[k * side : (k + 1) * side])
        grad_ref[span, :] = (weight * (student - prob_ref[span, :])).astype(grad_ref.dtype)


def partial_kernel(rows, wide_steps, core_ref, grad_ref, sib_ref, w_ref, sib_w_ref, *refs):
    outs, swapped = refs[:-1], refs[-1]
    wide_outs, narrow_outs = outs[:CHIPS], outs[CHIPS:]
    layers = len(narrow_outs)
    half = CHIPS * rows
    step = pl.program_id(0)

    @pl.when(step == 0)
    def _():
        for k in range(layers):
            for core in range(CORES):
                swapped[pl.ds((k * CORES + core) * half, half), :] = sib_ref[
                    pl.ds((k * CORES + 1 - core) * half, half), :
                ]

    contract = (((1,), (1,)), ((), ()))
    total = lax.dot_general(
        grad_ref[...], w_ref[...], contract, preferred_element_type=jnp.float32
    ) + lax.dot_general(swapped[...], sib_w_ref[...], contract, preferred_element_type=jnp.float32)

    def parts():
        for k in range(layers):
            for core in range(CORES):
                for j in range(CHIPS):
                    start = (k * GROUP + core * CHIPS + j) * rows
                    yield k, core, j, total[start : start + rows]

    @pl.when(step < wide_steps)
    def _():
        for k, core, j, part in parts():
            wide_outs[j][k, core] = part.astype(wide_outs[j].dtype)

    @pl.when(step >= wide_steps)
    def _():
        for k, core, j, part in parts():
            narrow_outs[k][j, core] = part.astype(narrow_outs[k].dtype)


def head_kernel(rows, *refs):
    pieces, (grad_ref, out_ref, hidden) = refs[:-3], refs[-3:]
    assemble(pieces, rows, hidden)
    out_ref[...] = lax.dot_general(
        hidden[...], grad_ref[...], (((0,), (0,)), ((), ())), preferred_element_type=jnp.float32
    ).astype(out_ref.dtype)


def sum_of(parts, index=...):
    total = parts[0][index]
    for part in parts[1:]:
        total = total + part[index].astype(jnp.float32)
    return total


def first_sum_kernel(layers, *refs):
    wide, narrow, outs = refs[:CHIPS], refs[CHIPS : CHIPS + layers], refs[CHIPS + layers :]
    for k, out in enumerate(outs[:layers]):
        out[...] = sum_of(wide, k).astype(out.dtype)
    for j, out in enumerate(outs[layers:]):
        out[...] = sum_of(narrow, j).astype(out.dtype)


def last_sum_kernel(layers, *refs):
    wide, narrow, (mine, theirs) = refs[:layers], refs[layers:-2], refs[-2:]
    split = wide[0].shape[-1]
    for parts, columns in ((wide, slice(0, split)), (narrow, slice(split, mine.shape[1]))):
        total = sum_of(parts)
        mine[:, columns] = total[0].astype(mine.dtype)
        theirs[:, columns] = total[1].astype(theirs.dtype)


def pack_kernel(code_ref, x_ref, out_ref):
    blocks, count, side = x_ref.shape
    devices, size, _ = out_ref.shape
    slot_rows = (size - STAT_ROWS) // blocks
    stored = slot_rows // SLOTS
    target = lax.broadcasted_iota(jnp.int32, (devices * slot_rows, 1), 0)
    row = lax.broadcasted_iota(jnp.int32, (count, 1), 0) % stored
    lane = lax.broadcasted_iota(jnp.int32, (1, side), 1)
    stat = jnp.zeros((1, side), jnp.float32)
    for t in range(blocks):
        onehot = jnp.where(code_ref[t] == target, 1.0, 0.0).astype(x_ref.dtype)
        packed = jnp.dot(onehot, x_ref[t], preferred_element_type=jnp.float32).astype(out_ref.dtype)
        for device in range(devices):
            out_ref[device, pl.ds(t * slot_rows, slot_rows), :] = packed[
                device * slot_rows : (device + 1) * slot_rows
            ]
        values = x_ref[t].astype(jnp.float32)
        row_top = jnp.max(values, axis=1, keepdims=True)
        tops = [jnp.max(jnp.where(row == r, row_top, -jnp.inf), axis=0, keepdims=True) for r in range(stored)]
        top = jnp.zeros_like(row_top)
        for r in range(stored):
            top = jnp.where(row == r, tops[r], top)
        powers = jnp.exp(values - top)
        sums = jnp.sum(powers, axis=1, keepdims=True)
        weighted = jnp.sum(powers * values, axis=1, keepdims=True)
        for r in range(stored):
            total = jnp.sum(jnp.where(row == r, sums, 0.0), axis=0, keepdims=True)
            mean = jnp.sum(jnp.where(row == r, weighted, 0.0), axis=0, keepdims=True) / total
            stat = jnp.where(lane == t * stored + r, tops[r] + jnp.log(total), stat)
            stat = jnp.where(lane == (blocks + t) * stored + r, mean, stat)
    high = stat.astype(jnp.bfloat16).astype(jnp.float32)
    middle = (stat - high).astype(jnp.bfloat16).astype(jnp.float32)
    low = stat - high - middle
    parts = jnp.concatenate([high, middle, low, jnp.zeros((STAT_ROWS - 3, side), jnp.float32)], axis=0)
    parts = parts.astype(out_ref.dtype)
    for device in range(devices):
        out_ref[device, pl.ds(size - STAT_ROWS, STAT_ROWS), :] = parts


def pack_teacher(teacher_logits, block_lists, places):
    blocks, listed_count, stored, side = teacher_logits.shape
    n = lax.axis_size("vocab")
    rank = lax.axis_index("vocab")
    owner = block_lists // places
    earlier = jnp.tril(jnp.ones((listed_count, listed_count), jnp.bool_), -1)
    slot = jnp.sum((owner[:, :, None] == owner[:, None, :]) & earlier, axis=2, dtype=jnp.int32)
    code = owner * SLOTS + slot
    rows_code = (code[:, :, None] * stored + jnp.arange(stored, dtype=jnp.int32)).reshape(blocks, 1, -1)
    payload = pl.pallas_call(
        pack_kernel,
        in_specs=[vmem_spec()] * 2,
        out_specs=vmem_spec(),
        out_shape=jax.ShapeDtypeStruct(
            (n, blocks * SLOTS * stored + STAT_ROWS, side), teacher_logits.dtype
        ),
        compiler_params=kernel_params(),
        cost_estimate=LIGHT,
        name="pack_teacher",
    )(rows_code, teacher_logits.reshape(blocks, listed_count * stored, side))
    mine = code[:, None, :] == rank * SLOTS + jnp.arange(SLOTS, dtype=jnp.int32)[None, :, None]
    place = jnp.sum(jnp.where(mine, (block_lists % places + 1)[:, None, :], 0), axis=2) - 1
    return payload, place.astype(jnp.int32)


def unpack_teacher(arrived, blocks, stored):
    n, _, side = arrived.shape
    arrived_blocks = (
        arrived[:, :-3]
        .reshape(n, blocks, SLOTS, stored, side)
        .transpose(1, 2, 0, 3, 4)
        .reshape(blocks, SLOTS, n * stored, side)
    )
    arrived_stat = (
        arrived[:, -3:, : 2 * blocks * stored]
        .astype(jnp.float32)
        .sum(axis=1)
        .reshape(n, 2, blocks, stored)
        .transpose(1, 2, 0, 3)
        .reshape(2, blocks, 1, n * stored)
    )
    return arrived_blocks, arrived_stat


def levels_plan(
    hidden_states, head_weight, teacher_logits, block_lists, row_reader, tail_mass, token_weight
):
    blocks, listed_count, stored, side = teacher_logits.shape
    rows, depth = hidden_states.shape
    slab = head_weight.shape[1]
    n = lax.axis_size("vocab")
    rank = lax.axis_index("vocab")
    tokens = n * rows
    layers = n // GROUP
    half = depth // CORES
    bf16, f32 = jnp.bfloat16, jnp.float32
    core, chip, layer = rank % CORES, (rank // CORES) % CHIPS, rank // GROUP
    pos = jnp.stack([core, chip, layer, rank]).astype(jnp.int32)
    unlisted = float(n * slab - side * listed_count)

    column = [hidden_states] + [shift(hidden_states, k * GROUP) for k in range(1, layers)]
    column = jnp.concatenate(column, axis=0)
    plane = [column] + [shift(column, j * CORES) for j in range(1, CHIPS)]
    payload, place = pack_teacher(teacher_logits, block_lists, slab // side)
    arrived = lax.all_to_all(
        payload[:, : 3 - STAT_ROWS], "vocab", split_axis=0, concat_axis=0, tiled=True
    )
    arrived_blocks, arrived_stat = unpack_teacher(arrived, blocks, stored)

    prob, entropy = pl.pallas_call(
        lambda *refs: teacher_kernel(unlisted, rows, *refs),
        out_shape=(
            jax.ShapeDtypeStruct((tokens, slab), f32),
            jax.ShapeDtypeStruct((rows, side), f32),
        ),
        in_specs=[smem_spec(), smem_spec()] + [vmem_spec()] * 4,
        out_specs=(vmem_spec(), vmem_spec()),
        compiler_params=kernel_params(),
        cost_estimate=LIGHT,
        name="teacher_prob",
    )(
        pos,
        place,
        arrived_blocks,
        arrived_stat,
        row_reader.reshape(blocks, 1, side),
        tail_mass.reshape(blocks, 1, side),
    )

    plane[-1], prob = lax.optimization_barrier((plane[-1], prob))
    pieces = plane + [shift(piece, 1) for piece in plane]
    pieces, late_weight = lax.optimization_barrier((pieces, head_weight))
    sib_w = shift(late_weight, 1)

    width = 256 if slab % 256 == 0 else 128
    tiles = slab // width
    whole = lambda t: (0, 0)
    logits, stat = pl.pallas_call(
        functools.partial(logits_kernel, rows),
        grid=(2 * tiles,),
        out_shape=[
            jax.ShapeDtypeStruct((tokens, slab), f32),
            jax.ShapeDtypeStruct((n, 2 * tokens // 128, 128), f32),
        ],
        in_specs=[vmem_spec()] * len(pieces)
        + [hbm_spec(), pl.BlockSpec((tokens, width), lambda t: (0, jnp.maximum(t - tiles, 0)))],
        out_specs=[
            pl.BlockSpec((tokens, slab), whole),
            pl.BlockSpec((n, 2 * tokens // 128, 128), lambda t: (0, 0, 0)),
        ],
        scratch_shapes=[
            pltpu.VMEM((tokens, depth), bf16),
            pltpu.VMEM((depth, slab), bf16),
            pltpu.SemaphoreType.DMA((2,)),
            pltpu.VMEM((tokens, 128), f32),
        ],
        compiler_params=kernel_params(LOGITS_VMEM),
        cost_estimate=LIGHT,
        name="logits",
    )(*pieces, head_weight, prob)
    stat = lax.all_to_all(stat, "vocab", split_axis=0, concat_axis=0, tiled=True)

    grad, loss = pl.pallas_call(
        lambda *refs: grad_kernel(rows, *refs),
        out_shape=(
            jax.ShapeDtypeStruct((tokens, slab), bf16),
            jax.ShapeDtypeStruct((rows, side), f32),
        ),
        in_specs=[smem_spec()] + [vmem_spec()] * 5,
        out_specs=(vmem_spec(), vmem_spec()),
        compiler_params=kernel_params(),
        cost_estimate=LIGHT,
        name="grad_logits",
    )(pos, stat, logits, prob, token_weight.reshape(blocks, 1, side), entropy)
    sib_grad = shift(grad, 1)

    tile = half // 5
    wide_steps = 3
    sizes = (wide_steps * tile, half - wide_steps * tile)
    wide_block = pl.BlockSpec(
        (layers, CORES, rows, tile), lambda t, pos: (0, 0, 0, jnp.minimum(t, wide_steps - 1))
    )
    narrow_block = pl.BlockSpec(
        (CHIPS, CORES, rows, tile), lambda t, pos: (0, 0, 0, jnp.maximum(t - wide_steps, 0))
    )
    partial = pl.pallas_call(
        functools.partial(partial_kernel, rows, wide_steps),
        grid_spec=pltpu.PrefetchScalarGridSpec(
            num_scalar_prefetch=1,
            grid=(5,),
            in_specs=[pl.BlockSpec((tokens, slab), lambda t, pos: (0, 0))] * 2
            + [pl.BlockSpec((tile, slab), lambda t, pos: (pos[0] * 5 + t, 0))] * 2,
            out_specs=[wide_block] * CHIPS + [narrow_block] * layers,
            scratch_shapes=[pltpu.VMEM((tokens, slab), bf16)],
        ),
        out_shape=[
            jax.ShapeDtypeStruct((layers, CORES, rows, sizes[0]), bf16 if j else f32) for j in range(CHIPS)
        ]
        + [jax.ShapeDtypeStruct((CHIPS, CORES, rows, sizes[1]), bf16 if k else f32) for k in range(layers)],
        compiler_params=kernel_params(LARGE_VMEM),
        cost_estimate=LIGHT,
        name="grad_hidden_partial",
    )(pos, grad, sib_grad, head_weight, sib_w)
    *partial, late_grad = lax.optimization_barrier((*partial, grad))
    wide_sums = [shift(partial[j], j * CORES) for j in range(1, CHIPS)]
    narrow_sums = [shift(partial[CHIPS + k], k * GROUP) for k in range(1, layers)]

    head_tile = half // 2
    grad_head = pl.pallas_call(
        functools.partial(head_kernel, rows),
        grid=(4,),
        in_specs=[pl.BlockSpec((layers * rows, head_tile), lambda t: (0, t)) for _ in pieces]
        + [pl.BlockSpec((tokens, slab), whole)],
        out_specs=pl.BlockSpec((head_tile, slab), lambda t: (t, 0)),
        out_shape=jax.ShapeDtypeStruct((depth, slab), bf16),
        scratch_shapes=[pltpu.VMEM((tokens, head_tile), bf16)],
        compiler_params=kernel_params(LARGE_VMEM),
        cost_estimate=LIGHT,
        name="grad_head",
    )(*pieces, late_grad)
    wide_sums, narrow_sums, grad_head = lax.optimization_barrier((wide_sums, narrow_sums, grad_head))

    summed = pl.pallas_call(
        functools.partial(first_sum_kernel, layers),
        in_specs=[vmem_spec()] * (CHIPS + layers),
        out_specs=[vmem_spec()] * (CHIPS + layers),
        out_shape=[jax.ShapeDtypeStruct((CORES, rows, sizes[0]), bf16 if k else f32) for k in range(layers)]
        + [jax.ShapeDtypeStruct((CORES, rows, sizes[1]), bf16 if j else f32) for j in range(CHIPS)],
        compiler_params=kernel_params(),
        cost_estimate=LIGHT,
        name="first_sum",
    )(partial[0], *wide_sums, partial[CHIPS], *narrow_sums)
    wide_sums = [shift(summed[k], k * GROUP) for k in range(1, layers)]
    narrow_sums = [shift(summed[layers + j], j * CORES) for j in range(1, CHIPS)]
    mine, theirs = pl.pallas_call(
        functools.partial(last_sum_kernel, layers),
        in_specs=[vmem_spec()] * (CHIPS + layers),
        out_specs=[vmem_spec()] * 2,
        out_shape=[jax.ShapeDtypeStruct((rows, half), bf16)] * 2,
        compiler_params=kernel_params(),
        cost_estimate=LIGHT,
        name="last_sum",
    )(summed[0], *wide_sums, summed[layers], *narrow_sums)
    other = shift(theirs, 1)

    low, high = jnp.where(core == 0, mine, other), jnp.where(core == 0, other, mine)
    return loss[:, 0], grad_head, jnp.concatenate([low, high], axis=1)


def fits_levels(hidden_states, teacher_logits):
    n = lax.axis_size("vocab")
    rows = hidden_states.shape[0]
    blocks, _, stored, side = teacher_logits.shape
    return (
        n == blocks * GROUP
        and blocks & (blocks - 1) == 0
        and rows * GROUP == side
        and rows % 16 == 0
        and 2 * n <= side
        and 6 * blocks * stored <= side
        and hidden_states.shape[1] % (CORES * 1280) == 0
    )


def on_device(
    hidden_states, head_weight, teacher_logits, block_lists, row_reader, tail_mass, token_weight
):
    plan = levels_plan if fits_levels(hidden_states, teacher_logits) else plain_plan
    return plan(
        hidden_states, head_weight, teacher_logits, block_lists, row_reader, tail_mass, token_weight
    )


def solution(mesh):
    in_specs = (
        P("vocab", None),
        P(None, "vocab"),
        P(None, None, "vocab", None),
        P(),
        P(),
        P(),
        P(),
    )
    out_specs = (P("vocab"), P(None, "vocab"), P("vocab", None))
    return jax.shard_map(
        on_device, mesh=mesh, in_specs=in_specs, out_specs=out_specs, check_vma=False
    )
```

```python
import functools

import jax
import jax.numpy as jnp
from jax import lax
from jax.experimental import pallas as pl
from jax.experimental.pallas import tpu as pltpu
from jax.sharding import PartitionSpec as P


def row_parts(scores, teacher_slab, listed_mask, student_exp, teacher_exp):
    return (
        jnp.sum(student_exp, axis=(2, 3)),
        jnp.sum(teacher_exp, axis=(2, 3)),
        jnp.sum(teacher_exp * scores, axis=(2, 3)),
        jnp.sum(teacher_exp * teacher_slab, axis=(2, 3)),
        jnp.sum(scores, axis=(2, 3)),
        jnp.sum(jnp.where(listed_mask, scores, 0.0), axis=(2, 3)),
    )


def plain_plan(
    hidden_states, head_weight, teacher_logits, block_lists, row_reader, tail_mass, token_weight
):
    blocks, listed_count, stored_rows, block_side = teacher_logits.shape
    slab_width = head_weight.shape[1]
    slab_blocks = slab_width // block_side
    devices = lax.axis_size("vocab")
    rank_self = lax.axis_index("vocab")
    tokens = blocks * block_side
    shard_rows = hidden_states.shape[0]
    gathered = lax.all_gather(hidden_states, "vocab", axis=0, tiled=True)
    logits = jnp.dot(gathered, head_weight, preferred_element_type=jnp.float32)
    owner_dev = block_lists // slab_blocks
    owned_here = owner_dev == rank_self
    within = block_lists - rank_self * slab_blocks
    token_iota = lax.broadcasted_iota(jnp.int32, (1, block_side, block_side), 1)
    token_map = (row_reader[:, None, :] == token_iota).astype(jnp.bfloat16)
    place_iota = lax.broadcasted_iota(jnp.int32, (1, slab_blocks, 1), 1)
    block_iota = lax.broadcasted_iota(jnp.int32, (1, devices * slab_blocks, 1), 1)
    picker = (block_lists[:, None, :] == block_iota).astype(jnp.bfloat16)
    outgoing = jnp.einsum(
        "tnk,tkrc->tnrc", picker, teacher_logits, preferred_element_type=jnp.float32
    ).astype(jnp.bfloat16)
    incoming = lax.all_to_all(outgoing, "vocab", split_axis=1, concat_axis=2, tiled=True)
    teacher_slab = jnp.einsum(
        "tpj,tbjc->tpbc", token_map, incoming, preferred_element_type=jnp.float32
    )
    listed = jnp.sum(
        ((within[:, None, :] == place_iota) & owned_here[:, None, :]).astype(jnp.int32), axis=2
    )
    scores = logits.reshape(blocks, block_side, slab_blocks, block_side)
    listed_mask = (listed > 0)[:, None, :, None]
    local_smax = jnp.max(scores, axis=(2, 3))
    local_tmax = jnp.max(jnp.where(listed_mask, teacher_slab, -1e30), axis=(2, 3))
    student_max, teacher_max = lax.pmax((local_smax, local_tmax), "vocab")
    student_exp = jnp.exp(scores - student_max[:, :, None, None])
    teacher_exp = jnp.exp(
        jnp.where(listed_mask, teacher_slab - teacher_max[:, :, None, None], -jnp.inf)
    )
    parts = row_parts(scores, teacher_slab, listed_mask, student_exp, teacher_exp)
    student_sum, teacher_sum, cross_sum, self_sum, logit_total, listed_total = lax.psum(
        (parts[0], parts[1], parts[2], parts[3], parts[4], parts[5]), "vocab"
    )
    tail_share = tail_mass.reshape(blocks, block_side)
    unlisted = float(devices * slab_width - block_side * listed_count)
    kept_mass = 1.0 - tail_share
    log_norm = student_max + jnp.log(student_sum)
    row_loss = (
        kept_mass * (jnp.log(kept_mass) - teacher_max - jnp.log(teacher_sum))
        + kept_mass * self_sum / teacher_sum
        + tail_share * jnp.log(tail_share / unlisted)
        - kept_mass * cross_sum / teacher_sum
        - tail_share / unlisted * (logit_total - listed_total)
        + log_norm
    )
    token_loss = lax.dynamic_slice_in_dim(
        row_loss.reshape(tokens), rank_self * shard_rows, shard_rows, 0
    )
    student_prob = student_exp / student_sum[:, :, None, None]
    teacher_prob = jnp.where(
        listed_mask,
        (kept_mass / teacher_sum)[:, :, None, None] * teacher_exp,
        (tail_share / unlisted)[:, :, None, None],
    )
    weight = token_weight.reshape(blocks, block_side)[:, :, None, None]
    grad_logits = (
        (weight * (student_prob - teacher_prob)).astype(jnp.bfloat16).reshape(tokens, slab_width)
    )
    grad_head = lax.dot_general(
        gathered, grad_logits, (((0,), (0,)), ((), ())), preferred_element_type=jnp.float32
    ).astype(jnp.bfloat16)
    grad_hidden = lax.psum_scatter(
        lax.dot_general(
            grad_logits, head_weight, (((1,), (1,)), ((), ())), preferred_element_type=jnp.float32
        ),
        "vocab",
        scatter_dimension=0,
        tiled=True,
    ).astype(jnp.bfloat16)
    return (token_loss, grad_head, grad_hidden)


CORES = 2
CHIPS = 4
GROUP = CORES * CHIPS
SLOTS = 4
LIGHT = pl.CostEstimate(flops=1, bytes_accessed=1, transcendentals=0)
SMALL_VMEM = 16 * 1024 * 1024
LOGITS_VMEM = 46 * 1024 * 1024
LARGE_VMEM = 48 * 1024 * 1024
STAT_ROWS = 16


def kernel_params(limit=SMALL_VMEM):
    return pltpu.CompilerParams(vmem_limit_bytes=limit)


def vmem_spec():
    return pl.BlockSpec(memory_space=pltpu.VMEM)


def hbm_spec():
    return pl.BlockSpec(memory_space=pltpu.HBM)


def smem_spec():
    return pl.BlockSpec(memory_space=pltpu.SMEM)


def shift(x, distance):
    n = lax.axis_size("vocab")
    return lax.ppermute(x, "vocab", [(i, i ^ distance) for i in range(n)])


def token_places(place, rows, side):
    row = lax.broadcasted_iota(jnp.int32, (side, 1), 0)
    group = row // rows
    chip = (group % CHIPS) ^ place[1]
    core = (group // CHIPS) ^ place[0]
    return (chip * CORES + core) * rows + row % rows


def pick_column(match, values):
    return jnp.sum(jnp.where(match, values, 0.0), axis=1, keepdims=True)


def teacher_kernel(
    unlisted, rows, pos_ref, place_ref, blocks_ref, stat_ref, reader_ref, tail_ref, prob_ref, entropy_ref
):
    layers, slots, side, _ = blocks_ref.shape
    pos = [pos_ref[i] for i in range(3)]
    lane = lax.broadcasted_iota(jnp.int32, (1, side), 1)
    where_token = token_places(pos, rows, side)
    for k in range(layers):
        block = pos[2] ^ k
        match = reader_ref[block] == where_token
        onehot = jnp.where(match, 1.0, 0.0).astype(jnp.bfloat16)
        normaliser = pick_column(match, stat_ref[0, block])
        tail = pick_column(lane == where_token, tail_ref[block])
        kept = 1.0 - tail
        rest = tail / unlisted
        span = pl.ds(k * side, side)
        prob_ref[span, :] = jnp.broadcast_to(rest, (side, prob_ref.shape[1]))
        for s in range(slots):
            place = place_ref[block, s]
            values = jnp.dot(onehot, blocks_ref[block, s], preferred_element_type=jnp.float32)
            prob = kept * jnp.exp(values - normaliser)

            @pl.when(place >= 0)
            def _():
                prob_ref[span, pl.ds(pl.multiple_of(place * side, side), side)] = prob

        if k == 0:
            mean = pick_column(match, stat_ref[1, block])
            entropy = kept * (jnp.log(kept) - normaliser + mean) + tail * jnp.log(rest)
            entropy_ref[...] = jnp.broadcast_to(entropy[:rows], entropy_ref.shape)


def assemble(pieces, rows, out_ref):
    per_core = len(pieces) // CORES
    layers = pieces[0].shape[0] // rows
    for core in range(CORES):
        mine = pieces[core * per_core : (core + 1) * per_core]
        for k in range(layers):
            span = pl.ds(k * rows, rows)
            for j, piece in enumerate(mine[:CHIPS]):
                at = pl.ds((k * GROUP + core * CHIPS + j) * rows, rows)
                columns = slice(0, piece.shape[1])
                out_ref[at, columns] = piece[span, :]
            if per_core > CHIPS:
                piece = mine[CHIPS]
                columns = slice(out_ref.shape[1] - piece.shape[1], out_ref.shape[1])
                out_ref[at, columns] = piece[span, :]


def logits_kernel(rows, *refs):
    pieces, refs = refs[:-8], refs[-8:]
    w_ref, prob_ref, logits_ref, stat_ref, hidden, weight, sems, cross_ref = refs
    depth, width = w_ref.shape[0], prob_ref.shape[1]
    parts = [slice(0, depth // 4), slice(depth // 4, depth)]
    tiles = w_ref.shape[1] // width
    step = pl.program_id(0)

    def copy(i):
        span = pl.ds(parts[i].start, parts[i].stop - parts[i].start)
        return pltpu.make_async_copy(w_ref.at[span, :], weight.at[span, :], sems.at[i])

    @pl.when(step == 0)
    def _():
        copy(0).start()
        copy(1).start()
        assemble(pieces, rows, hidden)
        copy(0).wait()

    @pl.when(step == tiles)
    def _():
        copy(1).wait()

    @pl.when(step < tiles)
    def _():
        span = pl.ds(pl.multiple_of(step * width, width), width)
        logits_ref[:, span] = jnp.dot(
            hidden[:, parts[0]], weight[parts[0], span], preferred_element_type=jnp.float32
        )

    @pl.when(step >= tiles)
    def _():
        span = pl.ds(pl.multiple_of((step - tiles) * width, width), width)
        total = logits_ref[:, span] + jnp.dot(
            hidden[:, parts[1]], weight[parts[1], span], preferred_element_type=jnp.float32
        )
        logits_ref[:, span] = total
        product = total * prob_ref[...]
        folded = product[:, :128]
        for i in range(1, width // 128):
            folded = folded + product[:, i * 128 : (i + 1) * 128]
        cross_ref[...] = jnp.where(step == tiles, 0.0, cross_ref[...]) + folded

    @pl.when(step == 2 * tiles - 1)
    def _():
        logits = logits_ref[...]
        top = jnp.max(logits, axis=1, keepdims=True)
        norm = top + jnp.log(jnp.sum(jnp.exp(logits - top), axis=1, keepdims=True))
        cross = jnp.sum(cross_ref[...], axis=1, keepdims=True)
        lane = lax.broadcasted_iota(jnp.int32, (1, 128), 1)
        both = jnp.where(lane == 0, norm, jnp.where(lane == 1, cross, 0.0)).T
        tokens = logits.shape[0]
        packed = [both[i : i + 1, t : t + 128] for i in range(2) for t in range(0, tokens, 128)]
        stat_ref[...] = jnp.broadcast_to(jnp.concatenate(packed, axis=0)[None], stat_ref.shape)


def grad_kernel(
    rows, pos_ref, stat_ref, logits_ref, prob_ref, weight_ref, entropy_ref, grad_ref, loss_ref
):
    tokens = logits_ref.shape[0]
    devices = tokens // rows
    layers, _, side = weight_ref.shape
    layer_bits = (devices // GROUP).bit_length() - 1
    pos = [pos_ref[i] for i in range(3)]
    rank = pos_ref[3]
    lane = lax.broadcasted_iota(jnp.int32, (1, 128), 1)
    per_stat = stat_ref.shape[1] // 2
    norms, crosses = [
        jnp.concatenate([stat_ref[:, i * per_stat + t, :] for t in range(per_stat)], axis=1) for i in range(2)
    ]
    stat = jnp.concatenate(
        [norms, crosses, jnp.zeros((128 - 2 * devices, tokens), jnp.float32)], axis=0
    ).T
    pairs = [(0, 2), (1, 0), (2, 1)] + [(3 + i, 3 + i) for i in range(layer_bits)]
    for index_bit, block_bit in pairs:
        halves = stat.reshape(devices >> (block_bit + 1), 2, rows << block_bit, 128)
        swapped = jnp.stack([halves[:, 1], halves[:, 0]], axis=1).reshape(tokens, 128)
        stat = jnp.where(((lane ^ rank) >> index_bit) & 1 == 1, swapped, stat)
    is_norm = lane < devices
    is_cross = (lane >= devices) & (lane < 2 * devices)
    top = jnp.max(jnp.where(is_norm, stat, -jnp.inf), axis=1, keepdims=True)
    total = jnp.sum(jnp.where(is_norm, jnp.exp(stat - top), 0.0), axis=1, keepdims=True)
    log_norm = top + jnp.log(total)
    cross = jnp.sum(jnp.where(is_cross, stat, 0.0), axis=1, keepdims=True)
    loss_ref[...] = entropy_ref[...] - cross[:rows] + log_norm[:rows]
    where_token = token_places(pos, rows, side)
    for k in range(layers):
        span = pl.ds(k * side, side)
        weight = pick_column(lane == where_token, weight_ref[pos[2] ^ k])
        student = jnp.exp(logits_ref[span, :] - log_norm[k * side : (k + 1) * side])
        grad_ref[span, :] = (weight * (student - prob_ref[span, :])).astype(grad_ref.dtype)


def partial_kernel(rows, wide_steps, core_ref, grad_ref, sib_ref, w_ref, sib_w_ref, *refs):
    outs, swapped = refs[:-1], refs[-1]
    wide_outs, narrow_outs = outs[:CHIPS], outs[CHIPS:]
    layers = len(narrow_outs)
    half = CHIPS * rows
    step = pl.program_id(0)

    @pl.when(step == 0)
    def _():
        for k in range(layers):
            for core in range(CORES):
                swapped[pl.ds((k * CORES + core) * half, half), :] = sib_ref[
                    pl.ds((k * CORES + 1 - core) * half, half), :
                ]

    contract = (((1,), (1,)), ((), ()))
    total = lax.dot_general(
        grad_ref[...], w_ref[...], contract, preferred_element_type=jnp.float32
    ) + lax.dot_general(swapped[...], sib_w_ref[...], contract, preferred_element_type=jnp.float32)

    def parts():
        for k in range(layers):
            for core in range(CORES):
                for j in range(CHIPS):
                    start = (k * GROUP + core * CHIPS + j) * rows
                    yield k, core, j, total[start : start + rows]

    @pl.when(step < wide_steps)
    def _():
        for k, core, j, part in parts():
            wide_outs[j][k, core] = part.astype(wide_outs[j].dtype)

    @pl.when(step >= wide_steps)
    def _():
        for k, core, j, part in parts():
            narrow_outs[k][j, core] = part.astype(narrow_outs[k].dtype)


def head_kernel(rows, *refs):
    pieces, (grad_ref, out_ref, hidden) = refs[:-3], refs[-3:]
    per_core = CHIPS + 1
    late = pl.program_id(0) >= pl.num_programs(0) // 2
    for i in range(2):

        @pl.when(late == (i == 1))
        def _():
            mine = [pieces[c * per_core : (c + 1) * per_core] for c in range(CORES)]
            assemble([p for some in mine for p in (*some[: CHIPS - 1], some[CHIPS - 1 + i])], rows, hidden)

    out_ref[...] = lax.dot_general(
        hidden[...], grad_ref[...], (((0,), (0,)), ((), ())), preferred_element_type=jnp.float32
    ).astype(out_ref.dtype)


def sum_of(parts, index=...):
    total = parts[0][index]
    for part in parts[1:]:
        total = total + part[index].astype(jnp.float32)
    return total


def first_sum_kernel(layers, *refs):
    wide, narrow, outs = refs[:CHIPS], refs[CHIPS : CHIPS + layers], refs[CHIPS + layers :]
    for k, out in enumerate(outs[:layers]):
        out[...] = sum_of(wide, k).astype(out.dtype)
    for j, out in enumerate(outs[layers:]):
        out[...] = sum_of(narrow, j).astype(out.dtype)


def last_sum_kernel(layers, *refs):
    wide, narrow, (mine, theirs) = refs[:layers], refs[layers:-2], refs[-2:]
    split = wide[0].shape[-1]
    for parts, columns in ((wide, slice(0, split)), (narrow, slice(split, mine.shape[1]))):
        total = sum_of(parts)
        mine[:, columns] = total[0].astype(mine.dtype)
        theirs[:, columns] = total[1].astype(theirs.dtype)


def pack_kernel(code_ref, x_ref, out_ref):
    blocks, count, side = x_ref.shape
    devices, size, _ = out_ref.shape
    slot_rows = (size - STAT_ROWS) // blocks
    stored = slot_rows // SLOTS
    target = lax.broadcasted_iota(jnp.int32, (devices * slot_rows, 1), 0)
    row = lax.broadcasted_iota(jnp.int32, (count, 1), 0) % stored
    lane = lax.broadcasted_iota(jnp.int32, (1, side), 1)
    stat = jnp.zeros((1, side), jnp.float32)
    for t in range(blocks):
        onehot = jnp.where(code_ref[t] == target, 1.0, 0.0).astype(x_ref.dtype)
        packed = jnp.dot(onehot, x_ref[t], preferred_element_type=jnp.float32).astype(out_ref.dtype)
        for device in range(devices):
            out_ref[device, pl.ds(t * slot_rows, slot_rows), :] = packed[
                device * slot_rows : (device + 1) * slot_rows
            ]
        values = x_ref[t].astype(jnp.float32)
        row_top = jnp.max(values, axis=1, keepdims=True)
        tops = [jnp.max(jnp.where(row == r, row_top, -jnp.inf), axis=0, keepdims=True) for r in range(stored)]
        top = jnp.zeros_like(row_top)
        for r in range(stored):
            top = jnp.where(row == r, tops[r], top)
        powers = jnp.exp(values - top)
        sums = jnp.sum(powers, axis=1, keepdims=True)
        weighted = jnp.sum(powers * values, axis=1, keepdims=True)
        for r in range(stored):
            total = jnp.sum(jnp.where(row == r, sums, 0.0), axis=0, keepdims=True)
            mean = jnp.sum(jnp.where(row == r, weighted, 0.0), axis=0, keepdims=True) / total
            stat = jnp.where(lane == t * stored + r, tops[r] + jnp.log(total), stat)
            stat = jnp.where(lane == (blocks + t) * stored + r, mean, stat)
    high = stat.astype(jnp.bfloat16).astype(jnp.float32)
    middle = (stat - high).astype(jnp.bfloat16).astype(jnp.float32)
    low = stat - high - middle
    parts = jnp.concatenate([high, middle, low, jnp.zeros((STAT_ROWS - 3, side), jnp.float32)], axis=0)
    parts = parts.astype(out_ref.dtype)
    for device in range(devices):
        out_ref[device, pl.ds(size - STAT_ROWS, STAT_ROWS), :] = parts


def pack_teacher(teacher_logits, block_lists, places):
    blocks, listed_count, stored, side = teacher_logits.shape
    n = lax.axis_size("vocab")
    rank = lax.axis_index("vocab")
    owner = block_lists // places
    earlier = jnp.tril(jnp.ones((listed_count, listed_count), jnp.bool_), -1)
    slot = jnp.sum((owner[:, :, None] == owner[:, None, :]) & earlier, axis=2, dtype=jnp.int32)
    code = owner * SLOTS + slot
    rows_code = (code[:, :, None] * stored + jnp.arange(stored, dtype=jnp.int32)).reshape(blocks, 1, -1)
    payload = pl.pallas_call(
        pack_kernel,
        in_specs=[vmem_spec()] * 2,
        out_specs=vmem_spec(),
        out_shape=jax.ShapeDtypeStruct(
            (n, blocks * SLOTS * stored + STAT_ROWS, side), teacher_logits.dtype
        ),
        compiler_params=kernel_params(),
        cost_estimate=LIGHT,
        name="pack_teacher",
    )(rows_code, teacher_logits.reshape(blocks, listed_count * stored, side))
    mine = code[:, None, :] == rank * SLOTS + jnp.arange(SLOTS, dtype=jnp.int32)[None, :, None]
    place = jnp.sum(jnp.where(mine, (block_lists % places + 1)[:, None, :], 0), axis=2) - 1
    return payload, place.astype(jnp.int32)


def unpack_teacher(arrived, blocks, stored):
    n, _, side = arrived.shape
    arrived_blocks = (
        arrived[:, :-3]
        .reshape(n, blocks, SLOTS, stored, side)
        .transpose(1, 2, 0, 3, 4)
        .reshape(blocks, SLOTS, n * stored, side)
    )
    arrived_stat = (
        arrived[:, -3:, : 2 * blocks * stored]
        .astype(jnp.float32)
        .sum(axis=1)
        .reshape(n, 2, blocks, stored)
        .transpose(1, 2, 0, 3)
        .reshape(2, blocks, 1, n * stored)
    )
    return arrived_blocks, arrived_stat


def levels_plan(
    hidden_states, head_weight, teacher_logits, block_lists, row_reader, tail_mass, token_weight
):
    blocks, listed_count, stored, side = teacher_logits.shape
    rows, depth = hidden_states.shape
    slab = head_weight.shape[1]
    n = lax.axis_size("vocab")
    rank = lax.axis_index("vocab")
    tokens = n * rows
    layers = n // GROUP
    half = depth // CORES
    bf16, f32 = jnp.bfloat16, jnp.float32
    core, chip, layer = rank % CORES, (rank // CORES) % CHIPS, rank // GROUP
    pos = jnp.stack([core, chip, layer, rank]).astype(jnp.int32)
    unlisted = float(n * slab - side * listed_count)

    column = [hidden_states] + [shift(hidden_states, k * GROUP) for k in range(1, layers)]
    column = jnp.concatenate(column, axis=0)
    X, Y = CORES, 2 * CORES
    plane = [column, shift(column, X), shift(column, Y)]
    plane += [shift(plane[1][:, :half], Y), shift(plane[2][:, half:], X)]
    payload, place = pack_teacher(teacher_logits, block_lists, slab // side)
    arrived = lax.all_to_all(
        payload[:, : 3 - STAT_ROWS], "vocab", split_axis=0, concat_axis=0, tiled=True
    )
    arrived_blocks, arrived_stat = unpack_teacher(arrived, blocks, stored)

    prob, entropy = pl.pallas_call(
        lambda *refs: teacher_kernel(unlisted, rows, *refs),
        out_shape=(
            jax.ShapeDtypeStruct((tokens, slab), f32),
            jax.ShapeDtypeStruct((rows, side), f32),
        ),
        in_specs=[smem_spec(), smem_spec()] + [vmem_spec()] * 4,
        out_specs=(vmem_spec(), vmem_spec()),
        compiler_params=kernel_params(),
        cost_estimate=LIGHT,
        name="teacher_prob",
    )(
        pos,
        place,
        arrived_blocks,
        arrived_stat,
        row_reader.reshape(blocks, 1, side),
        tail_mass.reshape(blocks, 1, side),
    )

    sent_w = lax.dynamic_slice(head_weight, ((1 - core) * half, 0), (half, slab))
    plane[-2], plane[-1], prob, sent_w = lax.optimization_barrier((plane[-2], plane[-1], prob, sent_w))
    pieces = plane + [shift(piece, 1) for piece in plane]
    pieces, sent_w = lax.optimization_barrier((pieces, sent_w))
    sib_w = shift(sent_w, 1)

    width = 256 if slab % 256 == 0 else 128
    tiles = slab // width
    whole = lambda t: (0, 0)
    logits, stat = pl.pallas_call(
        functools.partial(logits_kernel, rows),
        grid=(2 * tiles,),
        out_shape=[
            jax.ShapeDtypeStruct((tokens, slab), f32),
            jax.ShapeDtypeStruct((n, 2 * tokens // 128, 128), f32),
        ],
        in_specs=[vmem_spec()] * len(pieces)
        + [hbm_spec(), pl.BlockSpec((tokens, width), lambda t: (0, jnp.maximum(t - tiles, 0)))],
        out_specs=[
            pl.BlockSpec((tokens, slab), whole),
            pl.BlockSpec((n, 2 * tokens // 128, 128), lambda t: (0, 0, 0)),
        ],
        scratch_shapes=[
            pltpu.VMEM((tokens, depth), bf16),
            pltpu.VMEM((depth, slab), bf16),
            pltpu.SemaphoreType.DMA((2,)),
            pltpu.VMEM((tokens, 128), f32),
        ],
        compiler_params=kernel_params(LOGITS_VMEM),
        cost_estimate=LIGHT,
        name="logits",
    )(*pieces, head_weight, prob)
    stat = lax.all_to_all(stat, "vocab", split_axis=0, concat_axis=0, tiled=True)

    grad, loss = pl.pallas_call(
        lambda *refs: grad_kernel(rows, *refs),
        out_shape=(
            jax.ShapeDtypeStruct((tokens, slab), bf16),
            jax.ShapeDtypeStruct((rows, side), f32),
        ),
        in_specs=[smem_spec()] + [vmem_spec()] * 5,
        out_specs=(vmem_spec(), vmem_spec()),
        compiler_params=kernel_params(),
        cost_estimate=LIGHT,
        name="grad_logits",
    )(pos, stat, logits, prob, token_weight.reshape(blocks, 1, side), entropy)
    sib_grad = shift(grad, 1)

    tile = half // 5
    wide_steps = 3
    sizes = (wide_steps * tile, half - wide_steps * tile)
    wide_block = pl.BlockSpec(
        (layers, CORES, rows, tile), lambda t, pos: (0, 0, 0, jnp.minimum(t, wide_steps - 1))
    )
    narrow_block = pl.BlockSpec(
        (CHIPS, CORES, rows, tile), lambda t, pos: (0, 0, 0, jnp.maximum(t - wide_steps, 0))
    )
    partial = pl.pallas_call(
        functools.partial(partial_kernel, rows, wide_steps),
        grid_spec=pltpu.PrefetchScalarGridSpec(
            num_scalar_prefetch=1,
            grid=(5,),
            in_specs=[pl.BlockSpec((tokens, slab), lambda t, pos: (0, 0))] * 2
            + [pl.BlockSpec((tile, slab), lambda t, pos: (pos[0] * 5 + t, 0))]
            + [pl.BlockSpec((tile, slab), lambda t, pos: (t, 0))],
            out_specs=[wide_block] * CHIPS + [narrow_block] * layers,
            scratch_shapes=[pltpu.VMEM((tokens, slab), bf16)],
        ),
        out_shape=[
            jax.ShapeDtypeStruct((layers, CORES, rows, sizes[0]), bf16 if j else f32) for j in range(CHIPS)
        ]
        + [jax.ShapeDtypeStruct((CHIPS, CORES, rows, sizes[1]), bf16 if k else f32) for k in range(layers)],
        compiler_params=kernel_params(LARGE_VMEM),
        cost_estimate=LIGHT,
        name="grad_hidden_partial",
    )(pos, grad, sib_grad, head_weight, sib_w)
    *partial, late_grad = lax.optimization_barrier((*partial, grad))
    wide_sums = [shift(partial[j], j * CORES) for j in range(1, CHIPS)]
    narrow_sums = [shift(partial[CHIPS + k], k * GROUP) for k in range(1, layers)]

    head_tile = half // 2
    grad_head = pl.pallas_call(
        functools.partial(head_kernel, rows),
        grid=(4,),
        in_specs=[
            pl.BlockSpec(
                (layers * rows, head_tile),
                lambda t, i=i % (CHIPS + 1): (0, (t, jnp.minimum(t, 1), jnp.maximum(t - 2, 0))[max(i - 2, 0)]),
            )
            for i in range(len(pieces))
        ]
        + [pl.BlockSpec((tokens, slab), whole)],
        out_specs=pl.BlockSpec((head_tile, slab), lambda t: (t, 0)),
        out_shape=jax.ShapeDtypeStruct((depth, slab), bf16),
        scratch_shapes=[pltpu.VMEM((tokens, head_tile), bf16)],
        compiler_params=kernel_params(LARGE_VMEM),
        cost_estimate=LIGHT,
        name="grad_head",
    )(*pieces, late_grad)
    wide_sums, narrow_sums, grad_head = lax.optimization_barrier((wide_sums, narrow_sums, grad_head))

    summed = pl.pallas_call(
        functools.partial(first_sum_kernel, layers),
        in_specs=[vmem_spec()] * (CHIPS + layers),
        out_specs=[vmem_spec()] * (CHIPS + layers),
        out_shape=[jax.ShapeDtypeStruct((CORES, rows, sizes[0]), bf16 if k else f32) for k in range(layers)]
        + [jax.ShapeDtypeStruct((CORES, rows, sizes[1]), bf16 if j else f32) for j in range(CHIPS)],
        compiler_params=kernel_params(),
        cost_estimate=LIGHT,
        name="first_sum",
    )(partial[0], *wide_sums, partial[CHIPS], *narrow_sums)
    wide_sums = [shift(summed[k], k * GROUP) for k in range(1, layers)]
    narrow_sums = [shift(summed[layers + j], j * CORES) for j in range(1, CHIPS)]
    mine, theirs = pl.pallas_call(
        functools.partial(last_sum_kernel, layers),
        in_specs=[vmem_spec()] * (CHIPS + layers),
        out_specs=[vmem_spec()] * 2,
        out_shape=[jax.ShapeDtypeStruct((rows, half), bf16)] * 2,
        compiler_params=kernel_params(),
        cost_estimate=LIGHT,
        name="last_sum",
    )(summed[0], *wide_sums, summed[layers], *narrow_sums)
    other = shift(theirs, 1)

    low, high = jnp.where(core == 0, mine, other), jnp.where(core == 0, other, mine)
    return loss[:, 0], grad_head, jnp.concatenate([low, high], axis=1)


def fits_levels(hidden_states, teacher_logits):
    n = lax.axis_size("vocab")
    rows = hidden_states.shape[0]
    blocks, _, stored, side = teacher_logits.shape
    return (
        n == blocks * GROUP
        and blocks & (blocks - 1) == 0
        and rows * GROUP == side
        and rows % 16 == 0
        and 2 * n <= side
        and 6 * blocks * stored <= side
        and hidden_states.shape[1] % (CORES * 1280) == 0
    )


def on_device(
    hidden_states, head_weight, teacher_logits, block_lists, row_reader, tail_mass, token_weight
):
    plan = levels_plan if fits_levels(hidden_states, teacher_logits) else plain_plan
    return plan(
        hidden_states, head_weight, teacher_logits, block_lists, row_reader, tail_mass, token_weight
    )


def solution(mesh):
    in_specs = (
        P("vocab", None),
        P(None, "vocab"),
        P(None, None, "vocab", None),
        P(),
        P(),
        P(),
        P(),
    )
    out_specs = (P("vocab"), P(None, "vocab"), P("vocab", None))
    return jax.shard_map(
        on_device, mesh=mesh, in_specs=in_specs, out_specs=out_specs, check_vma=False
    )
```

```python
import functools

import jax
import jax.numpy as jnp
from jax import lax
from jax.experimental import pallas as pl
from jax.experimental.pallas import tpu as pltpu
from jax.sharding import PartitionSpec as P


def row_parts(scores, teacher_slab, listed_mask, student_exp, teacher_exp):
    return (
        jnp.sum(student_exp, axis=(2, 3)),
        jnp.sum(teacher_exp, axis=(2, 3)),
        jnp.sum(teacher_exp * scores, axis=(2, 3)),
        jnp.sum(teacher_exp * teacher_slab, axis=(2, 3)),
        jnp.sum(scores, axis=(2, 3)),
        jnp.sum(jnp.where(listed_mask, scores, 0.0), axis=(2, 3)),
    )


def plain_plan(
    hidden_states, head_weight, teacher_logits, block_lists, row_reader, tail_mass, token_weight
):
    blocks, listed_count, stored_rows, block_side = teacher_logits.shape
    slab_width = head_weight.shape[1]
    slab_blocks = slab_width // block_side
    devices = lax.axis_size("vocab")
    rank_self = lax.axis_index("vocab")
    tokens = blocks * block_side
    shard_rows = hidden_states.shape[0]
    gathered = lax.all_gather(hidden_states, "vocab", axis=0, tiled=True)
    logits = jnp.dot(gathered, head_weight, preferred_element_type=jnp.float32)
    owner_dev = block_lists // slab_blocks
    owned_here = owner_dev == rank_self
    within = block_lists - rank_self * slab_blocks
    token_iota = lax.broadcasted_iota(jnp.int32, (1, block_side, block_side), 1)
    token_map = (row_reader[:, None, :] == token_iota).astype(jnp.bfloat16)
    place_iota = lax.broadcasted_iota(jnp.int32, (1, slab_blocks, 1), 1)
    block_iota = lax.broadcasted_iota(jnp.int32, (1, devices * slab_blocks, 1), 1)
    picker = (block_lists[:, None, :] == block_iota).astype(jnp.bfloat16)
    outgoing = jnp.einsum(
        "tnk,tkrc->tnrc", picker, teacher_logits, preferred_element_type=jnp.float32
    ).astype(jnp.bfloat16)
    incoming = lax.all_to_all(outgoing, "vocab", split_axis=1, concat_axis=2, tiled=True)
    teacher_slab = jnp.einsum(
        "tpj,tbjc->tpbc", token_map, incoming, preferred_element_type=jnp.float32
    )
    listed = jnp.sum(
        ((within[:, None, :] == place_iota) & owned_here[:, None, :]).astype(jnp.int32), axis=2
    )
    scores = logits.reshape(blocks, block_side, slab_blocks, block_side)
    listed_mask = (listed > 0)[:, None, :, None]
    local_smax = jnp.max(scores, axis=(2, 3))
    local_tmax = jnp.max(jnp.where(listed_mask, teacher_slab, -1e30), axis=(2, 3))
    student_max, teacher_max = lax.pmax((local_smax, local_tmax), "vocab")
    student_exp = jnp.exp(scores - student_max[:, :, None, None])
    teacher_exp = jnp.exp(
        jnp.where(listed_mask, teacher_slab - teacher_max[:, :, None, None], -jnp.inf)
    )
    parts = row_parts(scores, teacher_slab, listed_mask, student_exp, teacher_exp)
    student_sum, teacher_sum, cross_sum, self_sum, logit_total, listed_total = lax.psum(
        (parts[0], parts[1], parts[2], parts[3], parts[4], parts[5]), "vocab"
    )
    tail_share = tail_mass.reshape(blocks, block_side)
    unlisted = float(devices * slab_width - block_side * listed_count)
    kept_mass = 1.0 - tail_share
    log_norm = student_max + jnp.log(student_sum)
    row_loss = (
        kept_mass * (jnp.log(kept_mass) - teacher_max - jnp.log(teacher_sum))
        + kept_mass * self_sum / teacher_sum
        + tail_share * jnp.log(tail_share / unlisted)
        - kept_mass * cross_sum / teacher_sum
        - tail_share / unlisted * (logit_total - listed_total)
        + log_norm
    )
    token_loss = lax.dynamic_slice_in_dim(
        row_loss.reshape(tokens), rank_self * shard_rows, shard_rows, 0
    )
    student_prob = student_exp / student_sum[:, :, None, None]
    teacher_prob = jnp.where(
        listed_mask,
        (kept_mass / teacher_sum)[:, :, None, None] * teacher_exp,
        (tail_share / unlisted)[:, :, None, None],
    )
    weight = token_weight.reshape(blocks, block_side)[:, :, None, None]
    grad_logits = (
        (weight * (student_prob - teacher_prob)).astype(jnp.bfloat16).reshape(tokens, slab_width)
    )
    grad_head = lax.dot_general(
        gathered, grad_logits, (((0,), (0,)), ((), ())), preferred_element_type=jnp.float32
    ).astype(jnp.bfloat16)
    grad_hidden = lax.psum_scatter(
        lax.dot_general(
            grad_logits, head_weight, (((1,), (1,)), ((), ())), preferred_element_type=jnp.float32
        ),
        "vocab",
        scatter_dimension=0,
        tiled=True,
    ).astype(jnp.bfloat16)
    return (token_loss, grad_head, grad_hidden)


CORES = 2
CHIPS = 4
GROUP = CORES * CHIPS
SLOTS = 4
LIGHT = pl.CostEstimate(flops=1, bytes_accessed=1, transcendentals=0)
SMALL_VMEM = 16 * 1024 * 1024
LOGITS_VMEM = 40 * 1024 * 1024
PARTIAL_VMEM = 42 * 1024 * 1024
LARGE_VMEM = 48 * 1024 * 1024
STAT_ROWS = 16


def kernel_params(limit=SMALL_VMEM):
    return pltpu.CompilerParams(vmem_limit_bytes=limit)


def vmem_spec():
    return pl.BlockSpec(memory_space=pltpu.VMEM)


def hbm_spec():
    return pl.BlockSpec(memory_space=pltpu.HBM)


def smem_spec():
    return pl.BlockSpec(memory_space=pltpu.SMEM)


def shift(x, distance):
    n = lax.axis_size("vocab")
    return lax.ppermute(x, "vocab", [(i, i ^ distance) for i in range(n)])


def token_places(place, rows, side):
    row = lax.broadcasted_iota(jnp.int32, (side, 1), 0)
    group = row // rows
    chip = (group % CHIPS) ^ place[1]
    core = (group // CHIPS) ^ place[0]
    return (chip * CORES + core) * rows + row % rows


def pick_column(match, values):
    return jnp.sum(jnp.where(match, values, 0.0), axis=1, keepdims=True)


def teacher_kernel(
    unlisted, rows, pos_ref, place_ref, blocks_ref, stat_ref, reader_ref, tail_ref, prob_ref, entropy_ref
):
    layers, slots, side, _ = blocks_ref.shape
    pos = [pos_ref[i] for i in range(3)]
    lane = lax.broadcasted_iota(jnp.int32, (1, side), 1)
    where_token = token_places(pos, rows, side)
    for k in range(layers):
        block = pos[2] ^ k
        match = reader_ref[block] == where_token
        onehot = jnp.where(match, 1.0, 0.0).astype(jnp.bfloat16)
        normaliser = pick_column(match, stat_ref[0, block])
        tail = pick_column(lane == where_token, tail_ref[block])
        kept = 1.0 - tail
        rest = tail / unlisted
        span = pl.ds(k * side, side)
        prob_ref[span, :] = jnp.broadcast_to(rest, (side, prob_ref.shape[1]))
        for s in range(slots):
            place = place_ref[block, s]
            values = jnp.dot(onehot, blocks_ref[block, s], preferred_element_type=jnp.float32)
            prob = kept * jnp.exp(values - normaliser)

            @pl.when(place >= 0)
            def _():
                prob_ref[span, pl.ds(pl.multiple_of(place * side, side), side)] = prob

        if k == 0:
            mean = pick_column(match, stat_ref[1, block])
            entropy = kept * (jnp.log(kept) - normaliser + mean) + tail * jnp.log(rest)
            entropy_ref[...] = jnp.broadcast_to(entropy[:rows], entropy_ref.shape)


def assemble(pieces, rows, out_ref):
    per_core = len(pieces) // CORES
    layers = pieces[0].shape[0] // rows
    for core in range(CORES):
        mine = pieces[core * per_core : (core + 1) * per_core]
        for k in range(layers):
            span = pl.ds(k * rows, rows)
            for j, piece in enumerate(mine[:CHIPS]):
                at = pl.ds((k * GROUP + core * CHIPS + j) * rows, rows)
                columns = slice(0, piece.shape[1])
                out_ref[at, columns] = piece[span, :]
            if per_core > CHIPS:
                piece = mine[CHIPS]
                columns = slice(out_ref.shape[1] - piece.shape[1], out_ref.shape[1])
                out_ref[at, columns] = piece[span, :]


def logits_kernel(rows, *refs):
    pieces, refs = refs[:-8], refs[-8:]
    w_ref, prob_ref, logits_ref, stat_ref, hidden, weight, sems, cross_ref = refs
    depth, width = w_ref.shape[0], prob_ref.shape[1]
    parts = [slice(0, depth // 4), slice(depth // 4, depth)]
    tiles = w_ref.shape[1] // width
    step = pl.program_id(0)

    def copy(i):
        span = pl.ds(parts[i].start, parts[i].stop - parts[i].start)
        return pltpu.make_async_copy(w_ref.at[span, :], weight.at[span, :], sems.at[i])

    @pl.when(step == 0)
    def _():
        copy(0).start()
        copy(1).start()
        assemble(pieces, rows, hidden)
        copy(0).wait()

    @pl.when(step == tiles)
    def _():
        copy(1).wait()

    @pl.when(step < tiles)
    def _():
        span = pl.ds(pl.multiple_of(step * width, width), width)
        logits_ref[:, span] = jnp.dot(
            hidden[:, parts[0]], weight[parts[0], span], preferred_element_type=jnp.float32
        )

    @pl.when(step >= tiles)
    def _():
        span = pl.ds(pl.multiple_of((step - tiles) * width, width), width)
        total = logits_ref[:, span] + jnp.dot(
            hidden[:, parts[1]], weight[parts[1], span], preferred_element_type=jnp.float32
        )
        logits_ref[:, span] = total
        product = total * prob_ref[...]
        folded = product[:, :128]
        for i in range(1, width // 128):
            folded = folded + product[:, i * 128 : (i + 1) * 128]
        cross_ref[...] = jnp.where(step == tiles, 0.0, cross_ref[...]) + folded

    @pl.when(step == 2 * tiles - 1)
    def _():
        logits = logits_ref[...]
        top = jnp.max(logits, axis=1, keepdims=True)
        norm = top + jnp.log(jnp.sum(jnp.exp(logits - top), axis=1, keepdims=True))
        cross = jnp.sum(cross_ref[...], axis=1, keepdims=True)
        lane = lax.broadcasted_iota(jnp.int32, (1, 128), 1)
        both = jnp.where(lane == 0, norm, jnp.where(lane == 1, cross, 0.0)).T
        tokens = logits.shape[0]
        packed = [both[i : i + 1, t : t + 128] for i in range(2) for t in range(0, tokens, 128)]
        stat_ref[...] = jnp.broadcast_to(jnp.concatenate(packed, axis=0)[None], stat_ref.shape)


def grad_kernel(
    rows, pos_ref, stat_ref, logits_ref, prob_ref, weight_ref, entropy_ref, grad_ref, loss_ref
):
    tokens = logits_ref.shape[0]
    devices = tokens // rows
    layers, _, side = weight_ref.shape
    layer_bits = (devices // GROUP).bit_length() - 1
    pos = [pos_ref[i] for i in range(3)]
    rank = pos_ref[3]
    lane = lax.broadcasted_iota(jnp.int32, (1, 128), 1)
    per_stat = stat_ref.shape[1] // 2
    norms, crosses = [
        jnp.concatenate([stat_ref[:, i * per_stat + t, :] for t in range(per_stat)], axis=1) for i in range(2)
    ]
    stat = jnp.concatenate(
        [norms, crosses, jnp.zeros((128 - 2 * devices, tokens), jnp.float32)], axis=0
    ).T
    pairs = [(0, 2), (1, 0), (2, 1)] + [(3 + i, 3 + i) for i in range(layer_bits)]
    for index_bit, block_bit in pairs:
        halves = stat.reshape(devices >> (block_bit + 1), 2, rows << block_bit, 128)
        swapped = jnp.stack([halves[:, 1], halves[:, 0]], axis=1).reshape(tokens, 128)
        stat = jnp.where(((lane ^ rank) >> index_bit) & 1 == 1, swapped, stat)
    is_norm = lane < devices
    is_cross = (lane >= devices) & (lane < 2 * devices)
    top = jnp.max(jnp.where(is_norm, stat, -jnp.inf), axis=1, keepdims=True)
    total = jnp.sum(jnp.where(is_norm, jnp.exp(stat - top), 0.0), axis=1, keepdims=True)
    log_norm = top + jnp.log(total)
    cross = jnp.sum(jnp.where(is_cross, stat, 0.0), axis=1, keepdims=True)
    loss_ref[...] = entropy_ref[...] - cross[:rows] + log_norm[:rows]
    where_token = token_places(pos, rows, side)
    for k in range(layers):
        span = pl.ds(k * side, side)
        weight = pick_column(lane == where_token, weight_ref[pos[2] ^ k])
        student = jnp.exp(logits_ref[span, :] - log_norm[k * side : (k + 1) * side])
        grad_ref[span, :] = (weight * (student - prob_ref[span, :])).astype(grad_ref.dtype)


def partial_kernel(rows, core_ref, grad_ref, sib_ref, w_ref, sib_w_ref, *refs):
    outs, swapped = refs[:-1], refs[-1]
    wide_outs, narrow_outs = outs[:CHIPS], outs[CHIPS:]
    layers = len(narrow_outs)
    half = CHIPS * rows
    step = pl.program_id(0)

    @pl.when(step == 0)
    def _():
        for k in range(layers):
            for core in range(CORES):
                swapped[pl.ds((k * CORES + core) * half, half), :] = sib_ref[
                    pl.ds((k * CORES + 1 - core) * half, half), :
                ]

    contract = (((1,), (1,)), ((), ()))
    total = lax.dot_general(
        grad_ref[...], w_ref[...], contract, preferred_element_type=jnp.float32
    ) + lax.dot_general(swapped[...], sib_w_ref[...], contract, preferred_element_type=jnp.float32)

    def store(outs, by_layer, columns, source):
        for k in range(layers):
            for core in range(CORES):
                for j in range(CHIPS):
                    start = (k * GROUP + core * CHIPS + j) * rows
                    out, i = (outs[k], j) if by_layer else (outs[j], k)
                    out[i, core, :, columns] = total[start : start + rows, source].astype(out.dtype)

    tile = w_ref.shape[0]
    wide = wide_outs[0].shape[-1]
    whole_steps, rest = wide // tile, wide % tile
    everything = slice(0, tile)

    @pl.when(step < whole_steps)
    def _():
        store(wide_outs, False, pl.ds(pl.multiple_of(step * tile, tile), tile), everything)

    if rest:

        @pl.when(step == whole_steps)
        def _():
            store(wide_outs, False, slice(whole_steps * tile, wide), slice(0, rest))
            store(narrow_outs, True, slice(0, tile - rest), slice(rest, tile))

    first = whole_steps + 1 if rest else whole_steps
    offset = tile - rest if rest else 0

    @pl.when(step >= first)
    def _():
        columns = pl.ds(pl.multiple_of(offset + (step - first) * tile, 128), tile)
        store(narrow_outs, True, columns, everything)


def head_kernel(rows, *refs):
    pieces, (grad_ref, out_ref, hidden) = refs[:-3], refs[-3:]
    per_core = CHIPS + 1
    late = pl.program_id(0) >= pl.num_programs(0) // 2
    for i in range(2):

        @pl.when(late == (i == 1))
        def _():
            mine = [pieces[c * per_core : (c + 1) * per_core] for c in range(CORES)]
            assemble([p for some in mine for p in (*some[: CHIPS - 1], some[CHIPS - 1 + i])], rows, hidden)

    out_ref[...] = lax.dot_general(
        hidden[...], grad_ref[...], (((0,), (0,)), ((), ())), preferred_element_type=jnp.float32
    ).astype(out_ref.dtype)


def sum_of(parts, index=...):
    total = parts[0][index]
    for part in parts[1:]:
        total = total + part[index].astype(jnp.float32)
    return total


def first_sum_kernel(layers, *refs):
    wide, narrow, outs = refs[:CHIPS], refs[CHIPS : CHIPS + layers], refs[CHIPS + layers :]
    for k, out in enumerate(outs[:layers]):
        out[...] = sum_of(wide, k).astype(out.dtype)
    for j, out in enumerate(outs[layers:]):
        out[...] = sum_of(narrow, j).astype(out.dtype)


def last_sum_kernel(layers, *refs):
    wide, narrow, (mine, theirs) = refs[:layers], refs[layers:-2], refs[-2:]
    split = wide[0].shape[-1]
    for parts, columns in ((wide, slice(0, split)), (narrow, slice(split, mine.shape[1]))):
        total = sum_of(parts)
        mine[:, columns] = total[0].astype(mine.dtype)
        theirs[:, columns] = total[1].astype(theirs.dtype)


def pack_kernel(code_ref, x_ref, out_ref):
    blocks, count, side = x_ref.shape
    devices, size, _ = out_ref.shape
    slot_rows = (size - STAT_ROWS) // blocks
    stored = slot_rows // SLOTS
    target = lax.broadcasted_iota(jnp.int32, (devices * slot_rows, 1), 0)
    row = lax.broadcasted_iota(jnp.int32, (count, 1), 0) % stored
    lane = lax.broadcasted_iota(jnp.int32, (1, side), 1)
    stat = jnp.zeros((1, side), jnp.float32)
    for t in range(blocks):
        onehot = jnp.where(code_ref[t] == target, 1.0, 0.0).astype(x_ref.dtype)
        packed = jnp.dot(onehot, x_ref[t], preferred_element_type=jnp.float32).astype(out_ref.dtype)
        for device in range(devices):
            out_ref[device, pl.ds(t * slot_rows, slot_rows), :] = packed[
                device * slot_rows : (device + 1) * slot_rows
            ]
        values = x_ref[t].astype(jnp.float32)
        row_top = jnp.max(values, axis=1, keepdims=True)
        tops = [jnp.max(jnp.where(row == r, row_top, -jnp.inf), axis=0, keepdims=True) for r in range(stored)]
        top = jnp.zeros_like(row_top)
        for r in range(stored):
            top = jnp.where(row == r, tops[r], top)
        powers = jnp.exp(values - top)
        sums = jnp.sum(powers, axis=1, keepdims=True)
        weighted = jnp.sum(powers * values, axis=1, keepdims=True)
        for r in range(stored):
            total = jnp.sum(jnp.where(row == r, sums, 0.0), axis=0, keepdims=True)
            mean = jnp.sum(jnp.where(row == r, weighted, 0.0), axis=0, keepdims=True) / total
            stat = jnp.where(lane == t * stored + r, tops[r] + jnp.log(total), stat)
            stat = jnp.where(lane == (blocks + t) * stored + r, mean, stat)
    high = stat.astype(jnp.bfloat16).astype(jnp.float32)
    middle = (stat - high).astype(jnp.bfloat16).astype(jnp.float32)
    low = stat - high - middle
    parts = jnp.concatenate([high, middle, low, jnp.zeros((STAT_ROWS - 3, side), jnp.float32)], axis=0)
    parts = parts.astype(out_ref.dtype)
    for device in range(devices):
        out_ref[device, pl.ds(size - STAT_ROWS, STAT_ROWS), :] = parts


def pack_teacher(teacher_logits, block_lists, places):
    blocks, listed_count, stored, side = teacher_logits.shape
    n = lax.axis_size("vocab")
    rank = lax.axis_index("vocab")
    owner = block_lists // places
    earlier = jnp.tril(jnp.ones((listed_count, listed_count), jnp.bool_), -1)
    slot = jnp.sum((owner[:, :, None] == owner[:, None, :]) & earlier, axis=2, dtype=jnp.int32)
    code = owner * SLOTS + slot
    rows_code = (code[:, :, None] * stored + jnp.arange(stored, dtype=jnp.int32)).reshape(blocks, 1, -1)
    payload = pl.pallas_call(
        pack_kernel,
        in_specs=[vmem_spec()] * 2,
        out_specs=vmem_spec(),
        out_shape=jax.ShapeDtypeStruct(
            (n, blocks * SLOTS * stored + STAT_ROWS, side), teacher_logits.dtype
        ),
        compiler_params=kernel_params(),
        cost_estimate=LIGHT,
        name="pack_teacher",
    )(rows_code, teacher_logits.reshape(blocks, listed_count * stored, side))
    mine = code[:, None, :] == rank * SLOTS + jnp.arange(SLOTS, dtype=jnp.int32)[None, :, None]
    place = jnp.sum(jnp.where(mine, (block_lists % places + 1)[:, None, :], 0), axis=2) - 1
    return payload, place.astype(jnp.int32)


def unpack_teacher(arrived, blocks, stored):
    n, _, side = arrived.shape
    arrived_blocks = (
        arrived[:, :-3]
        .reshape(n, blocks, SLOTS, stored, side)
        .transpose(1, 2, 0, 3, 4)
        .reshape(blocks, SLOTS, n * stored, side)
    )
    arrived_stat = (
        arrived[:, -3:, : 2 * blocks * stored]
        .astype(jnp.float32)
        .sum(axis=1)
        .reshape(n, 2, blocks, stored)
        .transpose(1, 2, 0, 3)
        .reshape(2, blocks, 1, n * stored)
    )
    return arrived_blocks, arrived_stat


def levels_plan(
    hidden_states, head_weight, teacher_logits, block_lists, row_reader, tail_mass, token_weight
):
    blocks, listed_count, stored, side = teacher_logits.shape
    rows, depth = hidden_states.shape
    slab = head_weight.shape[1]
    n = lax.axis_size("vocab")
    rank = lax.axis_index("vocab")
    tokens = n * rows
    layers = n // GROUP
    half = depth // CORES
    bf16, f32 = jnp.bfloat16, jnp.float32
    core, chip, layer = rank % CORES, (rank // CORES) % CHIPS, rank // GROUP
    pos = jnp.stack([core, chip, layer, rank]).astype(jnp.int32)
    unlisted = float(n * slab - side * listed_count)

    column = [hidden_states] + [shift(hidden_states, k * GROUP) for k in range(1, layers)]
    column = jnp.concatenate(column, axis=0)
    X, Y = CORES, 2 * CORES
    plane = [column, shift(column, X), shift(column, Y)]
    plane += [shift(plane[1][:, :half], Y), shift(plane[2][:, half:], X)]
    payload, place = pack_teacher(teacher_logits, block_lists, slab // side)
    arrived = lax.all_to_all(
        payload[:, : 3 - STAT_ROWS], "vocab", split_axis=0, concat_axis=0, tiled=True
    )
    arrived_blocks, arrived_stat = unpack_teacher(arrived, blocks, stored)

    prob, entropy = pl.pallas_call(
        lambda *refs: teacher_kernel(unlisted, rows, *refs),
        out_shape=(
            jax.ShapeDtypeStruct((tokens, slab), f32),
            jax.ShapeDtypeStruct((rows, side), f32),
        ),
        in_specs=[smem_spec(), smem_spec()] + [vmem_spec()] * 4,
        out_specs=(vmem_spec(), vmem_spec()),
        compiler_params=kernel_params(),
        cost_estimate=LIGHT,
        name="teacher_prob",
    )(
        pos,
        place,
        arrived_blocks,
        arrived_stat,
        row_reader.reshape(blocks, 1, side),
        tail_mass.reshape(blocks, 1, side),
    )

    sent_w = lax.dynamic_slice(head_weight, ((1 - core) * half, 0), (half, slab))
    plane[-2], plane[-1], prob, sent_w = lax.optimization_barrier((plane[-2], plane[-1], prob, sent_w))
    pieces = plane + [shift(piece, 1) for piece in plane]
    pieces, sent_w = lax.optimization_barrier((pieces, sent_w))
    sib_w = shift(sent_w, 1)

    width = 256 if slab % 256 == 0 else 128
    tiles = slab // width
    whole = lambda t: (0, 0)
    logits, stat = pl.pallas_call(
        functools.partial(logits_kernel, rows),
        grid=(2 * tiles,),
        out_shape=[
            jax.ShapeDtypeStruct((tokens, slab), f32),
            jax.ShapeDtypeStruct((n, 2 * tokens // 128, 128), f32),
        ],
        in_specs=[vmem_spec()] * len(pieces)
        + [hbm_spec(), pl.BlockSpec((tokens, width), lambda t: (0, jnp.maximum(t - tiles, 0)))],
        out_specs=[
            pl.BlockSpec((tokens, slab), whole),
            pl.BlockSpec((n, 2 * tokens // 128, 128), lambda t: (0, 0, 0)),
        ],
        scratch_shapes=[
            pltpu.VMEM((tokens, depth), bf16),
            pltpu.VMEM((depth, slab), bf16),
            pltpu.SemaphoreType.DMA((2,)),
            pltpu.VMEM((tokens, 128), f32),
        ],
        compiler_params=kernel_params(LOGITS_VMEM),
        cost_estimate=LIGHT,
        name="logits",
    )(*pieces, head_weight, prob)
    stat = lax.all_to_all(stat, "vocab", split_axis=0, concat_axis=0, tiled=True)

    grad, loss = pl.pallas_call(
        lambda *refs: grad_kernel(rows, *refs),
        out_shape=(
            jax.ShapeDtypeStruct((tokens, slab), bf16),
            jax.ShapeDtypeStruct((rows, side), f32),
        ),
        in_specs=[smem_spec()] + [vmem_spec()] * 5,
        out_specs=(vmem_spec(), vmem_spec()),
        compiler_params=kernel_params(),
        cost_estimate=LIGHT,
        name="grad_logits",
    )(pos, stat, logits, prob, token_weight.reshape(blocks, 1, side), entropy)
    sib_grad = shift(grad, 1)

    tile = half // 5
    sizes = (half * 7 // 10, half - half * 7 // 10)
    wide_block = pl.BlockSpec((layers, CORES, rows, sizes[0]), lambda t, pos: (0, 0, 0, 0))
    narrow_block = pl.BlockSpec((CHIPS, CORES, rows, sizes[1]), lambda t, pos: (0, 0, 0, 0))
    partial = pl.pallas_call(
        functools.partial(partial_kernel, rows),
        grid_spec=pltpu.PrefetchScalarGridSpec(
            num_scalar_prefetch=1,
            grid=(5,),
            in_specs=[pl.BlockSpec((tokens, slab), lambda t, pos: (0, 0))] * 2
            + [pl.BlockSpec((tile, slab), lambda t, pos: (pos[0] * 5 + t, 0))]
            + [pl.BlockSpec((tile, slab), lambda t, pos: (t, 0))],
            out_specs=[wide_block] * CHIPS + [narrow_block] * layers,
            scratch_shapes=[pltpu.VMEM((tokens, slab), bf16)],
        ),
        out_shape=[
            jax.ShapeDtypeStruct((layers, CORES, rows, sizes[0]), bf16 if j else f32) for j in range(CHIPS)
        ]
        + [jax.ShapeDtypeStruct((CHIPS, CORES, rows, sizes[1]), bf16 if k else f32) for k in range(layers)],
        compiler_params=kernel_params(PARTIAL_VMEM),
        cost_estimate=LIGHT,
        name="grad_hidden_partial",
    )(pos, grad, sib_grad, head_weight, sib_w)
    *partial, late_grad = lax.optimization_barrier((*partial, grad))
    wide_sums = [shift(partial[j], j * CORES) for j in range(1, CHIPS)]
    narrow_sums = [shift(partial[CHIPS + k], k * GROUP) for k in range(1, layers)]

    head_tile = half // 2
    grad_head = pl.pallas_call(
        functools.partial(head_kernel, rows),
        grid=(4,),
        in_specs=[
            pl.BlockSpec(
                (layers * rows, head_tile),
                lambda t, i=i % (CHIPS + 1): (0, (t, jnp.minimum(t, 1), jnp.maximum(t - 2, 0))[max(i - 2, 0)]),
            )
            for i in range(len(pieces))
        ]
        + [pl.BlockSpec((tokens, slab), whole)],
        out_specs=pl.BlockSpec((head_tile, slab), lambda t: (t, 0)),
        out_shape=jax.ShapeDtypeStruct((depth, slab), bf16),
        scratch_shapes=[pltpu.VMEM((tokens, head_tile), bf16)],
        compiler_params=kernel_params(LARGE_VMEM),
        cost_estimate=LIGHT,
        name="grad_head",
    )(*pieces, late_grad)
    wide_sums, narrow_sums, grad_head = lax.optimization_barrier((wide_sums, narrow_sums, grad_head))

    summed = pl.pallas_call(
        functools.partial(first_sum_kernel, layers),
        in_specs=[vmem_spec()] * (CHIPS + layers),
        out_specs=[vmem_spec()] * (CHIPS + layers),
        out_shape=[jax.ShapeDtypeStruct((CORES, rows, sizes[0]), bf16 if k else f32) for k in range(layers)]
        + [jax.ShapeDtypeStruct((CORES, rows, sizes[1]), bf16 if j else f32) for j in range(CHIPS)],
        compiler_params=kernel_params(),
        cost_estimate=LIGHT,
        name="first_sum",
    )(partial[0], *wide_sums, partial[CHIPS], *narrow_sums)
    wide_sums = [shift(summed[k], k * GROUP) for k in range(1, layers)]
    narrow_sums = [shift(summed[layers + j], j * CORES) for j in range(1, CHIPS)]
    mine, theirs = pl.pallas_call(
        functools.partial(last_sum_kernel, layers),
        in_specs=[vmem_spec()] * (CHIPS + layers),
        out_specs=[vmem_spec()] * 2,
        out_shape=[jax.ShapeDtypeStruct((rows, half), bf16)] * 2,
        compiler_params=kernel_params(),
        cost_estimate=LIGHT,
        name="last_sum",
    )(summed[0], *wide_sums, summed[layers], *narrow_sums)
    other = shift(theirs, 1)

    low, high = jnp.where(core == 0, mine, other), jnp.where(core == 0, other, mine)
    return loss[:, 0], grad_head, jnp.concatenate([low, high], axis=1)


def fits_levels(hidden_states, teacher_logits):
    n = lax.axis_size("vocab")
    rows = hidden_states.shape[0]
    blocks, _, stored, side = teacher_logits.shape
    return (
        n == blocks * GROUP
        and blocks & (blocks - 1) == 0
        and rows * GROUP == side
        and rows % 16 == 0
        and 2 * n <= side
        and 6 * blocks * stored <= side
        and hidden_states.shape[1] % (CORES * 1280) == 0
    )


def on_device(
    hidden_states, head_weight, teacher_logits, block_lists, row_reader, tail_mass, token_weight
):
    plan = levels_plan if fits_levels(hidden_states, teacher_logits) else plain_plan
    return plan(
        hidden_states, head_weight, teacher_logits, block_lists, row_reader, tail_mass, token_weight
    )


def solution(mesh):
    in_specs = (
        P("vocab", None),
        P(None, "vocab"),
        P(None, None, "vocab", None),
        P(),
        P(),
        P(),
        P(),
    )
    out_specs = (P("vocab"), P(None, "vocab"), P("vocab", None))
    return jax.shard_map(
        on_device, mesh=mesh, in_specs=in_specs, out_specs=out_specs, check_vma=False
    )
```

```python
import functools

import jax
import jax.numpy as jnp
from jax import lax
from jax.experimental import pallas as pl
from jax.experimental.pallas import tpu as pltpu
from jax.sharding import PartitionSpec as P


def row_parts(scores, teacher_slab, listed_mask, student_exp, teacher_exp):
    return (
        jnp.sum(student_exp, axis=(2, 3)),
        jnp.sum(teacher_exp, axis=(2, 3)),
        jnp.sum(teacher_exp * scores, axis=(2, 3)),
        jnp.sum(teacher_exp * teacher_slab, axis=(2, 3)),
        jnp.sum(scores, axis=(2, 3)),
        jnp.sum(jnp.where(listed_mask, scores, 0.0), axis=(2, 3)),
    )


def plain_plan(
    hidden_states, head_weight, teacher_logits, block_lists, row_reader, tail_mass, token_weight
):
    blocks, listed_count, stored_rows, block_side = teacher_logits.shape
    slab_width = head_weight.shape[1]
    slab_blocks = slab_width // block_side
    devices = lax.axis_size("vocab")
    rank_self = lax.axis_index("vocab")
    tokens = blocks * block_side
    shard_rows = hidden_states.shape[0]
    gathered = lax.all_gather(hidden_states, "vocab", axis=0, tiled=True)
    logits = jnp.dot(gathered, head_weight, preferred_element_type=jnp.float32)
    owner_dev = block_lists // slab_blocks
    owned_here = owner_dev == rank_self
    within = block_lists - rank_self * slab_blocks
    token_iota = lax.broadcasted_iota(jnp.int32, (1, block_side, block_side), 1)
    token_map = (row_reader[:, None, :] == token_iota).astype(jnp.bfloat16)
    place_iota = lax.broadcasted_iota(jnp.int32, (1, slab_blocks, 1), 1)
    block_iota = lax.broadcasted_iota(jnp.int32, (1, devices * slab_blocks, 1), 1)
    picker = (block_lists[:, None, :] == block_iota).astype(jnp.bfloat16)
    outgoing = jnp.einsum(
        "tnk,tkrc->tnrc", picker, teacher_logits, preferred_element_type=jnp.float32
    ).astype(jnp.bfloat16)
    incoming = lax.all_to_all(outgoing, "vocab", split_axis=1, concat_axis=2, tiled=True)
    teacher_slab = jnp.einsum(
        "tpj,tbjc->tpbc", token_map, incoming, preferred_element_type=jnp.float32
    )
    listed = jnp.sum(
        ((within[:, None, :] == place_iota) & owned_here[:, None, :]).astype(jnp.int32), axis=2
    )
    scores = logits.reshape(blocks, block_side, slab_blocks, block_side)
    listed_mask = (listed > 0)[:, None, :, None]
    local_smax = jnp.max(scores, axis=(2, 3))
    local_tmax = jnp.max(jnp.where(listed_mask, teacher_slab, -1e30), axis=(2, 3))
    student_max, teacher_max = lax.pmax((local_smax, local_tmax), "vocab")
    student_exp = jnp.exp(scores - student_max[:, :, None, None])
    teacher_exp = jnp.exp(
        jnp.where(listed_mask, teacher_slab - teacher_max[:, :, None, None], -jnp.inf)
    )
    parts = row_parts(scores, teacher_slab, listed_mask, student_exp, teacher_exp)
    student_sum, teacher_sum, cross_sum, self_sum, logit_total, listed_total = lax.psum(
        (parts[0], parts[1], parts[2], parts[3], parts[4], parts[5]), "vocab"
    )
    tail_share = tail_mass.reshape(blocks, block_side)
    unlisted = float(devices * slab_width - block_side * listed_count)
    kept_mass = 1.0 - tail_share
    log_norm = student_max + jnp.log(student_sum)
    row_loss = (
        kept_mass * (jnp.log(kept_mass) - teacher_max - jnp.log(teacher_sum))
        + kept_mass * self_sum / teacher_sum
        + tail_share * jnp.log(tail_share / unlisted)
        - kept_mass * cross_sum / teacher_sum
        - tail_share / unlisted * (logit_total - listed_total)
        + log_norm
    )
    token_loss = lax.dynamic_slice_in_dim(
        row_loss.reshape(tokens), rank_self * shard_rows, shard_rows, 0
    )
    student_prob = student_exp / student_sum[:, :, None, None]
    teacher_prob = jnp.where(
        listed_mask,
        (kept_mass / teacher_sum)[:, :, None, None] * teacher_exp,
        (tail_share / unlisted)[:, :, None, None],
    )
    weight = token_weight.reshape(blocks, block_side)[:, :, None, None]
    grad_logits = (
        (weight * (student_prob - teacher_prob)).astype(jnp.bfloat16).reshape(tokens, slab_width)
    )
    grad_head = lax.dot_general(
        gathered, grad_logits, (((0,), (0,)), ((), ())), preferred_element_type=jnp.float32
    ).astype(jnp.bfloat16)
    grad_hidden = lax.psum_scatter(
        lax.dot_general(
            grad_logits, head_weight, (((1,), (1,)), ((), ())), preferred_element_type=jnp.float32
        ),
        "vocab",
        scatter_dimension=0,
        tiled=True,
    ).astype(jnp.bfloat16)
    return (token_loss, grad_head, grad_hidden)


CORES = 2
CHIPS = 4
GROUP = CORES * CHIPS
SLOTS = 4
LIGHT = pl.CostEstimate(flops=1, bytes_accessed=1, transcendentals=0)
SMALL_VMEM = 16 * 1024 * 1024
LOGITS_VMEM = 40 * 1024 * 1024
PARTIAL_VMEM = 42 * 1024 * 1024
LARGE_VMEM = 48 * 1024 * 1024
STAT_ROWS = 16


def kernel_params(limit=SMALL_VMEM):
    return pltpu.CompilerParams(vmem_limit_bytes=limit)


def vmem_spec():
    return pl.BlockSpec(memory_space=pltpu.VMEM)


def hbm_spec():
    return pl.BlockSpec(memory_space=pltpu.HBM)


def smem_spec():
    return pl.BlockSpec(memory_space=pltpu.SMEM)


def shift(x, distance):
    n = lax.axis_size("vocab")
    return lax.ppermute(x, "vocab", [(i, i ^ distance) for i in range(n)])


def token_places(place, rows, side):
    row = lax.broadcasted_iota(jnp.int32, (side, 1), 0)
    group = row // rows
    chip = (group % CHIPS) ^ place[1]
    core = (group // CHIPS) ^ place[0]
    return (chip * CORES + core) * rows + row % rows


def pick_column(match, values):
    return jnp.sum(jnp.where(match, values, 0.0), axis=1, keepdims=True)


def teacher_kernel(
    unlisted, rows, pos_ref, place_ref, arrived_ref, reader_ref, tail_ref, prob_ref, entropy_ref
):
    devices, size, side = arrived_ref.shape
    blocks = reader_ref.shape[0]
    stored = side // devices
    per_block = SLOTS * stored
    layers = blocks
    pos = [pos_ref[i] for i in range(3)]
    lane = lax.broadcasted_iota(jnp.int32, (1, side), 1)
    sender_lane = lax.broadcasted_iota(jnp.int32, (1, devices), 1)
    row_lane = lax.broadcasted_iota(jnp.int32, (1, devices * per_block), 1)
    where_token = token_places(pos, rows, side)
    parts = [arrived_ref[:, size - 3 + i, :] for i in range(3)]
    for k in range(layers):
        block = pos[2] ^ k
        stored_row = jnp.sum(jnp.where(reader_ref[block] == where_token, lane, 0), axis=1, keepdims=True)
        sender, row = stored_row // stored, stored_row % stored
        from_sender = jnp.where(sender_lane == sender, 1.0, 0.0).astype(jnp.bfloat16)
        stat = sum(jnp.dot(from_sender, part, preferred_element_type=jnp.float32) for part in parts)
        normaliser = pick_column(lane == block * stored + row, stat)
        tail = pick_column(lane == where_token, tail_ref[block])
        kept = 1.0 - tail
        rest = tail / unlisted
        span = pl.ds(k * side, side)
        prob_ref[span, :] = jnp.broadcast_to(rest, (side, prob_ref.shape[1]))
        all_rows = arrived_ref[:, pl.ds(pl.multiple_of(block * per_block, per_block), per_block), :]
        all_rows = all_rows.reshape(devices * per_block, side)
        for s in range(SLOTS):
            place = place_ref[block, s]
            onehot = jnp.where(row_lane == sender * per_block + s * stored + row, 1.0, 0.0)
            values = jnp.dot(onehot.astype(jnp.bfloat16), all_rows, preferred_element_type=jnp.float32)
            prob = kept * jnp.exp(values - normaliser)

            @pl.when(place >= 0)
            def _():
                prob_ref[span, pl.ds(pl.multiple_of(place * side, side), side)] = prob

        if k == 0:
            mean = pick_column(lane == (blocks + block) * stored + row, stat)
            entropy = kept * (jnp.log(kept) - normaliser + mean) + tail * jnp.log(rest)
            entropy_ref[...] = jnp.broadcast_to(entropy[:rows], entropy_ref.shape)


def assemble(pieces, rows, out_ref):
    per_core = len(pieces) // CORES
    layers = pieces[0].shape[0] // rows
    for core in range(CORES):
        mine = pieces[core * per_core : (core + 1) * per_core]
        for k in range(layers):
            span = pl.ds(k * rows, rows)
            for j, piece in enumerate(mine[:CHIPS]):
                at = pl.ds((k * GROUP + core * CHIPS + j) * rows, rows)
                columns = slice(0, piece.shape[1])
                out_ref[at, columns] = piece[span, :]
            if per_core > CHIPS:
                piece = mine[CHIPS]
                columns = slice(out_ref.shape[1] - piece.shape[1], out_ref.shape[1])
                out_ref[at, columns] = piece[span, :]


def logits_kernel(rows, *refs):
    pieces, refs = refs[:-8], refs[-8:]
    w_ref, prob_ref, logits_ref, stat_ref, hidden, weight, sems, cross_ref = refs
    depth, width = w_ref.shape[0], prob_ref.shape[1]
    parts = [slice(0, depth // 4), slice(depth // 4, depth)]
    tiles = w_ref.shape[1] // width
    step = pl.program_id(0)

    def copy(i):
        span = pl.ds(parts[i].start, parts[i].stop - parts[i].start)
        return pltpu.make_async_copy(w_ref.at[span, :], weight.at[span, :], sems.at[i])

    @pl.when(step == 0)
    def _():
        copy(0).start()
        copy(1).start()
        assemble(pieces, rows, hidden)
        copy(0).wait()

    @pl.when(step == tiles)
    def _():
        copy(1).wait()

    @pl.when(step < tiles)
    def _():
        span = pl.ds(pl.multiple_of(step * width, width), width)
        logits_ref[:, span] = jnp.dot(
            hidden[:, parts[0]], weight[parts[0], span], preferred_element_type=jnp.float32
        )

    @pl.when(step >= tiles)
    def _():
        span = pl.ds(pl.multiple_of((step - tiles) * width, width), width)
        total = logits_ref[:, span] + jnp.dot(
            hidden[:, parts[1]], weight[parts[1], span], preferred_element_type=jnp.float32
        )
        logits_ref[:, span] = total
        product = total * prob_ref[...]
        folded = product[:, :128]
        for i in range(1, width // 128):
            folded = folded + product[:, i * 128 : (i + 1) * 128]
        cross_ref[...] = jnp.where(step == tiles, 0.0, cross_ref[...]) + folded

    @pl.when(step == 2 * tiles - 1)
    def _():
        logits = logits_ref[...]
        top = jnp.max(logits, axis=1, keepdims=True)
        norm = top + jnp.log(jnp.sum(jnp.exp(logits - top), axis=1, keepdims=True))
        cross = jnp.sum(cross_ref[...], axis=1, keepdims=True)
        lane = lax.broadcasted_iota(jnp.int32, (1, 128), 1)
        both = jnp.where(lane == 0, norm, jnp.where(lane == 1, cross, 0.0)).T
        tokens = logits.shape[0]
        packed = [both[i : i + 1, t : t + 128] for i in range(2) for t in range(0, tokens, 128)]
        stat_ref[...] = jnp.broadcast_to(jnp.concatenate(packed, axis=0)[None], stat_ref.shape)


def grad_kernel(
    rows, pos_ref, stat_ref, logits_ref, prob_ref, weight_ref, entropy_ref, grad_ref, loss_ref
):
    tokens = logits_ref.shape[0]
    devices = tokens // rows
    layers, _, side = weight_ref.shape
    layer_bits = (devices // GROUP).bit_length() - 1
    pos = [pos_ref[i] for i in range(3)]
    rank = pos_ref[3]
    lane = lax.broadcasted_iota(jnp.int32, (1, 128), 1)
    per_stat = stat_ref.shape[1] // 2
    norms, crosses = [
        jnp.concatenate([stat_ref[:, i * per_stat + t, :] for t in range(per_stat)], axis=1) for i in range(2)
    ]
    stat = jnp.concatenate(
        [norms, crosses, jnp.zeros((128 - 2 * devices, tokens), jnp.float32)], axis=0
    ).T
    pairs = [(0, 2), (1, 0), (2, 1)] + [(3 + i, 3 + i) for i in range(layer_bits)]
    for index_bit, block_bit in pairs:
        halves = stat.reshape(devices >> (block_bit + 1), 2, rows << block_bit, 128)
        swapped = jnp.stack([halves[:, 1], halves[:, 0]], axis=1).reshape(tokens, 128)
        stat = jnp.where(((lane ^ rank) >> index_bit) & 1 == 1, swapped, stat)
    is_norm = lane < devices
    is_cross = (lane >= devices) & (lane < 2 * devices)
    top = jnp.max(jnp.where(is_norm, stat, -jnp.inf), axis=1, keepdims=True)
    total = jnp.sum(jnp.where(is_norm, jnp.exp(stat - top), 0.0), axis=1, keepdims=True)
    log_norm = top + jnp.log(total)
    cross = jnp.sum(jnp.where(is_cross, stat, 0.0), axis=1, keepdims=True)
    loss_ref[...] = entropy_ref[...] - cross[:rows] + log_norm[:rows]
    where_token = token_places(pos, rows, side)
    for k in range(layers):
        span = pl.ds(k * side, side)
        weight = pick_column(lane == where_token, weight_ref[pos[2] ^ k])
        student = jnp.exp(logits_ref[span, :] - log_norm[k * side : (k + 1) * side])
        grad_ref[span, :] = (weight * (student - prob_ref[span, :])).astype(grad_ref.dtype)


def partial_kernel(rows, core_ref, grad_ref, sib_ref, w_ref, sib_w_ref, *refs):
    outs, swapped = refs[:-1], refs[-1]
    wide_outs, narrow_outs = outs[:CHIPS], outs[CHIPS:]
    layers = len(narrow_outs)
    half = CHIPS * rows
    step = pl.program_id(0)

    @pl.when(step == 0)
    def _():
        for k in range(layers):
            for core in range(CORES):
                swapped[pl.ds((k * CORES + core) * half, half), :] = sib_ref[
                    pl.ds((k * CORES + 1 - core) * half, half), :
                ]

    contract = (((1,), (1,)), ((), ()))
    total = lax.dot_general(
        grad_ref[...], w_ref[...], contract, preferred_element_type=jnp.float32
    ) + lax.dot_general(swapped[...], sib_w_ref[...], contract, preferred_element_type=jnp.float32)

    def store(outs, by_layer, columns, source):
        for k in range(layers):
            for core in range(CORES):
                for j in range(CHIPS):
                    start = (k * GROUP + core * CHIPS + j) * rows
                    out, i = (outs[k], j) if by_layer else (outs[j], k)
                    out[i, core, :, columns] = total[start : start + rows, source].astype(out.dtype)

    tile = w_ref.shape[0]
    wide = wide_outs[0].shape[-1]
    whole_steps, rest = wide // tile, wide % tile
    everything = slice(0, tile)

    @pl.when(step < whole_steps)
    def _():
        store(wide_outs, False, pl.ds(pl.multiple_of(step * tile, tile), tile), everything)

    if rest:

        @pl.when(step == whole_steps)
        def _():
            store(wide_outs, False, slice(whole_steps * tile, wide), slice(0, rest))
            store(narrow_outs, True, slice(0, tile - rest), slice(rest, tile))

    first = whole_steps + 1 if rest else whole_steps
    offset = tile - rest if rest else 0

    @pl.when(step >= first)
    def _():
        columns = pl.ds(pl.multiple_of(offset + (step - first) * tile, 128), tile)
        store(narrow_outs, True, columns, everything)


def head_kernel(rows, *refs):
    pieces, (grad_ref, out_ref, hidden) = refs[:-3], refs[-3:]
    per_core = CHIPS + 1
    late = pl.program_id(0) >= pl.num_programs(0) // 2
    for i in range(2):

        @pl.when(late == (i == 1))
        def _():
            mine = [pieces[c * per_core : (c + 1) * per_core] for c in range(CORES)]
            assemble([p for some in mine for p in (*some[: CHIPS - 1], some[CHIPS - 1 + i])], rows, hidden)

    out_ref[...] = lax.dot_general(
        hidden[...], grad_ref[...], (((0,), (0,)), ((), ())), preferred_element_type=jnp.float32
    ).astype(out_ref.dtype)


def sum_of(parts, index=...):
    total = parts[0][index]
    for part in parts[1:]:
        total = total + part[index].astype(jnp.float32)
    return total


def first_sum_kernel(layers, *refs):
    wide, narrow, outs = refs[:CHIPS], refs[CHIPS : CHIPS + layers], refs[CHIPS + layers :]
    for k, out in enumerate(outs[:layers]):
        out[...] = sum_of(wide, k).astype(out.dtype)
    for j, out in enumerate(outs[layers:]):
        out[...] = sum_of(narrow, j).astype(out.dtype)


def last_sum_kernel(layers, *refs):
    wide, narrow, (mine, theirs) = refs[:layers], refs[layers:-2], refs[-2:]
    split = wide[0].shape[-1]
    for parts, columns in ((wide, slice(0, split)), (narrow, slice(split, mine.shape[1]))):
        total = sum_of(parts)
        mine[:, columns] = total[0].astype(mine.dtype)
        theirs[:, columns] = total[1].astype(theirs.dtype)


def pack_kernel(code_ref, x_ref, out_ref):
    blocks, count, side = x_ref.shape
    devices, size, _ = out_ref.shape
    slot_rows = (size - STAT_ROWS) // blocks
    stored = slot_rows // SLOTS
    target = lax.broadcasted_iota(jnp.int32, (devices * slot_rows, 1), 0)
    row = lax.broadcasted_iota(jnp.int32, (count, 1), 0) % stored
    lane = lax.broadcasted_iota(jnp.int32, (1, side), 1)
    stat = jnp.zeros((1, side), jnp.float32)
    for t in range(blocks):
        onehot = jnp.where(code_ref[t] == target, 1.0, 0.0).astype(x_ref.dtype)
        packed = jnp.dot(onehot, x_ref[t], preferred_element_type=jnp.float32).astype(out_ref.dtype)
        for device in range(devices):
            out_ref[device, pl.ds(t * slot_rows, slot_rows), :] = packed[
                device * slot_rows : (device + 1) * slot_rows
            ]
        values = x_ref[t].astype(jnp.float32)
        row_top = jnp.max(values, axis=1, keepdims=True)
        tops = [jnp.max(jnp.where(row == r, row_top, -jnp.inf), axis=0, keepdims=True) for r in range(stored)]
        top = jnp.zeros_like(row_top)
        for r in range(stored):
            top = jnp.where(row == r, tops[r], top)
        powers = jnp.exp(values - top)
        sums = jnp.sum(powers, axis=1, keepdims=True)
        weighted = jnp.sum(powers * values, axis=1, keepdims=True)
        for r in range(stored):
            total = jnp.sum(jnp.where(row == r, sums, 0.0), axis=0, keepdims=True)
            mean = jnp.sum(jnp.where(row == r, weighted, 0.0), axis=0, keepdims=True) / total
            stat = jnp.where(lane == t * stored + r, tops[r] + jnp.log(total), stat)
            stat = jnp.where(lane == (blocks + t) * stored + r, mean, stat)
    high = stat.astype(jnp.bfloat16).astype(jnp.float32)
    middle = (stat - high).astype(jnp.bfloat16).astype(jnp.float32)
    low = stat - high - middle
    parts = jnp.concatenate([high, middle, low, jnp.zeros((STAT_ROWS - 3, side), jnp.float32)], axis=0)
    parts = parts.astype(out_ref.dtype)
    for device in range(devices):
        out_ref[device, pl.ds(size - STAT_ROWS, STAT_ROWS), :] = parts


def pack_teacher(teacher_logits, block_lists, places):
    blocks, listed_count, stored, side = teacher_logits.shape
    n = lax.axis_size("vocab")
    rank = lax.axis_index("vocab")
    owner = block_lists // places
    earlier = jnp.tril(jnp.ones((listed_count, listed_count), jnp.bool_), -1)
    slot = jnp.sum((owner[:, :, None] == owner[:, None, :]) & earlier, axis=2, dtype=jnp.int32)
    code = owner * SLOTS + slot
    rows_code = (code[:, :, None] * stored + jnp.arange(stored, dtype=jnp.int32)).reshape(blocks, 1, -1)
    payload = pl.pallas_call(
        pack_kernel,
        in_specs=[vmem_spec()] * 2,
        out_specs=vmem_spec(),
        out_shape=jax.ShapeDtypeStruct(
            (n, blocks * SLOTS * stored + STAT_ROWS, side), teacher_logits.dtype
        ),
        compiler_params=kernel_params(),
        cost_estimate=LIGHT,
        name="pack_teacher",
    )(rows_code, teacher_logits.reshape(blocks, listed_count * stored, side))
    mine = code[:, None, :] == rank * SLOTS + jnp.arange(SLOTS, dtype=jnp.int32)[None, :, None]
    place = jnp.sum(jnp.where(mine, (block_lists % places + 1)[:, None, :], 0), axis=2) - 1
    return payload, place.astype(jnp.int32)


def levels_plan(
    hidden_states, head_weight, teacher_logits, block_lists, row_reader, tail_mass, token_weight
):
    blocks, listed_count, stored, side = teacher_logits.shape
    rows, depth = hidden_states.shape
    slab = head_weight.shape[1]
    n = lax.axis_size("vocab")
    rank = lax.axis_index("vocab")
    tokens = n * rows
    layers = n // GROUP
    half = depth // CORES
    bf16, f32 = jnp.bfloat16, jnp.float32
    core, chip, layer = rank % CORES, (rank // CORES) % CHIPS, rank // GROUP
    pos = jnp.stack([core, chip, layer, rank]).astype(jnp.int32)
    unlisted = float(n * slab - side * listed_count)

    column = [hidden_states] + [shift(hidden_states, k * GROUP) for k in range(1, layers)]
    column = jnp.concatenate(column, axis=0)
    X, Y = CORES, 2 * CORES
    plane = [column, shift(column, X), shift(column, Y)]
    plane += [shift(plane[1][:, :half], Y), shift(plane[2][:, half:], X)]
    payload, place = pack_teacher(teacher_logits, block_lists, slab // side)
    arrived = lax.all_to_all(
        payload[:, : 3 - STAT_ROWS], "vocab", split_axis=0, concat_axis=0, tiled=True
    )

    prob, entropy = pl.pallas_call(
        lambda *refs: teacher_kernel(unlisted, rows, *refs),
        out_shape=(
            jax.ShapeDtypeStruct((tokens, slab), f32),
            jax.ShapeDtypeStruct((rows, side), f32),
        ),
        in_specs=[smem_spec(), smem_spec()] + [vmem_spec()] * 3,
        out_specs=(vmem_spec(), vmem_spec()),
        compiler_params=kernel_params(),
        cost_estimate=LIGHT,
        name="teacher_prob",
    )(
        pos,
        place,
        arrived,
        row_reader.reshape(blocks, 1, side),
        tail_mass.reshape(blocks, 1, side),
    )

    sent_w = lax.dynamic_slice(head_weight, ((1 - core) * half, 0), (half, slab))
    plane[-2], plane[-1], prob, sent_w = lax.optimization_barrier((plane[-2], plane[-1], prob, sent_w))
    pieces = plane + [shift(piece, 1) for piece in plane]
    pieces, sent_w = lax.optimization_barrier((pieces, sent_w))
    sib_w = shift(sent_w, 1)

    width = 256 if slab % 256 == 0 else 128
    tiles = slab // width
    whole = lambda t: (0, 0)
    logits, stat = pl.pallas_call(
        functools.partial(logits_kernel, rows),
        grid=(2 * tiles,),
        out_shape=[
            jax.ShapeDtypeStruct((tokens, slab), f32),
            jax.ShapeDtypeStruct((n, 2 * tokens // 128, 128), f32),
        ],
        in_specs=[vmem_spec()] * len(pieces)
        + [hbm_spec(), pl.BlockSpec((tokens, width), lambda t: (0, jnp.maximum(t - tiles, 0)))],
        out_specs=[
            pl.BlockSpec((tokens, slab), whole),
            pl.BlockSpec((n, 2 * tokens // 128, 128), lambda t: (0, 0, 0)),
        ],
        scratch_shapes=[
            pltpu.VMEM((tokens, depth), bf16),
            pltpu.VMEM((depth, slab), bf16),
            pltpu.SemaphoreType.DMA((2,)),
            pltpu.VMEM((tokens, 128), f32),
        ],
        compiler_params=kernel_params(LOGITS_VMEM),
        cost_estimate=LIGHT,
        name="logits",
    )(*pieces, head_weight, prob)
    stat = lax.all_to_all(stat, "vocab", split_axis=0, concat_axis=0, tiled=True)

    grad, loss = pl.pallas_call(
        lambda *refs: grad_kernel(rows, *refs),
        out_shape=(
            jax.ShapeDtypeStruct((tokens, slab), bf16),
            jax.ShapeDtypeStruct((rows, side), f32),
        ),
        in_specs=[smem_spec()] + [vmem_spec()] * 5,
        out_specs=(vmem_spec(), vmem_spec()),
        compiler_params=kernel_params(),
        cost_estimate=LIGHT,
        name="grad_logits",
    )(pos, stat, logits, prob, token_weight.reshape(blocks, 1, side), entropy)
    sib_grad = shift(grad, 1)

    tile = half // 5
    sizes = (half * 7 // 10, half - half * 7 // 10)
    wide_block = pl.BlockSpec((layers, CORES, rows, sizes[0]), lambda t, pos: (0, 0, 0, 0))
    narrow_block = pl.BlockSpec((CHIPS, CORES, rows, sizes[1]), lambda t, pos: (0, 0, 0, 0))
    partial = pl.pallas_call(
        functools.partial(partial_kernel, rows),
        grid_spec=pltpu.PrefetchScalarGridSpec(
            num_scalar_prefetch=1,
            grid=(5,),
            in_specs=[pl.BlockSpec((tokens, slab), lambda t, pos: (0, 0))] * 2
            + [pl.BlockSpec((tile, slab), lambda t, pos: (pos[0] * 5 + t, 0))]
            + [pl.BlockSpec((tile, slab), lambda t, pos: (t, 0))],
            out_specs=[wide_block] * CHIPS + [narrow_block] * layers,
            scratch_shapes=[pltpu.VMEM((tokens, slab), bf16)],
        ),
        out_shape=[
            jax.ShapeDtypeStruct((layers, CORES, rows, sizes[0]), bf16 if j else f32) for j in range(CHIPS)
        ]
        + [jax.ShapeDtypeStruct((CHIPS, CORES, rows, sizes[1]), bf16 if k else f32) for k in range(layers)],
        compiler_params=kernel_params(PARTIAL_VMEM),
        cost_estimate=LIGHT,
        name="grad_hidden_partial",
    )(pos, grad, sib_grad, head_weight, sib_w)
    *partial, late_grad = lax.optimization_barrier((*partial, grad))
    wide_sums = [shift(partial[j], j * CORES) for j in range(1, CHIPS)]
    narrow_sums = [shift(partial[CHIPS + k], k * GROUP) for k in range(1, layers)]

    head_tile = half // 2
    grad_head = pl.pallas_call(
        functools.partial(head_kernel, rows),
        grid=(4,),
        in_specs=[
            pl.BlockSpec(
                (layers * rows, head_tile),
                lambda t, i=i % (CHIPS + 1): (0, (t, jnp.minimum(t, 1), jnp.maximum(t - 2, 0))[max(i - 2, 0)]),
            )
            for i in range(len(pieces))
        ]
        + [pl.BlockSpec((tokens, slab), whole)],
        out_specs=pl.BlockSpec((head_tile, slab), lambda t: (t, 0)),
        out_shape=jax.ShapeDtypeStruct((depth, slab), bf16),
        scratch_shapes=[pltpu.VMEM((tokens, head_tile), bf16)],
        compiler_params=kernel_params(LARGE_VMEM),
        cost_estimate=LIGHT,
        name="grad_head",
    )(*pieces, late_grad)
    wide_sums, narrow_sums, grad_head = lax.optimization_barrier((wide_sums, narrow_sums, grad_head))

    summed = pl.pallas_call(
        functools.partial(first_sum_kernel, layers),
        in_specs=[vmem_spec()] * (CHIPS + layers),
        out_specs=[vmem_spec()] * (CHIPS + layers),
        out_shape=[jax.ShapeDtypeStruct((CORES, rows, sizes[0]), bf16 if k else f32) for k in range(layers)]
        + [jax.ShapeDtypeStruct((CORES, rows, sizes[1]), bf16 if j else f32) for j in range(CHIPS)],
        compiler_params=kernel_params(),
        cost_estimate=LIGHT,
        name="first_sum",
    )(partial[0], *wide_sums, partial[CHIPS], *narrow_sums)
    wide_sums = [shift(summed[k], k * GROUP) for k in range(1, layers)]
    narrow_sums = [shift(summed[layers + j], j * CORES) for j in range(1, CHIPS)]
    mine, theirs = pl.pallas_call(
        functools.partial(last_sum_kernel, layers),
        in_specs=[vmem_spec()] * (CHIPS + layers),
        out_specs=[vmem_spec()] * 2,
        out_shape=[jax.ShapeDtypeStruct((rows, half), bf16)] * 2,
        compiler_params=kernel_params(),
        cost_estimate=LIGHT,
        name="last_sum",
    )(summed[0], *wide_sums, summed[layers], *narrow_sums)
    other = shift(theirs, 1)

    low, high = jnp.where(core == 0, mine, other), jnp.where(core == 0, other, mine)
    return loss[:, 0], grad_head, jnp.concatenate([low, high], axis=1)


def fits_levels(hidden_states, teacher_logits):
    n = lax.axis_size("vocab")
    rows = hidden_states.shape[0]
    blocks, _, stored, side = teacher_logits.shape
    return (
        n == blocks * GROUP
        and blocks & (blocks - 1) == 0
        and rows * GROUP == side
        and rows % 16 == 0
        and 2 * n <= side
        and 6 * blocks * stored <= side
        and hidden_states.shape[1] % (CORES * 1280) == 0
    )


def on_device(
    hidden_states, head_weight, teacher_logits, block_lists, row_reader, tail_mass, token_weight
):
    plan = levels_plan if fits_levels(hidden_states, teacher_logits) else plain_plan
    return plan(
        hidden_states, head_weight, teacher_logits, block_lists, row_reader, tail_mass, token_weight
    )


def solution(mesh):
    in_specs = (
        P("vocab", None),
        P(None, "vocab"),
        P(None, None, "vocab", None),
        P(),
        P(),
        P(),
        P(),
    )
    out_specs = (P("vocab"), P(None, "vocab"), P("vocab", None))
    return jax.shard_map(
        on_device, mesh=mesh, in_specs=in_specs, out_specs=out_specs, check_vma=False
    )
```

```python
import functools

import jax
import jax.numpy as jnp
from jax import lax
from jax.experimental import pallas as pl
from jax.experimental.pallas import tpu as pltpu
from jax.sharding import PartitionSpec as P


def row_parts(scores, teacher_slab, listed_mask, student_exp, teacher_exp):
    return (
        jnp.sum(student_exp, axis=(2, 3)),
        jnp.sum(teacher_exp, axis=(2, 3)),
        jnp.sum(teacher_exp * scores, axis=(2, 3)),
        jnp.sum(teacher_exp * teacher_slab, axis=(2, 3)),
        jnp.sum(scores, axis=(2, 3)),
        jnp.sum(jnp.where(listed_mask, scores, 0.0), axis=(2, 3)),
    )


def plain_plan(
    hidden_states, head_weight, teacher_logits, block_lists, row_reader, tail_mass, token_weight
):
    blocks, listed_count, stored_rows, block_side = teacher_logits.shape
    slab_width = head_weight.shape[1]
    slab_blocks = slab_width // block_side
    devices = lax.axis_size("vocab")
    rank_self = lax.axis_index("vocab")
    tokens = blocks * block_side
    shard_rows = hidden_states.shape[0]
    gathered = lax.all_gather(hidden_states, "vocab", axis=0, tiled=True)
    logits = jnp.dot(gathered, head_weight, preferred_element_type=jnp.float32)
    owner_dev = block_lists // slab_blocks
    owned_here = owner_dev == rank_self
    within = block_lists - rank_self * slab_blocks
    token_iota = lax.broadcasted_iota(jnp.int32, (1, block_side, block_side), 1)
    token_map = (row_reader[:, None, :] == token_iota).astype(jnp.bfloat16)
    place_iota = lax.broadcasted_iota(jnp.int32, (1, slab_blocks, 1), 1)
    block_iota = lax.broadcasted_iota(jnp.int32, (1, devices * slab_blocks, 1), 1)
    picker = (block_lists[:, None, :] == block_iota).astype(jnp.bfloat16)
    outgoing = jnp.einsum(
        "tnk,tkrc->tnrc", picker, teacher_logits, preferred_element_type=jnp.float32
    ).astype(jnp.bfloat16)
    incoming = lax.all_to_all(outgoing, "vocab", split_axis=1, concat_axis=2, tiled=True)
    teacher_slab = jnp.einsum(
        "tpj,tbjc->tpbc", token_map, incoming, preferred_element_type=jnp.float32
    )
    listed = jnp.sum(
        ((within[:, None, :] == place_iota) & owned_here[:, None, :]).astype(jnp.int32), axis=2
    )
    scores = logits.reshape(blocks, block_side, slab_blocks, block_side)
    listed_mask = (listed > 0)[:, None, :, None]
    local_smax = jnp.max(scores, axis=(2, 3))
    local_tmax = jnp.max(jnp.where(listed_mask, teacher_slab, -1e30), axis=(2, 3))
    student_max, teacher_max = lax.pmax((local_smax, local_tmax), "vocab")
    student_exp = jnp.exp(scores - student_max[:, :, None, None])
    teacher_exp = jnp.exp(
        jnp.where(listed_mask, teacher_slab - teacher_max[:, :, None, None], -jnp.inf)
    )
    parts = row_parts(scores, teacher_slab, listed_mask, student_exp, teacher_exp)
    student_sum, teacher_sum, cross_sum, self_sum, logit_total, listed_total = lax.psum(
        (parts[0], parts[1], parts[2], parts[3], parts[4], parts[5]), "vocab"
    )
    tail_share = tail_mass.reshape(blocks, block_side)
    unlisted = float(devices * slab_width - block_side * listed_count)
    kept_mass = 1.0 - tail_share
    log_norm = student_max + jnp.log(student_sum)
    row_loss = (
        kept_mass * (jnp.log(kept_mass) - teacher_max - jnp.log(teacher_sum))
        + kept_mass * self_sum / teacher_sum
        + tail_share * jnp.log(tail_share / unlisted)
        - kept_mass * cross_sum / teacher_sum
        - tail_share / unlisted * (logit_total - listed_total)
        + log_norm
    )
    token_loss = lax.dynamic_slice_in_dim(
        row_loss.reshape(tokens), rank_self * shard_rows, shard_rows, 0
    )
    student_prob = student_exp / student_sum[:, :, None, None]
    teacher_prob = jnp.where(
        listed_mask,
        (kept_mass / teacher_sum)[:, :, None, None] * teacher_exp,
        (tail_share / unlisted)[:, :, None, None],
    )
    weight = token_weight.reshape(blocks, block_side)[:, :, None, None]
    grad_logits = (
        (weight * (student_prob - teacher_prob)).astype(jnp.bfloat16).reshape(tokens, slab_width)
    )
    grad_head = lax.dot_general(
        gathered, grad_logits, (((0,), (0,)), ((), ())), preferred_element_type=jnp.float32
    ).astype(jnp.bfloat16)
    grad_hidden = lax.psum_scatter(
        lax.dot_general(
            grad_logits, head_weight, (((1,), (1,)), ((), ())), preferred_element_type=jnp.float32
        ),
        "vocab",
        scatter_dimension=0,
        tiled=True,
    ).astype(jnp.bfloat16)
    return (token_loss, grad_head, grad_hidden)


CORES = 2
CHIPS = 4
GROUP = CORES * CHIPS
SLOTS = 4
LIGHT = pl.CostEstimate(flops=1, bytes_accessed=1, transcendentals=0)
SMALL_VMEM = 16 * 1024 * 1024
LOGITS_VMEM = 40 * 1024 * 1024
PARTIAL_VMEM = 42 * 1024 * 1024
LARGE_VMEM = 48 * 1024 * 1024
STAT_ROWS = 16


def kernel_params(limit=SMALL_VMEM):
    return pltpu.CompilerParams(vmem_limit_bytes=limit)


def vmem_spec():
    return pl.BlockSpec(memory_space=pltpu.VMEM)


def hbm_spec():
    return pl.BlockSpec(memory_space=pltpu.HBM)


def smem_spec():
    return pl.BlockSpec(memory_space=pltpu.SMEM)


def shift(x, distance):
    n = lax.axis_size("vocab")
    return lax.ppermute(x, "vocab", [(i, i ^ distance) for i in range(n)])


def token_places(place, rows, side):
    row = lax.broadcasted_iota(jnp.int32, (side, 1), 0)
    group = row // rows
    chip = (group % CHIPS) ^ place[1]
    core = (group // CHIPS) ^ place[0]
    return (chip * CORES + core) * rows + row % rows


def pick_column(match, values):
    return jnp.sum(jnp.where(match, values, 0.0), axis=1, keepdims=True)


def teacher_kernel(
    unlisted, rows, pos_ref, place_ref, arrived_ref, reader_ref, tail_ref, prob_ref, entropy_ref
):
    devices, size, side = arrived_ref.shape
    blocks = reader_ref.shape[0]
    stored = side // devices
    per_block = SLOTS * stored
    layers = blocks
    pos = [pos_ref[i] for i in range(3)]
    lane = lax.broadcasted_iota(jnp.int32, (1, side), 1)
    sender_lane = lax.broadcasted_iota(jnp.int32, (1, devices), 1)
    row_lane = lax.broadcasted_iota(jnp.int32, (1, devices * per_block), 1)
    where_token = token_places(pos, rows, side)
    parts = [arrived_ref[:, size - 3 + i, :] for i in range(3)]
    for k in range(layers):
        block = pos[2] ^ k
        stored_row = jnp.sum(jnp.where(reader_ref[block] == where_token, lane, 0), axis=1, keepdims=True)
        sender, row = stored_row // stored, stored_row % stored
        from_sender = jnp.where(sender_lane == sender, 1.0, 0.0).astype(jnp.bfloat16)
        stat = sum(jnp.dot(from_sender, part, preferred_element_type=jnp.float32) for part in parts)
        normaliser = pick_column(lane == block * stored + row, stat)
        tail = pick_column(lane == where_token, tail_ref[block])
        kept = 1.0 - tail
        rest = tail / unlisted
        span = pl.ds(k * side, side)
        prob_ref[span, :] = jnp.broadcast_to(rest, (side, prob_ref.shape[1]))
        all_rows = arrived_ref[:, pl.ds(pl.multiple_of(block * per_block, per_block), per_block), :]
        all_rows = all_rows.reshape(devices * per_block, side)
        for s in range(SLOTS):
            place = place_ref[block, s]
            onehot = jnp.where(row_lane == sender * per_block + s * stored + row, 1.0, 0.0)
            values = jnp.dot(onehot.astype(jnp.bfloat16), all_rows, preferred_element_type=jnp.float32)
            prob = kept * jnp.exp(values - normaliser)

            @pl.when(place >= 0)
            def _():
                prob_ref[span, pl.ds(pl.multiple_of(place * side, side), side)] = prob

        if k == 0:
            mean = pick_column(lane == (blocks + block) * stored + row, stat)
            entropy = kept * (jnp.log(kept) - normaliser + mean) + tail * jnp.log(rest)
            entropy_ref[...] = jnp.broadcast_to(entropy[:rows], entropy_ref.shape)


def assemble(pieces, rows, out_ref):
    per_core = len(pieces) // CORES
    layers = pieces[0].shape[0] // rows
    for core in range(CORES):
        mine = pieces[core * per_core : (core + 1) * per_core]
        for k in range(layers):
            span = pl.ds(k * rows, rows)
            for j, piece in enumerate(mine[:CHIPS]):
                at = pl.ds((k * GROUP + core * CHIPS + j) * rows, rows)
                columns = slice(0, piece.shape[1])
                out_ref[at, columns] = piece[span, :]
            if per_core > CHIPS:
                piece = mine[CHIPS]
                columns = slice(out_ref.shape[1] - piece.shape[1], out_ref.shape[1])
                out_ref[at, columns] = piece[span, :]


def logits_kernel(rows, *refs):
    pieces, refs = refs[:-8], refs[-8:]
    w_ref, prob_ref, logits_ref, stat_ref, hidden, weight, sems, cross_ref = refs
    depth, width = w_ref.shape[0], prob_ref.shape[1]
    parts = [slice(0, depth // 4), slice(depth // 4, depth)]
    tiles = w_ref.shape[1] // width
    step = pl.program_id(0)

    def copy(i):
        span = pl.ds(parts[i].start, parts[i].stop - parts[i].start)
        return pltpu.make_async_copy(w_ref.at[span, :], weight.at[span, :], sems.at[i])

    @pl.when(step == 0)
    def _():
        copy(0).start()
        copy(1).start()
        assemble(pieces, rows, hidden)
        copy(0).wait()

    @pl.when(step == tiles)
    def _():
        copy(1).wait()

    @pl.when(step < tiles)
    def _():
        span = pl.ds(pl.multiple_of(step * width, width), width)
        logits_ref[:, span] = jnp.dot(
            hidden[:, parts[0]], weight[parts[0], span], preferred_element_type=jnp.float32
        )

    @pl.when(step >= tiles)
    def _():
        span = pl.ds(pl.multiple_of((step - tiles) * width, width), width)
        total = logits_ref[:, span] + jnp.dot(
            hidden[:, parts[1]], weight[parts[1], span], preferred_element_type=jnp.float32
        )
        logits_ref[:, span] = total
        product = total * prob_ref[...]
        folded = product[:, :128]
        for i in range(1, width // 128):
            folded = folded + product[:, i * 128 : (i + 1) * 128]
        cross_ref[...] = jnp.where(step == tiles, 0.0, cross_ref[...]) + folded

    @pl.when(step == 2 * tiles - 1)
    def _():
        logits = logits_ref[...]
        top = jnp.max(logits, axis=1, keepdims=True)
        norm = top + jnp.log(jnp.sum(jnp.exp(logits - top), axis=1, keepdims=True))
        cross = jnp.sum(cross_ref[...], axis=1, keepdims=True)
        lane = lax.broadcasted_iota(jnp.int32, (1, 128), 1)
        both = jnp.where(lane == 0, norm, jnp.where(lane == 1, cross, 0.0)).T
        tokens = logits.shape[0]
        packed = [both[i : i + 1, t : t + 128] for i in range(2) for t in range(0, tokens, 128)]
        stat_ref[...] = jnp.broadcast_to(jnp.concatenate(packed, axis=0)[None], stat_ref.shape)


def grad_kernel(
    rows, pos_ref, stat_ref, logits_ref, prob_ref, weight_ref, entropy_ref, grad_ref, loss_ref
):
    tokens = logits_ref.shape[0]
    devices = tokens // rows
    layers, _, side = weight_ref.shape
    layer_bits = (devices // GROUP).bit_length() - 1
    pos = [pos_ref[i] for i in range(3)]
    rank = pos_ref[3]
    lane = lax.broadcasted_iota(jnp.int32, (1, 128), 1)
    per_stat = stat_ref.shape[1] // 2
    norms, crosses = [
        jnp.concatenate([stat_ref[:, i * per_stat + t, :] for t in range(per_stat)], axis=1) for i in range(2)
    ]
    stat = jnp.concatenate(
        [norms, crosses, jnp.zeros((128 - 2 * devices, tokens), jnp.float32)], axis=0
    ).T
    pairs = [(0, 2), (1, 0), (2, 1)] + [(3 + i, 3 + i) for i in range(layer_bits)]
    for index_bit, block_bit in pairs:
        halves = stat.reshape(devices >> (block_bit + 1), 2, rows << block_bit, 128)
        swapped = jnp.stack([halves[:, 1], halves[:, 0]], axis=1).reshape(tokens, 128)
        stat = jnp.where(((lane ^ rank) >> index_bit) & 1 == 1, swapped, stat)
    is_norm = lane < devices
    is_cross = (lane >= devices) & (lane < 2 * devices)
    top = jnp.max(jnp.where(is_norm, stat, -jnp.inf), axis=1, keepdims=True)
    total = jnp.sum(jnp.where(is_norm, jnp.exp(stat - top), 0.0), axis=1, keepdims=True)
    log_norm = top + jnp.log(total)
    cross = jnp.sum(jnp.where(is_cross, stat, 0.0), axis=1, keepdims=True)
    loss_ref[...] = entropy_ref[...] - cross[:rows] + log_norm[:rows]
    where_token = token_places(pos, rows, side)
    for k in range(layers):
        span = pl.ds(k * side, side)
        weight = pick_column(lane == where_token, weight_ref[pos[2] ^ k])
        student = jnp.exp(logits_ref[span, :] - log_norm[k * side : (k + 1) * side])
        grad_ref[span, :] = (weight * (student - prob_ref[span, :])).astype(grad_ref.dtype)


def partial_kernel(rows, core_ref, grad_ref, sib_ref, w_ref, sib_w_ref, *refs):
    outs, swapped = refs[:-1], refs[-1]
    wide_outs, narrow_outs = outs[:CHIPS], outs[CHIPS:]
    layers = len(narrow_outs)
    half = CHIPS * rows
    step = pl.program_id(0)

    @pl.when(step == 0)
    def _():
        for k in range(layers):
            for core in range(CORES):
                swapped[pl.ds((k * CORES + core) * half, half), :] = sib_ref[
                    pl.ds((k * CORES + 1 - core) * half, half), :
                ]

    contract = (((1,), (1,)), ((), ()))
    total = lax.dot_general(
        grad_ref[...], w_ref[...], contract, preferred_element_type=jnp.float32
    ) + lax.dot_general(swapped[...], sib_w_ref[...], contract, preferred_element_type=jnp.float32)

    def store(outs, by_layer, columns, source):
        for k in range(layers):
            for core in range(CORES):
                for j in range(CHIPS):
                    start = (k * GROUP + core * CHIPS + j) * rows
                    out, i = (outs[k], j) if by_layer else (outs[j], k)
                    out[i, core, :, columns] = total[start : start + rows, source].astype(out.dtype)

    tile = w_ref.shape[0]
    wide = wide_outs[0].shape[-1]
    whole_steps, rest = wide // tile, wide % tile
    everything = slice(0, tile)

    @pl.when(step < whole_steps)
    def _():
        store(wide_outs, False, pl.ds(pl.multiple_of(step * tile, tile), tile), everything)

    if rest:

        @pl.when(step == whole_steps)
        def _():
            store(wide_outs, False, slice(whole_steps * tile, wide), slice(0, rest))
            store(narrow_outs, True, slice(0, tile - rest), slice(rest, tile))

    first = whole_steps + 1 if rest else whole_steps
    offset = tile - rest if rest else 0

    @pl.when(step >= first)
    def _():
        columns = pl.ds(pl.multiple_of(offset + (step - first) * tile, 128), tile)
        store(narrow_outs, True, columns, everything)


def head_kernel(rows, *refs):
    pieces, grad_ref, (out_ref, hidden) = refs[:GROUP], refs[GROUP], refs[-2:]
    assemble(pieces, rows, hidden)
    out_ref[...] = lax.dot_general(
        hidden[...], grad_ref[...], (((0,), (0,)), ((), ())), preferred_element_type=jnp.float32
    ).astype(out_ref.dtype)


def sum_of(parts, index=...):
    total = parts[0][index]
    for part in parts[1:]:
        total = total + part[index].astype(jnp.float32)
    return total


def first_sum_kernel(layers, *refs):
    wide, narrow, outs = refs[:CHIPS], refs[CHIPS : CHIPS + layers], refs[CHIPS + layers :]
    for k, out in enumerate(outs[:layers]):
        out[...] = sum_of(wide, k).astype(out.dtype)
    for j, out in enumerate(outs[layers:]):
        out[...] = sum_of(narrow, j).astype(out.dtype)


def last_sum_kernel(layers, *refs):
    wide, narrow, (mine, theirs) = refs[:layers], refs[layers:-2], refs[-2:]
    split = wide[0].shape[-1]
    for parts, columns in ((wide, slice(0, split)), (narrow, slice(split, mine.shape[1]))):
        total = sum_of(parts)
        mine[:, columns] = total[0].astype(mine.dtype)
        theirs[:, columns] = total[1].astype(theirs.dtype)


def pack_kernel(code_ref, x_ref, out_ref):
    blocks, count, side = x_ref.shape
    devices, size, _ = out_ref.shape
    slot_rows = (size - STAT_ROWS) // blocks
    stored = slot_rows // SLOTS
    target = lax.broadcasted_iota(jnp.int32, (devices * slot_rows, 1), 0)
    row = lax.broadcasted_iota(jnp.int32, (count, 1), 0) % stored
    lane = lax.broadcasted_iota(jnp.int32, (1, side), 1)
    stat = jnp.zeros((1, side), jnp.float32)
    for t in range(blocks):
        onehot = jnp.where(code_ref[t] == target, 1.0, 0.0).astype(x_ref.dtype)
        packed = jnp.dot(onehot, x_ref[t], preferred_element_type=jnp.float32).astype(out_ref.dtype)
        for device in range(devices):
            out_ref[device, pl.ds(t * slot_rows, slot_rows), :] = packed[
                device * slot_rows : (device + 1) * slot_rows
            ]
        values = x_ref[t].astype(jnp.float32)
        row_top = jnp.max(values, axis=1, keepdims=True)
        tops = [jnp.max(jnp.where(row == r, row_top, -jnp.inf), axis=0, keepdims=True) for r in range(stored)]
        top = jnp.zeros_like(row_top)
        for r in range(stored):
            top = jnp.where(row == r, tops[r], top)
        powers = jnp.exp(values - top)
        sums = jnp.sum(powers, axis=1, keepdims=True)
        weighted = jnp.sum(powers * values, axis=1, keepdims=True)
        for r in range(stored):
            total = jnp.sum(jnp.where(row == r, sums, 0.0), axis=0, keepdims=True)
            mean = jnp.sum(jnp.where(row == r, weighted, 0.0), axis=0, keepdims=True) / total
            stat = jnp.where(lane == t * stored + r, tops[r] + jnp.log(total), stat)
            stat = jnp.where(lane == (blocks + t) * stored + r, mean, stat)
    high = stat.astype(jnp.bfloat16).astype(jnp.float32)
    middle = (stat - high).astype(jnp.bfloat16).astype(jnp.float32)
    low = stat - high - middle
    parts = jnp.concatenate([high, middle, low, jnp.zeros((STAT_ROWS - 3, side), jnp.float32)], axis=0)
    parts = parts.astype(out_ref.dtype)
    for device in range(devices):
        out_ref[device, pl.ds(size - STAT_ROWS, STAT_ROWS), :] = parts


def pack_teacher(teacher_logits, block_lists, places):
    blocks, listed_count, stored, side = teacher_logits.shape
    n = lax.axis_size("vocab")
    rank = lax.axis_index("vocab")
    owner = block_lists // places
    earlier = jnp.tril(jnp.ones((listed_count, listed_count), jnp.bool_), -1)
    slot = jnp.sum((owner[:, :, None] == owner[:, None, :]) & earlier, axis=2, dtype=jnp.int32)
    code = owner * SLOTS + slot
    rows_code = (code[:, :, None] * stored + jnp.arange(stored, dtype=jnp.int32)).reshape(blocks, 1, -1)
    payload = pl.pallas_call(
        pack_kernel,
        in_specs=[vmem_spec()] * 2,
        out_specs=vmem_spec(),
        out_shape=jax.ShapeDtypeStruct(
            (n, blocks * SLOTS * stored + STAT_ROWS, side), teacher_logits.dtype
        ),
        compiler_params=kernel_params(),
        cost_estimate=LIGHT,
        name="pack_teacher",
    )(rows_code, teacher_logits.reshape(blocks, listed_count * stored, side))
    mine = code[:, None, :] == rank * SLOTS + jnp.arange(SLOTS, dtype=jnp.int32)[None, :, None]
    place = jnp.sum(jnp.where(mine, (block_lists % places + 1)[:, None, :], 0), axis=2) - 1
    return payload, place.astype(jnp.int32)


def levels_plan(
    hidden_states, head_weight, teacher_logits, block_lists, row_reader, tail_mass, token_weight
):
    blocks, listed_count, stored, side = teacher_logits.shape
    rows, depth = hidden_states.shape
    slab = head_weight.shape[1]
    n = lax.axis_size("vocab")
    rank = lax.axis_index("vocab")
    tokens = n * rows
    layers = n // GROUP
    half = depth // CORES
    bf16, f32 = jnp.bfloat16, jnp.float32
    core, chip, layer = rank % CORES, (rank // CORES) % CHIPS, rank // GROUP
    pos = jnp.stack([core, chip, layer, rank]).astype(jnp.int32)
    unlisted = float(n * slab - side * listed_count)

    column = [hidden_states] + [shift(hidden_states, k * GROUP) for k in range(1, layers)]
    column = jnp.concatenate(column, axis=0)
    X, Y = CORES, 2 * CORES
    plane = [column, shift(column, X), shift(column, Y)]
    plane += [shift(plane[1][:, :half], Y), shift(plane[2][:, half:], X)]
    payload, place = pack_teacher(teacher_logits, block_lists, slab // side)
    arrived = lax.all_to_all(
        payload[:, : 3 - STAT_ROWS], "vocab", split_axis=0, concat_axis=0, tiled=True
    )

    prob, entropy = pl.pallas_call(
        lambda *refs: teacher_kernel(unlisted, rows, *refs),
        out_shape=(
            jax.ShapeDtypeStruct((tokens, slab), f32),
            jax.ShapeDtypeStruct((rows, side), f32),
        ),
        in_specs=[smem_spec(), smem_spec()] + [vmem_spec()] * 3,
        out_specs=(vmem_spec(), vmem_spec()),
        compiler_params=kernel_params(),
        cost_estimate=LIGHT,
        name="teacher_prob",
    )(
        pos,
        place,
        arrived,
        row_reader.reshape(blocks, 1, side),
        tail_mass.reshape(blocks, 1, side),
    )

    sent_w = lax.dynamic_slice(head_weight, ((1 - core) * half, 0), (half, slab))
    plane[-2], plane[-1], prob, sent_w = lax.optimization_barrier((plane[-2], plane[-1], prob, sent_w))
    pieces = plane + [shift(piece, 1) for piece in plane]
    pieces, sent_w = lax.optimization_barrier((pieces, sent_w))
    sib_w = shift(sent_w, 1)

    width = 256 if slab % 256 == 0 else 128
    tiles = slab // width
    whole = lambda t: (0, 0)
    logits, stat = pl.pallas_call(
        functools.partial(logits_kernel, rows),
        grid=(2 * tiles,),
        out_shape=[
            jax.ShapeDtypeStruct((tokens, slab), f32),
            jax.ShapeDtypeStruct((n, 2 * tokens // 128, 128), f32),
        ],
        in_specs=[vmem_spec()] * len(pieces)
        + [hbm_spec(), pl.BlockSpec((tokens, width), lambda t: (0, jnp.maximum(t - tiles, 0)))],
        out_specs=[vmem_spec()] * 2,
        scratch_shapes=[
            pltpu.VMEM((tokens, depth), bf16),
            pltpu.VMEM((depth, slab), bf16),
            pltpu.SemaphoreType.DMA((2,)),
            pltpu.VMEM((tokens, 128), f32),
        ],
        compiler_params=kernel_params(LOGITS_VMEM),
        cost_estimate=LIGHT,
        name="logits",
    )(*pieces, head_weight, prob)
    stat = lax.all_to_all(stat, "vocab", split_axis=0, concat_axis=0, tiled=True)

    grad, loss = pl.pallas_call(
        lambda *refs: grad_kernel(rows, *refs),
        out_shape=(
            jax.ShapeDtypeStruct((tokens, slab), bf16),
            jax.ShapeDtypeStruct((rows, side), f32),
        ),
        in_specs=[smem_spec()] + [vmem_spec()] * 5,
        out_specs=(vmem_spec(), vmem_spec()),
        compiler_params=kernel_params(),
        cost_estimate=LIGHT,
        name="grad_logits",
    )(pos, stat, logits, prob, token_weight.reshape(blocks, 1, side), entropy)
    sib_grad = shift(grad, 1)

    tile = half // 5
    sizes = (half * 7 // 10, half - half * 7 // 10)
    partial = pl.pallas_call(
        functools.partial(partial_kernel, rows),
        grid_spec=pltpu.PrefetchScalarGridSpec(
            num_scalar_prefetch=1,
            grid=(5,),
            in_specs=[vmem_spec()] * 2
            + [pl.BlockSpec((tile, slab), lambda t, pos: (pos[0] * 5 + t, 0))]
            + [pl.BlockSpec((tile, slab), lambda t, pos: (t, 0))],
            out_specs=[vmem_spec()] * (CHIPS + layers),
            scratch_shapes=[pltpu.VMEM((tokens, slab), bf16)],
        ),
        out_shape=[
            jax.ShapeDtypeStruct((layers, CORES, rows, sizes[0]), bf16 if j else f32) for j in range(CHIPS)
        ]
        + [jax.ShapeDtypeStruct((CHIPS, CORES, rows, sizes[1]), bf16 if k else f32) for k in range(layers)],
        compiler_params=kernel_params(PARTIAL_VMEM),
        cost_estimate=LIGHT,
        name="grad_hidden_partial",
    )(pos, grad, sib_grad, head_weight, sib_w)
    *partial, late_grad = lax.optimization_barrier((*partial, grad))
    wide_sums = [shift(partial[j], j * CORES) for j in range(1, CHIPS)]
    narrow_sums = [shift(partial[CHIPS + k], k * GROUP) for k in range(1, layers)]

    head_tile = half // 2

    def grad_head_half(i, *before):
        some = [piece for c in range(CORES) for piece in pieces[c * (CHIPS + 1) :][: CHIPS - 1]]
        across_chip = [pieces[c * (CHIPS + 1) + CHIPS - 1 + i] for c in range(CORES)]
        near = pl.BlockSpec((layers * rows, head_tile), lambda t: (0, 2 * i + t))
        far = pl.BlockSpec((layers * rows, head_tile), lambda t: (0, t))
        operands = []
        for c in range(CORES):
            operands += some[c * (CHIPS - 1) : (c + 1) * (CHIPS - 1)] + [across_chip[c]]
        return pl.pallas_call(
            functools.partial(head_kernel, rows),
            grid=(2,),
            in_specs=([near] * (CHIPS - 1) + [far]) * CORES + [vmem_spec()] + [hbm_spec()] * len(before),
            out_specs=pl.BlockSpec((head_tile, slab), lambda t: (2 * i + t, 0)),
            out_shape=jax.ShapeDtypeStruct((depth, slab), bf16),
            scratch_shapes=[pltpu.VMEM((tokens, head_tile), bf16)],
            input_output_aliases={GROUP + 1: 0} if before else {},
            compiler_params=kernel_params(LARGE_VMEM),
            cost_estimate=LIGHT,
            name="grad_head",
        )(*operands, late_grad, *before)

    grad_head = grad_head_half(0)
    wide_sums, narrow_sums, grad_head, late_grad = lax.optimization_barrier(
        (wide_sums, narrow_sums, grad_head, late_grad)
    )

    summed = pl.pallas_call(
        functools.partial(first_sum_kernel, layers),
        in_specs=[vmem_spec()] * (CHIPS + layers),
        out_specs=[vmem_spec()] * (CHIPS + layers),
        out_shape=[jax.ShapeDtypeStruct((CORES, rows, sizes[0]), bf16 if k else f32) for k in range(layers)]
        + [jax.ShapeDtypeStruct((CORES, rows, sizes[1]), bf16 if j else f32) for j in range(CHIPS)],
        compiler_params=kernel_params(),
        cost_estimate=LIGHT,
        name="first_sum",
    )(partial[0], *wide_sums, partial[CHIPS], *narrow_sums)
    wide_sums = [shift(summed[k], k * GROUP) for k in range(1, layers)]
    narrow_sums = [shift(summed[layers + j], j * CORES) for j in range(1, CHIPS)]
    grad_head = grad_head_half(1, grad_head)
    wide_sums, narrow_sums, grad_head = lax.optimization_barrier((wide_sums, narrow_sums, grad_head))
    mine, theirs = pl.pallas_call(
        functools.partial(last_sum_kernel, layers),
        in_specs=[vmem_spec()] * (CHIPS + layers),
        out_specs=[vmem_spec()] * 2,
        out_shape=[jax.ShapeDtypeStruct((rows, half), bf16)] * 2,
        compiler_params=kernel_params(),
        cost_estimate=LIGHT,
        name="last_sum",
    )(summed[0], *wide_sums, summed[layers], *narrow_sums)
    other = shift(theirs, 1)

    low, high = jnp.where(core == 0, mine, other), jnp.where(core == 0, other, mine)
    return loss[:, 0], grad_head, jnp.concatenate([low, high], axis=1)


def fits_levels(hidden_states, teacher_logits):
    n = lax.axis_size("vocab")
    rows = hidden_states.shape[0]
    blocks, _, stored, side = teacher_logits.shape
    return (
        n == blocks * GROUP
        and blocks & (blocks - 1) == 0
        and rows * GROUP == side
        and rows % 16 == 0
        and 2 * n <= side
        and 6 * blocks * stored <= side
        and hidden_states.shape[1] % (CORES * 1280) == 0
    )


def on_device(
    hidden_states, head_weight, teacher_logits, block_lists, row_reader, tail_mass, token_weight
):
    plan = levels_plan if fits_levels(hidden_states, teacher_logits) else plain_plan
    return plan(
        hidden_states, head_weight, teacher_logits, block_lists, row_reader, tail_mass, token_weight
    )


def solution(mesh):
    in_specs = (
        P("vocab", None),
        P(None, "vocab"),
        P(None, None, "vocab", None),
        P(),
        P(),
        P(),
        P(),
    )
    out_specs = (P("vocab"), P(None, "vocab"), P("vocab", None))
    return jax.shard_map(
        on_device, mesh=mesh, in_specs=in_specs, out_specs=out_specs, check_vma=False
    )
```

```python
import functools

import jax
import jax.numpy as jnp
from jax import lax
from jax.experimental import pallas as pl
from jax.experimental.pallas import tpu as pltpu
from jax.sharding import PartitionSpec as P


def row_parts(scores, teacher_slab, listed_mask, student_exp, teacher_exp):
    return (
        jnp.sum(student_exp, axis=(2, 3)),
        jnp.sum(teacher_exp, axis=(2, 3)),
        jnp.sum(teacher_exp * scores, axis=(2, 3)),
        jnp.sum(teacher_exp * teacher_slab, axis=(2, 3)),
        jnp.sum(scores, axis=(2, 3)),
        jnp.sum(jnp.where(listed_mask, scores, 0.0), axis=(2, 3)),
    )


def plain_plan(
    hidden_states, head_weight, teacher_logits, block_lists, row_reader, tail_mass, token_weight
):
    blocks, listed_count, stored_rows, block_side = teacher_logits.shape
    slab_width = head_weight.shape[1]
    slab_blocks = slab_width // block_side
    devices = lax.axis_size("vocab")
    rank_self = lax.axis_index("vocab")
    tokens = blocks * block_side
    shard_rows = hidden_states.shape[0]
    gathered = lax.all_gather(hidden_states, "vocab", axis=0, tiled=True)
    logits = jnp.dot(gathered, head_weight, preferred_element_type=jnp.float32)
    owner_dev = block_lists // slab_blocks
    owned_here = owner_dev == rank_self
    within = block_lists - rank_self * slab_blocks
    token_iota = lax.broadcasted_iota(jnp.int32, (1, block_side, block_side), 1)
    token_map = (row_reader[:, None, :] == token_iota).astype(jnp.bfloat16)
    place_iota = lax.broadcasted_iota(jnp.int32, (1, slab_blocks, 1), 1)
    block_iota = lax.broadcasted_iota(jnp.int32, (1, devices * slab_blocks, 1), 1)
    picker = (block_lists[:, None, :] == block_iota).astype(jnp.bfloat16)
    outgoing = jnp.einsum(
        "tnk,tkrc->tnrc", picker, teacher_logits, preferred_element_type=jnp.float32
    ).astype(jnp.bfloat16)
    incoming = lax.all_to_all(outgoing, "vocab", split_axis=1, concat_axis=2, tiled=True)
    teacher_slab = jnp.einsum(
        "tpj,tbjc->tpbc", token_map, incoming, preferred_element_type=jnp.float32
    )
    listed = jnp.sum(
        ((within[:, None, :] == place_iota) & owned_here[:, None, :]).astype(jnp.int32), axis=2
    )
    scores = logits.reshape(blocks, block_side, slab_blocks, block_side)
    listed_mask = (listed > 0)[:, None, :, None]
    local_smax = jnp.max(scores, axis=(2, 3))
    local_tmax = jnp.max(jnp.where(listed_mask, teacher_slab, -1e30), axis=(2, 3))
    student_max, teacher_max = lax.pmax((local_smax, local_tmax), "vocab")
    student_exp = jnp.exp(scores - student_max[:, :, None, None])
    teacher_exp = jnp.exp(
        jnp.where(listed_mask, teacher_slab - teacher_max[:, :, None, None], -jnp.inf)
    )
    parts = row_parts(scores, teacher_slab, listed_mask, student_exp, teacher_exp)
    student_sum, teacher_sum, cross_sum, self_sum, logit_total, listed_total = lax.psum(
        (parts[0], parts[1], parts[2], parts[3], parts[4], parts[5]), "vocab"
    )
    tail_share = tail_mass.reshape(blocks, block_side)
    unlisted = float(devices * slab_width - block_side * listed_count)
    kept_mass = 1.0 - tail_share
    log_norm = student_max + jnp.log(student_sum)
    row_loss = (
        kept_mass * (jnp.log(kept_mass) - teacher_max - jnp.log(teacher_sum))
        + kept_mass * self_sum / teacher_sum
        + tail_share * jnp.log(tail_share / unlisted)
        - kept_mass * cross_sum / teacher_sum
        - tail_share / unlisted * (logit_total - listed_total)
        + log_norm
    )
    token_loss = lax.dynamic_slice_in_dim(
        row_loss.reshape(tokens), rank_self * shard_rows, shard_rows, 0
    )
    student_prob = student_exp / student_sum[:, :, None, None]
    teacher_prob = jnp.where(
        listed_mask,
        (kept_mass / teacher_sum)[:, :, None, None] * teacher_exp,
        (tail_share / unlisted)[:, :, None, None],
    )
    weight = token_weight.reshape(blocks, block_side)[:, :, None, None]
    grad_logits = (
        (weight * (student_prob - teacher_prob)).astype(jnp.bfloat16).reshape(tokens, slab_width)
    )
    grad_head = lax.dot_general(
        gathered, grad_logits, (((0,), (0,)), ((), ())), preferred_element_type=jnp.float32
    ).astype(jnp.bfloat16)
    grad_hidden = lax.psum_scatter(
        lax.dot_general(
            grad_logits, head_weight, (((1,), (1,)), ((), ())), preferred_element_type=jnp.float32
        ),
        "vocab",
        scatter_dimension=0,
        tiled=True,
    ).astype(jnp.bfloat16)
    return (token_loss, grad_head, grad_hidden)


CORES = 2
CHIPS = 4
GROUP = CORES * CHIPS
SLOTS = 4
LIGHT = pl.CostEstimate(flops=1, bytes_accessed=1, transcendentals=0)
SMALL_VMEM = 16 * 1024 * 1024
LOGITS_VMEM = 40 * 1024 * 1024
PARTIAL_VMEM = 42 * 1024 * 1024
LARGE_VMEM = 48 * 1024 * 1024
STAT_ROWS = 16


def kernel_params(limit=SMALL_VMEM):
    return pltpu.CompilerParams(vmem_limit_bytes=limit)


def vmem_spec():
    return pl.BlockSpec(memory_space=pltpu.VMEM)


def hbm_spec():
    return pl.BlockSpec(memory_space=pltpu.HBM)


def smem_spec():
    return pl.BlockSpec(memory_space=pltpu.SMEM)


def shift(x, distance):
    n = lax.axis_size("vocab")
    return lax.ppermute(x, "vocab", [(i, i ^ distance) for i in range(n)])


def token_places(place, rows, side):
    row = lax.broadcasted_iota(jnp.int32, (side, 1), 0)
    group = row // rows
    chip = (group % CHIPS) ^ place[1]
    core = (group // CHIPS) ^ place[0]
    return (chip * CORES + core) * rows + row % rows


def pick_column(match, values):
    return jnp.sum(jnp.where(match, values, 0.0), axis=1, keepdims=True)


def teacher_kernel(
    unlisted, rows, pos_ref, place_ref, arrived_ref, reader_ref, tail_ref, prob_ref, entropy_ref
):
    devices, size, side = arrived_ref.shape
    blocks = reader_ref.shape[0]
    stored = side // devices
    per_block = SLOTS * stored
    layers = blocks
    pos = [pos_ref[i] for i in range(3)]
    lane = lax.broadcasted_iota(jnp.int32, (1, side), 1)
    sender_lane = lax.broadcasted_iota(jnp.int32, (1, devices), 1)
    row_lane = lax.broadcasted_iota(jnp.int32, (1, devices * per_block), 1)
    where_token = token_places(pos, rows, side)
    parts = [arrived_ref[:, size - 3 + i, :] for i in range(3)]
    for k in range(layers):
        block = pos[2] ^ k
        stored_row = jnp.sum(jnp.where(reader_ref[block] == where_token, lane, 0), axis=1, keepdims=True)
        sender, row = stored_row // stored, stored_row % stored
        from_sender = jnp.where(sender_lane == sender, 1.0, 0.0).astype(jnp.bfloat16)
        stat = sum(jnp.dot(from_sender, part, preferred_element_type=jnp.float32) for part in parts)
        normaliser = pick_column(lane == block * stored + row, stat)
        tail = pick_column(lane == where_token, tail_ref[block])
        kept = 1.0 - tail
        rest = tail / unlisted
        span = pl.ds(k * side, side)
        prob_ref[span, :] = jnp.broadcast_to(rest, (side, prob_ref.shape[1]))
        all_rows = arrived_ref[:, pl.ds(pl.multiple_of(block * per_block, per_block), per_block), :]
        all_rows = all_rows.reshape(devices * per_block, side)
        for s in range(SLOTS):
            place = place_ref[block, s]
            onehot = jnp.where(row_lane == sender * per_block + s * stored + row, 1.0, 0.0)
            values = jnp.dot(onehot.astype(jnp.bfloat16), all_rows, preferred_element_type=jnp.float32)
            prob = kept * jnp.exp(values - normaliser)

            @pl.when(place >= 0)
            def _():
                prob_ref[span, pl.ds(pl.multiple_of(place * side, side), side)] = prob

        if k == 0:
            mean = pick_column(lane == (blocks + block) * stored + row, stat)
            entropy = kept * (jnp.log(kept) - normaliser + mean) + tail * jnp.log(rest)
            entropy_ref[...] = jnp.broadcast_to(entropy[:rows], entropy_ref.shape)


def assemble(pieces, rows, out_ref):
    per_core = len(pieces) // CORES
    layers = pieces[0].shape[0] // rows
    for core in range(CORES):
        mine = pieces[core * per_core : (core + 1) * per_core]
        for k in range(layers):
            span = pl.ds(k * rows, rows)
            for j, piece in enumerate(mine[:CHIPS]):
                at = pl.ds((k * GROUP + core * CHIPS + j) * rows, rows)
                columns = slice(0, piece.shape[1])
                out_ref[at, columns] = piece[span, :]
            if per_core > CHIPS:
                piece = mine[CHIPS]
                columns = slice(out_ref.shape[1] - piece.shape[1], out_ref.shape[1])
                out_ref[at, columns] = piece[span, :]


def logits_kernel(rows, *refs):
    pieces, refs = refs[:-8], refs[-8:]
    w_ref, prob_ref, logits_ref, stat_ref, hidden, weight, sems, cross_ref = refs
    depth, width = w_ref.shape[0], prob_ref.shape[1]
    parts = [slice(0, depth // 4), slice(depth // 4, depth)]
    tiles = w_ref.shape[1] // width
    step = pl.program_id(0)

    def copy(i):
        span = pl.ds(parts[i].start, parts[i].stop - parts[i].start)
        return pltpu.make_async_copy(w_ref.at[span, :], weight.at[span, :], sems.at[i])

    @pl.when(step == 0)
    def _():
        copy(0).start()
        copy(1).start()
        assemble(pieces, rows, hidden)
        copy(0).wait()

    @pl.when(step == tiles)
    def _():
        copy(1).wait()

    @pl.when(step < tiles)
    def _():
        span = pl.ds(pl.multiple_of(step * width, width), width)
        logits_ref[:, span] = jnp.dot(
            hidden[:, parts[0]], weight[parts[0], span], preferred_element_type=jnp.float32
        )

    @pl.when(step >= tiles)
    def _():
        span = pl.ds(pl.multiple_of((step - tiles) * width, width), width)
        total = logits_ref[:, span] + jnp.dot(
            hidden[:, parts[1]], weight[parts[1], span], preferred_element_type=jnp.float32
        )
        logits_ref[:, span] = total
        product = total * prob_ref[...]
        folded = product[:, :128]
        for i in range(1, width // 128):
            folded = folded + product[:, i * 128 : (i + 1) * 128]
        cross_ref[...] = jnp.where(step == tiles, 0.0, cross_ref[...]) + folded

    @pl.when(step == 2 * tiles - 1)
    def _():
        logits = logits_ref[...]
        top = jnp.max(logits, axis=1, keepdims=True)
        norm = top + jnp.log(jnp.sum(jnp.exp(logits - top), axis=1, keepdims=True))
        cross = jnp.sum(cross_ref[...], axis=1, keepdims=True)
        lane = lax.broadcasted_iota(jnp.int32, (1, 128), 1)
        both = jnp.where(lane == 0, norm, jnp.where(lane == 1, cross, 0.0)).T
        tokens = logits.shape[0]
        packed = [both[i : i + 1, t : t + 128] for i in range(2) for t in range(0, tokens, 128)]
        stat_ref[...] = jnp.broadcast_to(jnp.concatenate(packed, axis=0)[None], stat_ref.shape)


def grad_kernel(
    rows, pos_ref, stat_ref, logits_ref, prob_ref, weight_ref, entropy_ref, grad_ref, loss_ref
):
    tokens = logits_ref.shape[0]
    devices = tokens // rows
    layers, _, side = weight_ref.shape
    layer_bits = (devices // GROUP).bit_length() - 1
    pos = [pos_ref[i] for i in range(3)]
    rank = pos_ref[3]
    lane = lax.broadcasted_iota(jnp.int32, (1, 128), 1)
    per_stat = stat_ref.shape[1] // 2
    norms, crosses = [
        jnp.concatenate([stat_ref[:, i * per_stat + t, :] for t in range(per_stat)], axis=1) for i in range(2)
    ]
    stat = jnp.concatenate(
        [norms, crosses, jnp.zeros((128 - 2 * devices, tokens), jnp.float32)], axis=0
    ).T
    pairs = [(0, 2), (1, 0), (2, 1)] + [(3 + i, 3 + i) for i in range(layer_bits)]
    for index_bit, block_bit in pairs:
        halves = stat.reshape(devices >> (block_bit + 1), 2, rows << block_bit, 128)
        swapped = jnp.stack([halves[:, 1], halves[:, 0]], axis=1).reshape(tokens, 128)
        stat = jnp.where(((lane ^ rank) >> index_bit) & 1 == 1, swapped, stat)
    is_norm = lane < devices
    is_cross = (lane >= devices) & (lane < 2 * devices)
    top = jnp.max(jnp.where(is_norm, stat, -jnp.inf), axis=1, keepdims=True)
    total = jnp.sum(jnp.where(is_norm, jnp.exp(stat - top), 0.0), axis=1, keepdims=True)
    log_norm = top + jnp.log(total)
    cross = jnp.sum(jnp.where(is_cross, stat, 0.0), axis=1, keepdims=True)
    loss_ref[...] = entropy_ref[...] - cross[:rows] + log_norm[:rows]
    where_token = token_places(pos, rows, side)
    for k in range(layers):
        span = pl.ds(k * side, side)
        weight = pick_column(lane == where_token, weight_ref[pos[2] ^ k])
        student = jnp.exp(logits_ref[span, :] - log_norm[k * side : (k + 1) * side])
        grad_ref[span, :] = (weight * (student - prob_ref[span, :])).astype(grad_ref.dtype)


def partial_kernel(rows, core_ref, grad_ref, sib_ref, w_ref, sib_w_ref, *refs):
    outs, swapped = refs[:-1], refs[-1]
    wide_outs, narrow_outs = outs[:CHIPS], outs[CHIPS:]
    layers = len(narrow_outs)
    half = CHIPS * rows
    step = pl.program_id(0)

    @pl.when(step == 0)
    def _():
        for k in range(layers):
            for core in range(CORES):
                swapped[pl.ds((k * CORES + core) * half, half), :] = sib_ref[
                    pl.ds((k * CORES + 1 - core) * half, half), :
                ]

    contract = (((1,), (1,)), ((), ()))
    total = lax.dot_general(
        grad_ref[...], w_ref[...], contract, preferred_element_type=jnp.float32
    ) + lax.dot_general(swapped[...], sib_w_ref[...], contract, preferred_element_type=jnp.float32)

    def store(outs, by_layer, columns, source):
        for k in range(layers):
            for core in range(CORES):
                for j in range(CHIPS):
                    start = (k * GROUP + core * CHIPS + j) * rows
                    out, i = (outs[k], j) if by_layer else (outs[j], k)
                    out[i, core, :, columns] = total[start : start + rows, source].astype(out.dtype)

    tile = w_ref.shape[0]
    wide = wide_outs[0].shape[-1]
    whole_steps, rest = wide // tile, wide % tile
    everything = slice(0, tile)

    @pl.when(step < whole_steps)
    def _():
        store(wide_outs, False, pl.ds(pl.multiple_of(step * tile, tile), tile), everything)

    if rest:

        @pl.when(step == whole_steps)
        def _():
            store(wide_outs, False, slice(whole_steps * tile, wide), slice(0, rest))
            store(narrow_outs, True, slice(0, tile - rest), slice(rest, tile))

    first = whole_steps + 1 if rest else whole_steps
    offset = tile - rest if rest else 0

    @pl.when(step >= first)
    def _():
        columns = pl.ds(pl.multiple_of(offset + (step - first) * tile, 128), tile)
        store(narrow_outs, True, columns, everything)


def head_kernel(rows, *refs):
    pieces, (grad_ref, out_ref, hidden) = refs[:-3], refs[-3:]
    per_core = CHIPS + 1
    late = pl.program_id(0) >= pl.num_programs(0) // 2
    for i in range(2):

        @pl.when(late == (i == 1))
        def _():
            mine = [pieces[c * per_core : (c + 1) * per_core] for c in range(CORES)]
            assemble([p for some in mine for p in (*some[: CHIPS - 1], some[CHIPS - 1 + i])], rows, hidden)

    out_ref[...] = lax.dot_general(
        hidden[...], grad_ref[...], (((0,), (0,)), ((), ())), preferred_element_type=jnp.float32
    ).astype(out_ref.dtype)


def sum_of(parts, index=...):
    total = parts[0][index]
    for part in parts[1:]:
        total = total + part[index].astype(jnp.float32)
    return total


def first_sum_kernel(layers, *refs):
    wide, narrow, outs = refs[:CHIPS], refs[CHIPS : CHIPS + layers], refs[CHIPS + layers :]
    for k, out in enumerate(outs[:layers]):
        out[...] = sum_of(wide, k).astype(out.dtype)
    for j, out in enumerate(outs[layers:]):
        out[...] = sum_of(narrow, j).astype(out.dtype)


def last_sum_kernel(layers, *refs):
    wide, narrow, (mine, theirs) = refs[:layers], refs[layers:-2], refs[-2:]
    split = wide[0].shape[-1]
    for parts, columns in ((wide, slice(0, split)), (narrow, slice(split, mine.shape[1]))):
        total = sum_of(parts)
        mine[:, columns] = total[0].astype(mine.dtype)
        theirs[:, columns] = total[1].astype(theirs.dtype)


def pack_kernel(code_ref, x_ref, out_ref):
    blocks, count, side = x_ref.shape
    devices, size, _ = out_ref.shape
    slot_rows = (size - STAT_ROWS) // blocks
    stored = slot_rows // SLOTS
    target = lax.broadcasted_iota(jnp.int32, (devices * slot_rows, 1), 0)
    row = lax.broadcasted_iota(jnp.int32, (count, 1), 0) % stored
    lane = lax.broadcasted_iota(jnp.int32, (1, side), 1)
    stat = jnp.zeros((1, side), jnp.float32)
    for t in range(blocks):
        onehot = jnp.where(code_ref[t] == target, 1.0, 0.0).astype(x_ref.dtype)
        packed = jnp.dot(onehot, x_ref[t], preferred_element_type=jnp.float32).astype(out_ref.dtype)
        for device in range(devices):
            out_ref[device, pl.ds(t * slot_rows, slot_rows), :] = packed[
                device * slot_rows : (device + 1) * slot_rows
            ]
        values = x_ref[t].astype(jnp.float32)
        row_top = jnp.max(values, axis=1, keepdims=True)
        tops = [jnp.max(jnp.where(row == r, row_top, -jnp.inf), axis=0, keepdims=True) for r in range(stored)]
        top = jnp.zeros_like(row_top)
        for r in range(stored):
            top = jnp.where(row == r, tops[r], top)
        powers = jnp.exp(values - top)
        sums = jnp.sum(powers, axis=1, keepdims=True)
        weighted = jnp.sum(powers * values, axis=1, keepdims=True)
        for r in range(stored):
            total = jnp.sum(jnp.where(row == r, sums, 0.0), axis=0, keepdims=True)
            mean = jnp.sum(jnp.where(row == r, weighted, 0.0), axis=0, keepdims=True) / total
            stat = jnp.where(lane == t * stored + r, tops[r] + jnp.log(total), stat)
            stat = jnp.where(lane == (blocks + t) * stored + r, mean, stat)
    high = stat.astype(jnp.bfloat16).astype(jnp.float32)
    middle = (stat - high).astype(jnp.bfloat16).astype(jnp.float32)
    low = stat - high - middle
    parts = jnp.concatenate([high, middle, low, jnp.zeros((STAT_ROWS - 3, side), jnp.float32)], axis=0)
    parts = parts.astype(out_ref.dtype)
    for device in range(devices):
        out_ref[device, pl.ds(size - STAT_ROWS, STAT_ROWS), :] = parts


def pack_teacher(teacher_logits, block_lists, places):
    blocks, listed_count, stored, side = teacher_logits.shape
    n = lax.axis_size("vocab")
    rank = lax.axis_index("vocab")
    owner = block_lists // places
    earlier = jnp.tril(jnp.ones((listed_count, listed_count), jnp.bool_), -1)
    slot = jnp.sum((owner[:, :, None] == owner[:, None, :]) & earlier, axis=2, dtype=jnp.int32)
    code = owner * SLOTS + slot
    rows_code = (code[:, :, None] * stored + jnp.arange(stored, dtype=jnp.int32)).reshape(blocks, 1, -1)
    payload = pl.pallas_call(
        pack_kernel,
        in_specs=[vmem_spec()] * 2,
        out_specs=vmem_spec(),
        out_shape=jax.ShapeDtypeStruct(
            (n, blocks * SLOTS * stored + STAT_ROWS, side), teacher_logits.dtype
        ),
        compiler_params=kernel_params(),
        cost_estimate=LIGHT,
        name="pack_teacher",
    )(rows_code, teacher_logits.reshape(blocks, listed_count * stored, side))
    mine = code[:, None, :] == rank * SLOTS + jnp.arange(SLOTS, dtype=jnp.int32)[None, :, None]
    place = jnp.sum(jnp.where(mine, (block_lists % places + 1)[:, None, :], 0), axis=2) - 1
    return payload, place.astype(jnp.int32)


def levels_plan(
    hidden_states, head_weight, teacher_logits, block_lists, row_reader, tail_mass, token_weight
):
    blocks, listed_count, stored, side = teacher_logits.shape
    rows, depth = hidden_states.shape
    slab = head_weight.shape[1]
    n = lax.axis_size("vocab")
    rank = lax.axis_index("vocab")
    tokens = n * rows
    layers = n // GROUP
    half = depth // CORES
    bf16, f32 = jnp.bfloat16, jnp.float32
    core, chip, layer = rank % CORES, (rank // CORES) % CHIPS, rank // GROUP
    pos = jnp.stack([core, chip, layer, rank]).astype(jnp.int32)
    unlisted = float(n * slab - side * listed_count)

    column = [hidden_states] + [shift(hidden_states, k * GROUP) for k in range(1, layers)]
    column = jnp.concatenate(column, axis=0)
    X, Y = CORES, 2 * CORES
    plane = [column, shift(column, X), shift(column, Y)]
    plane += [shift(plane[1][:, :half], Y), shift(plane[2][:, half:], X)]
    payload, place = pack_teacher(teacher_logits, block_lists, slab // side)
    arrived = lax.all_to_all(
        payload[:, : 3 - STAT_ROWS], "vocab", split_axis=0, concat_axis=0, tiled=True
    )

    prob, entropy = pl.pallas_call(
        lambda *refs: teacher_kernel(unlisted, rows, *refs),
        out_shape=(
            jax.ShapeDtypeStruct((tokens, slab), f32),
            jax.ShapeDtypeStruct((rows, side), f32),
        ),
        in_specs=[smem_spec(), smem_spec()] + [vmem_spec()] * 3,
        out_specs=(vmem_spec(), vmem_spec()),
        compiler_params=kernel_params(),
        cost_estimate=LIGHT,
        name="teacher_prob",
    )(
        pos,
        place,
        arrived,
        row_reader.reshape(blocks, 1, side),
        tail_mass.reshape(blocks, 1, side),
    )

    sent_w = lax.dynamic_slice(head_weight, ((1 - core) * half, 0), (half, slab))
    plane[-2], plane[-1], prob, sent_w = lax.optimization_barrier((plane[-2], plane[-1], prob, sent_w))
    pieces = plane + [shift(piece, 1) for piece in plane]
    pieces, sent_w = lax.optimization_barrier((pieces, sent_w))
    sib_w = shift(sent_w, 1)

    width = 256 if slab % 256 == 0 else 128
    tiles = slab // width
    whole = lambda t: (0, 0)
    logits, stat = pl.pallas_call(
        functools.partial(logits_kernel, rows),
        grid=(2 * tiles,),
        out_shape=[
            jax.ShapeDtypeStruct((tokens, slab), f32),
            jax.ShapeDtypeStruct((n, 2 * tokens // 128, 128), f32),
        ],
        in_specs=[vmem_spec()] * len(pieces)
        + [hbm_spec(), pl.BlockSpec((tokens, width), lambda t: (0, jnp.maximum(t - tiles, 0)))],
        out_specs=[vmem_spec()] * 2,
        scratch_shapes=[
            pltpu.VMEM((tokens, depth), bf16),
            pltpu.VMEM((depth, slab), bf16),
            pltpu.SemaphoreType.DMA((2,)),
            pltpu.VMEM((tokens, 128), f32),
        ],
        compiler_params=kernel_params(LOGITS_VMEM),
        cost_estimate=LIGHT,
        name="logits",
    )(*pieces, head_weight, prob)
    stat = lax.all_to_all(stat, "vocab", split_axis=0, concat_axis=0, tiled=True)

    grad, loss = pl.pallas_call(
        lambda *refs: grad_kernel(rows, *refs),
        out_shape=(
            jax.ShapeDtypeStruct((tokens, slab), bf16),
            jax.ShapeDtypeStruct((rows, side), f32),
        ),
        in_specs=[smem_spec()] + [vmem_spec()] * 5,
        out_specs=(vmem_spec(), vmem_spec()),
        compiler_params=kernel_params(),
        cost_estimate=LIGHT,
        name="grad_logits",
    )(pos, stat, logits, prob, token_weight.reshape(blocks, 1, side), entropy)
    sib_grad = shift(grad, 1)

    tile = half // 5
    sizes = (half * 7 // 10, half - half * 7 // 10)
    partial = pl.pallas_call(
        functools.partial(partial_kernel, rows),
        grid_spec=pltpu.PrefetchScalarGridSpec(
            num_scalar_prefetch=1,
            grid=(5,),
            in_specs=[vmem_spec()] * 2
            + [pl.BlockSpec((tile, slab), lambda t, pos: (pos[0] * 5 + t, 0))]
            + [pl.BlockSpec((tile, slab), lambda t, pos: (t, 0))],
            out_specs=[vmem_spec()] * (CHIPS + layers),
            scratch_shapes=[pltpu.VMEM((tokens, slab), bf16)],
        ),
        out_shape=[
            jax.ShapeDtypeStruct((layers, CORES, rows, sizes[0]), bf16 if j else f32) for j in range(CHIPS)
        ]
        + [jax.ShapeDtypeStruct((CHIPS, CORES, rows, sizes[1]), bf16 if k else f32) for k in range(layers)],
        compiler_params=kernel_params(PARTIAL_VMEM),
        cost_estimate=LIGHT,
        name="grad_hidden_partial",
    )(pos, grad, sib_grad, head_weight, sib_w)
    *partial, late_grad = lax.optimization_barrier((*partial, grad))
    wide_sums = [shift(partial[j], j * CORES) for j in range(1, CHIPS)]
    narrow_sums = [shift(partial[CHIPS + k], k * GROUP) for k in range(1, layers)]

    head_tile = half // 2
    grad_head = pl.pallas_call(
        functools.partial(head_kernel, rows),
        grid=(4,),
        in_specs=[
            pl.BlockSpec(
                (layers * rows, head_tile),
                lambda t, i=i % (CHIPS + 1): (0, (t, jnp.minimum(t, 1), jnp.maximum(t - 2, 0))[max(i - 2, 0)]),
            )
            for i in range(len(pieces))
        ]
        + [pl.BlockSpec((tokens, slab), whole)],
        out_specs=pl.BlockSpec((head_tile, slab), lambda t: (t, 0)),
        out_shape=jax.ShapeDtypeStruct((depth, slab), bf16),
        scratch_shapes=[pltpu.VMEM((tokens, head_tile), bf16)],
        compiler_params=kernel_params(LARGE_VMEM),
        cost_estimate=LIGHT,
        name="grad_head",
    )(*pieces, late_grad)
    wide_sums, narrow_sums, grad_head = lax.optimization_barrier((wide_sums, narrow_sums, grad_head))

    summed = pl.pallas_call(
        functools.partial(first_sum_kernel, layers),
        in_specs=[vmem_spec()] * (CHIPS + layers),
        out_specs=[vmem_spec()] * (CHIPS + layers),
        out_shape=[jax.ShapeDtypeStruct((CORES, rows, sizes[0]), bf16 if k else f32) for k in range(layers)]
        + [jax.ShapeDtypeStruct((CORES, rows, sizes[1]), bf16 if j else f32) for j in range(CHIPS)],
        compiler_params=kernel_params(),
        cost_estimate=LIGHT,
        name="first_sum",
    )(partial[0], *wide_sums, partial[CHIPS], *narrow_sums)
    wide_sums = [shift(summed[k], k * GROUP) for k in range(1, layers)]
    narrow_sums = [shift(summed[layers + j], j * CORES) for j in range(1, CHIPS)]
    mine, theirs = pl.pallas_call(
        functools.partial(last_sum_kernel, layers),
        in_specs=[vmem_spec()] * (CHIPS + layers),
        out_specs=[vmem_spec()] * 2,
        out_shape=[jax.ShapeDtypeStruct((rows, half), bf16)] * 2,
        compiler_params=kernel_params(),
        cost_estimate=LIGHT,
        name="last_sum",
    )(summed[0], *wide_sums, summed[layers], *narrow_sums)
    other = shift(theirs, 1)

    low, high = jnp.where(core == 0, mine, other), jnp.where(core == 0, other, mine)
    return loss[:, 0], grad_head, jnp.concatenate([low, high], axis=1)


def fits_levels(hidden_states, teacher_logits):
    n = lax.axis_size("vocab")
    rows = hidden_states.shape[0]
    blocks, _, stored, side = teacher_logits.shape
    return (
        n == blocks * GROUP
        and blocks & (blocks - 1) == 0
        and rows * GROUP == side
        and rows % 16 == 0
        and 2 * n <= side
        and 6 * blocks * stored <= side
        and hidden_states.shape[1] % (CORES * 1280) == 0
    )


def on_device(
    hidden_states, head_weight, teacher_logits, block_lists, row_reader, tail_mass, token_weight
):
    plan = levels_plan if fits_levels(hidden_states, teacher_logits) else plain_plan
    return plan(
        hidden_states, head_weight, teacher_logits, block_lists, row_reader, tail_mass, token_weight
    )


def solution(mesh):
    in_specs = (
        P("vocab", None),
        P(None, "vocab"),
        P(None, None, "vocab", None),
        P(),
        P(),
        P(),
        P(),
    )
    out_specs = (P("vocab"), P(None, "vocab"), P("vocab", None))
    return jax.shard_map(
        on_device, mesh=mesh, in_specs=in_specs, out_specs=out_specs, check_vma=False
    )
```

```python
import functools

import jax
import jax.numpy as jnp
from jax import lax
from jax.experimental import pallas as pl
from jax.experimental.pallas import tpu as pltpu
from jax.sharding import PartitionSpec as P


def row_parts(scores, teacher_slab, listed_mask, student_exp, teacher_exp):
    return (
        jnp.sum(student_exp, axis=(2, 3)),
        jnp.sum(teacher_exp, axis=(2, 3)),
        jnp.sum(teacher_exp * scores, axis=(2, 3)),
        jnp.sum(teacher_exp * teacher_slab, axis=(2, 3)),
        jnp.sum(scores, axis=(2, 3)),
        jnp.sum(jnp.where(listed_mask, scores, 0.0), axis=(2, 3)),
    )


def plain_plan(
    hidden_states, head_weight, teacher_logits, block_lists, row_reader, tail_mass, token_weight
):
    blocks, listed_count, stored_rows, block_side = teacher_logits.shape
    slab_width = head_weight.shape[1]
    slab_blocks = slab_width // block_side
    devices = lax.axis_size("vocab")
    rank_self = lax.axis_index("vocab")
    tokens = blocks * block_side
    shard_rows = hidden_states.shape[0]
    gathered = lax.all_gather(hidden_states, "vocab", axis=0, tiled=True)
    logits = jnp.dot(gathered, head_weight, preferred_element_type=jnp.float32)
    owner_dev = block_lists // slab_blocks
    owned_here = owner_dev == rank_self
    within = block_lists - rank_self * slab_blocks
    token_iota = lax.broadcasted_iota(jnp.int32, (1, block_side, block_side), 1)
    token_map = (row_reader[:, None, :] == token_iota).astype(jnp.bfloat16)
    place_iota = lax.broadcasted_iota(jnp.int32, (1, slab_blocks, 1), 1)
    block_iota = lax.broadcasted_iota(jnp.int32, (1, devices * slab_blocks, 1), 1)
    picker = (block_lists[:, None, :] == block_iota).astype(jnp.bfloat16)
    outgoing = jnp.einsum(
        "tnk,tkrc->tnrc", picker, teacher_logits, preferred_element_type=jnp.float32
    ).astype(jnp.bfloat16)
    incoming = lax.all_to_all(outgoing, "vocab", split_axis=1, concat_axis=2, tiled=True)
    teacher_slab = jnp.einsum(
        "tpj,tbjc->tpbc", token_map, incoming, preferred_element_type=jnp.float32
    )
    listed = jnp.sum(
        ((within[:, None, :] == place_iota) & owned_here[:, None, :]).astype(jnp.int32), axis=2
    )
    scores = logits.reshape(blocks, block_side, slab_blocks, block_side)
    listed_mask = (listed > 0)[:, None, :, None]
    local_smax = jnp.max(scores, axis=(2, 3))
    local_tmax = jnp.max(jnp.where(listed_mask, teacher_slab, -1e30), axis=(2, 3))
    student_max, teacher_max = lax.pmax((local_smax, local_tmax), "vocab")
    student_exp = jnp.exp(scores - student_max[:, :, None, None])
    teacher_exp = jnp.exp(
        jnp.where(listed_mask, teacher_slab - teacher_max[:, :, None, None], -jnp.inf)
    )
    parts = row_parts(scores, teacher_slab, listed_mask, student_exp, teacher_exp)
    student_sum, teacher_sum, cross_sum, self_sum, logit_total, listed_total = lax.psum(
        (parts[0], parts[1], parts[2], parts[3], parts[4], parts[5]), "vocab"
    )
    tail_share = tail_mass.reshape(blocks, block_side)
    unlisted = float(devices * slab_width - block_side * listed_count)
    kept_mass = 1.0 - tail_share
    log_norm = student_max + jnp.log(student_sum)
    row_loss = (
        kept_mass * (jnp.log(kept_mass) - teacher_max - jnp.log(teacher_sum))
        + kept_mass * self_sum / teacher_sum
        + tail_share * jnp.log(tail_share / unlisted)
        - kept_mass * cross_sum / teacher_sum
        - tail_share / unlisted * (logit_total - listed_total)
        + log_norm
    )
    token_loss = lax.dynamic_slice_in_dim(
        row_loss.reshape(tokens), rank_self * shard_rows, shard_rows, 0
    )
    student_prob = student_exp / student_sum[:, :, None, None]
    teacher_prob = jnp.where(
        listed_mask,
        (kept_mass / teacher_sum)[:, :, None, None] * teacher_exp,
        (tail_share / unlisted)[:, :, None, None],
    )
    weight = token_weight.reshape(blocks, block_side)[:, :, None, None]
    grad_logits = (
        (weight * (student_prob - teacher_prob)).astype(jnp.bfloat16).reshape(tokens, slab_width)
    )
    grad_head = lax.dot_general(
        gathered, grad_logits, (((0,), (0,)), ((), ())), preferred_element_type=jnp.float32
    ).astype(jnp.bfloat16)
    grad_hidden = lax.psum_scatter(
        lax.dot_general(
            grad_logits, head_weight, (((1,), (1,)), ((), ())), preferred_element_type=jnp.float32
        ),
        "vocab",
        scatter_dimension=0,
        tiled=True,
    ).astype(jnp.bfloat16)
    return (token_loss, grad_head, grad_hidden)


CORES = 2
CHIPS = 4
GROUP = CORES * CHIPS
SLOTS = 4
LIGHT = pl.CostEstimate(flops=1, bytes_accessed=1, transcendentals=0)
SMALL_VMEM = 16 * 1024 * 1024
LOGITS_VMEM = 40 * 1024 * 1024
PARTIAL_VMEM = 42 * 1024 * 1024
LARGE_VMEM = 48 * 1024 * 1024
STAT_ROWS = 16


def kernel_params(limit=SMALL_VMEM):
    return pltpu.CompilerParams(vmem_limit_bytes=limit)


def vmem_spec():
    return pl.BlockSpec(memory_space=pltpu.VMEM)


def hbm_spec():
    return pl.BlockSpec(memory_space=pltpu.HBM)


def smem_spec():
    return pl.BlockSpec(memory_space=pltpu.SMEM)


def shift(x, distance):
    n = lax.axis_size("vocab")
    return lax.ppermute(x, "vocab", [(i, i ^ distance) for i in range(n)])


def token_places(place, rows, side):
    row = lax.broadcasted_iota(jnp.int32, (side, 1), 0)
    group = row // rows
    chip = (group % CHIPS) ^ place[1]
    core = (group // CHIPS) ^ place[0]
    return (chip * CORES + core) * rows + row % rows


def pick_column(match, values):
    return jnp.sum(jnp.where(match, values, 0.0), axis=1, keepdims=True)


def teacher_kernel(
    unlisted, rows, pos_ref, place_ref, arrived_ref, reader_ref, tail_ref, prob_ref, entropy_ref
):
    devices, size, side = arrived_ref.shape
    blocks = reader_ref.shape[0]
    stored = side // devices
    per_block = SLOTS * stored
    layers = blocks
    pos = [pos_ref[i] for i in range(3)]
    lane = lax.broadcasted_iota(jnp.int32, (1, side), 1)
    sender_lane = lax.broadcasted_iota(jnp.int32, (1, devices), 1)
    row_lane = lax.broadcasted_iota(jnp.int32, (1, devices * per_block), 1)
    where_token = token_places(pos, rows, side)
    parts = [arrived_ref[:, size - 3 + i, :] for i in range(3)]
    for k in range(layers):
        block = pos[2] ^ k
        stored_row = jnp.sum(jnp.where(reader_ref[block] == where_token, lane, 0), axis=1, keepdims=True)
        sender, row = stored_row // stored, stored_row % stored
        from_sender = jnp.where(sender_lane == sender, 1.0, 0.0).astype(jnp.bfloat16)
        stat = sum(jnp.dot(from_sender, part, preferred_element_type=jnp.float32) for part in parts)
        normaliser = pick_column(lane == block * stored + row, stat)
        tail = pick_column(lane == where_token, tail_ref[block])
        kept = 1.0 - tail
        rest = tail / unlisted
        span = pl.ds(k * side, side)
        prob_ref[span, :] = jnp.broadcast_to(rest, (side, prob_ref.shape[1]))
        all_rows = arrived_ref[:, pl.ds(pl.multiple_of(block * per_block, per_block), per_block), :]
        all_rows = all_rows.reshape(devices * per_block, side)
        for s in range(SLOTS):
            place = place_ref[block, s]
            onehot = jnp.where(row_lane == sender * per_block + s * stored + row, 1.0, 0.0)
            values = jnp.dot(onehot.astype(jnp.bfloat16), all_rows, preferred_element_type=jnp.float32)
            prob = kept * jnp.exp(values - normaliser)

            @pl.when(place >= 0)
            def _():
                prob_ref[span, pl.ds(pl.multiple_of(place * side, side), side)] = prob

        if k == 0:
            mean = pick_column(lane == (blocks + block) * stored + row, stat)
            entropy = kept * (jnp.log(kept) - normaliser + mean) + tail * jnp.log(rest)
            entropy_ref[...] = jnp.broadcast_to(entropy[:rows], entropy_ref.shape)


def assemble(pieces, rows, out_ref):
    per_core = len(pieces) // CORES
    layers = pieces[0].shape[0] // rows
    for core in range(CORES):
        mine = pieces[core * per_core : (core + 1) * per_core]
        for k in range(layers):
            span = pl.ds(k * rows, rows)
            for j, piece in enumerate(mine[:CHIPS]):
                at = pl.ds((k * GROUP + core * CHIPS + j) * rows, rows)
                columns = slice(0, piece.shape[1])
                out_ref[at, columns] = piece[span, :]
            if per_core > CHIPS:
                piece = mine[CHIPS]
                columns = slice(out_ref.shape[1] - piece.shape[1], out_ref.shape[1])
                out_ref[at, columns] = piece[span, :]


def cut_kernel(x_ref, y_ref, low_ref, high_ref):
    half = low_ref.shape[1]
    low_ref[...] = x_ref[:, :half]
    high_ref[...] = y_ref[:, half:]


def join_kernel(pos_ref, mine_ref, other_ref, out_ref):
    half = mine_ref.shape[1]
    own = pos_ref[0]
    out_ref[:, pl.ds(pl.multiple_of(own * half, half), half)] = mine_ref[...]
    out_ref[:, pl.ds(pl.multiple_of((1 - own) * half, half), half)] = other_ref[...]


def logits_kernel(rows, *refs):
    pieces, refs = refs[:-8], refs[-8:]
    w_ref, prob_ref, logits_ref, stat_ref, hidden, weight, sems, cross_ref = refs
    depth, width = w_ref.shape[0], prob_ref.shape[1]
    parts = [slice(0, depth // 4), slice(depth // 4, depth)]
    tiles = w_ref.shape[1] // width
    step = pl.program_id(0)

    def copy(i):
        span = pl.ds(parts[i].start, parts[i].stop - parts[i].start)
        return pltpu.make_async_copy(w_ref.at[span, :], weight.at[span, :], sems.at[i])

    @pl.when(step == 0)
    def _():
        copy(0).start()
        copy(1).start()
        assemble(pieces, rows, hidden)
        copy(0).wait()

    @pl.when(step == tiles)
    def _():
        copy(1).wait()

    @pl.when(step < tiles)
    def _():
        span = pl.ds(pl.multiple_of(step * width, width), width)
        logits_ref[:, span] = jnp.dot(
            hidden[:, parts[0]], weight[parts[0], span], preferred_element_type=jnp.float32
        )

    @pl.when(step >= tiles)
    def _():
        span = pl.ds(pl.multiple_of((step - tiles) * width, width), width)
        total = logits_ref[:, span] + jnp.dot(
            hidden[:, parts[1]], weight[parts[1], span], preferred_element_type=jnp.float32
        )
        logits_ref[:, span] = total
        product = total * prob_ref[...]
        folded = product[:, :128]
        for i in range(1, width // 128):
            folded = folded + product[:, i * 128 : (i + 1) * 128]
        cross_ref[...] = jnp.where(step == tiles, 0.0, cross_ref[...]) + folded

    @pl.when(step == 2 * tiles - 1)
    def _():
        logits = logits_ref[...]
        top = jnp.max(logits, axis=1, keepdims=True)
        norm = top + jnp.log(jnp.sum(jnp.exp(logits - top), axis=1, keepdims=True))
        cross = jnp.sum(cross_ref[...], axis=1, keepdims=True)
        lane = lax.broadcasted_iota(jnp.int32, (1, 128), 1)
        both = jnp.where(lane == 0, norm, jnp.where(lane == 1, cross, 0.0)).T
        tokens = logits.shape[0]
        packed = [both[i : i + 1, t : t + 128] for i in range(2) for t in range(0, tokens, 128)]
        stat_ref[...] = jnp.broadcast_to(jnp.concatenate(packed, axis=0)[None], stat_ref.shape)


def grad_kernel(
    rows, pos_ref, stat_ref, logits_ref, prob_ref, weight_ref, entropy_ref, grad_ref, loss_ref
):
    tokens = logits_ref.shape[0]
    devices = tokens // rows
    layers, _, side = weight_ref.shape
    layer_bits = (devices // GROUP).bit_length() - 1
    pos = [pos_ref[i] for i in range(3)]
    rank = pos_ref[3]
    lane = lax.broadcasted_iota(jnp.int32, (1, 128), 1)
    per_stat = stat_ref.shape[1] // 2
    norms, crosses = [
        jnp.concatenate([stat_ref[:, i * per_stat + t, :] for t in range(per_stat)], axis=1) for i in range(2)
    ]
    stat = jnp.concatenate(
        [norms, crosses, jnp.zeros((128 - 2 * devices, tokens), jnp.float32)], axis=0
    ).T
    pairs = [(0, 2), (1, 0), (2, 1)] + [(3 + i, 3 + i) for i in range(layer_bits)]
    for index_bit, block_bit in pairs:
        halves = stat.reshape(devices >> (block_bit + 1), 2, rows << block_bit, 128)
        swapped = jnp.stack([halves[:, 1], halves[:, 0]], axis=1).reshape(tokens, 128)
        stat = jnp.where(((lane ^ rank) >> index_bit) & 1 == 1, swapped, stat)
    is_norm = lane < devices
    is_cross = (lane >= devices) & (lane < 2 * devices)
    top = jnp.max(jnp.where(is_norm, stat, -jnp.inf), axis=1, keepdims=True)
    total = jnp.sum(jnp.where(is_norm, jnp.exp(stat - top), 0.0), axis=1, keepdims=True)
    log_norm = top + jnp.log(total)
    cross = jnp.sum(jnp.where(is_cross, stat, 0.0), axis=1, keepdims=True)
    loss_ref[...] = entropy_ref[...] - cross[:rows] + log_norm[:rows]
    where_token = token_places(pos, rows, side)
    for k in range(layers):
        span = pl.ds(k * side, side)
        weight = pick_column(lane == where_token, weight_ref[pos[2] ^ k])
        student = jnp.exp(logits_ref[span, :] - log_norm[k * side : (k + 1) * side])
        grad_ref[span, :] = (weight * (student - prob_ref[span, :])).astype(grad_ref.dtype)


def partial_kernel(rows, core_ref, grad_ref, sib_ref, w_ref, sib_w_ref, *refs):
    outs, swapped = refs[:-1], refs[-1]
    wide_outs, narrow_outs = outs[:CHIPS], outs[CHIPS:]
    layers = len(narrow_outs)
    half = CHIPS * rows
    step = pl.program_id(0)

    @pl.when(step == 0)
    def _():
        for k in range(layers):
            for core in range(CORES):
                swapped[pl.ds((k * CORES + core) * half, half), :] = sib_ref[
                    pl.ds((k * CORES + 1 - core) * half, half), :
                ]

    contract = (((1,), (1,)), ((), ()))
    total = lax.dot_general(
        grad_ref[...], w_ref[...], contract, preferred_element_type=jnp.float32
    ) + lax.dot_general(swapped[...], sib_w_ref[...], contract, preferred_element_type=jnp.float32)

    def store(outs, by_layer, columns, source):
        for k in range(layers):
            for core in range(CORES):
                for j in range(CHIPS):
                    start = (k * GROUP + core * CHIPS + j) * rows
                    out, i = (outs[k], j) if by_layer else (outs[j], k)
                    out[i, core, :, columns] = total[start : start + rows, source].astype(out.dtype)

    tile = w_ref.shape[0]
    wide = wide_outs[0].shape[-1]
    whole_steps, rest = wide // tile, wide % tile
    everything = slice(0, tile)

    @pl.when(step < whole_steps)
    def _():
        store(wide_outs, False, pl.ds(pl.multiple_of(step * tile, tile), tile), everything)

    if rest:

        @pl.when(step == whole_steps)
        def _():
            store(wide_outs, False, slice(whole_steps * tile, wide), slice(0, rest))
            store(narrow_outs, True, slice(0, tile - rest), slice(rest, tile))

    first = whole_steps + 1 if rest else whole_steps
    offset = tile - rest if rest else 0

    @pl.when(step >= first)
    def _():
        columns = pl.ds(pl.multiple_of(offset + (step - first) * tile, 128), tile)
        store(narrow_outs, True, columns, everything)


def head_kernel(rows, *refs):
    pieces, (grad_ref, out_ref, hidden) = refs[:-3], refs[-3:]
    per_core = CHIPS + 1
    late = pl.program_id(0) >= pl.num_programs(0) // 2
    for i in range(2):

        @pl.when(late == (i == 1))
        def _():
            mine = [pieces[c * per_core : (c + 1) * per_core] for c in range(CORES)]
            assemble([p for some in mine for p in (*some[: CHIPS - 1], some[CHIPS - 1 + i])], rows, hidden)

    out_ref[...] = lax.dot_general(
        hidden[...], grad_ref[...], (((0,), (0,)), ((), ())), preferred_element_type=jnp.float32
    ).astype(out_ref.dtype)


def sum_of(parts, index=...):
    total = parts[0][index]
    for part in parts[1:]:
        total = total + part[index].astype(jnp.float32)
    return total


def first_sum_kernel(layers, *refs):
    wide, narrow, outs = refs[:CHIPS], refs[CHIPS : CHIPS + layers], refs[CHIPS + layers :]
    for k, out in enumerate(outs[:layers]):
        out[...] = sum_of(wide, k).astype(out.dtype)
    for j, out in enumerate(outs[layers:]):
        out[...] = sum_of(narrow, j).astype(out.dtype)


def last_sum_kernel(layers, *refs):
    wide, narrow, (mine, theirs) = refs[:layers], refs[layers:-2], refs[-2:]
    split = wide[0].shape[-1]
    for parts, columns in ((wide, slice(0, split)), (narrow, slice(split, mine.shape[1]))):
        total = sum_of(parts)
        mine[:, columns] = total[0].astype(mine.dtype)
        theirs[:, columns] = total[1].astype(theirs.dtype)


def pack_kernel(code_ref, x_ref, out_ref):
    blocks, count, side = x_ref.shape
    devices, size, _ = out_ref.shape
    slot_rows = (size - STAT_ROWS) // blocks
    stored = slot_rows // SLOTS
    target = lax.broadcasted_iota(jnp.int32, (devices * slot_rows, 1), 0)
    row = lax.broadcasted_iota(jnp.int32, (count, 1), 0) % stored
    lane = lax.broadcasted_iota(jnp.int32, (1, side), 1)
    stat = jnp.zeros((1, side), jnp.float32)
    for t in range(blocks):
        onehot = jnp.where(code_ref[t] == target, 1.0, 0.0).astype(x_ref.dtype)
        packed = jnp.dot(onehot, x_ref[t], preferred_element_type=jnp.float32).astype(out_ref.dtype)
        for device in range(devices):
            out_ref[device, pl.ds(t * slot_rows, slot_rows), :] = packed[
                device * slot_rows : (device + 1) * slot_rows
            ]
        values = x_ref[t].astype(jnp.float32)
        row_top = jnp.max(values, axis=1, keepdims=True)
        tops = [jnp.max(jnp.where(row == r, row_top, -jnp.inf), axis=0, keepdims=True) for r in range(stored)]
        top = jnp.zeros_like(row_top)
        for r in range(stored):
            top = jnp.where(row == r, tops[r], top)
        powers = jnp.exp(values - top)
        sums = jnp.sum(powers, axis=1, keepdims=True)
        weighted = jnp.sum(powers * values, axis=1, keepdims=True)
        for r in range(stored):
            total = jnp.sum(jnp.where(row == r, sums, 0.0), axis=0, keepdims=True)
            mean = jnp.sum(jnp.where(row == r, weighted, 0.0), axis=0, keepdims=True) / total
            stat = jnp.where(lane == t * stored + r, tops[r] + jnp.log(total), stat)
            stat = jnp.where(lane == (blocks + t) * stored + r, mean, stat)
    high = stat.astype(jnp.bfloat16).astype(jnp.float32)
    middle = (stat - high).astype(jnp.bfloat16).astype(jnp.float32)
    low = stat - high - middle
    parts = jnp.concatenate([high, middle, low, jnp.zeros((STAT_ROWS - 3, side), jnp.float32)], axis=0)
    parts = parts.astype(out_ref.dtype)
    for device in range(devices):
        out_ref[device, pl.ds(size - STAT_ROWS, STAT_ROWS), :] = parts


def pack_teacher(teacher_logits, block_lists, places):
    blocks, listed_count, stored, side = teacher_logits.shape
    n = lax.axis_size("vocab")
    rank = lax.axis_index("vocab")
    owner = block_lists // places
    earlier = jnp.tril(jnp.ones((listed_count, listed_count), jnp.bool_), -1)
    slot = jnp.sum((owner[:, :, None] == owner[:, None, :]) & earlier, axis=2, dtype=jnp.int32)
    code = owner * SLOTS + slot
    rows_code = (code[:, :, None] * stored + jnp.arange(stored, dtype=jnp.int32)).reshape(blocks, 1, -1)
    payload = pl.pallas_call(
        pack_kernel,
        in_specs=[vmem_spec()] * 2,
        out_specs=vmem_spec(),
        out_shape=jax.ShapeDtypeStruct(
            (n, blocks * SLOTS * stored + STAT_ROWS, side), teacher_logits.dtype
        ),
        compiler_params=kernel_params(),
        cost_estimate=LIGHT,
        name="pack_teacher",
    )(rows_code, teacher_logits.reshape(blocks, listed_count * stored, side))
    mine = code[:, None, :] == rank * SLOTS + jnp.arange(SLOTS, dtype=jnp.int32)[None, :, None]
    place = jnp.sum(jnp.where(mine, (block_lists % places + 1)[:, None, :], 0), axis=2) - 1
    return payload, place.astype(jnp.int32)


def levels_plan(
    hidden_states, head_weight, teacher_logits, block_lists, row_reader, tail_mass, token_weight
):
    blocks, listed_count, stored, side = teacher_logits.shape
    rows, depth = hidden_states.shape
    slab = head_weight.shape[1]
    n = lax.axis_size("vocab")
    rank = lax.axis_index("vocab")
    tokens = n * rows
    layers = n // GROUP
    half = depth // CORES
    bf16, f32 = jnp.bfloat16, jnp.float32
    core, chip, layer = rank % CORES, (rank // CORES) % CHIPS, rank // GROUP
    pos = jnp.stack([core, chip, layer, rank]).astype(jnp.int32)
    unlisted = float(n * slab - side * listed_count)

    column = [hidden_states] + [shift(hidden_states, k * GROUP) for k in range(1, layers)]
    column = jnp.concatenate(column, axis=0)
    X, Y = CORES, 2 * CORES
    plane = [column, shift(column, X), shift(column, Y)]
    sent_w = lax.dynamic_slice(head_weight, ((1 - core) * half, 0), (half, slab))
    plane[1], plane[2], sent_w = lax.optimization_barrier((plane[1], plane[2], sent_w))
    low, high = pl.pallas_call(
        cut_kernel,
        in_specs=[vmem_spec()] * 2,
        out_specs=[vmem_spec()] * 2,
        out_shape=[jax.ShapeDtypeStruct((layers * rows, half), bf16)] * 2,
        compiler_params=kernel_params(),
        cost_estimate=LIGHT,
        name="cut_halves",
    )(plane[1], plane[2])
    plane += [shift(low, Y), shift(high, X)]
    payload, place = pack_teacher(teacher_logits, block_lists, slab // side)
    arrived = lax.all_to_all(
        payload[:, : 3 - STAT_ROWS], "vocab", split_axis=0, concat_axis=0, tiled=True
    )

    prob, entropy = pl.pallas_call(
        lambda *refs: teacher_kernel(unlisted, rows, *refs),
        out_shape=(
            jax.ShapeDtypeStruct((tokens, slab), f32),
            jax.ShapeDtypeStruct((rows, side), f32),
        ),
        in_specs=[smem_spec(), smem_spec()] + [vmem_spec()] * 3,
        out_specs=(vmem_spec(), vmem_spec()),
        compiler_params=kernel_params(),
        cost_estimate=LIGHT,
        name="teacher_prob",
    )(
        pos,
        place,
        arrived,
        row_reader.reshape(blocks, 1, side),
        tail_mass.reshape(blocks, 1, side),
    )

    plane[-2], plane[-1], prob = lax.optimization_barrier((plane[-2], plane[-1], prob))
    pieces = plane + [shift(piece, 1) for piece in plane]
    pieces, sent_w = lax.optimization_barrier((pieces, sent_w))
    sib_w = shift(sent_w, 1)

    width = 256 if slab % 256 == 0 else 128
    tiles = slab // width
    whole = lambda t: (0, 0)
    logits, stat = pl.pallas_call(
        functools.partial(logits_kernel, rows),
        grid=(2 * tiles,),
        out_shape=[
            jax.ShapeDtypeStruct((tokens, slab), f32),
            jax.ShapeDtypeStruct((n, 2 * tokens // 128, 128), f32),
        ],
        in_specs=[vmem_spec()] * len(pieces)
        + [hbm_spec(), pl.BlockSpec((tokens, width), lambda t: (0, jnp.maximum(t - tiles, 0)))],
        out_specs=[vmem_spec()] * 2,
        scratch_shapes=[
            pltpu.VMEM((tokens, depth), bf16),
            pltpu.VMEM((depth, slab), bf16),
            pltpu.SemaphoreType.DMA((2,)),
            pltpu.VMEM((tokens, 128), f32),
        ],
        compiler_params=kernel_params(LOGITS_VMEM),
        cost_estimate=LIGHT,
        name="logits",
    )(*pieces, head_weight, prob)
    stat = lax.all_to_all(stat, "vocab", split_axis=0, concat_axis=0, tiled=True)

    grad, loss = pl.pallas_call(
        lambda *refs: grad_kernel(rows, *refs),
        out_shape=(
            jax.ShapeDtypeStruct((tokens, slab), bf16),
            jax.ShapeDtypeStruct((rows, side), f32),
        ),
        in_specs=[smem_spec()] + [vmem_spec()] * 5,
        out_specs=(vmem_spec(), vmem_spec()),
        compiler_params=kernel_params(),
        cost_estimate=LIGHT,
        name="grad_logits",
    )(pos, stat, logits, prob, token_weight.reshape(blocks, 1, side), entropy)
    sib_grad = shift(grad, 1)

    tile = half // 5
    sizes = (half * 7 // 10, half - half * 7 // 10)
    partial = pl.pallas_call(
        functools.partial(partial_kernel, rows),
        grid_spec=pltpu.PrefetchScalarGridSpec(
            num_scalar_prefetch=1,
            grid=(5,),
            in_specs=[vmem_spec()] * 2
            + [pl.BlockSpec((tile, slab), lambda t, pos: (pos[0] * 5 + t, 0))]
            + [pl.BlockSpec((tile, slab), lambda t, pos: (t, 0))],
            out_specs=[vmem_spec()] * (CHIPS + layers),
            scratch_shapes=[pltpu.VMEM((tokens, slab), bf16)],
        ),
        out_shape=[
            jax.ShapeDtypeStruct((layers, CORES, rows, sizes[0]), bf16 if j else f32) for j in range(CHIPS)
        ]
        + [jax.ShapeDtypeStruct((CHIPS, CORES, rows, sizes[1]), bf16 if k else f32) for k in range(layers)],
        compiler_params=kernel_params(PARTIAL_VMEM),
        cost_estimate=LIGHT,
        name="grad_hidden_partial",
    )(pos, grad, sib_grad, head_weight, sib_w)
    *partial, late_grad = lax.optimization_barrier((*partial, grad))
    wide_sums = [shift(partial[j], j * CORES) for j in range(1, CHIPS)]
    narrow_sums = [shift(partial[CHIPS + k], k * GROUP) for k in range(1, layers)]

    head_tile = half // 2
    grad_head = pl.pallas_call(
        functools.partial(head_kernel, rows),
        grid=(4,),
        in_specs=[
            pl.BlockSpec(
                (layers * rows, head_tile),
                lambda t, i=i % (CHIPS + 1): (0, (t, jnp.minimum(t, 1), jnp.maximum(t - 2, 0))[max(i - 2, 0)]),
            )
            for i in range(len(pieces))
        ]
        + [pl.BlockSpec((tokens, slab), whole)],
        out_specs=pl.BlockSpec((head_tile, slab), lambda t: (t, 0)),
        out_shape=jax.ShapeDtypeStruct((depth, slab), bf16),
        scratch_shapes=[pltpu.VMEM((tokens, head_tile), bf16)],
        compiler_params=kernel_params(LARGE_VMEM),
        cost_estimate=LIGHT,
        name="grad_head",
    )(*pieces, late_grad)
    wide_sums, narrow_sums, grad_head = lax.optimization_barrier((wide_sums, narrow_sums, grad_head))

    summed = pl.pallas_call(
        functools.partial(first_sum_kernel, layers),
        in_specs=[vmem_spec()] * (CHIPS + layers),
        out_specs=[vmem_spec()] * (CHIPS + layers),
        out_shape=[jax.ShapeDtypeStruct((CORES, rows, sizes[0]), bf16 if k else f32) for k in range(layers)]
        + [jax.ShapeDtypeStruct((CORES, rows, sizes[1]), bf16 if j else f32) for j in range(CHIPS)],
        compiler_params=kernel_params(),
        cost_estimate=LIGHT,
        name="first_sum",
    )(partial[0], *wide_sums, partial[CHIPS], *narrow_sums)
    wide_sums = [shift(summed[k], k * GROUP) for k in range(1, layers)]
    narrow_sums = [shift(summed[layers + j], j * CORES) for j in range(1, CHIPS)]
    mine, theirs = pl.pallas_call(
        functools.partial(last_sum_kernel, layers),
        in_specs=[vmem_spec()] * (CHIPS + layers),
        out_specs=[vmem_spec()] * 2,
        out_shape=[jax.ShapeDtypeStruct((rows, half), bf16)] * 2,
        compiler_params=kernel_params(),
        cost_estimate=LIGHT,
        name="last_sum",
    )(summed[0], *wide_sums, summed[layers], *narrow_sums)
    other = shift(theirs, 1)

    grad_hidden = pl.pallas_call(
        join_kernel,
        in_specs=[smem_spec()] + [vmem_spec()] * 2,
        out_specs=vmem_spec(),
        out_shape=jax.ShapeDtypeStruct((rows, depth), bf16),
        compiler_params=kernel_params(),
        cost_estimate=LIGHT,
        name="join_halves",
    )(pos, mine, other)
    return loss[:, 0], grad_head, grad_hidden


def fits_levels(hidden_states, teacher_logits):
    n = lax.axis_size("vocab")
    rows = hidden_states.shape[0]
    blocks, _, stored, side = teacher_logits.shape
    return (
        n == blocks * GROUP
        and blocks & (blocks - 1) == 0
        and rows * GROUP == side
        and rows % 16 == 0
        and 2 * n <= side
        and 6 * blocks * stored <= side
        and hidden_states.shape[1] % (CORES * 1280) == 0
    )


def on_device(
    hidden_states, head_weight, teacher_logits, block_lists, row_reader, tail_mass, token_weight
):
    plan = levels_plan if fits_levels(hidden_states, teacher_logits) else plain_plan
    return plan(
        hidden_states, head_weight, teacher_logits, block_lists, row_reader, tail_mass, token_weight
    )


def solution(mesh):
    in_specs = (
        P("vocab", None),
        P(None, "vocab"),
        P(None, None, "vocab", None),
        P(),
        P(),
        P(),
        P(),
    )
    out_specs = (P("vocab"), P(None, "vocab"), P("vocab", None))
    return jax.shard_map(
        on_device, mesh=mesh, in_specs=in_specs, out_specs=out_specs, check_vma=False
    )
```

```python
import functools

import jax
import jax.numpy as jnp
from jax import lax
from jax.experimental import pallas as pl
from jax.experimental.pallas import tpu as pltpu
from jax.sharding import PartitionSpec as P


def row_parts(scores, teacher_slab, listed_mask, student_exp, teacher_exp):
    return (
        jnp.sum(student_exp, axis=(2, 3)),
        jnp.sum(teacher_exp, axis=(2, 3)),
        jnp.sum(teacher_exp * scores, axis=(2, 3)),
        jnp.sum(teacher_exp * teacher_slab, axis=(2, 3)),
        jnp.sum(scores, axis=(2, 3)),
        jnp.sum(jnp.where(listed_mask, scores, 0.0), axis=(2, 3)),
    )


def plain_plan(
    hidden_states, head_weight, teacher_logits, block_lists, row_reader, tail_mass, token_weight
):
    blocks, listed_count, stored_rows, block_side = teacher_logits.shape
    slab_width = head_weight.shape[1]
    slab_blocks = slab_width // block_side
    devices = lax.axis_size("vocab")
    rank_self = lax.axis_index("vocab")
    tokens = blocks * block_side
    shard_rows = hidden_states.shape[0]
    gathered = lax.all_gather(hidden_states, "vocab", axis=0, tiled=True)
    logits = jnp.dot(gathered, head_weight, preferred_element_type=jnp.float32)
    owner_dev = block_lists // slab_blocks
    owned_here = owner_dev == rank_self
    within = block_lists - rank_self * slab_blocks
    token_iota = lax.broadcasted_iota(jnp.int32, (1, block_side, block_side), 1)
    token_map = (row_reader[:, None, :] == token_iota).astype(jnp.bfloat16)
    place_iota = lax.broadcasted_iota(jnp.int32, (1, slab_blocks, 1), 1)
    block_iota = lax.broadcasted_iota(jnp.int32, (1, devices * slab_blocks, 1), 1)
    picker = (block_lists[:, None, :] == block_iota).astype(jnp.bfloat16)
    outgoing = jnp.einsum(
        "tnk,tkrc->tnrc", picker, teacher_logits, preferred_element_type=jnp.float32
    ).astype(jnp.bfloat16)
    incoming = lax.all_to_all(outgoing, "vocab", split_axis=1, concat_axis=2, tiled=True)
    teacher_slab = jnp.einsum(
        "tpj,tbjc->tpbc", token_map, incoming, preferred_element_type=jnp.float32
    )
    listed = jnp.sum(
        ((within[:, None, :] == place_iota) & owned_here[:, None, :]).astype(jnp.int32), axis=2
    )
    scores = logits.reshape(blocks, block_side, slab_blocks, block_side)
    listed_mask = (listed > 0)[:, None, :, None]
    local_smax = jnp.max(scores, axis=(2, 3))
    local_tmax = jnp.max(jnp.where(listed_mask, teacher_slab, -1e30), axis=(2, 3))
    student_max, teacher_max = lax.pmax((local_smax, local_tmax), "vocab")
    student_exp = jnp.exp(scores - student_max[:, :, None, None])
    teacher_exp = jnp.exp(
        jnp.where(listed_mask, teacher_slab - teacher_max[:, :, None, None], -jnp.inf)
    )
    parts = row_parts(scores, teacher_slab, listed_mask, student_exp, teacher_exp)
    student_sum, teacher_sum, cross_sum, self_sum, logit_total, listed_total = lax.psum(
        (parts[0], parts[1], parts[2], parts[3], parts[4], parts[5]), "vocab"
    )
    tail_share = tail_mass.reshape(blocks, block_side)
    unlisted = float(devices * slab_width - block_side * listed_count)
    kept_mass = 1.0 - tail_share
    log_norm = student_max + jnp.log(student_sum)
    row_loss = (
        kept_mass * (jnp.log(kept_mass) - teacher_max - jnp.log(teacher_sum))
        + kept_mass * self_sum / teacher_sum
        + tail_share * jnp.log(tail_share / unlisted)
        - kept_mass * cross_sum / teacher_sum
        - tail_share / unlisted * (logit_total - listed_total)
        + log_norm
    )
    token_loss = lax.dynamic_slice_in_dim(
        row_loss.reshape(tokens), rank_self * shard_rows, shard_rows, 0
    )
    student_prob = student_exp / student_sum[:, :, None, None]
    teacher_prob = jnp.where(
        listed_mask,
        (kept_mass / teacher_sum)[:, :, None, None] * teacher_exp,
        (tail_share / unlisted)[:, :, None, None],
    )
    weight = token_weight.reshape(blocks, block_side)[:, :, None, None]
    grad_logits = (
        (weight * (student_prob - teacher_prob)).astype(jnp.bfloat16).reshape(tokens, slab_width)
    )
    grad_head = lax.dot_general(
        gathered, grad_logits, (((0,), (0,)), ((), ())), preferred_element_type=jnp.float32
    ).astype(jnp.bfloat16)
    grad_hidden = lax.psum_scatter(
        lax.dot_general(
            grad_logits, head_weight, (((1,), (1,)), ((), ())), preferred_element_type=jnp.float32
        ),
        "vocab",
        scatter_dimension=0,
        tiled=True,
    ).astype(jnp.bfloat16)
    return (token_loss, grad_head, grad_hidden)


CORES = 2
CHIPS = 4
GROUP = CORES * CHIPS
SLOTS = 4
LIGHT = pl.CostEstimate(flops=1, bytes_accessed=1, transcendentals=0)
SMALL_VMEM = 16 * 1024 * 1024
LOGITS_VMEM = 40 * 1024 * 1024
PARTIAL_VMEM = 42 * 1024 * 1024
LARGE_VMEM = 48 * 1024 * 1024
STAT_ROWS = 16


def kernel_params(limit=SMALL_VMEM):
    return pltpu.CompilerParams(vmem_limit_bytes=limit)


def vmem_spec():
    return pl.BlockSpec(memory_space=pltpu.VMEM)


def hbm_spec():
    return pl.BlockSpec(memory_space=pltpu.HBM)


def smem_spec():
    return pl.BlockSpec(memory_space=pltpu.SMEM)


def shift(x, distance):
    n = lax.axis_size("vocab")
    return lax.ppermute(x, "vocab", [(i, i ^ distance) for i in range(n)])


def token_places(place, rows, side):
    row = lax.broadcasted_iota(jnp.int32, (side, 1), 0)
    group = row // rows
    chip = (group % CHIPS) ^ place[1]
    core = (group // CHIPS) ^ place[0]
    return (chip * CORES + core) * rows + row % rows


def pick_column(match, values):
    return jnp.sum(jnp.where(match, values, 0.0), axis=1, keepdims=True)


def teacher_kernel(
    unlisted, rows, pos_ref, place_ref, arrived_ref, reader_ref, tail_ref, prob_ref, entropy_ref
):
    devices, size, side = arrived_ref.shape
    blocks = reader_ref.shape[0]
    stored = side // devices
    per_block = SLOTS * stored
    layers = blocks
    pos = [pos_ref[i] for i in range(3)]
    lane = lax.broadcasted_iota(jnp.int32, (1, side), 1)
    sender_lane = lax.broadcasted_iota(jnp.int32, (1, devices), 1)
    row_lane = lax.broadcasted_iota(jnp.int32, (1, devices * per_block), 1)
    where_token = token_places(pos, rows, side)
    parts = [arrived_ref[:, size - 3 + i, :] for i in range(3)]
    for k in range(layers):
        block = pos[2] ^ k
        stored_row = jnp.sum(jnp.where(reader_ref[block] == where_token, lane, 0), axis=1, keepdims=True)
        sender, row = stored_row // stored, stored_row % stored
        from_sender = jnp.where(sender_lane == sender, 1.0, 0.0).astype(jnp.bfloat16)
        stat = sum(jnp.dot(from_sender, part, preferred_element_type=jnp.float32) for part in parts)
        normaliser = pick_column(lane == block * stored + row, stat)
        tail = pick_column(lane == where_token, tail_ref[block])
        kept = 1.0 - tail
        rest = tail / unlisted
        span = pl.ds(k * side, side)
        prob_ref[span, :] = jnp.broadcast_to(rest, (side, prob_ref.shape[1]))
        all_rows = arrived_ref[:, pl.ds(pl.multiple_of(block * per_block, per_block), per_block), :]
        all_rows = all_rows.reshape(devices * per_block, side)
        for s in range(SLOTS):
            place = place_ref[block, s]
            onehot = jnp.where(row_lane == sender * per_block + s * stored + row, 1.0, 0.0)
            values = jnp.dot(onehot.astype(jnp.bfloat16), all_rows, preferred_element_type=jnp.float32)
            prob = kept * jnp.exp(values - normaliser)

            @pl.when(place >= 0)
            def _():
                prob_ref[span, pl.ds(pl.multiple_of(place * side, side), side)] = prob

        if k == 0:
            mean = pick_column(lane == (blocks + block) * stored + row, stat)
            entropy = kept * (jnp.log(kept) - normaliser + mean) + tail * jnp.log(rest)
            entropy_ref[...] = jnp.broadcast_to(entropy[:rows], entropy_ref.shape)


def assemble(pieces, rows, out_ref):
    per_core = len(pieces) // CORES
    layers = pieces[0].shape[0] // rows
    for core in range(CORES):
        mine = pieces[core * per_core : (core + 1) * per_core]
        for k in range(layers):
            span = pl.ds(k * rows, rows)
            for j, piece in enumerate(mine[:CHIPS]):
                at = pl.ds((k * GROUP + core * CHIPS + j) * rows, rows)
                columns = slice(0, piece.shape[1])
                out_ref[at, columns] = piece[span, :]
            if per_core > CHIPS:
                piece = mine[CHIPS]
                columns = slice(out_ref.shape[1] - piece.shape[1], out_ref.shape[1])
                out_ref[at, columns] = piece[span, :]


def cut_kernel(x_ref, y_ref, low_ref, high_ref):
    half = low_ref.shape[1]
    low_ref[...] = x_ref[:, :half]
    high_ref[...] = y_ref[:, half:]


def logits_kernel(rows, *refs):
    pieces, refs = refs[:-8], refs[-8:]
    w_ref, prob_ref, logits_ref, stat_ref, hidden, weight, sems, cross_ref = refs
    depth, width = w_ref.shape[0], prob_ref.shape[1]
    parts = [slice(0, depth // 4), slice(depth // 4, depth)]
    tiles = w_ref.shape[1] // width
    step = pl.program_id(0)

    def copy(i):
        span = pl.ds(parts[i].start, parts[i].stop - parts[i].start)
        return pltpu.make_async_copy(w_ref.at[span, :], weight.at[span, :], sems.at[i])

    @pl.when(step == 0)
    def _():
        copy(0).start()
        copy(1).start()
        assemble(pieces, rows, hidden)
        copy(0).wait()

    @pl.when(step == tiles)
    def _():
        copy(1).wait()

    @pl.when(step < tiles)
    def _():
        span = pl.ds(pl.multiple_of(step * width, width), width)
        logits_ref[:, span] = jnp.dot(
            hidden[:, parts[0]], weight[parts[0], span], preferred_element_type=jnp.float32
        )

    @pl.when(step >= tiles)
    def _():
        span = pl.ds(pl.multiple_of((step - tiles) * width, width), width)
        total = logits_ref[:, span] + jnp.dot(
            hidden[:, parts[1]], weight[parts[1], span], preferred_element_type=jnp.float32
        )
        logits_ref[:, span] = total
        product = total * prob_ref[...]
        folded = product[:, :128]
        for i in range(1, width // 128):
            folded = folded + product[:, i * 128 : (i + 1) * 128]
        cross_ref[...] = jnp.where(step == tiles, 0.0, cross_ref[...]) + folded

    @pl.when(step == 2 * tiles - 1)
    def _():
        logits = logits_ref[...]
        top = jnp.max(logits, axis=1, keepdims=True)
        norm = top + jnp.log(jnp.sum(jnp.exp(logits - top), axis=1, keepdims=True))
        cross = jnp.sum(cross_ref[...], axis=1, keepdims=True)
        lane = lax.broadcasted_iota(jnp.int32, (1, 128), 1)
        both = jnp.where(lane == 0, norm, jnp.where(lane == 1, cross, 0.0)).T
        tokens = logits.shape[0]
        packed = [both[i : i + 1, t : t + 128] for i in range(2) for t in range(0, tokens, 128)]
        stat_ref[...] = jnp.broadcast_to(jnp.concatenate(packed, axis=0)[None], stat_ref.shape)


def grad_kernel(
    rows, pos_ref, stat_ref, logits_ref, prob_ref, weight_ref, entropy_ref, grad_ref, loss_ref
):
    tokens = logits_ref.shape[0]
    devices = tokens // rows
    layers, _, side = weight_ref.shape
    layer_bits = (devices // GROUP).bit_length() - 1
    pos = [pos_ref[i] for i in range(3)]
    rank = pos_ref[3]
    lane = lax.broadcasted_iota(jnp.int32, (1, 128), 1)
    per_stat = stat_ref.shape[1] // 2
    norms, crosses = [
        jnp.concatenate([stat_ref[:, i * per_stat + t, :] for t in range(per_stat)], axis=1) for i in range(2)
    ]
    stat = jnp.concatenate(
        [norms, crosses, jnp.zeros((128 - 2 * devices, tokens), jnp.float32)], axis=0
    ).T
    pairs = [(0, 2), (1, 0), (2, 1)] + [(3 + i, 3 + i) for i in range(layer_bits)]
    for index_bit, block_bit in pairs:
        halves = stat.reshape(devices >> (block_bit + 1), 2, rows << block_bit, 128)
        swapped = jnp.stack([halves[:, 1], halves[:, 0]], axis=1).reshape(tokens, 128)
        stat = jnp.where(((lane ^ rank) >> index_bit) & 1 == 1, swapped, stat)
    is_norm = lane < devices
    is_cross = (lane >= devices) & (lane < 2 * devices)
    top = jnp.max(jnp.where(is_norm, stat, -jnp.inf), axis=1, keepdims=True)
    total = jnp.sum(jnp.where(is_norm, jnp.exp(stat - top), 0.0), axis=1, keepdims=True)
    log_norm = top + jnp.log(total)
    cross = jnp.sum(jnp.where(is_cross, stat, 0.0), axis=1, keepdims=True)
    loss_ref[...] = entropy_ref[...] - cross[:rows] + log_norm[:rows]
    where_token = token_places(pos, rows, side)
    for k in range(layers):
        span = pl.ds(k * side, side)
        weight = pick_column(lane == where_token, weight_ref[pos[2] ^ k])
        student = jnp.exp(logits_ref[span, :] - log_norm[k * side : (k + 1) * side])
        grad_ref[span, :] = (weight * (student - prob_ref[span, :])).astype(grad_ref.dtype)


def partial_kernel(rows, core_ref, grad_ref, sib_ref, w_ref, sib_w_ref, *refs):
    outs, swapped = refs[:-1], refs[-1]
    wide_outs, narrow_outs = outs[:CHIPS], outs[CHIPS:]
    layers = len(narrow_outs)
    half = CHIPS * rows
    step = pl.program_id(0)

    @pl.when(step == 0)
    def _():
        for k in range(layers):
            for core in range(CORES):
                swapped[pl.ds((k * CORES + core) * half, half), :] = sib_ref[
                    pl.ds((k * CORES + 1 - core) * half, half), :
                ]

    contract = (((1,), (1,)), ((), ()))
    total = lax.dot_general(
        grad_ref[...], w_ref[...], contract, preferred_element_type=jnp.float32
    ) + lax.dot_general(swapped[...], sib_w_ref[...], contract, preferred_element_type=jnp.float32)

    def store(outs, by_layer, columns, source):
        for k in range(layers):
            for core in range(CORES):
                for j in range(CHIPS):
                    start = (k * GROUP + core * CHIPS + j) * rows
                    out, i = (outs[k], j) if by_layer else (outs[j], k)
                    out[i, core, :, columns] = total[start : start + rows, source].astype(out.dtype)

    tile = w_ref.shape[0]
    wide = wide_outs[0].shape[-1]
    whole_steps, rest = wide // tile, wide % tile
    everything = slice(0, tile)

    @pl.when(step < whole_steps)
    def _():
        store(wide_outs, False, pl.ds(pl.multiple_of(step * tile, tile), tile), everything)

    if rest:

        @pl.when(step == whole_steps)
        def _():
            store(wide_outs, False, slice(whole_steps * tile, wide), slice(0, rest))
            store(narrow_outs, True, slice(0, tile - rest), slice(rest, tile))

    first = whole_steps + 1 if rest else whole_steps
    offset = tile - rest if rest else 0

    @pl.when(step >= first)
    def _():
        columns = pl.ds(pl.multiple_of(offset + (step - first) * tile, 128), tile)
        store(narrow_outs, True, columns, everything)


def head_kernel(rows, *refs):
    pieces, (grad_ref, out_ref, hidden) = refs[:-3], refs[-3:]
    per_core = CHIPS + 1
    late = pl.program_id(0) >= pl.num_programs(0) // 2
    for i in range(2):

        @pl.when(late == (i == 1))
        def _():
            mine = [pieces[c * per_core : (c + 1) * per_core] for c in range(CORES)]
            assemble([p for some in mine for p in (*some[: CHIPS - 1], some[CHIPS - 1 + i])], rows, hidden)

    out_ref[...] = lax.dot_general(
        hidden[...], grad_ref[...], (((0,), (0,)), ((), ())), preferred_element_type=jnp.float32
    ).astype(out_ref.dtype)


def sum_of(parts, index=...):
    total = parts[0][index]
    for part in parts[1:]:
        total = total + part[index].astype(jnp.float32)
    return total


def first_sum_kernel(layers, *refs):
    wide, narrow, outs = refs[:CHIPS], refs[CHIPS : CHIPS + layers], refs[CHIPS + layers :]
    for k, out in enumerate(outs[:layers]):
        out[...] = sum_of(wide, k).astype(out.dtype)
    for j, out in enumerate(outs[layers:]):
        out[...] = sum_of(narrow, j).astype(out.dtype)


def last_sum_kernel(layers, *refs):
    wide, narrow, (mine, theirs) = refs[:layers], refs[layers:-2], refs[-2:]
    split = wide[0].shape[-1]
    for parts, columns in ((wide, slice(0, split)), (narrow, slice(split, mine.shape[1]))):
        total = sum_of(parts)
        mine[:, columns] = total[0].astype(mine.dtype)
        theirs[:, columns] = total[1].astype(theirs.dtype)


def pack_kernel(code_ref, x_ref, out_ref):
    blocks, count, side = x_ref.shape
    devices, size, _ = out_ref.shape
    slot_rows = (size - STAT_ROWS) // blocks
    stored = slot_rows // SLOTS
    target = lax.broadcasted_iota(jnp.int32, (devices * slot_rows, 1), 0)
    row = lax.broadcasted_iota(jnp.int32, (count, 1), 0) % stored
    lane = lax.broadcasted_iota(jnp.int32, (1, side), 1)
    stat = jnp.zeros((1, side), jnp.float32)
    for t in range(blocks):
        onehot = jnp.where(code_ref[t] == target, 1.0, 0.0).astype(x_ref.dtype)
        packed = jnp.dot(onehot, x_ref[t], preferred_element_type=jnp.float32).astype(out_ref.dtype)
        for device in range(devices):
            out_ref[device, pl.ds(t * slot_rows, slot_rows), :] = packed[
                device * slot_rows : (device + 1) * slot_rows
            ]
        values = x_ref[t].astype(jnp.float32)
        row_top = jnp.max(values, axis=1, keepdims=True)
        tops = [jnp.max(jnp.where(row == r, row_top, -jnp.inf), axis=0, keepdims=True) for r in range(stored)]
        top = jnp.zeros_like(row_top)
        for r in range(stored):
            top = jnp.where(row == r, tops[r], top)
        powers = jnp.exp(values - top)
        sums = jnp.sum(powers, axis=1, keepdims=True)
        weighted = jnp.sum(powers * values, axis=1, keepdims=True)
        for r in range(stored):
            total = jnp.sum(jnp.where(row == r, sums, 0.0), axis=0, keepdims=True)
            mean = jnp.sum(jnp.where(row == r, weighted, 0.0), axis=0, keepdims=True) / total
            stat = jnp.where(lane == t * stored + r, tops[r] + jnp.log(total), stat)
            stat = jnp.where(lane == (blocks + t) * stored + r, mean, stat)
    high = stat.astype(jnp.bfloat16).astype(jnp.float32)
    middle = (stat - high).astype(jnp.bfloat16).astype(jnp.float32)
    low = stat - high - middle
    parts = jnp.concatenate([high, middle, low, jnp.zeros((STAT_ROWS - 3, side), jnp.float32)], axis=0)
    parts = parts.astype(out_ref.dtype)
    for device in range(devices):
        out_ref[device, pl.ds(size - STAT_ROWS, STAT_ROWS), :] = parts


def pack_teacher(teacher_logits, block_lists, places):
    blocks, listed_count, stored, side = teacher_logits.shape
    n = lax.axis_size("vocab")
    rank = lax.axis_index("vocab")
    owner = block_lists // places
    earlier = jnp.tril(jnp.ones((listed_count, listed_count), jnp.bool_), -1)
    slot = jnp.sum((owner[:, :, None] == owner[:, None, :]) & earlier, axis=2, dtype=jnp.int32)
    code = owner * SLOTS + slot
    rows_code = (code[:, :, None] * stored + jnp.arange(stored, dtype=jnp.int32)).reshape(blocks, 1, -1)
    payload = pl.pallas_call(
        pack_kernel,
        in_specs=[vmem_spec()] * 2,
        out_specs=vmem_spec(),
        out_shape=jax.ShapeDtypeStruct(
            (n, blocks * SLOTS * stored + STAT_ROWS, side), teacher_logits.dtype
        ),
        compiler_params=kernel_params(),
        cost_estimate=LIGHT,
        name="pack_teacher",
    )(rows_code, teacher_logits.reshape(blocks, listed_count * stored, side))
    mine = code[:, None, :] == rank * SLOTS + jnp.arange(SLOTS, dtype=jnp.int32)[None, :, None]
    place = jnp.sum(jnp.where(mine, (block_lists % places + 1)[:, None, :], 0), axis=2) - 1
    return payload, place.astype(jnp.int32)


def levels_plan(
    hidden_states, head_weight, teacher_logits, block_lists, row_reader, tail_mass, token_weight
):
    blocks, listed_count, stored, side = teacher_logits.shape
    rows, depth = hidden_states.shape
    slab = head_weight.shape[1]
    n = lax.axis_size("vocab")
    rank = lax.axis_index("vocab")
    tokens = n * rows
    layers = n // GROUP
    half = depth // CORES
    bf16, f32 = jnp.bfloat16, jnp.float32
    core, chip, layer = rank % CORES, (rank // CORES) % CHIPS, rank // GROUP
    pos = jnp.stack([core, chip, layer, rank]).astype(jnp.int32)
    unlisted = float(n * slab - side * listed_count)

    column = [hidden_states] + [shift(hidden_states, k * GROUP) for k in range(1, layers)]
    column = jnp.concatenate(column, axis=0)
    X, Y = CORES, 2 * CORES
    plane = [column, shift(column, X), shift(column, Y)]
    sent_w = lax.dynamic_slice(head_weight, ((1 - core) * half, 0), (half, slab))
    plane[1], plane[2], sent_w = lax.optimization_barrier((plane[1], plane[2], sent_w))
    low, high = pl.pallas_call(
        cut_kernel,
        in_specs=[vmem_spec()] * 2,
        out_specs=[vmem_spec()] * 2,
        out_shape=[jax.ShapeDtypeStruct((layers * rows, half), bf16)] * 2,
        compiler_params=kernel_params(),
        cost_estimate=LIGHT,
        name="cut_halves",
    )(plane[1], plane[2])
    plane += [shift(low, Y), shift(high, X)]
    payload, place = pack_teacher(teacher_logits, block_lists, slab // side)
    arrived = lax.all_to_all(
        payload[:, : 3 - STAT_ROWS], "vocab", split_axis=0, concat_axis=0, tiled=True
    )

    prob, entropy = pl.pallas_call(
        lambda *refs: teacher_kernel(unlisted, rows, *refs),
        out_shape=(
            jax.ShapeDtypeStruct((tokens, slab), f32),
            jax.ShapeDtypeStruct((rows, side), f32),
        ),
        in_specs=[smem_spec(), smem_spec()] + [vmem_spec()] * 3,
        out_specs=(vmem_spec(), vmem_spec()),
        compiler_params=kernel_params(),
        cost_estimate=LIGHT,
        name="teacher_prob",
    )(
        pos,
        place,
        arrived,
        row_reader.reshape(blocks, 1, side),
        tail_mass.reshape(blocks, 1, side),
    )

    plane[-2], plane[-1], prob = lax.optimization_barrier((plane[-2], plane[-1], prob))
    pieces = plane + [shift(piece, 1) for piece in plane]
    pieces, sent_w = lax.optimization_barrier((pieces, sent_w))
    sib_w = shift(sent_w, 1)

    width = 256 if slab % 256 == 0 else 128
    tiles = slab // width
    whole = lambda t: (0, 0)
    logits, stat = pl.pallas_call(
        functools.partial(logits_kernel, rows),
        grid=(2 * tiles,),
        out_shape=[
            jax.ShapeDtypeStruct((tokens, slab), f32),
            jax.ShapeDtypeStruct((n, 2 * tokens // 128, 128), f32),
        ],
        in_specs=[vmem_spec()] * len(pieces)
        + [hbm_spec(), pl.BlockSpec((tokens, width), lambda t: (0, jnp.maximum(t - tiles, 0)))],
        out_specs=[vmem_spec()] * 2,
        scratch_shapes=[
            pltpu.VMEM((tokens, depth), bf16),
            pltpu.VMEM((depth, slab), bf16),
            pltpu.SemaphoreType.DMA((2,)),
            pltpu.VMEM((tokens, 128), f32),
        ],
        compiler_params=kernel_params(LOGITS_VMEM),
        cost_estimate=LIGHT,
        name="logits",
    )(*pieces, head_weight, prob)
    stat = lax.all_to_all(stat, "vocab", split_axis=0, concat_axis=0, tiled=True)

    grad, loss = pl.pallas_call(
        lambda *refs: grad_kernel(rows, *refs),
        out_shape=(
            jax.ShapeDtypeStruct((tokens, slab), bf16),
            jax.ShapeDtypeStruct((rows, side), f32),
        ),
        in_specs=[smem_spec()] + [vmem_spec()] * 5,
        out_specs=(vmem_spec(), vmem_spec()),
        compiler_params=kernel_params(),
        cost_estimate=LIGHT,
        name="grad_logits",
    )(pos, stat, logits, prob, token_weight.reshape(blocks, 1, side), entropy)
    sib_grad = shift(grad, 1)

    tile = half // 5
    sizes = (half * 7 // 10, half - half * 7 // 10)
    partial = pl.pallas_call(
        functools.partial(partial_kernel, rows),
        grid_spec=pltpu.PrefetchScalarGridSpec(
            num_scalar_prefetch=1,
            grid=(5,),
            in_specs=[vmem_spec()] * 2
            + [pl.BlockSpec((tile, slab), lambda t, pos: (pos[0] * 5 + t, 0))]
            + [pl.BlockSpec((tile, slab), lambda t, pos: (t, 0))],
            out_specs=[vmem_spec()] * (CHIPS + layers),
            scratch_shapes=[pltpu.VMEM((tokens, slab), bf16)],
        ),
        out_shape=[
            jax.ShapeDtypeStruct((layers, CORES, rows, sizes[0]), bf16 if j else f32) for j in range(CHIPS)
        ]
        + [jax.ShapeDtypeStruct((CHIPS, CORES, rows, sizes[1]), bf16 if k else f32) for k in range(layers)],
        compiler_params=kernel_params(PARTIAL_VMEM),
        cost_estimate=LIGHT,
        name="grad_hidden_partial",
    )(pos, grad, sib_grad, head_weight, sib_w)
    *partial, late_grad = lax.optimization_barrier((*partial, grad))
    wide_sums = [shift(partial[j], j * CORES) for j in range(1, CHIPS)]
    narrow_sums = [shift(partial[CHIPS + k], k * GROUP) for k in range(1, layers)]

    head_tile = half // 2
    grad_head = pl.pallas_call(
        functools.partial(head_kernel, rows),
        grid=(4,),
        in_specs=[
            pl.BlockSpec(
                (layers * rows, head_tile),
                lambda t, i=i % (CHIPS + 1): (0, (t, jnp.minimum(t, 1), jnp.maximum(t - 2, 0))[max(i - 2, 0)]),
            )
            for i in range(len(pieces))
        ]
        + [vmem_spec()],
        out_specs=pl.BlockSpec((head_tile, slab), lambda t: (t, 0)),
        out_shape=jax.ShapeDtypeStruct((depth, slab), bf16),
        scratch_shapes=[pltpu.VMEM((tokens, head_tile), bf16)],
        compiler_params=kernel_params(LARGE_VMEM),
        cost_estimate=LIGHT,
        name="grad_head",
    )(*pieces, late_grad)
    wide_sums, narrow_sums, grad_head = lax.optimization_barrier((wide_sums, narrow_sums, grad_head))

    summed = pl.pallas_call(
        functools.partial(first_sum_kernel, layers),
        in_specs=[vmem_spec()] * (CHIPS + layers),
        out_specs=[vmem_spec()] * (CHIPS + layers),
        out_shape=[jax.ShapeDtypeStruct((CORES, rows, sizes[0]), bf16 if k else f32) for k in range(layers)]
        + [jax.ShapeDtypeStruct((CORES, rows, sizes[1]), bf16 if j else f32) for j in range(CHIPS)],
        compiler_params=kernel_params(),
        cost_estimate=LIGHT,
        name="first_sum",
    )(partial[0], *wide_sums, partial[CHIPS], *narrow_sums)
    wide_sums = [shift(summed[k], k * GROUP) for k in range(1, layers)]
    narrow_sums = [shift(summed[layers + j], j * CORES) for j in range(1, CHIPS)]
    mine, theirs = pl.pallas_call(
        functools.partial(last_sum_kernel, layers),
        in_specs=[vmem_spec()] * (CHIPS + layers),
        out_specs=[vmem_spec()] * 2,
        out_shape=[jax.ShapeDtypeStruct((rows, half), bf16)] * 2,
        compiler_params=kernel_params(),
        cost_estimate=LIGHT,
        name="last_sum",
    )(summed[0], *wide_sums, summed[layers], *narrow_sums)
    other = shift(theirs, 1)

    low, high = jnp.where(core == 0, mine, other), jnp.where(core == 0, other, mine)
    return loss[:, 0], grad_head, jnp.concatenate([low, high], axis=1)


def fits_levels(hidden_states, teacher_logits):
    n = lax.axis_size("vocab")
    rows = hidden_states.shape[0]
    blocks, _, stored, side = teacher_logits.shape
    return (
        n == blocks * GROUP
        and blocks & (blocks - 1) == 0
        and rows * GROUP == side
        and rows % 16 == 0
        and 2 * n <= side
        and 6 * blocks * stored <= side
        and hidden_states.shape[1] % (CORES * 1280) == 0
    )


def on_device(
    hidden_states, head_weight, teacher_logits, block_lists, row_reader, tail_mass, token_weight
):
    plan = levels_plan if fits_levels(hidden_states, teacher_logits) else plain_plan
    return plan(
        hidden_states, head_weight, teacher_logits, block_lists, row_reader, tail_mass, token_weight
    )


def solution(mesh):
    in_specs = (
        P("vocab", None),
        P(None, "vocab"),
        P(None, None, "vocab", None),
        P(),
        P(),
        P(),
        P(),
    )
    out_specs = (P("vocab"), P(None, "vocab"), P("vocab", None))
    return jax.shard_map(
        on_device, mesh=mesh, in_specs=in_specs, out_specs=out_specs, check_vma=False
    )
```

```python
import functools

import jax
import jax.numpy as jnp
from jax import lax
from jax.experimental import pallas as pl
from jax.experimental.pallas import tpu as pltpu
from jax.sharding import PartitionSpec as P


def row_parts(scores, teacher_slab, listed_mask, student_exp, teacher_exp):
    return (
        jnp.sum(student_exp, axis=(2, 3)),
        jnp.sum(teacher_exp, axis=(2, 3)),
        jnp.sum(teacher_exp * scores, axis=(2, 3)),
        jnp.sum(teacher_exp * teacher_slab, axis=(2, 3)),
        jnp.sum(scores, axis=(2, 3)),
        jnp.sum(jnp.where(listed_mask, scores, 0.0), axis=(2, 3)),
    )


def plain_plan(
    hidden_states, head_weight, teacher_logits, block_lists, row_reader, tail_mass, token_weight
):
    blocks, listed_count, stored_rows, block_side = teacher_logits.shape
    slab_width = head_weight.shape[1]
    slab_blocks = slab_width // block_side
    devices = lax.axis_size("vocab")
    rank_self = lax.axis_index("vocab")
    tokens = blocks * block_side
    shard_rows = hidden_states.shape[0]
    gathered = lax.all_gather(hidden_states, "vocab", axis=0, tiled=True)
    logits = jnp.dot(gathered, head_weight, preferred_element_type=jnp.float32)
    owner_dev = block_lists // slab_blocks
    owned_here = owner_dev == rank_self
    within = block_lists - rank_self * slab_blocks
    token_iota = lax.broadcasted_iota(jnp.int32, (1, block_side, block_side), 1)
    token_map = (row_reader[:, None, :] == token_iota).astype(jnp.bfloat16)
    place_iota = lax.broadcasted_iota(jnp.int32, (1, slab_blocks, 1), 1)
    block_iota = lax.broadcasted_iota(jnp.int32, (1, devices * slab_blocks, 1), 1)
    picker = (block_lists[:, None, :] == block_iota).astype(jnp.bfloat16)
    outgoing = jnp.einsum(
        "tnk,tkrc->tnrc", picker, teacher_logits, preferred_element_type=jnp.float32
    ).astype(jnp.bfloat16)
    incoming = lax.all_to_all(outgoing, "vocab", split_axis=1, concat_axis=2, tiled=True)
    teacher_slab = jnp.einsum(
        "tpj,tbjc->tpbc", token_map, incoming, preferred_element_type=jnp.float32
    )
    listed = jnp.sum(
        ((within[:, None, :] == place_iota) & owned_here[:, None, :]).astype(jnp.int32), axis=2
    )
    scores = logits.reshape(blocks, block_side, slab_blocks, block_side)
    listed_mask = (listed > 0)[:, None, :, None]
    local_smax = jnp.max(scores, axis=(2, 3))
    local_tmax = jnp.max(jnp.where(listed_mask, teacher_slab, -1e30), axis=(2, 3))
    student_max, teacher_max = lax.pmax((local_smax, local_tmax), "vocab")
    student_exp = jnp.exp(scores - student_max[:, :, None, None])
    teacher_exp = jnp.exp(
        jnp.where(listed_mask, teacher_slab - teacher_max[:, :, None, None], -jnp.inf)
    )
    parts = row_parts(scores, teacher_slab, listed_mask, student_exp, teacher_exp)
    student_sum, teacher_sum, cross_sum, self_sum, logit_total, listed_total = lax.psum(
        (parts[0], parts[1], parts[2], parts[3], parts[4], parts[5]), "vocab"
    )
    tail_share = tail_mass.reshape(blocks, block_side)
    unlisted = float(devices * slab_width - block_side * listed_count)
    kept_mass = 1.0 - tail_share
    log_norm = student_max + jnp.log(student_sum)
    row_loss = (
        kept_mass * (jnp.log(kept_mass) - teacher_max - jnp.log(teacher_sum))
        + kept_mass * self_sum / teacher_sum
        + tail_share * jnp.log(tail_share / unlisted)
        - kept_mass * cross_sum / teacher_sum
        - tail_share / unlisted * (logit_total - listed_total)
        + log_norm
    )
    token_loss = lax.dynamic_slice_in_dim(
        row_loss.reshape(tokens), rank_self * shard_rows, shard_rows, 0
    )
    student_prob = student_exp / student_sum[:, :, None, None]
    teacher_prob = jnp.where(
        listed_mask,
        (kept_mass / teacher_sum)[:, :, None, None] * teacher_exp,
        (tail_share / unlisted)[:, :, None, None],
    )
    weight = token_weight.reshape(blocks, block_side)[:, :, None, None]
    grad_logits = (
        (weight * (student_prob - teacher_prob)).astype(jnp.bfloat16).reshape(tokens, slab_width)
    )
    grad_head = lax.dot_general(
        gathered, grad_logits, (((0,), (0,)), ((), ())), preferred_element_type=jnp.float32
    ).astype(jnp.bfloat16)
    grad_hidden = lax.psum_scatter(
        lax.dot_general(
            grad_logits, head_weight, (((1,), (1,)), ((), ())), preferred_element_type=jnp.float32
        ),
        "vocab",
        scatter_dimension=0,
        tiled=True,
    ).astype(jnp.bfloat16)
    return (token_loss, grad_head, grad_hidden)


CORES = 2
CHIPS = 4
GROUP = CORES * CHIPS
SLOTS = 4
LIGHT = pl.CostEstimate(flops=1, bytes_accessed=1, transcendentals=0)
SMALL_VMEM = 16 * 1024 * 1024
LOGITS_VMEM = 40 * 1024 * 1024
PARTIAL_VMEM = 42 * 1024 * 1024
LARGE_VMEM = 48 * 1024 * 1024
STAT_ROWS = 16


def kernel_params(limit=SMALL_VMEM):
    return pltpu.CompilerParams(vmem_limit_bytes=limit)


def vmem_spec():
    return pl.BlockSpec(memory_space=pltpu.VMEM)


def hbm_spec():
    return pl.BlockSpec(memory_space=pltpu.HBM)


def smem_spec():
    return pl.BlockSpec(memory_space=pltpu.SMEM)


def shift(x, distance):
    n = lax.axis_size("vocab")
    return lax.ppermute(x, "vocab", [(i, i ^ distance) for i in range(n)])


def token_places(place, rows, side):
    row = lax.broadcasted_iota(jnp.int32, (side, 1), 0)
    group = row // rows
    chip = (group % CHIPS) ^ place[1]
    core = (group // CHIPS) ^ place[0]
    return (chip * CORES + core) * rows + row % rows


def pick_column(match, values):
    return jnp.sum(jnp.where(match, values, 0.0), axis=1, keepdims=True)


def teacher_kernel(
    unlisted, rows, pos_ref, place_ref, arrived_ref, reader_ref, tail_ref, prob_ref, entropy_ref
):
    devices, size, side = arrived_ref.shape
    blocks = reader_ref.shape[0]
    stored = side // devices
    per_block = SLOTS * stored
    layers = blocks
    pos = [pos_ref[i] for i in range(3)]
    lane = lax.broadcasted_iota(jnp.int32, (1, side), 1)
    sender_lane = lax.broadcasted_iota(jnp.int32, (1, devices), 1)
    row_lane = lax.broadcasted_iota(jnp.int32, (1, devices * per_block), 1)
    where_token = token_places(pos, rows, side)
    parts = [arrived_ref[:, size - 3 + i, :] for i in range(3)]
    for k in range(layers):
        block = pos[2] ^ k
        stored_row = jnp.sum(jnp.where(reader_ref[block] == where_token, lane, 0), axis=1, keepdims=True)
        sender, row = stored_row // stored, stored_row % stored
        from_sender = jnp.where(sender_lane == sender, 1.0, 0.0).astype(jnp.bfloat16)
        stat = sum(jnp.dot(from_sender, part, preferred_element_type=jnp.float32) for part in parts)
        normaliser = pick_column(lane == block * stored + row, stat)
        tail = pick_column(lane == where_token, tail_ref[block])
        kept = 1.0 - tail
        rest = tail / unlisted
        span = pl.ds(k * side, side)
        prob_ref[span, :] = jnp.broadcast_to(rest, (side, prob_ref.shape[1]))
        all_rows = arrived_ref[:, pl.ds(pl.multiple_of(block * per_block, per_block), per_block), :]
        all_rows = all_rows.reshape(devices * per_block, side)
        for s in range(SLOTS):
            place = place_ref[block, s]
            onehot = jnp.where(row_lane == sender * per_block + s * stored + row, 1.0, 0.0)
            values = jnp.dot(onehot.astype(jnp.bfloat16), all_rows, preferred_element_type=jnp.float32)
            prob = kept * jnp.exp(values - normaliser)

            @pl.when(place >= 0)
            def _():
                prob_ref[span, pl.ds(pl.multiple_of(place * side, side), side)] = prob

        if k == 0:
            mean = pick_column(lane == (blocks + block) * stored + row, stat)
            entropy = kept * (jnp.log(kept) - normaliser + mean) + tail * jnp.log(rest)
            entropy_ref[...] = jnp.broadcast_to(entropy[:rows], entropy_ref.shape)


def assemble(pieces, rows, out_ref):
    per_core = len(pieces) // CORES
    layers = pieces[0].shape[0] // rows
    for core in range(CORES):
        mine = pieces[core * per_core : (core + 1) * per_core]
        for k in range(layers):
            span = pl.ds(k * rows, rows)
            for j, piece in enumerate(mine[:CHIPS]):
                at = pl.ds((k * GROUP + core * CHIPS + j) * rows, rows)
                columns = slice(0, piece.shape[1])
                out_ref[at, columns] = piece[span, :]
            if per_core > CHIPS:
                piece = mine[CHIPS]
                columns = slice(out_ref.shape[1] - piece.shape[1], out_ref.shape[1])
                out_ref[at, columns] = piece[span, :]


def cut_kernel(x_ref, y_ref, low_ref, high_ref):
    half = low_ref.shape[1]
    low_ref[...] = x_ref[:, :half]
    high_ref[...] = y_ref[:, half:]


def logits_kernel(rows, *refs):
    pieces, refs = refs[:-8], refs[-8:]
    w_ref, prob_ref, logits_ref, stat_ref, hidden, weight, sems, cross_ref = refs
    depth, width = w_ref.shape[0], prob_ref.shape[1]
    parts = [slice(0, depth // 4), slice(depth // 4, depth)]
    tiles = w_ref.shape[1] // width
    step = pl.program_id(0)

    def copy(i):
        span = pl.ds(parts[i].start, parts[i].stop - parts[i].start)
        return pltpu.make_async_copy(w_ref.at[span, :], weight.at[span, :], sems.at[i])

    @pl.when(step == 0)
    def _():
        copy(0).start()
        copy(1).start()
        assemble(pieces, rows, hidden)
        copy(0).wait()

    @pl.when(step == tiles)
    def _():
        copy(1).wait()

    @pl.when(step < tiles)
    def _():
        span = pl.ds(pl.multiple_of(step * width, width), width)
        logits_ref[:, span] = jnp.dot(
            hidden[:, parts[0]], weight[parts[0], span], preferred_element_type=jnp.float32
        )

    @pl.when(step >= tiles)
    def _():
        span = pl.ds(pl.multiple_of((step - tiles) * width, width), width)
        total = logits_ref[:, span] + jnp.dot(
            hidden[:, parts[1]], weight[parts[1], span], preferred_element_type=jnp.float32
        )
        logits_ref[:, span] = total
        product = total * prob_ref[...]
        folded = product[:, :128]
        for i in range(1, width // 128):
            folded = folded + product[:, i * 128 : (i + 1) * 128]
        cross_ref[...] = jnp.where(step == tiles, 0.0, cross_ref[...]) + folded

    @pl.when(step == 2 * tiles - 1)
    def _():
        logits = logits_ref[...]
        top = jnp.max(logits, axis=1, keepdims=True)
        norm = top + jnp.log(jnp.sum(jnp.exp(logits - top), axis=1, keepdims=True))
        cross = jnp.sum(cross_ref[...], axis=1, keepdims=True)
        lane = lax.broadcasted_iota(jnp.int32, (1, 128), 1)
        both = jnp.where(lane == 0, norm, jnp.where(lane == 1, cross, 0.0)).T
        tokens = logits.shape[0]
        packed = [both[i : i + 1, t : t + 128] for i in range(2) for t in range(0, tokens, 128)]
        stat_ref[...] = jnp.broadcast_to(jnp.concatenate(packed, axis=0)[None], stat_ref.shape)


def grad_kernel(
    rows, pos_ref, stat_ref, logits_ref, prob_ref, weight_ref, entropy_ref, grad_ref, loss_ref
):
    tokens = logits_ref.shape[0]
    devices = tokens // rows
    layers, _, side = weight_ref.shape
    layer_bits = (devices // GROUP).bit_length() - 1
    pos = [pos_ref[i] for i in range(3)]
    rank = pos_ref[3]
    lane = lax.broadcasted_iota(jnp.int32, (1, 128), 1)
    per_stat = stat_ref.shape[1] // 2
    norms, crosses = [
        jnp.concatenate([stat_ref[:, i * per_stat + t, :] for t in range(per_stat)], axis=1) for i in range(2)
    ]
    stat = jnp.concatenate(
        [norms, crosses, jnp.zeros((128 - 2 * devices, tokens), jnp.float32)], axis=0
    ).T
    pairs = [(0, 2), (1, 0), (2, 1)] + [(3 + i, 3 + i) for i in range(layer_bits)]
    for index_bit, block_bit in pairs:
        halves = stat.reshape(devices >> (block_bit + 1), 2, rows << block_bit, 128)
        swapped = jnp.stack([halves[:, 1], halves[:, 0]], axis=1).reshape(tokens, 128)
        stat = jnp.where(((lane ^ rank) >> index_bit) & 1 == 1, swapped, stat)
    is_norm = lane < devices
    is_cross = (lane >= devices) & (lane < 2 * devices)
    top = jnp.max(jnp.where(is_norm, stat, -jnp.inf), axis=1, keepdims=True)
    total = jnp.sum(jnp.where(is_norm, jnp.exp(stat - top), 0.0), axis=1, keepdims=True)
    log_norm = top + jnp.log(total)
    cross = jnp.sum(jnp.where(is_cross, stat, 0.0), axis=1, keepdims=True)
    loss_ref[...] = entropy_ref[...] - cross[:rows] + log_norm[:rows]
    where_token = token_places(pos, rows, side)
    for k in range(layers):
        span = pl.ds(k * side, side)
        weight = pick_column(lane == where_token, weight_ref[pos[2] ^ k])
        student = jnp.exp(logits_ref[span, :] - log_norm[k * side : (k + 1) * side])
        grad_ref[span, :] = (weight * (student - prob_ref[span, :])).astype(grad_ref.dtype)


def partial_kernel(rows, core_ref, grad_ref, sib_ref, w_ref, sib_w_ref, *refs):
    outs, swapped = refs[:-1], refs[-1]
    wide_outs, narrow_outs = outs[:CHIPS], outs[CHIPS:]
    layers = len(narrow_outs)
    half = CHIPS * rows
    step = pl.program_id(0)

    @pl.when(step == 0)
    def _():
        for k in range(layers):
            for core in range(CORES):
                swapped[pl.ds((k * CORES + core) * half, half), :] = sib_ref[
                    pl.ds((k * CORES + 1 - core) * half, half), :
                ]

    contract = (((1,), (1,)), ((), ()))
    total = lax.dot_general(
        grad_ref[...], w_ref[...], contract, preferred_element_type=jnp.float32
    ) + lax.dot_general(swapped[...], sib_w_ref[...], contract, preferred_element_type=jnp.float32)

    def store(outs, by_layer, columns, source):
        for k in range(layers):
            for core in range(CORES):
                for j in range(CHIPS):
                    start = (k * GROUP + core * CHIPS + j) * rows
                    out, i = (outs[k], j) if by_layer else (outs[j], k)
                    out[i, core, :, columns] = total[start : start + rows, source].astype(out.dtype)

    tile = w_ref.shape[0]
    wide = wide_outs[0].shape[-1]
    whole_steps, rest = wide // tile, wide % tile
    everything = slice(0, tile)

    @pl.when(step < whole_steps)
    def _():
        store(wide_outs, False, pl.ds(pl.multiple_of(step * tile, tile), tile), everything)

    if rest:

        @pl.when(step == whole_steps)
        def _():
            store(wide_outs, False, slice(whole_steps * tile, wide), slice(0, rest))
            store(narrow_outs, True, slice(0, tile - rest), slice(rest, tile))

    first = whole_steps + 1 if rest else whole_steps
    offset = tile - rest if rest else 0

    @pl.when(step >= first)
    def _():
        columns = pl.ds(pl.multiple_of(offset + (step - first) * tile, 128), tile)
        store(narrow_outs, True, columns, everything)


def head_kernel(rows, *refs):
    pieces, (grad_ref, out_ref, hidden) = refs[:-3], refs[-3:]
    per_core = CHIPS + 1
    late = pl.program_id(0) >= pl.num_programs(0) // 2
    for i in range(2):

        @pl.when(late == (i == 1))
        def _():
            mine = [pieces[c * per_core : (c + 1) * per_core] for c in range(CORES)]
            assemble([p for some in mine for p in (*some[: CHIPS - 1], some[CHIPS - 1 + i])], rows, hidden)

    out_ref[...] = lax.dot_general(
        hidden[...], grad_ref[...], (((0,), (0,)), ((), ())), preferred_element_type=jnp.float32
    ).astype(out_ref.dtype)


def sum_of(parts, index=...):
    total = parts[0][index]
    for part in parts[1:]:
        total = total + part[index].astype(jnp.float32)
    return total


def first_sum_kernel(layers, *refs):
    wide, narrow, outs = refs[:CHIPS], refs[CHIPS : CHIPS + layers], refs[CHIPS + layers :]
    for k, out in enumerate(outs[:layers]):
        out[...] = sum_of(wide, k).astype(out.dtype)
    for j, out in enumerate(outs[layers:]):
        out[...] = sum_of(narrow, j).astype(out.dtype)


def last_sum_kernel(layers, *refs):
    wide, narrow, (mine, theirs) = refs[:layers], refs[layers:-2], refs[-2:]
    split = wide[0].shape[-1]
    for parts, columns in ((wide, slice(0, split)), (narrow, slice(split, mine.shape[1]))):
        total = sum_of(parts)
        mine[:, columns] = total[0].astype(mine.dtype)
        theirs[:, columns] = total[1].astype(theirs.dtype)


def pack_kernel(code_ref, x_ref, out_ref):
    blocks, count, side = x_ref.shape
    devices, size, _ = out_ref.shape
    slot_rows = (size - STAT_ROWS) // blocks
    stored = slot_rows // SLOTS
    target = lax.broadcasted_iota(jnp.int32, (devices * slot_rows, 1), 0)
    row = lax.broadcasted_iota(jnp.int32, (count, 1), 0) % stored
    lane = lax.broadcasted_iota(jnp.int32, (1, side), 1)
    stat = jnp.zeros((1, side), jnp.float32)
    for t in range(blocks):
        onehot = jnp.where(code_ref[t] == target, 1.0, 0.0).astype(x_ref.dtype)
        packed = jnp.dot(onehot, x_ref[t], preferred_element_type=jnp.float32).astype(out_ref.dtype)
        for device in range(devices):
            out_ref[device, pl.ds(t * slot_rows, slot_rows), :] = packed[
                device * slot_rows : (device + 1) * slot_rows
            ]
        values = x_ref[t].astype(jnp.float32)
        row_top = jnp.max(values, axis=1, keepdims=True)
        tops = [jnp.max(jnp.where(row == r, row_top, -jnp.inf), axis=0, keepdims=True) for r in range(stored)]
        top = jnp.zeros_like(row_top)
        for r in range(stored):
            top = jnp.where(row == r, tops[r], top)
        powers = jnp.exp(values - top)
        sums = jnp.sum(powers, axis=1, keepdims=True)
        weighted = jnp.sum(powers * values, axis=1, keepdims=True)
        for r in range(stored):
            total = jnp.sum(jnp.where(row == r, sums, 0.0), axis=0, keepdims=True)
            mean = jnp.sum(jnp.where(row == r, weighted, 0.0), axis=0, keepdims=True) / total
            stat = jnp.where(lane == t * stored + r, tops[r] + jnp.log(total), stat)
            stat = jnp.where(lane == (blocks + t) * stored + r, mean, stat)
    high = stat.astype(jnp.bfloat16).astype(jnp.float32)
    middle = (stat - high).astype(jnp.bfloat16).astype(jnp.float32)
    low = stat - high - middle
    parts = jnp.concatenate([high, middle, low, jnp.zeros((STAT_ROWS - 3, side), jnp.float32)], axis=0)
    parts = parts.astype(out_ref.dtype)
    for device in range(devices):
        out_ref[device, pl.ds(size - STAT_ROWS, STAT_ROWS), :] = parts


def pack_teacher(teacher_logits, block_lists, places):
    blocks, listed_count, stored, side = teacher_logits.shape
    n = lax.axis_size("vocab")
    rank = lax.axis_index("vocab")
    owner = block_lists // places
    earlier = jnp.tril(jnp.ones((listed_count, listed_count), jnp.bool_), -1)
    slot = jnp.sum((owner[:, :, None] == owner[:, None, :]) & earlier, axis=2, dtype=jnp.int32)
    code = owner * SLOTS + slot
    rows_code = (code[:, :, None] * stored + jnp.arange(stored, dtype=jnp.int32)).reshape(blocks, 1, -1)
    payload = pl.pallas_call(
        pack_kernel,
        in_specs=[vmem_spec()] * 2,
        out_specs=vmem_spec(),
        out_shape=jax.ShapeDtypeStruct(
            (n, blocks * SLOTS * stored + STAT_ROWS, side), teacher_logits.dtype
        ),
        compiler_params=kernel_params(),
        cost_estimate=LIGHT,
        name="pack_teacher",
    )(rows_code, teacher_logits.reshape(blocks, listed_count * stored, side))
    mine = code[:, None, :] == rank * SLOTS + jnp.arange(SLOTS, dtype=jnp.int32)[None, :, None]
    place = jnp.sum(jnp.where(mine, (block_lists % places + 1)[:, None, :], 0), axis=2) - 1
    return payload, place.astype(jnp.int32)


def levels_plan(
    hidden_states, head_weight, teacher_logits, block_lists, row_reader, tail_mass, token_weight
):
    blocks, listed_count, stored, side = teacher_logits.shape
    rows, depth = hidden_states.shape
    slab = head_weight.shape[1]
    n = lax.axis_size("vocab")
    rank = lax.axis_index("vocab")
    tokens = n * rows
    layers = n // GROUP
    half = depth // CORES
    bf16, f32 = jnp.bfloat16, jnp.float32
    core, chip, layer = rank % CORES, (rank // CORES) % CHIPS, rank // GROUP
    pos = jnp.stack([core, chip, layer, rank]).astype(jnp.int32)
    unlisted = float(n * slab - side * listed_count)

    column = [hidden_states] + [shift(hidden_states, k * GROUP) for k in range(1, layers)]
    column = jnp.concatenate(column, axis=0)
    X, Y = CORES, 2 * CORES
    plane = [column, shift(column, X), shift(column, Y)]
    sent_w = lax.dynamic_slice(head_weight, ((1 - core) * half, 0), (half, slab))
    plane[1], plane[2], sent_w = lax.optimization_barrier((plane[1], plane[2], sent_w))
    low, high = pl.pallas_call(
        cut_kernel,
        in_specs=[vmem_spec()] * 2,
        out_specs=[vmem_spec()] * 2,
        out_shape=[jax.ShapeDtypeStruct((layers * rows, half), bf16)] * 2,
        compiler_params=kernel_params(),
        cost_estimate=LIGHT,
        name="cut_halves",
    )(plane[1], plane[2])
    plane += [shift(low, Y), shift(high, X)]
    payload, place = pack_teacher(teacher_logits, block_lists, slab // side)
    arrived = lax.all_to_all(
        payload[:, : 3 - STAT_ROWS], "vocab", split_axis=0, concat_axis=0, tiled=True
    )

    prob, entropy = pl.pallas_call(
        lambda *refs: teacher_kernel(unlisted, rows, *refs),
        out_shape=(
            jax.ShapeDtypeStruct((tokens, slab), f32),
            jax.ShapeDtypeStruct((rows, side), f32),
        ),
        in_specs=[smem_spec(), smem_spec()] + [vmem_spec()] * 3,
        out_specs=(vmem_spec(), vmem_spec()),
        compiler_params=kernel_params(),
        cost_estimate=LIGHT,
        name="teacher_prob",
    )(
        pos,
        place,
        arrived,
        row_reader.reshape(blocks, 1, side),
        tail_mass.reshape(blocks, 1, side),
    )

    plane[-2], plane[-1], prob = lax.optimization_barrier((plane[-2], plane[-1], prob))
    pieces = plane + [shift(piece, 1) for piece in plane]
    pieces, sent_w = lax.optimization_barrier((pieces, sent_w))
    sib_w = shift(sent_w, 1)

    width = 512 if slab % 512 == 0 else 128
    tiles = slab // width
    whole = lambda t: (0, 0)
    logits, stat = pl.pallas_call(
        functools.partial(logits_kernel, rows),
        grid=(2 * tiles,),
        out_shape=[
            jax.ShapeDtypeStruct((tokens, slab), f32),
            jax.ShapeDtypeStruct((n, 2 * tokens // 128, 128), f32),
        ],
        in_specs=[vmem_spec()] * len(pieces)
        + [hbm_spec(), pl.BlockSpec((tokens, width), lambda t: (0, jnp.maximum(t - tiles, 0)))],
        out_specs=[vmem_spec()] * 2,
        scratch_shapes=[
            pltpu.VMEM((tokens, depth), bf16),
            pltpu.VMEM((depth, slab), bf16),
            pltpu.SemaphoreType.DMA((2,)),
            pltpu.VMEM((tokens, 128), f32),
        ],
        compiler_params=kernel_params(LOGITS_VMEM),
        cost_estimate=LIGHT,
        name="logits",
    )(*pieces, head_weight, prob)
    stat = lax.all_to_all(stat, "vocab", split_axis=0, concat_axis=0, tiled=True)

    grad, loss = pl.pallas_call(
        lambda *refs: grad_kernel(rows, *refs),
        out_shape=(
            jax.ShapeDtypeStruct((tokens, slab), bf16),
            jax.ShapeDtypeStruct((rows, side), f32),
        ),
        in_specs=[smem_spec()] + [vmem_spec()] * 5,
        out_specs=(vmem_spec(), vmem_spec()),
        compiler_params=kernel_params(),
        cost_estimate=LIGHT,
        name="grad_logits",
    )(pos, stat, logits, prob, token_weight.reshape(blocks, 1, side), entropy)
    sib_grad = shift(grad, 1)

    tile = half // 5
    sizes = (half * 7 // 10, half - half * 7 // 10)
    partial = pl.pallas_call(
        functools.partial(partial_kernel, rows),
        grid_spec=pltpu.PrefetchScalarGridSpec(
            num_scalar_prefetch=1,
            grid=(5,),
            in_specs=[vmem_spec()] * 2
            + [pl.BlockSpec((tile, slab), lambda t, pos: (pos[0] * 5 + t, 0))]
            + [pl.BlockSpec((tile, slab), lambda t, pos: (t, 0))],
            out_specs=[vmem_spec()] * (CHIPS + layers),
            scratch_shapes=[pltpu.VMEM((tokens, slab), bf16)],
        ),
        out_shape=[
            jax.ShapeDtypeStruct((layers, CORES, rows, sizes[0]), bf16 if j else f32) for j in range(CHIPS)
        ]
        + [jax.ShapeDtypeStruct((CHIPS, CORES, rows, sizes[1]), bf16 if k else f32) for k in range(layers)],
        compiler_params=kernel_params(PARTIAL_VMEM),
        cost_estimate=LIGHT,
        name="grad_hidden_partial",
    )(pos, grad, sib_grad, head_weight, sib_w)
    *partial, late_grad = lax.optimization_barrier((*partial, grad))
    wide_sums = [shift(partial[j], j * CORES) for j in range(1, CHIPS)]
    narrow_sums = [shift(partial[CHIPS + k], k * GROUP) for k in range(1, layers)]

    head_tile = half // 2
    grad_head = pl.pallas_call(
        functools.partial(head_kernel, rows),
        grid=(4,),
        in_specs=[
            pl.BlockSpec(
                (layers * rows, head_tile),
                lambda t, i=i % (CHIPS + 1): (0, (t, jnp.minimum(t, 1), jnp.maximum(t - 2, 0))[max(i - 2, 0)]),
            )
            for i in range(len(pieces))
        ]
        + [vmem_spec()],
        out_specs=pl.BlockSpec((head_tile, slab), lambda t: (t, 0)),
        out_shape=jax.ShapeDtypeStruct((depth, slab), bf16),
        scratch_shapes=[pltpu.VMEM((tokens, head_tile), bf16)],
        compiler_params=kernel_params(LARGE_VMEM),
        cost_estimate=LIGHT,
        name="grad_head",
    )(*pieces, late_grad)
    wide_sums, narrow_sums, grad_head = lax.optimization_barrier((wide_sums, narrow_sums, grad_head))

    summed = pl.pallas_call(
        functools.partial(first_sum_kernel, layers),
        in_specs=[vmem_spec()] * (CHIPS + layers),
        out_specs=[vmem_spec()] * (CHIPS + layers),
        out_shape=[jax.ShapeDtypeStruct((CORES, rows, sizes[0]), bf16 if k else f32) for k in range(layers)]
        + [jax.ShapeDtypeStruct((CORES, rows, sizes[1]), bf16 if j else f32) for j in range(CHIPS)],
        compiler_params=kernel_params(),
        cost_estimate=LIGHT,
        name="first_sum",
    )(partial[0], *wide_sums, partial[CHIPS], *narrow_sums)
    wide_sums = [shift(summed[k], k * GROUP) for k in range(1, layers)]
    narrow_sums = [shift(summed[layers + j], j * CORES) for j in range(1, CHIPS)]
    mine, theirs = pl.pallas_call(
        functools.partial(last_sum_kernel, layers),
        in_specs=[vmem_spec()] * (CHIPS + layers),
        out_specs=[vmem_spec()] * 2,
        out_shape=[jax.ShapeDtypeStruct((rows, half), bf16)] * 2,
        compiler_params=kernel_params(),
        cost_estimate=LIGHT,
        name="last_sum",
    )(summed[0], *wide_sums, summed[layers], *narrow_sums)
    other = shift(theirs, 1)

    low, high = jnp.where(core == 0, mine, other), jnp.where(core == 0, other, mine)
    return loss[:, 0], grad_head, jnp.concatenate([low, high], axis=1)


def fits_levels(hidden_states, teacher_logits):
    n = lax.axis_size("vocab")
    rows = hidden_states.shape[0]
    blocks, _, stored, side = teacher_logits.shape
    return (
        n == blocks * GROUP
        and blocks & (blocks - 1) == 0
        and rows * GROUP == side
        and rows % 16 == 0
        and 2 * n <= side
        and 6 * blocks * stored <= side
        and hidden_states.shape[1] % (CORES * 1280) == 0
    )


def on_device(
    hidden_states, head_weight, teacher_logits, block_lists, row_reader, tail_mass, token_weight
):
    plan = levels_plan if fits_levels(hidden_states, teacher_logits) else plain_plan
    return plan(
        hidden_states, head_weight, teacher_logits, block_lists, row_reader, tail_mass, token_weight
    )


def solution(mesh):
    in_specs = (
        P("vocab", None),
        P(None, "vocab"),
        P(None, None, "vocab", None),
        P(),
        P(),
        P(),
        P(),
    )
    out_specs = (P("vocab"), P(None, "vocab"), P("vocab", None))
    return jax.shard_map(
        on_device, mesh=mesh, in_specs=in_specs, out_specs=out_specs, check_vma=False
    )
```

```python
import functools

import jax
import jax.numpy as jnp
from jax import lax
from jax.experimental import pallas as pl
from jax.experimental.pallas import tpu as pltpu
from jax.sharding import PartitionSpec as P


def row_parts(scores, teacher_slab, listed_mask, student_exp, teacher_exp):
    return (
        jnp.sum(student_exp, axis=(2, 3)),
        jnp.sum(teacher_exp, axis=(2, 3)),
        jnp.sum(teacher_exp * scores, axis=(2, 3)),
        jnp.sum(teacher_exp * teacher_slab, axis=(2, 3)),
        jnp.sum(scores, axis=(2, 3)),
        jnp.sum(jnp.where(listed_mask, scores, 0.0), axis=(2, 3)),
    )


def plain_plan(
    hidden_states, head_weight, teacher_logits, block_lists, row_reader, tail_mass, token_weight
):
    blocks, listed_count, stored_rows, block_side = teacher_logits.shape
    slab_width = head_weight.shape[1]
    slab_blocks = slab_width // block_side
    devices = lax.axis_size("vocab")
    rank_self = lax.axis_index("vocab")
    tokens = blocks * block_side
    shard_rows = hidden_states.shape[0]
    gathered = lax.all_gather(hidden_states, "vocab", axis=0, tiled=True)
    logits = jnp.dot(gathered, head_weight, preferred_element_type=jnp.float32)
    owner_dev = block_lists // slab_blocks
    owned_here = owner_dev == rank_self
    within = block_lists - rank_self * slab_blocks
    token_iota = lax.broadcasted_iota(jnp.int32, (1, block_side, block_side), 1)
    token_map = (row_reader[:, None, :] == token_iota).astype(jnp.bfloat16)
    place_iota = lax.broadcasted_iota(jnp.int32, (1, slab_blocks, 1), 1)
    block_iota = lax.broadcasted_iota(jnp.int32, (1, devices * slab_blocks, 1), 1)
    picker = (block_lists[:, None, :] == block_iota).astype(jnp.bfloat16)
    outgoing = jnp.einsum(
        "tnk,tkrc->tnrc", picker, teacher_logits, preferred_element_type=jnp.float32
    ).astype(jnp.bfloat16)
    incoming = lax.all_to_all(outgoing, "vocab", split_axis=1, concat_axis=2, tiled=True)
    teacher_slab = jnp.einsum(
        "tpj,tbjc->tpbc", token_map, incoming, preferred_element_type=jnp.float32
    )
    listed = jnp.sum(
        ((within[:, None, :] == place_iota) & owned_here[:, None, :]).astype(jnp.int32), axis=2
    )
    scores = logits.reshape(blocks, block_side, slab_blocks, block_side)
    listed_mask = (listed > 0)[:, None, :, None]
    local_smax = jnp.max(scores, axis=(2, 3))
    local_tmax = jnp.max(jnp.where(listed_mask, teacher_slab, -1e30), axis=(2, 3))
    student_max, teacher_max = lax.pmax((local_smax, local_tmax), "vocab")
    student_exp = jnp.exp(scores - student_max[:, :, None, None])
    teacher_exp = jnp.exp(
        jnp.where(listed_mask, teacher_slab - teacher_max[:, :, None, None], -jnp.inf)
    )
    parts = row_parts(scores, teacher_slab, listed_mask, student_exp, teacher_exp)
    student_sum, teacher_sum, cross_sum, self_sum, logit_total, listed_total = lax.psum(
        (parts[0], parts[1], parts[2], parts[3], parts[4], parts[5]), "vocab"
    )
    tail_share = tail_mass.reshape(blocks, block_side)
    unlisted = float(devices * slab_width - block_side * listed_count)
    kept_mass = 1.0 - tail_share
    log_norm = student_max + jnp.log(student_sum)
    row_loss = (
        kept_mass * (jnp.log(kept_mass) - teacher_max - jnp.log(teacher_sum))
        + kept_mass * self_sum / teacher_sum
        + tail_share * jnp.log(tail_share / unlisted)
        - kept_mass * cross_sum / teacher_sum
        - tail_share / unlisted * (logit_total - listed_total)
        + log_norm
    )
    token_loss = lax.dynamic_slice_in_dim(
        row_loss.reshape(tokens), rank_self * shard_rows, shard_rows, 0
    )
    student_prob = student_exp / student_sum[:, :, None, None]
    teacher_prob = jnp.where(
        listed_mask,
        (kept_mass / teacher_sum)[:, :, None, None] * teacher_exp,
        (tail_share / unlisted)[:, :, None, None],
    )
    weight = token_weight.reshape(blocks, block_side)[:, :, None, None]
    grad_logits = (
        (weight * (student_prob - teacher_prob)).astype(jnp.bfloat16).reshape(tokens, slab_width)
    )
    grad_head = lax.dot_general(
        gathered, grad_logits, (((0,), (0,)), ((), ())), preferred_element_type=jnp.float32
    ).astype(jnp.bfloat16)
    grad_hidden = lax.psum_scatter(
        lax.dot_general(
            grad_logits, head_weight, (((1,), (1,)), ((), ())), preferred_element_type=jnp.float32
        ),
        "vocab",
        scatter_dimension=0,
        tiled=True,
    ).astype(jnp.bfloat16)
    return (token_loss, grad_head, grad_hidden)


CORES = 2
CHIPS = 4
GROUP = CORES * CHIPS
SLOTS = 4
LIGHT = pl.CostEstimate(flops=1, bytes_accessed=1, transcendentals=0)
SMALL_VMEM = 16 * 1024 * 1024
LOGITS_VMEM = 40 * 1024 * 1024
PARTIAL_VMEM = 42 * 1024 * 1024
LARGE_VMEM = 48 * 1024 * 1024
STAT_ROWS = 16


def kernel_params(limit=SMALL_VMEM):
    return pltpu.CompilerParams(vmem_limit_bytes=limit)


def vmem_spec():
    return pl.BlockSpec(memory_space=pltpu.VMEM)


def hbm_spec():
    return pl.BlockSpec(memory_space=pltpu.HBM)


def smem_spec():
    return pl.BlockSpec(memory_space=pltpu.SMEM)


def shift(x, distance):
    n = lax.axis_size("vocab")
    return lax.ppermute(x, "vocab", [(i, i ^ distance) for i in range(n)])


def token_places(place, rows, side):
    row = lax.broadcasted_iota(jnp.int32, (side, 1), 0)
    group = row // rows
    chip = (group % CHIPS) ^ place[1]
    core = (group // CHIPS) ^ place[0]
    return (chip * CORES + core) * rows + row % rows


def pick_column(match, values):
    return jnp.sum(jnp.where(match, values, 0.0), axis=1, keepdims=True)


def teacher_kernel(
    unlisted, rows, pos_ref, place_ref, arrived_ref, reader_ref, tail_ref, prob_ref, entropy_ref
):
    devices, size, side = arrived_ref.shape
    blocks = reader_ref.shape[0]
    stored = side // devices
    per_block = SLOTS * stored
    layers = blocks
    pos = [pos_ref[i] for i in range(3)]
    lane = lax.broadcasted_iota(jnp.int32, (1, side), 1)
    sender_lane = lax.broadcasted_iota(jnp.int32, (1, devices), 1)
    row_lane = lax.broadcasted_iota(jnp.int32, (1, devices * per_block), 1)
    where_token = token_places(pos, rows, side)
    parts = [arrived_ref[:, size - 3 + i, :] for i in range(3)]
    for k in range(layers):
        block = pos[2] ^ k
        stored_row = jnp.sum(jnp.where(reader_ref[block] == where_token, lane, 0), axis=1, keepdims=True)
        sender, row = stored_row // stored, stored_row % stored
        from_sender = jnp.where(sender_lane == sender, 1.0, 0.0).astype(jnp.bfloat16)
        stat = sum(jnp.dot(from_sender, part, preferred_element_type=jnp.float32) for part in parts)
        normaliser = pick_column(lane == block * stored + row, stat)
        tail = pick_column(lane == where_token, tail_ref[block])
        kept = 1.0 - tail
        rest = tail / unlisted
        span = pl.ds(k * side, side)
        prob_ref[span, :] = jnp.broadcast_to(rest, (side, prob_ref.shape[1]))
        all_rows = arrived_ref[:, pl.ds(pl.multiple_of(block * per_block, per_block), per_block), :]
        all_rows = all_rows.reshape(devices * per_block, side)
        for s in range(SLOTS):
            place = place_ref[block, s]
            onehot = jnp.where(row_lane == sender * per_block + s * stored + row, 1.0, 0.0)
            values = jnp.dot(onehot.astype(jnp.bfloat16), all_rows, preferred_element_type=jnp.float32)
            prob = kept * jnp.exp(values - normaliser)

            @pl.when(place >= 0)
            def _():
                prob_ref[span, pl.ds(pl.multiple_of(place * side, side), side)] = prob

        if k == 0:
            mean = pick_column(lane == (blocks + block) * stored + row, stat)
            entropy = kept * (jnp.log(kept) - normaliser + mean) + tail * jnp.log(rest)
            entropy_ref[...] = jnp.broadcast_to(entropy[:rows], entropy_ref.shape)


def assemble(pieces, rows, out_ref):
    per_core = len(pieces) // CORES
    layers = pieces[0].shape[0] // rows
    for core in range(CORES):
        mine = pieces[core * per_core : (core + 1) * per_core]
        for k in range(layers):
            span = pl.ds(k * rows, rows)
            for j, piece in enumerate(mine[:CHIPS]):
                at = pl.ds((k * GROUP + core * CHIPS + j) * rows, rows)
                columns = slice(0, piece.shape[1])
                out_ref[at, columns] = piece[span, :]
            if per_core > CHIPS:
                piece = mine[CHIPS]
                columns = slice(out_ref.shape[1] - piece.shape[1], out_ref.shape[1])
                out_ref[at, columns] = piece[span, :]


def cut_kernel(x_ref, y_ref, low_ref, high_ref):
    half = low_ref.shape[1]
    low_ref[...] = x_ref[:, :half]
    high_ref[...] = y_ref[:, half:]


def logits_kernel(rows, *refs):
    pieces, refs = refs[:-8], refs[-8:]
    w_ref, prob_ref, logits_ref, stat_ref, hidden, weight, sems, cross_ref = refs
    depth, width = w_ref.shape[0], prob_ref.shape[1]
    parts = [slice(0, depth // 4), slice(depth // 4, depth)]
    tiles = w_ref.shape[1] // width
    step = pl.program_id(0)

    def copy(i):
        span = pl.ds(parts[i].start, parts[i].stop - parts[i].start)
        return pltpu.make_async_copy(w_ref.at[span, :], weight.at[span, :], sems.at[i])

    @pl.when(step == 0)
    def _():
        copy(0).start()
        copy(1).start()
        assemble(pieces, rows, hidden)
        copy(0).wait()

    @pl.when(step == tiles)
    def _():
        copy(1).wait()

    @pl.when(step < tiles)
    def _():
        span = pl.ds(pl.multiple_of(step * width, width), width)
        logits_ref[:, span] = jnp.dot(
            hidden[:, parts[0]], weight[parts[0], span], preferred_element_type=jnp.float32
        )

    @pl.when(step >= tiles)
    def _():
        span = pl.ds(pl.multiple_of((step - tiles) * width, width), width)
        total = logits_ref[:, span] + jnp.dot(
            hidden[:, parts[1]], weight[parts[1], span], preferred_element_type=jnp.float32
        )
        logits_ref[:, span] = total
        product = total * prob_ref[...]
        folded = product[:, :128]
        for i in range(1, width // 128):
            folded = folded + product[:, i * 128 : (i + 1) * 128]
        cross_ref[...] = jnp.where(step == tiles, 0.0, cross_ref[...]) + folded

    @pl.when(step == 2 * tiles - 1)
    def _():
        logits = logits_ref[...]
        top = jnp.max(logits, axis=1, keepdims=True)
        norm = top + jnp.log(jnp.sum(jnp.exp(logits - top), axis=1, keepdims=True))
        cross = jnp.sum(cross_ref[...], axis=1, keepdims=True)
        lane = lax.broadcasted_iota(jnp.int32, (1, 128), 1)
        both = jnp.where(lane == 0, norm, jnp.where(lane == 1, cross, 0.0)).T
        tokens = logits.shape[0]
        packed = [both[i : i + 1, t : t + 128] for i in range(2) for t in range(0, tokens, 128)]
        stat_ref[...] = jnp.broadcast_to(jnp.concatenate(packed, axis=0)[None], stat_ref.shape)


def grad_kernel(
    rows, pos_ref, stat_ref, logits_ref, prob_ref, weight_ref, entropy_ref, grad_ref, loss_ref
):
    tokens = logits_ref.shape[0]
    devices = tokens // rows
    layers, _, side = weight_ref.shape
    layer_bits = (devices // GROUP).bit_length() - 1
    pos = [pos_ref[i] for i in range(3)]
    rank = pos_ref[3]
    lane = lax.broadcasted_iota(jnp.int32, (1, 128), 1)
    per_stat = stat_ref.shape[1] // 2
    norms, crosses = [
        jnp.concatenate([stat_ref[:, i * per_stat + t, :] for t in range(per_stat)], axis=1) for i in range(2)
    ]
    stat = jnp.concatenate(
        [norms, crosses, jnp.zeros((128 - 2 * devices, tokens), jnp.float32)], axis=0
    ).T
    pairs = [(0, 2), (1, 0), (2, 1)] + [(3 + i, 3 + i) for i in range(layer_bits)]
    for index_bit, block_bit in pairs:
        halves = stat.reshape(devices >> (block_bit + 1), 2, rows << block_bit, 128)
        swapped = jnp.stack([halves[:, 1], halves[:, 0]], axis=1).reshape(tokens, 128)
        stat = jnp.where(((lane ^ rank) >> index_bit) & 1 == 1, swapped, stat)
    is_norm = lane < devices
    is_cross = (lane >= devices) & (lane < 2 * devices)
    top = jnp.max(jnp.where(is_norm, stat, -jnp.inf), axis=1, keepdims=True)
    total = jnp.sum(jnp.where(is_norm, jnp.exp(stat - top), 0.0), axis=1, keepdims=True)
    log_norm = top + jnp.log(total)
    cross = jnp.sum(jnp.where(is_cross, stat, 0.0), axis=1, keepdims=True)
    loss_ref[...] = entropy_ref[...] - cross[:rows] + log_norm[:rows]
    where_token = token_places(pos, rows, side)
    for k in range(layers):
        span = pl.ds(k * side, side)
        weight = pick_column(lane == where_token, weight_ref[pos[2] ^ k])
        student = jnp.exp(logits_ref[span, :] - log_norm[k * side : (k + 1) * side])
        grad_ref[span, :] = (weight * (student - prob_ref[span, :])).astype(grad_ref.dtype)


def partial_kernel(rows, core_ref, grad_ref, sib_ref, w_ref, sib_w_ref, *refs):
    outs, swapped = refs[:-1], refs[-1]
    wide_outs, narrow_outs = outs[:CHIPS], outs[CHIPS:]
    layers = len(narrow_outs)
    half = CHIPS * rows
    step = pl.program_id(0)

    @pl.when(step == 0)
    def _():
        for k in range(layers):
            for core in range(CORES):
                swapped[pl.ds((k * CORES + core) * half, half), :] = sib_ref[
                    pl.ds((k * CORES + 1 - core) * half, half), :
                ]

    contract = (((1,), (1,)), ((), ()))
    total = lax.dot_general(
        grad_ref[...], w_ref[...], contract, preferred_element_type=jnp.float32
    ) + lax.dot_general(swapped[...], sib_w_ref[...], contract, preferred_element_type=jnp.float32)

    def store(outs, by_layer, columns, source):
        for k in range(layers):
            for core in range(CORES):
                for j in range(CHIPS):
                    start = (k * GROUP + core * CHIPS + j) * rows
                    out, i = (outs[k], j) if by_layer else (outs[j], k)
                    out[i, core, :, columns] = total[start : start + rows, source].astype(out.dtype)

    tile = w_ref.shape[0]
    wide = wide_outs[0].shape[-1]
    whole_steps, rest = wide // tile, wide % tile
    everything = slice(0, tile)

    @pl.when(step < whole_steps)
    def _():
        store(wide_outs, False, pl.ds(pl.multiple_of(step * tile, tile), tile), everything)

    if rest:

        @pl.when(step == whole_steps)
        def _():
            store(wide_outs, False, slice(whole_steps * tile, wide), slice(0, rest))
            store(narrow_outs, True, slice(0, tile - rest), slice(rest, tile))

    first = whole_steps + 1 if rest else whole_steps
    offset = tile - rest if rest else 0

    @pl.when(step >= first)
    def _():
        columns = pl.ds(pl.multiple_of(offset + (step - first) * tile, 128), tile)
        store(narrow_outs, True, columns, everything)


def head_kernel(rows, *refs):
    pieces, (grad_ref, out_ref, hidden) = refs[:-3], refs[-3:]
    per_core = CHIPS + 1
    late = pl.program_id(0) >= pl.num_programs(0) // 2
    for i in range(2):

        @pl.when(late == (i == 1))
        def _():
            mine = [pieces[c * per_core : (c + 1) * per_core] for c in range(CORES)]
            assemble([p for some in mine for p in (*some[: CHIPS - 1], some[CHIPS - 1 + i])], rows, hidden)

    out_ref[...] = lax.dot_general(
        hidden[...], grad_ref[...], (((0,), (0,)), ((), ())), preferred_element_type=jnp.float32
    ).astype(out_ref.dtype)


def sum_of(parts, index=...):
    total = parts[0][index]
    for part in parts[1:]:
        total = total + part[index].astype(jnp.float32)
    return total


def first_sum_kernel(layers, *refs):
    wide, narrow, outs = refs[:CHIPS], refs[CHIPS : CHIPS + layers], refs[CHIPS + layers :]
    for k, out in enumerate(outs[:layers]):
        out[...] = sum_of(wide, k).astype(out.dtype)
    for j, out in enumerate(outs[layers:]):
        out[...] = sum_of(narrow, j).astype(out.dtype)


def last_sum_kernel(layers, *refs):
    wide, narrow, (mine, theirs) = refs[:layers], refs[layers:-2], refs[-2:]
    split = wide[0].shape[-1]
    for parts, columns in ((wide, slice(0, split)), (narrow, slice(split, mine.shape[1]))):
        total = sum_of(parts)
        mine[:, columns] = total[0].astype(mine.dtype)
        theirs[:, columns] = total[1].astype(theirs.dtype)


def pack_kernel(code_ref, x_ref, out_ref):
    blocks, count, side = x_ref.shape
    devices, size, _ = out_ref.shape
    slot_rows = (size - STAT_ROWS) // blocks
    stored = slot_rows // SLOTS
    target = lax.broadcasted_iota(jnp.int32, (devices * slot_rows, 1), 0)
    row = lax.broadcasted_iota(jnp.int32, (count, 1), 0) % stored
    lane = lax.broadcasted_iota(jnp.int32, (1, side), 1)
    stat = jnp.zeros((1, side), jnp.float32)
    for t in range(blocks):
        onehot = jnp.where(code_ref[t] == target, 1.0, 0.0).astype(x_ref.dtype)
        packed = jnp.dot(onehot, x_ref[t], preferred_element_type=jnp.float32).astype(out_ref.dtype)
        for device in range(devices):
            out_ref[device, pl.ds(t * slot_rows, slot_rows), :] = packed[
                device * slot_rows : (device + 1) * slot_rows
            ]
        values = x_ref[t].astype(jnp.float32)
        row_top = jnp.max(values, axis=1, keepdims=True)
        tops = [jnp.max(jnp.where(row == r, row_top, -jnp.inf), axis=0, keepdims=True) for r in range(stored)]
        top = jnp.zeros_like(row_top)
        for r in range(stored):
            top = jnp.where(row == r, tops[r], top)
        powers = jnp.exp(values - top)
        sums = jnp.sum(powers, axis=1, keepdims=True)
        weighted = jnp.sum(powers * values, axis=1, keepdims=True)
        for r in range(stored):
            total = jnp.sum(jnp.where(row == r, sums, 0.0), axis=0, keepdims=True)
            mean = jnp.sum(jnp.where(row == r, weighted, 0.0), axis=0, keepdims=True) / total
            stat = jnp.where(lane == t * stored + r, tops[r] + jnp.log(total), stat)
            stat = jnp.where(lane == (blocks + t) * stored + r, mean, stat)
    high = stat.astype(jnp.bfloat16).astype(jnp.float32)
    middle = (stat - high).astype(jnp.bfloat16).astype(jnp.float32)
    low = stat - high - middle
    parts = jnp.concatenate([high, middle, low, jnp.zeros((STAT_ROWS - 3, side), jnp.float32)], axis=0)
    parts = parts.astype(out_ref.dtype)
    for device in range(devices):
        out_ref[device, pl.ds(size - STAT_ROWS, STAT_ROWS), :] = parts


def pack_teacher(teacher_logits, block_lists, places):
    blocks, listed_count, stored, side = teacher_logits.shape
    n = lax.axis_size("vocab")
    rank = lax.axis_index("vocab")
    owner = block_lists // places
    earlier = jnp.tril(jnp.ones((listed_count, listed_count), jnp.bool_), -1)
    slot = jnp.sum((owner[:, :, None] == owner[:, None, :]) & earlier, axis=2, dtype=jnp.int32)
    code = owner * SLOTS + slot
    rows_code = (code[:, :, None] * stored + jnp.arange(stored, dtype=jnp.int32)).reshape(blocks, 1, -1)
    payload = pl.pallas_call(
        pack_kernel,
        in_specs=[vmem_spec()] * 2,
        out_specs=vmem_spec(),
        out_shape=jax.ShapeDtypeStruct(
            (n, blocks * SLOTS * stored + STAT_ROWS, side), teacher_logits.dtype
        ),
        compiler_params=kernel_params(),
        cost_estimate=LIGHT,
        name="pack_teacher",
    )(rows_code, teacher_logits.reshape(blocks, listed_count * stored, side))
    mine = code[:, None, :] == rank * SLOTS + jnp.arange(SLOTS, dtype=jnp.int32)[None, :, None]
    place = jnp.sum(jnp.where(mine, (block_lists % places + 1)[:, None, :], 0), axis=2) - 1
    return payload, place.astype(jnp.int32)


def levels_plan(
    hidden_states, head_weight, teacher_logits, block_lists, row_reader, tail_mass, token_weight
):
    blocks, listed_count, stored, side = teacher_logits.shape
    rows, depth = hidden_states.shape
    slab = head_weight.shape[1]
    n = lax.axis_size("vocab")
    rank = lax.axis_index("vocab")
    tokens = n * rows
    layers = n // GROUP
    half = depth // CORES
    bf16, f32 = jnp.bfloat16, jnp.float32
    core, chip, layer = rank % CORES, (rank // CORES) % CHIPS, rank // GROUP
    pos = jnp.stack([core, chip, layer, rank]).astype(jnp.int32)
    unlisted = float(n * slab - side * listed_count)

    column = [hidden_states] + [shift(hidden_states, k * GROUP) for k in range(1, layers)]
    column = jnp.concatenate(column, axis=0)
    X, Y = CORES, 2 * CORES
    plane = [column, shift(column, X), shift(column, Y)]
    low, high = pl.pallas_call(
        cut_kernel,
        in_specs=[vmem_spec()] * 2,
        out_specs=[vmem_spec()] * 2,
        out_shape=[jax.ShapeDtypeStruct((layers * rows, half), bf16)] * 2,
        compiler_params=kernel_params(),
        cost_estimate=LIGHT,
        name="cut_halves",
    )(plane[1], plane[2])
    plane += [shift(low, Y), shift(high, X)]
    payload, place = pack_teacher(teacher_logits, block_lists, slab // side)
    sent_w = lax.dynamic_slice(head_weight, ((1 - core) * half, 0), (half, slab))
    payload, sent_w = lax.optimization_barrier((payload[:, : 3 - STAT_ROWS], sent_w))
    arrived = lax.all_to_all(
        payload, "vocab", split_axis=0, concat_axis=0, tiled=True
    )

    prob, entropy = pl.pallas_call(
        lambda *refs: teacher_kernel(unlisted, rows, *refs),
        out_shape=(
            jax.ShapeDtypeStruct((tokens, slab), f32),
            jax.ShapeDtypeStruct((rows, side), f32),
        ),
        in_specs=[smem_spec(), smem_spec()] + [vmem_spec()] * 3,
        out_specs=(vmem_spec(), vmem_spec()),
        compiler_params=kernel_params(),
        cost_estimate=LIGHT,
        name="teacher_prob",
    )(
        pos,
        place,
        arrived,
        row_reader.reshape(blocks, 1, side),
        tail_mass.reshape(blocks, 1, side),
    )

    plane[-2], plane[-1], prob = lax.optimization_barrier((plane[-2], plane[-1], prob))
    pieces = plane + [shift(piece, 1) for piece in plane]
    pieces, sent_w = lax.optimization_barrier((pieces, sent_w))
    sib_w = shift(sent_w, 1)

    width = 512 if slab % 512 == 0 else 128
    tiles = slab // width
    whole = lambda t: (0, 0)
    logits, stat = pl.pallas_call(
        functools.partial(logits_kernel, rows),
        grid=(2 * tiles,),
        out_shape=[
            jax.ShapeDtypeStruct((tokens, slab), f32),
            jax.ShapeDtypeStruct((n, 2 * tokens // 128, 128), f32),
        ],
        in_specs=[vmem_spec()] * len(pieces)
        + [hbm_spec(), pl.BlockSpec((tokens, width), lambda t: (0, jnp.maximum(t - tiles, 0)))],
        out_specs=[vmem_spec()] * 2,
        scratch_shapes=[
            pltpu.VMEM((tokens, depth), bf16),
            pltpu.VMEM((depth, slab), bf16),
            pltpu.SemaphoreType.DMA((2,)),
            pltpu.VMEM((tokens, 128), f32),
        ],
        compiler_params=kernel_params(LOGITS_VMEM),
        cost_estimate=LIGHT,
        name="logits",
    )(*pieces, head_weight, prob)
    stat = lax.all_to_all(stat, "vocab", split_axis=0, concat_axis=0, tiled=True)

    grad, loss = pl.pallas_call(
        lambda *refs: grad_kernel(rows, *refs),
        out_shape=(
            jax.ShapeDtypeStruct((tokens, slab), bf16),
            jax.ShapeDtypeStruct((rows, side), f32),
        ),
        in_specs=[smem_spec()] + [vmem_spec()] * 5,
        out_specs=(vmem_spec(), vmem_spec()),
        compiler_params=kernel_params(),
        cost_estimate=LIGHT,
        name="grad_logits",
    )(pos, stat, logits, prob, token_weight.reshape(blocks, 1, side), entropy)
    sib_grad = shift(grad, 1)

    tile = half // 5
    sizes = (half * 7 // 10, half - half * 7 // 10)
    partial = pl.pallas_call(
        functools.partial(partial_kernel, rows),
        grid_spec=pltpu.PrefetchScalarGridSpec(
            num_scalar_prefetch=1,
            grid=(5,),
            in_specs=[vmem_spec()] * 2
            + [pl.BlockSpec((tile, slab), lambda t, pos: (pos[0] * 5 + t, 0))]
            + [pl.BlockSpec((tile, slab), lambda t, pos: (t, 0))],
            out_specs=[vmem_spec()] * (CHIPS + layers),
            scratch_shapes=[pltpu.VMEM((tokens, slab), bf16)],
        ),
        out_shape=[
            jax.ShapeDtypeStruct((layers, CORES, rows, sizes[0]), bf16 if j else f32) for j in range(CHIPS)
        ]
        + [jax.ShapeDtypeStruct((CHIPS, CORES, rows, sizes[1]), bf16 if k else f32) for k in range(layers)],
        compiler_params=kernel_params(PARTIAL_VMEM),
        cost_estimate=LIGHT,
        name="grad_hidden_partial",
    )(pos, grad, sib_grad, head_weight, sib_w)
    *partial, late_grad = lax.optimization_barrier((*partial, grad))
    wide_sums = [shift(partial[j], j * CORES) for j in range(1, CHIPS)]
    narrow_sums = [shift(partial[CHIPS + k], k * GROUP) for k in range(1, layers)]

    head_tile = half // 2
    grad_head = pl.pallas_call(
        functools.partial(head_kernel, rows),
        grid=(4,),
        in_specs=[
            pl.BlockSpec(
                (layers * rows, head_tile),
                lambda t, i=i % (CHIPS + 1): (0, (t, jnp.minimum(t, 1), jnp.maximum(t - 2, 0))[max(i - 2, 0)]),
            )
            for i in range(len(pieces))
        ]
        + [vmem_spec()],
        out_specs=pl.BlockSpec((head_tile, slab), lambda t: (t, 0)),
        out_shape=jax.ShapeDtypeStruct((depth, slab), bf16),
        scratch_shapes=[pltpu.VMEM((tokens, head_tile), bf16)],
        compiler_params=kernel_params(LARGE_VMEM),
        cost_estimate=LIGHT,
        name="grad_head",
    )(*pieces, late_grad)
    wide_sums, narrow_sums, grad_head = lax.optimization_barrier((wide_sums, narrow_sums, grad_head))

    summed = pl.pallas_call(
        functools.partial(first_sum_kernel, layers),
        in_specs=[vmem_spec()] * (CHIPS + layers),
        out_specs=[vmem_spec()] * (CHIPS + layers),
        out_shape=[jax.ShapeDtypeStruct((CORES, rows, sizes[0]), bf16 if k else f32) for k in range(layers)]
        + [jax.ShapeDtypeStruct((CORES, rows, sizes[1]), bf16 if j else f32) for j in range(CHIPS)],
        compiler_params=kernel_params(),
        cost_estimate=LIGHT,
        name="first_sum",
    )(partial[0], *wide_sums, partial[CHIPS], *narrow_sums)
    wide_sums = [shift(summed[k], k * GROUP) for k in range(1, layers)]
    narrow_sums = [shift(summed[layers + j], j * CORES) for j in range(1, CHIPS)]
    mine, theirs = pl.pallas_call(
        functools.partial(last_sum_kernel, layers),
        in_specs=[vmem_spec()] * (CHIPS + layers),
        out_specs=[vmem_spec()] * 2,
        out_shape=[jax.ShapeDtypeStruct((rows, half), bf16)] * 2,
        compiler_params=kernel_params(),
        cost_estimate=LIGHT,
        name="last_sum",
    )(summed[0], *wide_sums, summed[layers], *narrow_sums)
    other = shift(theirs, 1)

    low, high = jnp.where(core == 0, mine, other), jnp.where(core == 0, other, mine)
    return loss[:, 0], grad_head, jnp.concatenate([low, high], axis=1)


def fits_levels(hidden_states, teacher_logits):
    n = lax.axis_size("vocab")
    rows = hidden_states.shape[0]
    blocks, _, stored, side = teacher_logits.shape
    return (
        n == blocks * GROUP
        and blocks & (blocks - 1) == 0
        and rows * GROUP == side
        and rows % 16 == 0
        and 2 * n <= side
        and 6 * blocks * stored <= side
        and hidden_states.shape[1] % (CORES * 1280) == 0
    )


def on_device(
    hidden_states, head_weight, teacher_logits, block_lists, row_reader, tail_mass, token_weight
):
    plan = levels_plan if fits_levels(hidden_states, teacher_logits) else plain_plan
    return plan(
        hidden_states, head_weight, teacher_logits, block_lists, row_reader, tail_mass, token_weight
    )


def solution(mesh):
    in_specs = (
        P("vocab", None),
        P(None, "vocab"),
        P(None, None, "vocab", None),
        P(),
        P(),
        P(),
        P(),
    )
    out_specs = (P("vocab"), P(None, "vocab"), P("vocab", None))
    return jax.shard_map(
        on_device, mesh=mesh, in_specs=in_specs, out_specs=out_specs, check_vma=False
    )
```

```python
import functools

import jax
import jax.numpy as jnp
from jax import lax
from jax.experimental import pallas as pl
from jax.experimental.pallas import tpu as pltpu
from jax.sharding import PartitionSpec as P


def row_parts(scores, teacher_slab, listed_mask, student_exp, teacher_exp):
    return (
        jnp.sum(student_exp, axis=(2, 3)),
        jnp.sum(teacher_exp, axis=(2, 3)),
        jnp.sum(teacher_exp * scores, axis=(2, 3)),
        jnp.sum(teacher_exp * teacher_slab, axis=(2, 3)),
        jnp.sum(scores, axis=(2, 3)),
        jnp.sum(jnp.where(listed_mask, scores, 0.0), axis=(2, 3)),
    )


def plain_plan(
    hidden_states, head_weight, teacher_logits, block_lists, row_reader, tail_mass, token_weight
):
    blocks, listed_count, stored_rows, block_side = teacher_logits.shape
    slab_width = head_weight.shape[1]
    slab_blocks = slab_width // block_side
    devices = lax.axis_size("vocab")
    rank_self = lax.axis_index("vocab")
    tokens = blocks * block_side
    shard_rows = hidden_states.shape[0]
    gathered = lax.all_gather(hidden_states, "vocab", axis=0, tiled=True)
    logits = jnp.dot(gathered, head_weight, preferred_element_type=jnp.float32)
    owner_dev = block_lists // slab_blocks
    owned_here = owner_dev == rank_self
    within = block_lists - rank_self * slab_blocks
    token_iota = lax.broadcasted_iota(jnp.int32, (1, block_side, block_side), 1)
    token_map = (row_reader[:, None, :] == token_iota).astype(jnp.bfloat16)
    place_iota = lax.broadcasted_iota(jnp.int32, (1, slab_blocks, 1), 1)
    block_iota = lax.broadcasted_iota(jnp.int32, (1, devices * slab_blocks, 1), 1)
    picker = (block_lists[:, None, :] == block_iota).astype(jnp.bfloat16)
    outgoing = jnp.einsum(
        "tnk,tkrc->tnrc", picker, teacher_logits, preferred_element_type=jnp.float32
    ).astype(jnp.bfloat16)
    incoming = lax.all_to_all(outgoing, "vocab", split_axis=1, concat_axis=2, tiled=True)
    teacher_slab = jnp.einsum(
        "tpj,tbjc->tpbc", token_map, incoming, preferred_element_type=jnp.float32
    )
    listed = jnp.sum(
        ((within[:, None, :] == place_iota) & owned_here[:, None, :]).astype(jnp.int32), axis=2
    )
    scores = logits.reshape(blocks, block_side, slab_blocks, block_side)
    listed_mask = (listed > 0)[:, None, :, None]
    local_smax = jnp.max(scores, axis=(2, 3))
    local_tmax = jnp.max(jnp.where(listed_mask, teacher_slab, -1e30), axis=(2, 3))
    student_max, teacher_max = lax.pmax((local_smax, local_tmax), "vocab")
    student_exp = jnp.exp(scores - student_max[:, :, None, None])
    teacher_exp = jnp.exp(
        jnp.where(listed_mask, teacher_slab - teacher_max[:, :, None, None], -jnp.inf)
    )
    parts = row_parts(scores, teacher_slab, listed_mask, student_exp, teacher_exp)
    student_sum, teacher_sum, cross_sum, self_sum, logit_total, listed_total = lax.psum(
        (parts[0], parts[1], parts[2], parts[3], parts[4], parts[5]), "vocab"
    )
    tail_share = tail_mass.reshape(blocks, block_side)
    unlisted = float(devices * slab_width - block_side * listed_count)
    kept_mass = 1.0 - tail_share
    log_norm = student_max + jnp.log(student_sum)
    row_loss = (
        kept_mass * (jnp.log(kept_mass) - teacher_max - jnp.log(teacher_sum))
        + kept_mass * self_sum / teacher_sum
        + tail_share * jnp.log(tail_share / unlisted)
        - kept_mass * cross_sum / teacher_sum
        - tail_share / unlisted * (logit_total - listed_total)
        + log_norm
    )
    token_loss = lax.dynamic_slice_in_dim(
        row_loss.reshape(tokens), rank_self * shard_rows, shard_rows, 0
    )
    student_prob = student_exp / student_sum[:, :, None, None]
    teacher_prob = jnp.where(
        listed_mask,
        (kept_mass / teacher_sum)[:, :, None, None] * teacher_exp,
        (tail_share / unlisted)[:, :, None, None],
    )
    weight = token_weight.reshape(blocks, block_side)[:, :, None, None]
    grad_logits = (
        (weight * (student_prob - teacher_prob)).astype(jnp.bfloat16).reshape(tokens, slab_width)
    )
    grad_head = lax.dot_general(
        gathered, grad_logits, (((0,), (0,)), ((), ())), preferred_element_type=jnp.float32
    ).astype(jnp.bfloat16)
    grad_hidden = lax.psum_scatter(
        lax.dot_general(
            grad_logits, head_weight, (((1,), (1,)), ((), ())), preferred_element_type=jnp.float32
        ),
        "vocab",
        scatter_dimension=0,
        tiled=True,
    ).astype(jnp.bfloat16)
    return (token_loss, grad_head, grad_hidden)


CORES = 2
CHIPS = 4
GROUP = CORES * CHIPS
SLOTS = 4
LIGHT = pl.CostEstimate(flops=1, bytes_accessed=1, transcendentals=0)
SMALL_VMEM = 16 * 1024 * 1024
LOGITS_VMEM = 40 * 1024 * 1024
PARTIAL_VMEM = 42 * 1024 * 1024
LARGE_VMEM = 48 * 1024 * 1024
STAT_ROWS = 16


def kernel_params(limit=SMALL_VMEM):
    return pltpu.CompilerParams(vmem_limit_bytes=limit)


def vmem_spec():
    return pl.BlockSpec(memory_space=pltpu.VMEM)


def hbm_spec():
    return pl.BlockSpec(memory_space=pltpu.HBM)


def smem_spec():
    return pl.BlockSpec(memory_space=pltpu.SMEM)


def shift(x, distance):
    n = lax.axis_size("vocab")
    return lax.ppermute(x, "vocab", [(i, i ^ distance) for i in range(n)])


def token_places(place, rows, side):
    row = lax.broadcasted_iota(jnp.int32, (side, 1), 0)
    group = row // rows
    chip = (group % CHIPS) ^ place[1]
    core = (group // CHIPS) ^ place[0]
    return (chip * CORES + core) * rows + row % rows


def pick_column(match, values):
    return jnp.sum(jnp.where(match, values, 0.0), axis=1, keepdims=True)


def teacher_kernel(
    unlisted, rows, pos_ref, place_ref, arrived_ref, reader_ref, tail_ref, prob_ref, entropy_ref
):
    devices, size, side = arrived_ref.shape
    blocks = reader_ref.shape[0]
    stored = side // devices
    per_block = SLOTS * stored
    layers = blocks
    pos = [pos_ref[i] for i in range(3)]
    lane = lax.broadcasted_iota(jnp.int32, (1, side), 1)
    sender_lane = lax.broadcasted_iota(jnp.int32, (1, devices), 1)
    row_lane = lax.broadcasted_iota(jnp.int32, (1, devices * per_block), 1)
    where_token = token_places(pos, rows, side)
    parts = [arrived_ref[:, size - 3 + i, :] for i in range(3)]
    for k in range(layers):
        block = pos[2] ^ k
        stored_row = jnp.sum(jnp.where(reader_ref[block] == where_token, lane, 0), axis=1, keepdims=True)
        sender, row = stored_row // stored, stored_row % stored
        from_sender = jnp.where(sender_lane == sender, 1.0, 0.0).astype(jnp.bfloat16)
        stat = sum(jnp.dot(from_sender, part, preferred_element_type=jnp.float32) for part in parts)
        normaliser = pick_column(lane == block * stored + row, stat)
        tail = pick_column(lane == where_token, tail_ref[block])
        kept = 1.0 - tail
        rest = tail / unlisted
        span = pl.ds(k * side, side)
        prob_ref[span, :] = jnp.broadcast_to(rest, (side, prob_ref.shape[1]))
        all_rows = arrived_ref[:, pl.ds(pl.multiple_of(block * per_block, per_block), per_block), :]
        all_rows = all_rows.reshape(devices * per_block, side)
        for s in range(SLOTS):
            place = place_ref[block, s]
            onehot = jnp.where(row_lane == sender * per_block + s * stored + row, 1.0, 0.0)
            values = jnp.dot(onehot.astype(jnp.bfloat16), all_rows, preferred_element_type=jnp.float32)
            prob = kept * jnp.exp(values - normaliser)

            @pl.when(place >= 0)
            def _():
                prob_ref[span, pl.ds(pl.multiple_of(place * side, side), side)] = prob

        if k == 0:
            mean = pick_column(lane == (blocks + block) * stored + row, stat)
            entropy = kept * (jnp.log(kept) - normaliser + mean) + tail * jnp.log(rest)
            entropy_ref[...] = jnp.broadcast_to(entropy[:rows], entropy_ref.shape)


def assemble(pieces, rows, out_ref):
    per_core = len(pieces) // CORES
    layers = pieces[0].shape[0] // rows
    for core in range(CORES):
        mine = pieces[core * per_core : (core + 1) * per_core]
        for k in range(layers):
            span = pl.ds(k * rows, rows)
            for j, piece in enumerate(mine[:CHIPS]):
                at = pl.ds((k * GROUP + core * CHIPS + j) * rows, rows)
                columns = slice(0, piece.shape[1])
                out_ref[at, columns] = piece[span, :]
            if per_core > CHIPS:
                piece = mine[CHIPS]
                columns = slice(out_ref.shape[1] - piece.shape[1], out_ref.shape[1])
                out_ref[at, columns] = piece[span, :]


def cut_kernel(x_ref, y_ref, low_ref, high_ref):
    half = low_ref.shape[1]
    low_ref[...] = x_ref[:, :half]
    high_ref[...] = y_ref[:, half:]


def logits_kernel(rows, *refs):
    pieces, refs = refs[:-8], refs[-8:]
    w_ref, prob_ref, logits_ref, stat_ref, hidden, weight, sems, cross_ref = refs
    depth, width = w_ref.shape[0], prob_ref.shape[1]
    parts = [slice(0, depth // 4), slice(depth // 4, depth)]
    tiles = w_ref.shape[1] // width
    step = pl.program_id(0)

    def copy(i):
        span = pl.ds(parts[i].start, parts[i].stop - parts[i].start)
        return pltpu.make_async_copy(w_ref.at[span, :], weight.at[span, :], sems.at[i])

    @pl.when(step == 0)
    def _():
        copy(0).start()
        copy(1).start()
        assemble(pieces, rows, hidden)
        copy(0).wait()

    @pl.when(step == tiles)
    def _():
        copy(1).wait()

    @pl.when(step < tiles)
    def _():
        span = pl.ds(pl.multiple_of(step * width, width), width)
        logits_ref[:, span] = jnp.dot(
            hidden[:, parts[0]], weight[parts[0], span], preferred_element_type=jnp.float32
        )

    @pl.when(step >= tiles)
    def _():
        span = pl.ds(pl.multiple_of((step - tiles) * width, width), width)
        total = logits_ref[:, span] + jnp.dot(
            hidden[:, parts[1]], weight[parts[1], span], preferred_element_type=jnp.float32
        )
        logits_ref[:, span] = total
        product = total * prob_ref[...]
        folded = product[:, :128]
        for i in range(1, width // 128):
            folded = folded + product[:, i * 128 : (i + 1) * 128]
        cross_ref[...] = jnp.where(step == tiles, 0.0, cross_ref[...]) + folded

    @pl.when(step == 2 * tiles - 1)
    def _():
        logits = logits_ref[...]
        top = jnp.max(logits, axis=1, keepdims=True)
        norm = top + jnp.log(jnp.sum(jnp.exp(logits - top), axis=1, keepdims=True))
        cross = jnp.sum(cross_ref[...], axis=1, keepdims=True)
        lane = lax.broadcasted_iota(jnp.int32, (1, 128), 1)
        both = jnp.where(lane == 0, norm, jnp.where(lane == 1, cross, 0.0)).T
        tokens = logits.shape[0]
        packed = [both[i : i + 1, t : t + 128] for i in range(2) for t in range(0, tokens, 128)]
        stat_ref[...] = jnp.broadcast_to(jnp.concatenate(packed, axis=0)[None], stat_ref.shape)


def grad_kernel(
    rows, pos_ref, stat_ref, logits_ref, prob_ref, weight_ref, entropy_ref, grad_ref, loss_ref
):
    tokens = logits_ref.shape[0]
    devices = tokens // rows
    layers, _, side = weight_ref.shape
    layer_bits = (devices // GROUP).bit_length() - 1
    pos = [pos_ref[i] for i in range(3)]
    rank = pos_ref[3]
    lane = lax.broadcasted_iota(jnp.int32, (1, 128), 1)
    per_stat = stat_ref.shape[1] // 2
    norms, crosses = [
        jnp.concatenate([stat_ref[:, i * per_stat + t, :] for t in range(per_stat)], axis=1) for i in range(2)
    ]
    stat = jnp.concatenate(
        [norms, crosses, jnp.zeros((128 - 2 * devices, tokens), jnp.float32)], axis=0
    ).T
    pairs = [(0, 2), (1, 0), (2, 1)] + [(3 + i, 3 + i) for i in range(layer_bits)]
    for index_bit, block_bit in pairs:
        halves = stat.reshape(devices >> (block_bit + 1), 2, rows << block_bit, 128)
        swapped = jnp.stack([halves[:, 1], halves[:, 0]], axis=1).reshape(tokens, 128)
        stat = jnp.where(((lane ^ rank) >> index_bit) & 1 == 1, swapped, stat)
    is_norm = lane < devices
    is_cross = (lane >= devices) & (lane < 2 * devices)
    top = jnp.max(jnp.where(is_norm, stat, -jnp.inf), axis=1, keepdims=True)
    total = jnp.sum(jnp.where(is_norm, jnp.exp(stat - top), 0.0), axis=1, keepdims=True)
    log_norm = top + jnp.log(total)
    cross = jnp.sum(jnp.where(is_cross, stat, 0.0), axis=1, keepdims=True)
    loss_ref[...] = entropy_ref[...] - cross[:rows] + log_norm[:rows]
    where_token = token_places(pos, rows, side)
    for k in range(layers):
        span = pl.ds(k * side, side)
        weight = pick_column(lane == where_token, weight_ref[pos[2] ^ k])
        student = jnp.exp(logits_ref[span, :] - log_norm[k * side : (k + 1) * side])
        grad_ref[span, :] = (weight * (student - prob_ref[span, :])).astype(grad_ref.dtype)


def partial_kernel(rows, core_ref, grad_ref, sib_ref, w_ref, sib_w_ref, *refs):
    outs, swapped = refs[:-1], refs[-1]
    wide_outs, narrow_outs = outs[:CHIPS], outs[CHIPS:]
    layers = len(narrow_outs)
    half = CHIPS * rows
    step = pl.program_id(0)

    @pl.when(step == 0)
    def _():
        for k in range(layers):
            for core in range(CORES):
                swapped[pl.ds((k * CORES + core) * half, half), :] = sib_ref[
                    pl.ds((k * CORES + 1 - core) * half, half), :
                ]

    contract = (((1,), (1,)), ((), ()))
    total = lax.dot_general(
        grad_ref[...], w_ref[...], contract, preferred_element_type=jnp.float32
    ) + lax.dot_general(swapped[...], sib_w_ref[...], contract, preferred_element_type=jnp.float32)

    def store(outs, by_layer, columns, source):
        for k in range(layers):
            for core in range(CORES):
                for j in range(CHIPS):
                    start = (k * GROUP + core * CHIPS + j) * rows
                    out, i = (outs[k], j) if by_layer else (outs[j], k)
                    out[i, core, :, columns] = total[start : start + rows, source].astype(out.dtype)

    tile = w_ref.shape[0]
    wide = wide_outs[0].shape[-1]
    whole_steps, rest = wide // tile, wide % tile
    everything = slice(0, tile)

    @pl.when(step < whole_steps)
    def _():
        store(wide_outs, False, pl.ds(pl.multiple_of(step * tile, tile), tile), everything)

    if rest:

        @pl.when(step == whole_steps)
        def _():
            store(wide_outs, False, slice(whole_steps * tile, wide), slice(0, rest))
            store(narrow_outs, True, slice(0, tile - rest), slice(rest, tile))

    first = whole_steps + 1 if rest else whole_steps
    offset = tile - rest if rest else 0

    @pl.when(step >= first)
    def _():
        columns = pl.ds(pl.multiple_of(offset + (step - first) * tile, 128), tile)
        store(narrow_outs, True, columns, everything)


def head_kernel(rows, *refs):
    pieces, (grad_ref, out_ref, hidden) = refs[:-3], refs[-3:]
    per_core = CHIPS + 1
    late = pl.program_id(0) >= pl.num_programs(0) // 2
    for i in range(2):

        @pl.when(late == (i == 1))
        def _():
            mine = [pieces[c * per_core : (c + 1) * per_core] for c in range(CORES)]
            assemble([p for some in mine for p in (*some[: CHIPS - 1], some[CHIPS - 1 + i])], rows, hidden)

    out_ref[...] = lax.dot_general(
        hidden[...], grad_ref[...], (((0,), (0,)), ((), ())), preferred_element_type=jnp.float32
    ).astype(out_ref.dtype)


def sum_of(parts, index=...):
    total = parts[0][index]
    for part in parts[1:]:
        total = total + part[index].astype(jnp.float32)
    return total


def first_sum_kernel(layers, *refs):
    wide, narrow, outs = refs[:CHIPS], refs[CHIPS : CHIPS + layers], refs[CHIPS + layers :]
    for k, out in enumerate(outs[:layers]):
        out[...] = sum_of(wide, k).astype(out.dtype)
    for j, out in enumerate(outs[layers:]):
        out[...] = sum_of(narrow, j).astype(out.dtype)


def last_sum_kernel(layers, *refs):
    wide, narrow, (mine, theirs) = refs[:layers], refs[layers:-2], refs[-2:]
    split = wide[0].shape[-1]
    for parts, columns in ((wide, slice(0, split)), (narrow, slice(split, mine.shape[1]))):
        total = sum_of(parts)
        mine[:, columns] = total[0].astype(mine.dtype)
        theirs[:, columns] = total[1].astype(theirs.dtype)


def pack_kernel(code_ref, x_ref, out_ref):
    blocks, count, side = x_ref.shape
    devices, size, _ = out_ref.shape
    slot_rows = (size - STAT_ROWS) // blocks
    stored = slot_rows // SLOTS
    target = lax.broadcasted_iota(jnp.int32, (devices * slot_rows, 1), 0)
    row = lax.broadcasted_iota(jnp.int32, (count, 1), 0) % stored
    lane = lax.broadcasted_iota(jnp.int32, (1, side), 1)
    stat = jnp.zeros((1, side), jnp.float32)
    for t in range(blocks):
        onehot = jnp.where(code_ref[t] == target, 1.0, 0.0).astype(x_ref.dtype)
        packed = jnp.dot(onehot, x_ref[t], preferred_element_type=jnp.float32).astype(out_ref.dtype)
        for device in range(devices):
            out_ref[device, pl.ds(t * slot_rows, slot_rows), :] = packed[
                device * slot_rows : (device + 1) * slot_rows
            ]
        values = x_ref[t].astype(jnp.float32)
        row_top = jnp.max(values, axis=1, keepdims=True)
        tops = [jnp.max(jnp.where(row == r, row_top, -jnp.inf), axis=0, keepdims=True) for r in range(stored)]
        top = jnp.zeros_like(row_top)
        for r in range(stored):
            top = jnp.where(row == r, tops[r], top)
        powers = jnp.exp(values - top)
        sums = jnp.sum(powers, axis=1, keepdims=True)
        weighted = jnp.sum(powers * values, axis=1, keepdims=True)
        for r in range(stored):
            total = jnp.sum(jnp.where(row == r, sums, 0.0), axis=0, keepdims=True)
            mean = jnp.sum(jnp.where(row == r, weighted, 0.0), axis=0, keepdims=True) / total
            stat = jnp.where(lane == t * stored + r, tops[r] + jnp.log(total), stat)
            stat = jnp.where(lane == (blocks + t) * stored + r, mean, stat)
    high = stat.astype(jnp.bfloat16).astype(jnp.float32)
    middle = (stat - high).astype(jnp.bfloat16).astype(jnp.float32)
    low = stat - high - middle
    parts = jnp.concatenate([high, middle, low, jnp.zeros((STAT_ROWS - 3, side), jnp.float32)], axis=0)
    parts = parts.astype(out_ref.dtype)
    for device in range(devices):
        out_ref[device, pl.ds(size - STAT_ROWS, STAT_ROWS), :] = parts


def pack_teacher(teacher_logits, block_lists, places):
    blocks, listed_count, stored, side = teacher_logits.shape
    n = lax.axis_size("vocab")
    rank = lax.axis_index("vocab")
    owner = block_lists // places
    earlier = jnp.tril(jnp.ones((listed_count, listed_count), jnp.bool_), -1)
    slot = jnp.sum((owner[:, :, None] == owner[:, None, :]) & earlier, axis=2, dtype=jnp.int32)
    code = owner * SLOTS + slot
    rows_code = (code[:, :, None] * stored + jnp.arange(stored, dtype=jnp.int32)).reshape(blocks, 1, -1)
    payload = pl.pallas_call(
        pack_kernel,
        in_specs=[vmem_spec()] * 2,
        out_specs=vmem_spec(),
        out_shape=jax.ShapeDtypeStruct(
            (n, blocks * SLOTS * stored + STAT_ROWS, side), teacher_logits.dtype
        ),
        compiler_params=kernel_params(),
        cost_estimate=LIGHT,
        name="pack_teacher",
    )(rows_code, teacher_logits.reshape(blocks, listed_count * stored, side))
    mine = code[:, None, :] == rank * SLOTS + jnp.arange(SLOTS, dtype=jnp.int32)[None, :, None]
    place = jnp.sum(jnp.where(mine, (block_lists % places + 1)[:, None, :], 0), axis=2) - 1
    return payload, place.astype(jnp.int32)


def levels_plan(
    hidden_states, head_weight, teacher_logits, block_lists, row_reader, tail_mass, token_weight
):
    blocks, listed_count, stored, side = teacher_logits.shape
    rows, depth = hidden_states.shape
    slab = head_weight.shape[1]
    n = lax.axis_size("vocab")
    rank = lax.axis_index("vocab")
    tokens = n * rows
    layers = n // GROUP
    half = depth // CORES
    bf16, f32 = jnp.bfloat16, jnp.float32
    core, chip, layer = rank % CORES, (rank // CORES) % CHIPS, rank // GROUP
    pos = jnp.stack([core, chip, layer, rank]).astype(jnp.int32)
    unlisted = float(n * slab - side * listed_count)

    column = [hidden_states] + [shift(hidden_states, k * GROUP) for k in range(1, layers)]
    column = jnp.concatenate(column, axis=0)
    X, Y = CORES, 2 * CORES
    plane = [column, shift(column, X), shift(column, Y)]
    sent_w = lax.dynamic_slice(head_weight, ((1 - core) * half, 0), (half, slab))
    plane[1], plane[2], sent_w = lax.optimization_barrier((plane[1], plane[2], sent_w))
    low, high = pl.pallas_call(
        cut_kernel,
        in_specs=[vmem_spec()] * 2,
        out_specs=[vmem_spec()] * 2,
        out_shape=[jax.ShapeDtypeStruct((layers * rows, half), bf16)] * 2,
        compiler_params=kernel_params(),
        cost_estimate=LIGHT,
        name="cut_halves",
    )(plane[1], plane[2])
    plane += [shift(low, Y), shift(high, X)]
    payload, place = pack_teacher(teacher_logits, block_lists, slab // side)
    arrived = lax.all_to_all(
        payload[:, : 3 - STAT_ROWS], "vocab", split_axis=0, concat_axis=0, tiled=True
    )

    prob, entropy = pl.pallas_call(
        lambda *refs: teacher_kernel(unlisted, rows, *refs),
        out_shape=(
            jax.ShapeDtypeStruct((tokens, slab), f32),
            jax.ShapeDtypeStruct((rows, side), f32),
        ),
        in_specs=[smem_spec(), smem_spec()] + [vmem_spec()] * 3,
        out_specs=(vmem_spec(), vmem_spec()),
        compiler_params=kernel_params(),
        cost_estimate=LIGHT,
        name="teacher_prob",
    )(
        pos,
        place,
        arrived,
        row_reader.reshape(blocks, 1, side),
        tail_mass.reshape(blocks, 1, side),
    )

    plane[-2], plane[-1], prob = lax.optimization_barrier((plane[-2], plane[-1], prob))
    pieces = plane + [shift(piece, 1) for piece in plane]
    pieces, sent_w = lax.optimization_barrier((pieces, sent_w))
    sib_w = shift(sent_w, 1)

    width = slab
    tiles = slab // width
    whole = lambda t: (0, 0)
    logits, stat = pl.pallas_call(
        functools.partial(logits_kernel, rows),
        grid=(2 * tiles,),
        out_shape=[
            jax.ShapeDtypeStruct((tokens, slab), f32),
            jax.ShapeDtypeStruct((n, 2 * tokens // 128, 128), f32),
        ],
        in_specs=[vmem_spec()] * len(pieces)
        + [hbm_spec(), pl.BlockSpec((tokens, width), lambda t: (0, jnp.maximum(t - tiles, 0)))],
        out_specs=[vmem_spec()] * 2,
        scratch_shapes=[
            pltpu.VMEM((tokens, depth), bf16),
            pltpu.VMEM((depth, slab), bf16),
            pltpu.SemaphoreType.DMA((2,)),
            pltpu.VMEM((tokens, 128), f32),
        ],
        compiler_params=kernel_params(LOGITS_VMEM),
        cost_estimate=LIGHT,
        name="logits",
    )(*pieces, head_weight, prob)
    stat = lax.all_to_all(stat, "vocab", split_axis=0, concat_axis=0, tiled=True)

    grad, loss = pl.pallas_call(
        lambda *refs: grad_kernel(rows, *refs),
        out_shape=(
            jax.ShapeDtypeStruct((tokens, slab), bf16),
            jax.ShapeDtypeStruct((rows, side), f32),
        ),
        in_specs=[smem_spec()] + [vmem_spec()] * 5,
        out_specs=(vmem_spec(), vmem_spec()),
        compiler_params=kernel_params(),
        cost_estimate=LIGHT,
        name="grad_logits",
    )(pos, stat, logits, prob, token_weight.reshape(blocks, 1, side), entropy)
    sib_grad = shift(grad, 1)

    tile = half // 5
    sizes = (half * 7 // 10, half - half * 7 // 10)
    partial = pl.pallas_call(
        functools.partial(partial_kernel, rows),
        grid_spec=pltpu.PrefetchScalarGridSpec(
            num_scalar_prefetch=1,
            grid=(5,),
            in_specs=[vmem_spec()] * 2
            + [pl.BlockSpec((tile, slab), lambda t, pos: (pos[0] * 5 + t, 0))]
            + [pl.BlockSpec((tile, slab), lambda t, pos: (t, 0))],
            out_specs=[vmem_spec()] * (CHIPS + layers),
            scratch_shapes=[pltpu.VMEM((tokens, slab), bf16)],
        ),
        out_shape=[
            jax.ShapeDtypeStruct((layers, CORES, rows, sizes[0]), bf16 if j else f32) for j in range(CHIPS)
        ]
        + [jax.ShapeDtypeStruct((CHIPS, CORES, rows, sizes[1]), bf16 if k else f32) for k in range(layers)],
        compiler_params=kernel_params(PARTIAL_VMEM),
        cost_estimate=LIGHT,
        name="grad_hidden_partial",
    )(pos, grad, sib_grad, head_weight, sib_w)
    *partial, late_grad = lax.optimization_barrier((*partial, grad))
    wide_sums = [shift(partial[j], j * CORES) for j in range(1, CHIPS)]
    narrow_sums = [shift(partial[CHIPS + k], k * GROUP) for k in range(1, layers)]

    head_tile = half // 2
    grad_head = pl.pallas_call(
        functools.partial(head_kernel, rows),
        grid=(4,),
        in_specs=[
            pl.BlockSpec(
                (layers * rows, head_tile),
                lambda t, i=i % (CHIPS + 1): (0, (t, jnp.minimum(t, 1), jnp.maximum(t - 2, 0))[max(i - 2, 0)]),
            )
            for i in range(len(pieces))
        ]
        + [vmem_spec()],
        out_specs=pl.BlockSpec((head_tile, slab), lambda t: (t, 0)),
        out_shape=jax.ShapeDtypeStruct((depth, slab), bf16),
        scratch_shapes=[pltpu.VMEM((tokens, head_tile), bf16)],
        compiler_params=kernel_params(LARGE_VMEM),
        cost_estimate=LIGHT,
        name="grad_head",
    )(*pieces, late_grad)
    wide_sums, narrow_sums, grad_head = lax.optimization_barrier((wide_sums, narrow_sums, grad_head))

    summed = pl.pallas_call(
        functools.partial(first_sum_kernel, layers),
        in_specs=[vmem_spec()] * (CHIPS + layers),
        out_specs=[vmem_spec()] * (CHIPS + layers),
        out_shape=[jax.ShapeDtypeStruct((CORES, rows, sizes[0]), bf16 if k else f32) for k in range(layers)]
        + [jax.ShapeDtypeStruct((CORES, rows, sizes[1]), bf16 if j else f32) for j in range(CHIPS)],
        compiler_params=kernel_params(),
        cost_estimate=LIGHT,
        name="first_sum",
    )(partial[0], *wide_sums, partial[CHIPS], *narrow_sums)
    wide_sums = [shift(summed[k], k * GROUP) for k in range(1, layers)]
    narrow_sums = [shift(summed[layers + j], j * CORES) for j in range(1, CHIPS)]
    mine, theirs = pl.pallas_call(
        functools.partial(last_sum_kernel, layers),
        in_specs=[vmem_spec()] * (CHIPS + layers),
        out_specs=[vmem_spec()] * 2,
        out_shape=[jax.ShapeDtypeStruct((rows, half), bf16)] * 2,
        compiler_params=kernel_params(),
        cost_estimate=LIGHT,
        name="last_sum",
    )(summed[0], *wide_sums, summed[layers], *narrow_sums)
    other = shift(theirs, 1)

    low, high = jnp.where(core == 0, mine, other), jnp.where(core == 0, other, mine)
    return loss[:, 0], grad_head, jnp.concatenate([low, high], axis=1)


def fits_levels(hidden_states, teacher_logits):
    n = lax.axis_size("vocab")
    rows = hidden_states.shape[0]
    blocks, _, stored, side = teacher_logits.shape
    return (
        n == blocks * GROUP
        and blocks & (blocks - 1) == 0
        and rows * GROUP == side
        and rows % 16 == 0
        and 2 * n <= side
        and 6 * blocks * stored <= side
        and hidden_states.shape[1] % (CORES * 1280) == 0
    )


def on_device(
    hidden_states, head_weight, teacher_logits, block_lists, row_reader, tail_mass, token_weight
):
    plan = levels_plan if fits_levels(hidden_states, teacher_logits) else plain_plan
    return plan(
        hidden_states, head_weight, teacher_logits, block_lists, row_reader, tail_mass, token_weight
    )


def solution(mesh):
    in_specs = (
        P("vocab", None),
        P(None, "vocab"),
        P(None, None, "vocab", None),
        P(),
        P(),
        P(),
        P(),
    )
    out_specs = (P("vocab"), P(None, "vocab"), P("vocab", None))
    return jax.shard_map(
        on_device, mesh=mesh, in_specs=in_specs, out_specs=out_specs, check_vma=False
    )
```
